32 devices in a mesh: span: 8 (over z, x), cross: 4 (over y, core).
Axes of the slice: x: 2, y: 2, z: 4, core: 2. Of those that a mesh axis runs over, the one named last changes fastest.
Arguments:
- populations: bfloat16 [19, 128, 128, 128], P(None, 'span', 'cross'), may hold values from 0.2 to 1.8
- cell_index: int32 [4096, 8], P(('span', 'cross')), may hold values from 0 to 65535
- marker_weight: float32 [4096, 8], P(('span', 'cross')), may hold values from 0 to 0.25
- segment_id: int32 [4096], P(('span', 'cross')), may hold values from 0 to 255, as said below
Outputs:
- populations_next: bfloat16 [19, 128, 128, 128], P(None, 'span', 'cross')
- eddy_coeff: float32 [128, 128], P('cross')
- segment_force: float32 [3, 256], P(None, ('span', 'cross'))
The draws below stay inside these ranges and needn't reach their ends.
Inputs may be any that keep to these rules, and one draw needn't show every extreme that they name: cell_index addresses a cell of the block of the device that holds the marker, flat in the order (span, crossflow, stream) of that 16 x 32 x 128 block. `segment_id`: segments are owned 8 to a device in device order (span slowest); a marker's segment may be owned by any device.
All inputs are finite; a program needn't handle non-finite values.
Results may differ from the reference program's by a relative error of at most 0.0019.
The reference program's roundings to bfloat16 on the way (of `post`) count: a program that leaves them out, or rounds other values in their place, can miss the bound.
Values may be sent and summed in bfloat16 or wider, within the bound.
No kernel may reach another device: no remote copies, remote signals or barrier semaphores. Data moves between devices by JAX's collectives and lax.ppermute only.
A program may use at most 128 MiB of HBM per device.

```python
import jax
import jax.numpy as jnp
from jax import lax

Q = 19
CX = 128
CY = 32
CZ = 16
MK_DEV = 128
SEG_DEV = 8
K = 8
NY = 128
NZ = 128
MARKERS = 4096
SEGMENTS = 256
N_SPAN = 8
N_CROSS = 4


def draw_populations(key, part):
    key = jax.random.fold_in(key, 23)
    span_frac = jnp.arange(NZ, dtype=jnp.float32) / max(NZ - 1, 1)
    first = jnp.sin(0.5 * jnp.pi * jax.random.uniform(jax.random.fold_in(key, 1), (Q, 1, NY, CX), jnp.float32, -1.0, 1.0))
    second = jnp.sin(0.5 * jnp.pi * jax.random.uniform(jax.random.fold_in(key, 2), (Q, 1, NY, CX), jnp.float32, -1.0, 1.0))
    tile_low = -1.0
    rough_low = 0.5
    mixing = (0.15 + 0.85 * span_frac) * jax.random.uniform(jax.random.fold_in(key, 3), (NZ,), jnp.float32, rough_low, 1.0)
    mixing = mixing[None, :, None, None]
    noise = jax.random.uniform(jax.random.fold_in(key, 4), (Q, NZ, NY, CX), jnp.float32, -1.0, 1.0)
    shaped = 0.8 * (mixing * first + (1.0 - mixing) * second) + 0.2 * noise
    tiles = jax.random.uniform(jax.random.fold_in(key, 5), (NY // 4 + 1, CX // 4 + 1), jnp.float32, tile_low, 0.0)
    tile_rows = jnp.arange(NY, dtype=jnp.int32) // 4
    tile_cols = jnp.arange(CX, dtype=jnp.int32) // 4
    tile_env = jnp.exp(tiles[tile_rows][:, tile_cols])
    span_env = jnp.exp(0.5 * (span_frac - 1.0))
    pops = 1.0 + 0.8 * span_env[None, :, None, None] * tile_env[None, None] * shaped
    return pops.astype(jnp.bfloat16)


def draw_segment_id(key, part):
    key = jax.random.fold_in(key, 11)
    owners = SEGMENTS // SEG_DEV
    marker = jnp.arange(MARKERS, dtype=jnp.int32)
    device = marker // MK_DEV
    local = marker % MK_DEV
    random_owner = jax.random.randint(jax.random.fold_in(key, 1), (MARKERS,), 0, owners)
    far_owner = (device + owners // 2) % owners
    prior_owner = (device + owners - 1) % owners
    owner = jnp.where(local == 0, far_owner, jnp.where(local == 1, prior_owner, random_owner))
    within = jax.random.randint(jax.random.fold_in(key, 2), (MARKERS,), 0, SEG_DEV)
    segment = owner * SEG_DEV + within
    segment = jnp.where(marker == 2, SEGMENTS - 1, segment)
    segment = jnp.where(marker == 3, 0, segment)
    return segment.astype(jnp.int32)


def with_ends(entries, rng, low, top_value):
    longest = entries.shape.index(max(entries.shape))
    spots = []
    for shift in (0, 1):
        where = [jax.random.randint(jax.random.fold_in(rng, axis), (), 0, length) for axis, length in enumerate(entries.shape)]
        where[longest] = (where[longest] + shift) % entries.shape[longest]
        spots.append(tuple(where))
    return entries.at[spots[0]].set(low).at[spots[1]].set(top_value)


def level_of(stream_key, dims, shards, low, high):
    level = 1.0
    for axis_at, shards_of in shards:
        draws = jax.random.uniform(jax.random.fold_in(jax.random.fold_in(stream_key, 6), axis_at), (shards_of,), jnp.float32, low / len(shards), high / len(shards))
        level = level * jnp.repeat(jnp.exp(draws), dims[axis_at] // shards_of).reshape((-1,) + (1,) * (len(dims) - 1 - axis_at))
    return level


def setup_inputs(seed: int = 0) -> dict:
    arg_keys = jax.random.split(jax.random.key(seed), 5)
    populations = draw_populations(jax.random.fold_in(arg_keys[4], 71), 0)
    cell_index = with_ends(jax.random.randint(arg_keys[1], (MARKERS, K), 0, CZ * CY * CX), jax.random.fold_in(arg_keys[1], 1), 0, (CZ * CY * CX) - 1).astype(jnp.int32)
    marker_weight = jnp.clip(0.25 * jax.random.uniform(arg_keys[2], (MARKERS, K), jnp.float32) ** level_of(arg_keys[2], (MARKERS, K), ((0, 32),), -0.2, 0.2), 0.0, 0.25)
    segment_id = draw_segment_id(jax.random.fold_in(arg_keys[4], 71), 0)
    return dict(populations=populations, cell_index=cell_index, marker_weight=marker_weight, segment_id=segment_id)


eps_sum = 1e-06
base_visc = 0.005

def lattice_tables():
    velocities = [[0, 0, 0], [1, 0, 0], [-1, 0, 0], [0, 1, 0], [0, -1, 0], [0, 0, 1], [0, 0, -1], [1, 1, 0], [-1, -1, 0], [1, -1, 0], [-1, 1, 0], [1, 0, 1], [-1, 0, -1], [1, 0, -1], [-1, 0, 1], [0, 1, 1], [0, -1, -1], [0, 1, -1], [0, -1, 1]]
    weights = [1.0 / 3.0] + [1.0 / 18.0] * 6 + [1.0 / 36.0] * 12
    return (velocities, weights)

def inner_product(first, second):
    return sum((first[index] * second[index] for index in range(19)))

def relax_tables():
    velocities, weights = lattice_tables()
    along_x = [float(entry[0]) for entry in velocities]
    along_y = [float(entry[1]) for entry in velocities]
    along_z = [float(entry[2]) for entry in velocities]
    polynomials = []
    for index in range(19):
        cx, cy, cz = (along_x[index], along_y[index], along_z[index])
        square = cx * cx + cy * cy + cz * cz
        normal_x = 3.0 * cx * cx - square
        normal_yz = cy * cy - cz * cz
        polynomials.append([1.0, square, square * square, cx, cx * square, cy, cy * square, cz, cz * square, normal_x, normal_x * square, normal_yz, normal_yz * square, cx * cy, cy * cz, cx * cz, cx * (cy * cy - cz * cz), cy * (cz * cz - cx * cx), cz * (cx * cx - cy * cy)])
    ortho_rows = []
    for moment in range(19):
        vector = [polynomials[index][moment] for index in range(19)]
        for prior in ortho_rows:
            factor = inner_product(vector, prior) / inner_product(prior, prior)
            vector = [vector[index] - factor * prior[index] for index in range(19)]
        ortho_rows.append(vector)
    norms = [inner_product(row_vec, row_vec) for row_vec in ortho_rows]
    fixed = [0.0, 1.19, 1.4, 0.0, 1.2, 0.0, 1.2, 0.0, 1.2, 0.0, 1.4, 0.0, 1.4, 0.0, 0.0, 0.0, 1.98, 1.98, 1.98]
    shear = [1.0 if moment in (9, 11, 13, 14, 15) else 0.0 for moment in range(19)]

    def build(rates):
        return [[sum((ortho_rows[moment][outer] / norms[moment] * rates[moment] * ortho_rows[moment][inner] for moment in range(19))) for inner in range(19)] for outer in range(19)]
    return (build(fixed), build(shear))

def moment_basis():
    velocities, weights = lattice_tables()
    return [[1.0] * 19] + [[float(entry[dim]) for entry in velocities] for dim in range(3)]

def moments(pops):
    basis = jnp.asarray(moment_basis(), jnp.bfloat16)
    sums = jnp.dot(basis, pops.reshape(19, -1), preferred_element_type=jnp.float32)
    density = sums[0]
    return (density, sums[1:] / density)

def collide(pops, density, velocity, rate):
    velocities, weights = lattice_tables()
    fixed_mat, shear_mat = relax_tables()
    flat = pops.reshape(19, -1).astype(jnp.float32)
    along = jnp.dot(jnp.asarray(velocities, jnp.float32), velocity, precision=lax.Precision.HIGHEST)
    speed = lax.optimization_barrier(jnp.sum(velocity * velocity, axis=0))
    equil = jnp.asarray(weights, jnp.float32)[:, None] * density * (1.0 + 3.0 * along + 4.5 * along * along - 1.5 * speed)
    offeq = flat - equil
    relaxed = jnp.dot(jnp.asarray(fixed_mat, jnp.float32), offeq, precision=lax.Precision.HIGHEST)
    sheared = jnp.dot(jnp.asarray(shear_mat, jnp.float32), offeq, precision=lax.Precision.HIGHEST)
    post = flat - relaxed - rate.reshape(-1) * sheared
    return post.astype(jnp.bfloat16).reshape(pops.shape)

def crop(array):
    return array[..., 1:-1, 1:-1, :]

def diff_z(array):
    return 0.5 * (array[..., 2:, 1:-1, :] - array[..., :-2, 1:-1, :])

def diff_y(array):
    return 0.5 * (array[..., 1:-1, 2:, :] - array[..., 1:-1, :-2, :])

def diff_x(array):
    return crop(0.5 * (jnp.roll(array, -1, -1) - jnp.roll(array, 1, -1)))

def smooth(array):
    first = 0.25 * (array[..., :-2, :, :] + 2.0 * array[..., 1:-1, :, :] + array[..., 2:, :, :])
    second = 0.25 * (first[..., :-2, :] + 2.0 * first[..., 1:-1, :] + first[..., 2:, :])
    return 0.25 * (jnp.roll(second, 1, -1) + 2.0 * second + jnp.roll(second, -1, -1))

def strain(field):
    grad_x, grad_y, grad_z = (diff_x(field), diff_y(field), diff_z(field))
    parts = jnp.stack([grad_x[0], grad_y[1], grad_z[2], 0.5 * (grad_y[0] + grad_x[1]), 0.5 * (grad_z[0] + grad_x[2]), 0.5 * (grad_z[1] + grad_y[2])])
    magnitude = jnp.sqrt(2.0 * (lax.optimization_barrier(jnp.sum(parts[:3] ** 2, axis=0)) + 2.0 * lax.optimization_barrier(jnp.sum(parts[3:] ** 2, axis=0))))
    return (parts, magnitude)

def pair_products(field):
    return jnp.stack([field[0] * field[0], field[1] * field[1], field[2] * field[2], field[0] * field[1], field[0] * field[2], field[1] * field[2]])

def germano(padded):
    strain_one, mag_one = strain(padded)
    hat_ss = smooth(mag_one * strain_one)
    vel_hat = smooth(padded)
    strain_hat, mag_hat = strain(vel_hat)
    hat_prods = smooth(pair_products(crop(padded)))
    leonard = hat_prods - pair_products(crop(vel_hat))
    model = 2.0 * (hat_ss - 4.0 * mag_hat * strain_hat)
    counts = jnp.asarray([1.0, 1.0, 1.0, 2.0, 2.0, 2.0], jnp.float32)[:, None, None, None]
    plane_lm = lax.optimization_barrier(jnp.sum(counts * leonard * model, axis=(0, 1)))
    plane_mm = lax.optimization_barrier(jnp.sum(counts * model * model, axis=(0, 1)))
    return (plane_lm, plane_mm, crop(mag_one))

def reference(populations, cell_index, marker_weight, segment_id):
    velocities, weights = lattice_tables()
    density, velocity = moments(populations)
    field = velocity.reshape(3, NZ, NY, CX)
    padded = jnp.concatenate([field[:, -2:], field, field[:, :2]], axis=1)
    padded = jnp.concatenate([padded[:, :, -2:], padded, padded[:, :, :2]], axis=2)

    def slab_terms(index):
        return germano(lax.dynamic_slice_in_dim(padded, index * CZ, CZ + 4, 1))
    plane_lm, plane_mm, magnitude = lax.map(slab_terms, jnp.arange(N_SPAN, dtype=jnp.int32))
    eddy_coeff = jnp.maximum(lax.optimization_barrier(jnp.sum(plane_lm, axis=0)) / (lax.optimization_barrier(jnp.sum(plane_mm, axis=0)) + eps_sum), 0.0)
    rate = 1.0 / (0.5 + 3.0 * (base_visc + eddy_coeff * magnitude.reshape(NZ, NY, CX)))
    density_grid = density.reshape(NZ, NY, CX)

    def slab_collide(index):
        start = index * CZ
        pops = lax.dynamic_slice_in_dim(populations, start, CZ, 1)
        slab_density = lax.dynamic_slice_in_dim(density_grid, start, CZ, 0)
        slab_velocity = lax.dynamic_slice_in_dim(field, start, CZ, 1)
        slab_rate = lax.dynamic_slice_in_dim(rate, start, CZ, 0)
        return collide(pops, slab_density.reshape(-1), slab_velocity.reshape(3, -1), slab_rate)
    post = lax.map(slab_collide, jnp.arange(N_SPAN, dtype=jnp.int32))
    post = jnp.moveaxis(post, 0, 1).reshape(Q, NZ, NY, CX)
    planes = []
    for index in range(19):
        shift_x, shift_y, shift_z = (velocities[index][0], velocities[index][1], velocities[index][2])
        planes.append(jnp.roll(post[index], (shift_z, shift_y, shift_x), axis=(0, 1, 2)))
    populations_next = jnp.stack(planes)
    momentum = jnp.dot(jnp.asarray(moment_basis()[1:], jnp.bfloat16), populations_next.reshape(19, -1), preferred_element_type=jnp.float32)
    marker = jnp.arange(MARKERS, dtype=jnp.int32)
    device = marker // MK_DEV
    span_pos = device // N_CROSS
    cross_pos = device % N_CROSS
    local_z = cell_index // (CY * CX)
    local_y = cell_index // CX % CY
    local_x = cell_index % CX
    global_cell = ((span_pos[:, None] * CZ + local_z) * NY + cross_pos[:, None] * CY + local_y) * CX + local_x
    picked = momentum[:, global_cell]
    force = -lax.optimization_barrier(jnp.sum(marker_weight * picked, axis=-1))
    segment_force = jax.ops.segment_sum(force.T, segment_id, num_segments=SEGMENTS).T
    return (populations_next, eddy_coeff, segment_force)
```

```python
import jax
import jax.numpy as jnp
from jax import lax
from jax.sharding import PartitionSpec as P

SEG_DEV = 8


eps_sum = 1e-06
base_visc = 0.005


def extended(block, sides, width):
    for axis, dim in sides:
        count = lax.axis_size(axis)
        forward = [(i, i + 1) for i in range(count - 1)]
        forward.append((count - 1, 0))
        backward = [(target, source) for source, target in forward]
        low = lax.ppermute(
            lax.slice_in_dim(block, block.shape[dim] - width, None, axis=dim), axis, forward
        )
        high = lax.ppermute(lax.slice_in_dim(block, 0, width, axis=dim), axis, backward)
        block = jnp.concatenate([low, block, high], axis=dim)
    return block


def lattice_tables():
    velocities = [
        [0, 0, 0],
        [1, 0, 0],
        [-1, 0, 0],
        [0, 1, 0],
        [0, -1, 0],
        [0, 0, 1],
        [0, 0, -1],
        [1, 1, 0],
        [-1, -1, 0],
        [1, -1, 0],
        [-1, 1, 0],
        [1, 0, 1],
        [-1, 0, -1],
        [1, 0, -1],
        [-1, 0, 1],
        [0, 1, 1],
        [0, -1, -1],
        [0, 1, -1],
        [0, -1, 1],
    ]
    weights = [1.0 / 3.0] + [1.0 / 18.0] * 6 + [1.0 / 36.0] * 12
    return (velocities, weights)


def inner_product(first, second):
    return sum((first[index] * second[index] for index in range(19)))


def relax_tables():
    velocities, weights = lattice_tables()
    along_x = [float(entry[0]) for entry in velocities]
    along_y = [float(entry[1]) for entry in velocities]
    along_z = [float(entry[2]) for entry in velocities]
    polynomials = []
    for index in range(19):
        cx, cy, cz = (along_x[index], along_y[index], along_z[index])
        square = cx * cx + cy * cy + cz * cz
        normal_x = 3.0 * cx * cx - square
        normal_yz = cy * cy - cz * cz
        polynomials.append(
            [
                1.0,
                square,
                square * square,
                cx,
                cx * square,
                cy,
                cy * square,
                cz,
                cz * square,
                normal_x,
                normal_x * square,
                normal_yz,
                normal_yz * square,
                cx * cy,
                cy * cz,
                cx * cz,
                cx * (cy * cy - cz * cz),
                cy * (cz * cz - cx * cx),
                cz * (cx * cx - cy * cy),
            ]
        )
    ortho_rows = []
    for moment in range(19):
        vector = [polynomials[index][moment] for index in range(19)]
        for prior in ortho_rows:
            factor = inner_product(vector, prior) / inner_product(prior, prior)
            vector = [vector[index] - factor * prior[index] for index in range(19)]
        ortho_rows.append(vector)
    norms = [inner_product(row_vec, row_vec) for row_vec in ortho_rows]
    fixed = [
        0.0,
        1.19,
        1.4,
        0.0,
        1.2,
        0.0,
        1.2,
        0.0,
        1.2,
        0.0,
        1.4,
        0.0,
        1.4,
        0.0,
        0.0,
        0.0,
        1.98,
        1.98,
        1.98,
    ]
    shear = [1.0 if moment in (9, 11, 13, 14, 15) else 0.0 for moment in range(19)]

    def build(rates):
        return [
            [
                sum(
                    (
                        ortho_rows[moment][outer]
                        / norms[moment]
                        * rates[moment]
                        * ortho_rows[moment][inner]
                        for moment in range(19)
                    )
                )
                for inner in range(19)
            ]
            for outer in range(19)
        ]

    return (build(fixed), build(shear))


def moment_basis():
    velocities, weights = lattice_tables()
    return [[1.0] * 19] + [[float(entry[dim]) for entry in velocities] for dim in range(3)]


def moments(pops):
    basis = jnp.asarray(moment_basis(), jnp.bfloat16)
    sums = jnp.dot(basis, pops.reshape(19, -1), preferred_element_type=jnp.float32)
    density = sums[0]
    return (density, sums[1:] / density)


def collide(pops, density, velocity, rate):
    velocities, weights = lattice_tables()
    fixed_mat, shear_mat = relax_tables()
    flat = pops.reshape(19, -1).astype(jnp.float32)
    along = jnp.dot(jnp.asarray(velocities, jnp.float32), velocity, precision=lax.Precision.HIGHEST)
    speed = jnp.sum(velocity * velocity, axis=0)
    equil = (
        jnp.asarray(weights, jnp.float32)[:, None]
        * density
        * (1.0 + 3.0 * along + 4.5 * along * along - 1.5 * speed)
    )
    offeq = flat - equil
    relaxed = jnp.dot(jnp.asarray(fixed_mat, jnp.float32), offeq, precision=lax.Precision.HIGHEST)
    sheared = jnp.dot(jnp.asarray(shear_mat, jnp.float32), offeq, precision=lax.Precision.HIGHEST)
    post = flat - relaxed - rate.reshape(-1) * sheared
    return post.astype(jnp.bfloat16).reshape(pops.shape)


def crop(array):
    return array[..., 1:-1, 1:-1, :]


def diff_z(array):
    return 0.5 * (array[..., 2:, 1:-1, :] - array[..., :-2, 1:-1, :])


def diff_y(array):
    return 0.5 * (array[..., 1:-1, 2:, :] - array[..., 1:-1, :-2, :])


def diff_x(array):
    return crop(0.5 * (jnp.roll(array, -1, -1) - jnp.roll(array, 1, -1)))


def smooth(array):
    first = 0.25 * (array[..., :-2, :, :] + 2.0 * array[..., 1:-1, :, :] + array[..., 2:, :, :])
    second = 0.25 * (first[..., :-2, :] + 2.0 * first[..., 1:-1, :] + first[..., 2:, :])
    return 0.25 * (jnp.roll(second, 1, -1) + 2.0 * second + jnp.roll(second, -1, -1))


def strain(field):
    grad_x, grad_y, grad_z = (diff_x(field), diff_y(field), diff_z(field))
    parts = jnp.stack(
        [
            grad_x[0],
            grad_y[1],
            grad_z[2],
            0.5 * (grad_y[0] + grad_x[1]),
            0.5 * (grad_z[0] + grad_x[2]),
            0.5 * (grad_z[1] + grad_y[2]),
        ]
    )
    magnitude = jnp.sqrt(
        2.0 * (jnp.sum(parts[:3] ** 2, axis=0) + 2.0 * jnp.sum(parts[3:] ** 2, axis=0))
    )
    return (parts, magnitude)


def pair_products(field):
    return jnp.stack(
        [
            field[0] * field[0],
            field[1] * field[1],
            field[2] * field[2],
            field[0] * field[1],
            field[0] * field[2],
            field[1] * field[2],
        ]
    )


def germano(padded):
    strain_one, mag_one = strain(padded)
    hat_ss = smooth(mag_one * strain_one)
    vel_hat = smooth(padded)
    strain_hat, mag_hat = strain(vel_hat)
    hat_prods = smooth(pair_products(crop(padded)))
    leonard = hat_prods - pair_products(crop(vel_hat))
    model = 2.0 * (hat_ss - 4.0 * mag_hat * strain_hat)
    counts = jnp.asarray([1.0, 1.0, 1.0, 2.0, 2.0, 2.0], jnp.float32)[:, None, None, None]
    plane_lm = jnp.sum(counts * leonard * model, axis=(0, 1))
    plane_mm = jnp.sum(counts * model * model, axis=(0, 1))
    return (plane_lm, plane_mm, crop(mag_one))


def stream(rimmed):
    velocities, weights = lattice_tables()
    depth, width = (rimmed.shape[1] - 2, rimmed.shape[2] - 2)
    planes = []
    for index in range(19):
        shift_x, shift_y, shift_z = (
            velocities[index][0],
            velocities[index][1],
            velocities[index][2],
        )
        piece = rimmed[
            index, 1 - shift_z : 1 - shift_z + depth, 1 - shift_y : 1 - shift_y + width, :
        ]
        planes.append(jnp.roll(piece, shift_x, axis=-1))
    return jnp.stack(planes)


def line_coefficient(plane_lm, plane_mm):
    count = lax.axis_size("span")
    rows, cols = plane_lm.shape
    if rows % count:
        total_lm, total_mm = lax.psum((plane_lm, plane_mm), "span")
        return jnp.maximum(total_lm / (total_mm + eps_sum), 0.0)
    parts = jnp.stack([plane_lm, plane_mm]).reshape(2, count, rows // count, cols)
    parts = lax.all_to_all(parts.transpose(1, 0, 2, 3), "span", 0, 0)
    sums = jnp.sum(parts, axis=0)
    piece = jnp.maximum(sums[0] / (sums[1] + eps_sum), 0.0)
    pieces = lax.all_to_all(jnp.broadcast_to(piece, (count,) + piece.shape), "span", 0, 0)
    return pieces.reshape(rows, cols)


def segment_sums(momentum, cell_index, marker_weight, segment_id):
    lanes = 128
    owners = lax.axis_size("span") * lax.axis_size("cross")
    segments_all = SEG_DEV * owners
    flat = cell_index.reshape(-1)
    row, lane = (flat // lanes, flat % lanes)
    rows = momentum.shape[1] // lanes
    pick_row = (row[:, None] == jnp.arange(rows)[None, :]).astype(jnp.float32)
    table = momentum.reshape(3, rows, lanes).transpose(1, 0, 2).reshape(rows, 3 * lanes)
    picked = jnp.dot(pick_row, table, precision=lax.Precision.HIGHEST).reshape(-1, 3, lanes)
    pick_lane = jnp.where(
        lane[:, None] == jnp.arange(lanes)[None, :], -marker_weight.reshape(-1)[:, None], 0.0
    )
    force = jnp.sum(picked * pick_lane[:, None, :], axis=-1)
    force = force.reshape(segment_id.shape[0], -1, 3).sum(axis=1)
    pick_segment = (segment_id[None, :] == jnp.arange(segments_all)[:, None]).astype(jnp.float32)
    partial = jnp.dot(pick_segment, force, precision=lax.Precision.HIGHEST)
    partial = partial.reshape(owners, 1, SEG_DEV * 3)
    partial = jnp.pad(partial, ((0, 0), (0, 0), (0, lanes - SEG_DEV * 3)))
    arrived = lax.all_to_all(partial, ("span", "cross"), 0, 0)
    mine = jnp.sum(arrived, axis=(0, 1))[: SEG_DEV * 3]
    return mine.reshape(SEG_DEV, 3).T


def local(populations, cell_index, marker_weight, segment_id):
    block_shape = populations.shape[1:]
    density, velocity = moments(populations)
    field = velocity.reshape((3,) + block_shape)
    padded = extended(field, (("span", 1), ("cross", 2)), 2)
    plane_lm, plane_mm, magnitude = germano(padded)
    eddy_coeff = line_coefficient(plane_lm, plane_mm)
    rate = 1.0 / (0.5 + 3.0 * (base_visc + eddy_coeff * magnitude))
    post = collide(populations, density, velocity, rate)
    rimmed = extended(post, (("span", 1), ("cross", 2)), 1)
    populations_next = stream(rimmed)
    momentum = jnp.dot(
        jnp.asarray(moment_basis()[1:], jnp.bfloat16),
        populations_next.reshape(19, -1),
        preferred_element_type=jnp.float32,
    )
    segment_force = segment_sums(momentum, cell_index, marker_weight, segment_id)
    return (populations_next, eddy_coeff, segment_force)


def solution(mesh):
    in_specs = (
        P(None, "span", "cross", None),
        P(("span", "cross"), None),
        P(("span", "cross"), None),
        P(("span", "cross")),
    )
    out_specs = (P(None, "span", "cross", None), P("cross", None), P(None, ("span", "cross")))
    return jax.shard_map(local, mesh=mesh, in_specs=in_specs, out_specs=out_specs, check_vma=False)
```

```python
import functools

import jax
import jax.numpy as jnp
from jax import lax
from jax.experimental import pallas as pl
from jax.experimental.pallas import tpu as pltpu
from jax.sharding import PartitionSpec as P

SEG_DEV = 8
LANES = 128
HALO = 4
EXT = 40
PAD = 56
OWN = 10
TOP = 8
CHUNKS = (8, 16, 24, 32, 40)
VMEM = 40 * 1024 * 1024

eps_sum = 1e-06
base_visc = 0.005

VELOCITIES = [
    [0, 0, 0],
    [1, 0, 0],
    [-1, 0, 0],
    [0, 1, 0],
    [0, -1, 0],
    [0, 0, 1],
    [0, 0, -1],
    [1, 1, 0],
    [-1, -1, 0],
    [1, -1, 0],
    [-1, 1, 0],
    [1, 0, 1],
    [-1, 0, -1],
    [1, 0, -1],
    [-1, 0, 1],
    [0, 1, 1],
    [0, -1, -1],
    [0, 1, -1],
    [0, -1, 1],
]


def neighbours(axis):
    count = lax.axis_size(axis)
    forward = [(i, (i + 1) % count) for i in range(count)]
    backward = [(target, source) for source, target in forward]
    return forward, backward


def exchange(first, last, axis):
    forward, backward = neighbours(axis)
    low = lax.ppermute(last, axis, forward)
    high = lax.ppermute(first, axis, backward)
    return low, high


def full(shape, dtype):
    return jax.ShapeDtypeStruct(shape, dtype)


def in_vmem(count):
    return [pl.BlockSpec(memory_space=pltpu.VMEM)] * count


def params():
    return pltpu.CompilerParams(vmem_limit_bytes=VMEM)


def plus(array):
    return pltpu.roll(array, LANES - 1, 1)


def minus(array):
    return pltpu.roll(array, 1, 1)


def moments_kernel(pops_hbm, vel_ref, first_ref, last_ref, pops, sems):
    depth = pops.shape[1]
    part = depth // 4
    copies = []
    for index in range(4):
        planes = pl.ds(index * part, part)
        copies.append(
            pltpu.make_async_copy(pops_hbm.at[:, planes], pops.at[:, planes], sems.at[index])
        )
        copies[-1].start()

    def plane(z, carry):
        for half in range(2):
            rows = pl.ds(16 * half, 16)
            f = [pops[q, z, rows, :].astype(jnp.float32) for q in range(19)]
            flux = [0.0, 0.0, 0.0]
            density = f[0]
            for q in range(1, 19, 2):
                even, odd = f[q] + f[q + 1], f[q] - f[q + 1]
                density = density + even
                for dim in range(3):
                    sign = VELOCITIES[q][dim]
                    if sign:
                        flux[dim] = flux[dim] + odd if sign > 0 else flux[dim] - odd
            inverse = 1.0 / density
            for dim in range(3):
                speed = flux[dim] * inverse
                vel_ref[dim, z, rows, :] = speed
                if half == 0:
                    first_ref[dim, z] = speed[:HALO]
                else:
                    last_ref[dim, z] = speed[16 - HALO :]
        return carry

    for index in range(4):
        copies[index].wait()
        lax.fori_loop(index * part, (index + 1) * part, plane, 0)


def block_moments(populations):
    _, depth, width, lanes = populations.shape
    edge = full((3, depth, HALO, lanes), jnp.float32)
    return pl.pallas_call(
        moments_kernel,
        out_shape=(full((3, depth, width, lanes), jnp.float32), edge, edge),
        in_specs=[pl.BlockSpec(memory_space=pl.ANY)],
        out_specs=tuple(in_vmem(3)),
        scratch_shapes=[
            pltpu.VMEM(populations.shape, populations.dtype),
            pltpu.SemaphoreType.DMA((4,)),
        ],
        compiler_params=params(),
        name="moments",
    )(populations)


def edges_kernel(vel_ref, low_ref, high_ref, *outs):
    depth, width = vel_ref.shape[1:3]
    for start, out in zip((0, 2, depth - 4, depth - 2), outs):
        for dim in range(3):
            for index in range(2):
                z = start + index
                out[dim, index, pl.ds(0, HALO), :] = low_ref[dim, z]
                out[dim, index, pl.ds(HALO, width), :] = vel_ref[dim, z]
                out[dim, index, pl.ds(HALO + width, HALO), :] = high_ref[dim, z]


def edge_planes(vel, low, high):
    pair = full((3, 2, EXT, LANES), jnp.float32)
    return pl.pallas_call(
        edges_kernel,
        out_shape=(pair,) * 4,
        in_specs=in_vmem(3),
        out_specs=tuple(in_vmem(4)),
        compiler_params=params(),
        name="edges",
    )(vel, low, high)


def strain_parts(ref, p, row):
    grads = []
    for dim in range(3):
        here = ref[dim, p, pl.ds(row, 8), :]
        grads.append(
            (
                plus(here) - minus(here),
                ref[dim, p, pl.ds(row + 1, 8), :] - ref[dim, p, pl.ds(row - 1, 8), :],
                ref[dim, p + 1, pl.ds(row, 8), :] - ref[dim, p - 1, pl.ds(row, 8), :],
            )
        )
    parts = [
        grads[0][0],
        grads[1][1],
        grads[2][2],
        grads[0][1] + grads[1][0],
        grads[0][2] + grads[2][0],
        grads[1][2] + grads[2][1],
    ]
    straight = parts[0] * parts[0] + parts[1] * parts[1] + parts[2] * parts[2]
    mixed = parts[3] * parts[3] + parts[4] * parts[4] + parts[5] * parts[5]
    return parts, jnp.sqrt(0.5 * straight + 0.25 * mixed)


def weigh(low, middle, high):
    return (low + high) + (middle + middle)


PAIRS = ((0, 0), (1, 1), (2, 2), (0, 1), (0, 2), (1, 2))


def model_sums(planes, ext, hat, prods, zsum, acc_ref, store_mag):
    def first_pass(p, carry):
        for row in CHUNKS:
            rows = pl.ds(row, 8)
            parts, size = strain_parts(ext, p, row)
            store_mag(p, row, size)
            for k in range(6):
                prods[k, p, rows, :] = size * parts[k]
            for k, (i, j) in enumerate(PAIRS):
                prods[6 + k, p, rows, :] = ext[i, p, rows, :] * ext[j, p, rows, :]
            for dim in range(3):
                lines = []
                for shift in (-1, 0, 1):
                    at = pl.ds(row + shift, 8)
                    lines.append(
                        weigh(ext[dim, p - 1, at, :], ext[dim, p, at, :], ext[dim, p + 1, at, :])
                    )
                line = weigh(*lines)
                hat[dim, p, rows, :] = (1.0 / 64.0) * weigh(minus(line), line, plus(line))
        return carry

    lax.fori_loop(1, planes - 1, first_pass, 0)

    def second_pass(p, carry):
        for row in CHUNKS:
            rows = pl.ds(row, 8)
            for k in range(12):
                zsum[k, rows, :] = weigh(
                    prods[k, p - 1, rows, :], prods[k, p, rows, :], prods[k, p + 1, rows, :]
                )
        for row in CHUNKS:
            rows = pl.ds(row, 8)
            parts, size = strain_parts(hat, p, row)
            size = 256.0 * size
            here = [hat[dim, p, rows, :] for dim in range(3)]
            scaled = [64.0 * speed for speed in here]
            smooth = []
            for k in range(12):
                line = weigh(
                    zsum[k, pl.ds(row - 1, 8), :], zsum[k, rows, :], zsum[k, pl.ds(row + 1, 8), :]
                )
                smooth.append(weigh(minus(line), line, plus(line)))
            lm = 0.0
            squares = [0.0, 0.0]
            for k, (i, j) in enumerate(PAIRS):
                model = smooth[k] - size * parts[k]
                leonard = smooth[6 + k] - scaled[i] * here[j]
                lm = lm + leonard * model
                squares[k // 3] = squares[k // 3] + model * model
            out = pl.ds(row - TOP, 8)
            acc_ref[0, out, :] += (1.0 / 4096.0) * lm
            acc_ref[1, out, :] += (1.0 / 4096.0) * (squares[0] + 0.5 * squares[1])
        return carry

    lax.fori_loop(2, planes - 2, second_pass, 0)


def inner_kernel(vel_ref, low_ref, high_ref, acc_ref, mag_ref, ext, hat, prods, zsum):
    depth, width = vel_ref.shape[1:3]

    def assemble(p, carry):
        for dim in range(3):
            ext[dim, p, pl.ds(OWN - HALO, HALO), :] = low_ref[dim, p]
            ext[dim, p, pl.ds(OWN, width), :] = vel_ref[dim, p]
            ext[dim, p, pl.ds(OWN + width, HALO), :] = high_ref[dim, p]
        return carry

    lax.fori_loop(0, depth, assemble, 0)
    acc_ref[...] = jnp.zeros_like(acc_ref)

    def store_mag(p, row, size):
        mag_ref[p - 1, pl.ds(row - TOP, 8), :] = size

    model_sums(depth, ext, hat, prods, zsum, acc_ref, store_mag)


def model_scratch(planes):
    return [
        pltpu.VMEM((3, planes, PAD, LANES), jnp.float32),
        pltpu.VMEM((3, planes, PAD, LANES), jnp.float32),
        pltpu.VMEM((12, planes, PAD, LANES), jnp.float32),
        pltpu.VMEM((12, PAD, LANES), jnp.float32),
    ]


def inner_sums(vel, low, high):
    depth = vel.shape[1]
    return pl.pallas_call(
        inner_kernel,
        out_shape=(
            full((2, EXT, LANES), jnp.float32),
            full((depth - 2, EXT, LANES), jnp.float32),
        ),
        in_specs=in_vmem(3),
        out_specs=tuple(in_vmem(2)),
        scratch_shapes=model_scratch(depth),
        compiler_params=params(),
        name="inner_sums",
    )(vel, low, high)


def outer_kernel(*refs):
    blocks, (partial_ref, acc_ref, mag_ref, ext, hat, prods, zsum) = refs[:6], refs[6:]
    acc_ref[...] = partial_ref[...]
    for side in range(2):
        for place in range(3):
            for dim in range(3):
                for index in range(2):
                    ext[dim, 2 * place + index, pl.ds(OWN - HALO, EXT), :] = blocks[
                        3 * side + place
                    ][dim, index]

        def store_mag(p, row, size):
            slot = p - 1 if side == 0 else p - 1

            @pl.when((slot < 2) if side == 0 else (slot >= 2))
            def _():
                mag_ref[slot, pl.ds(row - TOP, 8), :] = size

        model_sums(6, ext, hat, prods, zsum, acc_ref, store_mag)


def outer_sums(blocks, partial):
    return pl.pallas_call(
        outer_kernel,
        out_shape=(
            full((2, EXT, LANES), jnp.float32),
            full((4, EXT, LANES), jnp.float32),
        ),
        in_specs=in_vmem(7),
        out_specs=tuple(in_vmem(2)),
        scratch_shapes=model_scratch(6),
        compiler_params=params(),
        name="outer_sums",
    )(*blocks, partial)


def load_block(pops_hbm, low_hbm, high_hbm, pops, sems):
    depth = pops.shape[1] - 2
    part = depth // 4
    pieces = [(low_hbm, pl.ds(0, 1))]
    pieces += [
        (pops_hbm.at[:, pl.ds(index * part, part)], pl.ds(1 + index * part, part))
        for index in range(4)
    ]
    pieces.append((high_hbm, pl.ds(depth + 1, 1)))
    copies = [
        pltpu.make_async_copy(source, pops.at[:, place], sems.at[index])
        for index, (source, place) in enumerate(pieces)
    ]
    for copy in copies:
        copy.start()
    return copies


def rows_kernel(pops_hbm, low_hbm, high_hbm, first_ref, last_ref, pops, rows, sems):
    copies = load_block(pops_hbm, low_hbm, high_hbm, pops, sems)
    planes, width = pops.shape[1:3]
    rows[...] = jnp.zeros_like(rows)
    for copy in copies:
        copy.wait()

    def plane(p, carry):
        for q in range(19):
            low = pops[q, p, pl.ds(0, 16), :].astype(jnp.float32)
            high = pops[q, p, pl.ds(width - 16, 16), :].astype(jnp.float32)
            rows[0, q, pl.ds(p, 1), :] = low[:1]
            rows[1, q, pl.ds(p, 1), :] = high[15:]
        return carry

    lax.fori_loop(0, planes, plane, 0)
    first_ref[...] = rows[0].astype(jnp.bfloat16)
    last_ref[...] = rows[1].astype(jnp.bfloat16)


def face_rows(populations, low, high):
    _, depth, width, lanes = populations.shape
    tall = -(-(depth + 2) // 16) * 16
    edge = full((19, tall, lanes), jnp.bfloat16)
    return pl.pallas_call(
        rows_kernel,
        out_shape=(edge, edge),
        in_specs=[pl.BlockSpec(memory_space=pl.ANY)] * 3,
        out_specs=tuple(in_vmem(2)),
        scratch_shapes=[
            pltpu.VMEM((19, depth + 2, width, lanes), jnp.bfloat16),
            pltpu.VMEM((2, 19, tall, lanes), jnp.float32),
            pltpu.SemaphoreType.DMA((6,)),
        ],
        compiler_params=params(),
        name="face_rows",
    )(populations, low, high)


def relax(f, rate):
    even = {q: f[q] + f[q + 1] for q in range(1, 19, 2)}
    odd = {q: f[q] - f[q + 1] for q in range(1, 19, 2)}
    x_xy, x_xz = odd[7] + odd[9], odd[11] + odd[13]
    y_yz, y_xy = odd[15] + odd[17], odd[7] - odd[9]
    z_xz, z_yz = odd[11] - odd[13], odd[15] - odd[17]
    flux, up, down, axis_odd = [], [], [], []
    for first, second, along in ((x_xy, x_xz, 1), (y_yz, y_xy, 3), (z_xz, z_yz, 5)):
        sides = first + second
        total = odd[along] + sides
        heat = 0.15 * (sides - (2.0 / 3.0) * total)
        twist = (1.98 / 8.0) * (first - second)
        flux.append(total)
        up.append(heat + twist)
        down.append(heat - twist)
        axis_odd.append(4.0 * heat)
    a, b, c = even[7] + even[9], even[11] + even[13], even[15] + even[17]
    axes = even[1] + even[3] + even[5]
    diagonals = a + b + c
    density = f[0] + axes + diagonals
    inverse = 1.0 / density
    speed = [total * inverse for total in flux]
    square = [total * part for total, part in zip(flux, speed)]
    energy = square[0] + square[1] + square[2]
    d_e = (1.19 / 126.0) * (diagonals - f[0] - energy)
    d_eps = (1.4 / 252.0) * (9.0 * f[0] - 7.0 * axes - 2.0 * diagonals + 5.5 * energy)
    ax_n, dg_n, eq_n = 3.0 * even[1] - axes, diagonals - 3.0 * c, 3.0 * square[0] - energy
    ax_w, dg_w, eq_w = even[3] - even[5], a - b, square[1] - square[2]
    quarter = 0.25 * rate
    d_n = (rate * (1.0 / 36.0)) * (ax_n + dg_n - eq_n)
    d_pn = (1.4 / 72.0) * (dg_n - 2.0 * ax_n + 0.5 * eq_n)
    d_w = (rate * (1.0 / 12.0)) * (ax_w + dg_w - eq_w)
    d_pw = (1.4 / 24.0) * (dg_w - 2.0 * ax_w + 0.5 * eq_w)
    d_xy = quarter * (even[7] - even[9] - flux[0] * speed[1])
    d_xz = quarter * (even[11] - even[13] - flux[0] * speed[2])
    d_yz = quarter * (even[15] - even[17] - flux[1] * speed[2])
    base_axis = 11.0 * d_e + 4.0 * d_eps
    base_diag = -8.0 * d_e - d_eps
    k_n, k_w = d_n - 2.0 * d_pn, d_w - 2.0 * d_pw
    l_n, l_w = d_n + d_pn, d_w + d_pw
    post = [None] * 19
    post[0] = f[0] + (30.0 * d_e - 12.0 * d_eps)
    rest = base_axis + k_n
    for q, change, skew in (
        (1, base_axis - 2.0 * k_n, axis_odd[0]),
        (3, rest - k_w, axis_odd[1]),
        (5, rest + k_w, axis_odd[2]),
    ):
        post[q] = f[q] + (change + skew)
        post[q + 1] = f[q + 1] + (change - skew)
    rest = base_diag - l_n
    for q, change, shear, one, two in (
        (7, rest - l_w, d_xy, up[0], down[1]),
        (11, rest + l_w, d_xz, down[0], up[2]),
        (15, base_diag + 2.0 * l_n, d_yz, up[1], down[2]),
    ):
        minus_shear, plus_shear = change - shear, change + shear
        same, other = one + two, one - two
        post[q] = f[q] + (minus_shear - same)
        post[q + 1] = f[q + 1] + (minus_shear + same)
        post[q + 2] = f[q + 2] + (plus_shear - other)
        post[q + 3] = f[q + 3] + (plus_shear + other)
    return post


def relax_rate(eddy, size):
    return 1.0 / (0.5 + 3.0 * (base_visc + eddy * size))


BEFORE = [q for q in range(19) if VELOCITIES[q][1] > 0]
AFTER = [q for q in range(19) if VELOCITIES[q][1] < 0]
FIRST = 8


def step_kernel(
    pops_hbm,
    low_hbm,
    high_hbm,
    before_ref,
    after_ref,
    sums_ref,
    mag_in_ref,
    mag_out_ref,
    cell_ref,
    weight_ref,
    segment_ref,
    next_hbm,
    eddy_ref,
    partial_ref,
    pops,
    post,
    nexts,
    table,
    eddy,
    line,
    sems,
    out_sems,
):
    copies = load_block(pops_hbm, low_hbm, high_hbm, pops, sems)
    planes, width = pops.shape[1:3]
    depth = planes - 2
    part = depth // 4
    eddy[...] = jnp.maximum(sums_ref[0] / (sums_ref[1] + eps_sum), 0.0)
    eddy_ref[...] = eddy[pl.ds(OWN - TOP, width), :]

    tall = before_ref.shape[1]
    for side, (source, wanted, row, place) in enumerate(
        (
            (before_ref, BEFORE, OWN - TOP - 1, FIRST - 1),
            (after_ref, AFTER, OWN - TOP + width, FIRST + width),
        )
    ):
        line[...] = jnp.zeros_like(line)
        for p in range(planes):
            if p < 2:
                size = mag_out_ref[p, pl.ds(row, 1), :]
            elif p < planes - 2:
                size = mag_in_ref[p - 2, pl.ds(row, 1), :]
            else:
                size = mag_out_ref[p - planes + 4, pl.ds(row, 1), :]
            line[pl.ds(p, 1), :] = size
        here = eddy[pl.ds(row, 1), :]
        for start in range(0, planes, 16):
            rows = pl.ds(start, 16)
            f = [source[q, rows, :].astype(jnp.float32) for q in range(19)]
            out = relax(f, relax_rate(here, line[rows, :]))
            for q in wanted:
                for index in range(min(16, planes - start)):
                    post[q, start + index, pl.ds(place, 1), :] = out[q][index : index + 1]

    def collide(p, size_ref, at):
        for half in range(2):
            rows = pl.ds(16 * half, 16)
            lines = pl.ds(OWN - TOP + 16 * half, 16)
            rate = relax_rate(eddy[lines, :], size_ref[at, lines, :])
            f = [pops[q, p, rows, :].astype(jnp.float32) for q in range(19)]
            out = relax(f, rate)
            for q in range(19):
                post[q, p, pl.ds(FIRST + 16 * half, 16), :] = out[q]

    def inner(p, carry):
        collide(p, mag_in_ref, p - 2)
        return carry

    for copy in copies:
        copy.wait()
    collide(0, mag_out_ref, 0)
    collide(1, mag_out_ref, 1)
    lax.fori_loop(2, planes - 2, inner, 0)
    collide(planes - 2, mag_out_ref, 2)
    collide(planes - 1, mag_out_ref, 3)

    def run(z, carry):
        for half in range(2):
            flux = [0.0, 0.0, 0.0]
            for q in range(19):
                shift_x, shift_y, shift_z = VELOCITIES[q]
                piece = post[q, z + 1 - shift_z, pl.ds(FIRST + 16 * half - shift_y, 16), :]
                if shift_x:
                    piece = minus(piece) if shift_x > 0 else plus(piece)
                moved = piece.astype(jnp.bfloat16)
                nexts[q, z, pl.ds(16 * half, 16), :] = moved
                if q:
                    moved = moved.astype(jnp.float32)
                for dim in range(3):
                    sign = VELOCITIES[q][dim]
                    if sign:
                        flux[dim] = flux[dim] + moved if sign > 0 else flux[dim] - moved
            at = pl.ds(pl.multiple_of(z * width + 16 * half, 16), 16)
            for dim in range(3):
                coarse = flux[dim].astype(jnp.bfloat16)
                fine = (flux[dim] - coarse.astype(jnp.float32)).astype(jnp.bfloat16)
                table[0, at, dim * LANES : (dim + 1) * LANES] = coarse
                table[1, at, dim * LANES : (dim + 1) * LANES] = fine
        return carry

    outs = []
    for index in range(4):
        lax.fori_loop(index * part, (index + 1) * part, run, 0)
        place = pl.ds(index * part, part)
        outs.append(
            pltpu.make_async_copy(nexts.at[:, place], next_hbm.at[:, place], out_sems.at[index])
        )
        outs[-1].start()

    taps, markers = cell_ref.shape
    flat_rows = depth * width
    row_of = lax.broadcasted_iota(jnp.int32, (flat_rows, markers), 0)
    lane_of = lax.broadcasted_iota(jnp.int32, (LANES, markers), 0)
    force = [jnp.zeros((1, markers), jnp.float32) for _ in range(3)]
    contract = (((0,), (0,)), ((), ()))
    for tap in range(taps):
        cell = cell_ref[pl.ds(tap, 1), :]
        row, lane = lax.shift_right_logical(cell, 7), lax.bitwise_and(cell, LANES - 1)
        pick = jnp.where(row_of == row, 1.0, 0.0).astype(jnp.bfloat16)
        picked = lax.dot_general(
            table[0], pick, contract, preferred_element_type=jnp.float32
        ) + lax.dot_general(table[1], pick, contract, preferred_element_type=jnp.float32)
        weight = jnp.where(lane_of == lane, -weight_ref[pl.ds(tap, 1), :], 0.0)
        for dim in range(3):
            lanes = picked[dim * LANES : (dim + 1) * LANES, :]
            force[dim] = force[dim] + jnp.sum(lanes * weight, axis=0, keepdims=True)

    owners = partial_ref.shape[0]
    segments = owners * SEG_DEV
    force = jnp.concatenate(force + [jnp.zeros((5, markers), jnp.float32)], axis=0)
    segment_of = lax.broadcasted_iota(jnp.int32, (segments, markers), 0)
    hit = jnp.where(segment_of == segment_ref[...], 1.0, 0.0)
    totals = lax.dot_general(
        force,
        hit,
        (((1,), (1,)), ((), ())),
        precision=lax.Precision.HIGHEST,
        preferred_element_type=jnp.float32,
    )
    owner_of = lax.broadcasted_iota(jnp.int32, (owners, segments), 0)
    at_segment = lax.broadcasted_iota(jnp.int32, (owners, segments), 1)
    mine = lax.shift_right_logical(at_segment, 3) == owner_of
    spot = lax.broadcasted_iota(jnp.int32, (segments, LANES), 0)
    at_lane = lax.broadcasted_iota(jnp.int32, (segments, LANES), 1)
    packed = jnp.zeros((owners, LANES), jnp.float32)
    for dim in range(3):
        spread = jnp.where(mine, totals[dim : dim + 1, :], 0.0)
        to_lane = lax.bitwise_and(spot, SEG_DEV - 1) + dim * SEG_DEV == at_lane
        packed = packed + jnp.dot(
            spread,
            jnp.where(to_lane, 1.0, 0.0),
            precision=lax.Precision.HIGHEST,
            preferred_element_type=jnp.float32,
        )
    partial_ref[:, 0, :] = packed
    for copy in outs:
        copy.wait()


def step(populations, low, high, before, after, sums, mag_in, mag_out, cells, weights, segments, owners):
    _, depth, width, lanes = populations.shape
    planes = depth + 2
    tall = before.shape[1]
    hbm = pl.BlockSpec(memory_space=pl.ANY)
    return pl.pallas_call(
        step_kernel,
        out_shape=(
            full(populations.shape, jnp.bfloat16),
            full((width, lanes), jnp.float32),
            full((owners, 1, lanes), jnp.float32),
        ),
        in_specs=[hbm] * 3 + in_vmem(8),
        out_specs=(hbm,) + tuple(in_vmem(2)),
        scratch_shapes=[
            pltpu.VMEM((19, planes, width, lanes), jnp.bfloat16),
            pltpu.VMEM((19, planes, FIRST + width + 8, lanes), jnp.float32),
            pltpu.VMEM(populations.shape, jnp.bfloat16),
            pltpu.VMEM((2, depth * width, 3 * lanes), jnp.bfloat16),
            pltpu.VMEM((EXT, lanes), jnp.float32),
            pltpu.VMEM((tall, lanes), jnp.float32),
            pltpu.SemaphoreType.DMA((6,)),
            pltpu.SemaphoreType.DMA((4,)),
        ],
        compiler_params=params(),
        name="step",
    )(populations, low, high, before, after, sums, mag_in, mag_out, cells, weights, segments)


def finish_kernel(arrived_ref, out_ref):
    total = jnp.sum(arrived_ref[:, 0, :], axis=0, keepdims=True)
    for dim in range(3):
        out_ref[pl.ds(dim, 1), :] = total[:, dim * SEG_DEV : (dim + 1) * SEG_DEV]


def span_sum(values):
    count = lax.axis_size("span")
    if count & (count - 1):
        return lax.psum(values, "span")
    distance = 1
    while distance < count:
        pairs = [(i, i ^ distance) for i in range(count)]
        values = values + lax.ppermute(values, "span", pairs)
        distance *= 2
    return values


def local(populations, cell_index, marker_weight, segment_id):
    owners = lax.axis_size("span") * lax.axis_size("cross")
    face_low, face_high = exchange(populations[:, :1], populations[:, -1:], "span")
    vel, first, last = block_moments(populations)
    low, high = exchange(first, last, "cross")
    edges = edge_planes(vel, low, high)
    below, above = exchange(edges[0], edges[3], "span")
    rows_first, rows_last = face_rows(populations, face_low, face_high)
    before, after = exchange(rows_first, rows_last, "cross")
    partial, mag_in = inner_sums(vel, low, high)
    sums, mag_out = outer_sums((below,) + tuple(edges) + (above,), partial)
    sums = span_sum(sums)
    populations_next, eddy_coeff, packed = step(
        populations,
        face_low,
        face_high,
        before,
        after,
        sums,
        mag_in,
        mag_out,
        cell_index.T,
        marker_weight.T,
        segment_id[None, :],
        owners,
    )
    arrived = lax.all_to_all(packed, ("span", "cross"), 0, 0)
    segment_force = pl.pallas_call(
        finish_kernel,
        out_shape=full((3, SEG_DEV), jnp.float32),
        in_specs=in_vmem(1),
        out_specs=in_vmem(1)[0],
        name="finish",
    )(arrived)
    return (populations_next, eddy_coeff, segment_force)


def solution(mesh):
    in_specs = (
        P(None, "span", "cross", None),
        P(("span", "cross"), None),
        P(("span", "cross"), None),
        P(("span", "cross")),
    )
    out_specs = (P(None, "span", "cross", None), P("cross", None), P(None, ("span", "cross")))
    return jax.shard_map(local, mesh=mesh, in_specs=in_specs, out_specs=out_specs, check_vma=False)
```

```python
import functools

import jax
import jax.numpy as jnp
from jax import lax
from jax.experimental import pallas as pl
from jax.experimental.pallas import tpu as pltpu
from jax.sharding import PartitionSpec as P

SEG_DEV = 8
LANES = 128
HALO = 3
EXT = 40
PAD = 56
OWN = 10
TOP = 8
CHUNKS = (8, 16, 24, 32, 40)
VMEM = 28 * 1024 * 1024

eps_sum = 1e-06
base_visc = 0.005

VELOCITIES = [
    [0, 0, 0],
    [1, 0, 0],
    [-1, 0, 0],
    [0, 1, 0],
    [0, -1, 0],
    [0, 0, 1],
    [0, 0, -1],
    [1, 1, 0],
    [-1, -1, 0],
    [1, -1, 0],
    [-1, 1, 0],
    [1, 0, 1],
    [-1, 0, -1],
    [1, 0, -1],
    [-1, 0, 1],
    [0, 1, 1],
    [0, -1, -1],
    [0, 1, -1],
    [0, -1, 1],
]


def neighbours(axis):
    count = lax.axis_size(axis)
    forward = [(i, (i + 1) % count) for i in range(count)]
    backward = [(target, source) for source, target in forward]
    return forward, backward


def exchange(first, last, axis):
    forward, backward = neighbours(axis)
    low = lax.ppermute(last, axis, forward)
    high = lax.ppermute(first, axis, backward)
    return low, high


def full(shape, dtype):
    return jax.ShapeDtypeStruct(shape, dtype)


def in_vmem(count):
    return [pl.BlockSpec(memory_space=pltpu.VMEM)] * count


def params():
    return pltpu.CompilerParams(vmem_limit_bytes=VMEM)


def cost(micros):
    return pl.CostEstimate(flops=0, bytes_accessed=int(micros * 3.6e6), transcendentals=0)


def plus(array):
    return pltpu.roll(array, LANES - 1, 1)


def minus(array):
    return pltpu.roll(array, 1, 1)


def split(value):
    high = value.astype(jnp.bfloat16)
    return high, (value - high.astype(jnp.float32)).astype(jnp.bfloat16)


def join(high, low):
    return high.astype(jnp.float32) + low.astype(jnp.float32)


def moments_kernel(pops, vel_ref, y_first, y_last, z_first, z_last, rows):
    depth, width = pops.shape[1:3]

    def plane(z, carry):
        for half in range(width // 16):
            at = pl.ds(16 * half, 16)
            f = [pops[q, z, at, :].astype(jnp.float32) for q in range(19)]
            flux = [0.0, 0.0, 0.0]
            density = f[0]
            for q in range(1, 19, 2):
                even, odd = f[q] + f[q + 1], f[q] - f[q + 1]
                density = density + even
                for dim in range(3):
                    sign = VELOCITIES[q][dim]
                    if sign:
                        flux[dim] = flux[dim] + odd if sign > 0 else flux[dim] - odd
            inverse = 1.0 / density
            for dim in range(3):
                speed = flux[dim] * inverse
                vel_ref[dim, z, at, :] = speed
                for k in range(HALO):
                    if half == 0:
                        rows[0, dim * HALO + k, pl.ds(z, 1), :] = speed[k : k + 1]
                    if half == width // 16 - 1:
                        rows[1, dim * HALO + k, pl.ds(z, 1), :] = speed[15 - k : 16 - k]
        return carry

    lax.fori_loop(0, depth, plane, 0)
    for side, out in enumerate((y_first, y_last)):
        for dim in range(3):
            line = [rows[side, dim * HALO + k] for k in range(HALO)]
            out[4 * dim], out[4 * dim + 1] = split(line[0])
            for k in range(1, HALO):
                out[4 * dim + 1 + k] = (line[k] - line[k - 1]).astype(jnp.bfloat16)
    for near, far, out in ((0, 1, z_first), (depth - 1, depth - 2, z_last)):
        for dim in range(3):
            layer = vel_ref[dim, near]
            out[3 * dim], out[3 * dim + 1] = split(layer)
            out[3 * dim + 2] = (vel_ref[dim, far] - layer).astype(jnp.bfloat16)


def block_moments(populations):
    _, depth, width, lanes = populations.shape
    y_edge = full((12, depth, lanes), jnp.bfloat16)
    z_edge = full((9, width, lanes), jnp.bfloat16)
    return pl.pallas_call(
        moments_kernel,
        out_shape=(full((3, depth, width, lanes), jnp.float32), y_edge, y_edge, z_edge, z_edge),
        in_specs=in_vmem(1),
        out_specs=tuple(in_vmem(5)),
        scratch_shapes=[pltpu.VMEM((2, 3 * HALO, depth, lanes), jnp.float32)],
        compiler_params=params(),
        cost_estimate=cost(1),
        name="moments",
    )(populations)


def decode_rows(message, rows, side):
    for dim in range(3):
        line = join(message[4 * dim], message[4 * dim + 1])
        rows[side, dim * HALO] = line
        for k in range(1, HALO):
            line = line + message[4 * dim + 1 + k].astype(jnp.float32)
            rows[side, dim * HALO + k] = line


def place_plane(ext, p, vel_ref, rows, z):
    width = vel_ref.shape[2]
    for dim in range(3):
        ext[dim, p, pl.ds(OWN, width), :] = vel_ref[dim, z]
        for k in range(HALO):
            line = pl.ds(z, 1)
            ext[dim, p, pl.ds(OWN - 1 - k, 1), :] = rows[0, dim * HALO + k, line, :]
            ext[dim, p, pl.ds(OWN + width + k, 1), :] = rows[1, dim * HALO + k, line, :]


NOTE = 48
NOTE_ROWS = 72


def edges_kernel(low_ref, high_ref, cell_ref, weight_ref, segment_ref, first, last, rows):
    depth = low_ref.shape[1]
    decode_rows(low_ref, rows, 0)
    decode_rows(high_ref, rows, 1)
    taps = cell_ref.shape[0]
    for planes, out in (((0, 1), first), ((depth - 1, depth - 2), last)):
        out[...] = jnp.zeros_like(out)
        for dim in range(3):
            for index, z in enumerate(planes):
                for side in range(2):
                    for k in range(HALO):
                        row = 16 * dim + 8 * index + HALO * side + k
                        out[pl.ds(row, 1), :] = rows[side, dim * HALO + k, pl.ds(z, 1), :]
        out[pl.ds(NOTE, taps), :] = cell_ref[...].astype(jnp.float32)
        out[pl.ds(NOTE + taps, taps), :] = weight_ref[...]
        out[pl.ds(NOTE + 2 * taps, 1), :] = segment_ref[...].astype(jnp.float32)


def edge_notes(low, high, cells, weights, segments):
    note = full((NOTE_ROWS, LANES), jnp.float32)
    return pl.pallas_call(
        edges_kernel,
        out_shape=(note, note),
        in_specs=in_vmem(5),
        out_specs=tuple(in_vmem(2)),
        scratch_shapes=[pltpu.VMEM((2, 3 * HALO, low.shape[1], LANES), jnp.float32)],
        compiler_params=params(),
        cost_estimate=cost(0.2),
        name="edges",
    )(low, high, cells, weights, segments)


def strain_parts(ref, p, row):
    grads = []
    for dim in range(3):
        here = ref[dim, p, pl.ds(row, 8), :]
        grads.append(
            (
                plus(here) - minus(here),
                ref[dim, p, pl.ds(row + 1, 8), :] - ref[dim, p, pl.ds(row - 1, 8), :],
                ref[dim, p + 1, pl.ds(row, 8), :] - ref[dim, p - 1, pl.ds(row, 8), :],
            )
        )
    parts = [
        grads[0][0],
        grads[1][1],
        grads[2][2],
        grads[0][1] + grads[1][0],
        grads[0][2] + grads[2][0],
        grads[1][2] + grads[2][1],
    ]
    straight = parts[0] * parts[0] + parts[1] * parts[1] + parts[2] * parts[2]
    mixed = parts[3] * parts[3] + parts[4] * parts[4] + parts[5] * parts[5]
    return parts, jnp.sqrt(0.5 * straight + 0.25 * mixed)


def weigh(low, middle, high):
    return (low + high) + (middle + middle)


PAIRS = ((0, 0), (1, 1), (2, 2), (0, 1), (0, 2), (1, 2))


def model_sums(planes, ext, hat, prods, zsum, acc_ref, store_mag):
    def first_pass(p, carry):
        for row in CHUNKS:
            rows = pl.ds(row, 8)
            parts, size = strain_parts(ext, p, row)
            store_mag(p, row, size)
            for k in range(6):
                prods[k, p, rows, :] = size * parts[k]
            for k, (i, j) in enumerate(PAIRS):
                prods[6 + k, p, rows, :] = ext[i, p, rows, :] * ext[j, p, rows, :]
            for dim in range(3):
                lines = []
                for shift in (-1, 0, 1):
                    at = pl.ds(row + shift, 8)
                    lines.append(
                        weigh(ext[dim, p - 1, at, :], ext[dim, p, at, :], ext[dim, p + 1, at, :])
                    )
                line = weigh(*lines)
                hat[dim, p, rows, :] = (1.0 / 64.0) * weigh(minus(line), line, plus(line))
        return carry

    lax.fori_loop(1, planes - 1, first_pass, 0)

    def second_pass(p, carry):
        for row in CHUNKS:
            rows = pl.ds(row, 8)
            for k in range(12):
                zsum[k, rows, :] = weigh(
                    prods[k, p - 1, rows, :], prods[k, p, rows, :], prods[k, p + 1, rows, :]
                )
        for row in CHUNKS:
            rows = pl.ds(row, 8)
            parts, size = strain_parts(hat, p, row)
            size = 256.0 * size
            here = [hat[dim, p, rows, :] for dim in range(3)]
            scaled = [64.0 * speed for speed in here]
            smooth = []
            for k in range(12):
                line = weigh(
                    zsum[k, pl.ds(row - 1, 8), :], zsum[k, rows, :], zsum[k, pl.ds(row + 1, 8), :]
                )
                smooth.append(weigh(minus(line), line, plus(line)))
            lm = 0.0
            squares = [0.0, 0.0]
            for k, (i, j) in enumerate(PAIRS):
                model = smooth[k] - size * parts[k]
                leonard = smooth[6 + k] - scaled[i] * here[j]
                lm = lm + leonard * model
                squares[k // 3] = squares[k // 3] + model * model
            out = pl.ds(row - TOP, 8)
            acc_ref[0, out, :] += (1.0 / 4096.0) * lm
            acc_ref[1, out, :] += (1.0 / 4096.0) * (squares[0] + 0.5 * squares[1])
        return carry

    lax.fori_loop(2, planes - 2, second_pass, 0)


def inner_kernel(vel_ref, low_ref, high_ref, acc_ref, mag_ref, ext, hat, prods, zsum, rows):
    depth = vel_ref.shape[1]
    decode_rows(low_ref, rows, 0)
    decode_rows(high_ref, rows, 1)

    def assemble(p, carry):
        place_plane(ext, p, vel_ref, rows, p)
        return carry

    lax.fori_loop(0, depth, assemble, 0)
    acc_ref[...] = jnp.zeros_like(acc_ref)

    def store_mag(p, row, size):
        mag_ref[p - 1, pl.ds(row - TOP, 8), :] = size

    model_sums(depth, ext, hat, prods, zsum, acc_ref, store_mag)


def model_scratch(planes, depth):
    return [
        pltpu.VMEM((3, planes, PAD, LANES), jnp.float32),
        pltpu.VMEM((3, planes, PAD, LANES), jnp.float32),
        pltpu.VMEM((12, planes, PAD, LANES), jnp.float32),
        pltpu.VMEM((12, PAD, LANES), jnp.float32),
        pltpu.VMEM((2, 3 * HALO, depth, LANES), jnp.float32),
    ]


def inner_sums(vel, low, high):
    depth = vel.shape[1]
    return pl.pallas_call(
        inner_kernel,
        out_shape=(
            full((2, EXT, LANES), jnp.float32),
            full((depth - 2, EXT, LANES), jnp.float32),
        ),
        in_specs=in_vmem(3),
        out_specs=tuple(in_vmem(2)),
        scratch_shapes=model_scratch(depth, depth),
        compiler_params=params(),
        cost_estimate=cost(5),
        name="inner_sums",
    )(vel, low, high)


def outer_kernel(
    vel_ref,
    low_ref,
    high_ref,
    below_ref,
    above_ref,
    note_below,
    note_above,
    partial_ref,
    sums_ref,
    mag_ref,
    ext,
    hat,
    prods,
    zsum,
    rows,
    acc,
):
    depth, width = vel_ref.shape[1:3]
    decode_rows(low_ref, rows, 0)
    decode_rows(high_ref, rows, 1)
    acc[...] = partial_ref[...]
    for side, (message, note, places, start) in enumerate(
        ((below_ref, note_below, (1, 0), 0), (above_ref, note_above, (4, 5), depth - 4))
    ):
        for index in range(4):
            place_plane(ext, index + (2 if side == 0 else 0), vel_ref, rows, start + index)
        for dim in range(3):
            near = join(message[3 * dim], message[3 * dim + 1])
            far = near + message[3 * dim + 2].astype(jnp.float32)
            for index, (p, layer) in enumerate(zip(places, (near, far))):
                ext[dim, p, pl.ds(OWN, width), :] = layer
                row = 16 * dim + 8 * index
                for k in range(HALO):
                    ext[dim, p, pl.ds(OWN - 1 - k, 1), :] = note[pl.ds(row + k, 1), :]
                    ext[dim, p, pl.ds(OWN + width + k, 1), :] = note[pl.ds(row + HALO + k, 1), :]

        def store_mag(p, row, size):
            mag_ref[4 * side + p - 1, pl.ds(row - TOP, 8), :] = size

        model_sums(6, ext, hat, prods, zsum, acc, store_mag)
    lines = width + 2
    sums_ref[...] = jnp.zeros_like(sums_ref)
    for index in range(2):
        sums_ref[pl.ds(index * lines, lines), :] = acc[index, pl.ds(OWN - TOP - 1, lines), :]


def outer_sums(vel, low, high, below, above, note_below, note_above, partial):
    depth, width = vel.shape[1:3]
    return pl.pallas_call(
        outer_kernel,
        out_shape=(
            full((-(-2 * (width + 2) // 8) * 8, LANES), jnp.float32),
            full((8, EXT, LANES), jnp.float32),
        ),
        in_specs=in_vmem(8),
        out_specs=tuple(in_vmem(2)),
        scratch_shapes=model_scratch(6, depth) + [pltpu.VMEM((2, EXT, LANES), jnp.float32)],
        compiler_params=params(),
        cost_estimate=cost(2),
        name="outer_sums",
    )(vel, low, high, below, above, note_below, note_above, partial)


def rows_kernel(pops, after_this, first_ref, last_ref, rows):
    depth, width = pops.shape[1:3]

    def plane(z, carry):
        for q in range(19):
            low = pops[q, z, pl.ds(0, 16), :].astype(jnp.float32)
            high = pops[q, z, pl.ds(width - 16, 16), :].astype(jnp.float32)
            rows[0, q, pl.ds(z, 1), :] = low[:1]
            rows[1, q, pl.ds(z, 1), :] = high[15:]
        return carry

    lax.fori_loop(0, depth, plane, 0)
    first_ref[...] = rows[0].astype(jnp.bfloat16)
    last_ref[...] = rows[1].astype(jnp.bfloat16)


def face_rows(populations, after_this):
    _, depth, width, lanes = populations.shape
    edge = full((19, depth, lanes), jnp.bfloat16)
    return pl.pallas_call(
        rows_kernel,
        out_shape=(edge, edge),
        in_specs=in_vmem(1) + [pl.BlockSpec(memory_space=pl.ANY)],
        out_specs=tuple(in_vmem(2)),
        scratch_shapes=[pltpu.VMEM((2, 19, depth, lanes), jnp.float32)],
        compiler_params=params(),
        cost_estimate=cost(0.5),
        name="face_rows",
    )(populations, after_this)


def relax_parts(f):
    even = {q: f[q] + f[q + 1] for q in range(1, 19, 2)}
    odd = {q: f[q] - f[q + 1] for q in range(1, 19, 2)}
    x_xy, x_xz = odd[7] + odd[9], odd[11] + odd[13]
    y_yz, y_xy = odd[15] + odd[17], odd[7] - odd[9]
    z_xz, z_yz = odd[11] - odd[13], odd[15] - odd[17]
    flux, up, down, axis_odd = [], [], [], []
    for first, second, along in ((x_xy, x_xz, 1), (y_yz, y_xy, 3), (z_xz, z_yz, 5)):
        sides = first + second
        total = odd[along] + sides
        heat = 0.15 * (sides - (2.0 / 3.0) * total)
        twist = (1.98 / 8.0) * (first - second)
        flux.append(total)
        up.append(heat + twist)
        down.append(heat - twist)
        axis_odd.append(4.0 * heat)
    a, b, c = even[7] + even[9], even[11] + even[13], even[15] + even[17]
    axes = even[1] + even[3] + even[5]
    diagonals = a + b + c
    density = f[0] + axes + diagonals
    inverse = 1.0 / density
    speed = [total * inverse for total in flux]
    square = [total * part for total, part in zip(flux, speed)]
    energy = square[0] + square[1] + square[2]
    d_e = (1.19 / 126.0) * (diagonals - f[0] - energy)
    d_eps = (1.4 / 252.0) * (9.0 * f[0] - 7.0 * axes - 2.0 * diagonals + 5.5 * energy)
    ax_n, dg_n, eq_n = 3.0 * even[1] - axes, diagonals - 3.0 * c, 3.0 * square[0] - energy
    ax_w, dg_w, eq_w = even[3] - even[5], a - b, square[1] - square[2]
    d_pn = (1.4 / 72.0) * (dg_n - 2.0 * ax_n + 0.5 * eq_n)
    d_pw = (1.4 / 24.0) * (dg_w - 2.0 * ax_w + 0.5 * eq_w)
    shear = [
        (1.0 / 36.0) * (ax_n + dg_n - eq_n),
        (1.0 / 12.0) * (ax_w + dg_w - eq_w),
        0.25 * (even[7] - even[9] - flux[0] * speed[1]),
        0.25 * (even[11] - even[13] - flux[0] * speed[2]),
        0.25 * (even[15] - even[17] - flux[1] * speed[2]),
    ]
    base_axis = 11.0 * d_e + 4.0 * d_eps
    base_diag = -8.0 * d_e - d_eps
    base = [None] * 19
    base[0] = f[0] + (30.0 * d_e - 12.0 * d_eps)
    rest = base_axis - 2.0 * d_pn
    for q, change, skew in (
        (1, base_axis + 4.0 * d_pn, axis_odd[0]),
        (3, rest + 2.0 * d_pw, axis_odd[1]),
        (5, rest - 2.0 * d_pw, axis_odd[2]),
    ):
        base[q] = f[q] + (change + skew)
        base[q + 1] = f[q + 1] + (change - skew)
    rest = base_diag - d_pn
    for q, change, one, two in (
        (7, rest - d_pw, up[0], down[1]),
        (11, rest + d_pw, down[0], up[2]),
        (15, base_diag + 2.0 * d_pn, up[1], down[2]),
    ):
        same, other = one + two, one - two
        base[q] = f[q] + (change - same)
        base[q + 1] = f[q + 1] + (change + same)
        base[q + 2] = f[q + 2] + (change - other)
        base[q + 3] = f[q + 3] + (change + other)
    return base, shear


def shear_changes(shear, rate):
    n, w, xy, xz, yz = [rate * part for part in shear]
    lean = n + w
    tilt = n - w
    twice = n + n
    changes = [None] * 19
    changes[1] = changes[2] = -twice
    changes[3] = changes[4] = tilt
    changes[5] = changes[6] = lean
    changes[7] = changes[8] = -(lean + xy)
    changes[9] = changes[10] = xy - lean
    changes[11] = changes[12] = -(tilt + xz)
    changes[13] = changes[14] = xz - tilt
    changes[15] = changes[16] = twice - yz
    changes[17] = changes[18] = twice + yz
    return changes


def relax_rate(eddy, size):
    return 1.0 / (0.5 + 3.0 * (base_visc + eddy * size))


BEFORE = [q for q in range(19) if VELOCITIES[q][1] > 0]
AFTER = [q for q in range(19) if VELOCITIES[q][1] < 0]
RISING = [q for q in range(19) if VELOCITIES[q][2] > 0]
FALLING = [q for q in range(19) if VELOCITIES[q][2] < 0]
FIRST = 8


def ready_kernel(pops, before_ref, after_ref, after_this, base_ref, shear_ref, edge_ref, edge_shear):
    depth, width = pops.shape[1:3]
    for side, (source, wanted) in enumerate(((before_ref, BEFORE), (after_ref, AFTER))):
        base, shear = relax_parts([source[q].astype(jnp.float32) for q in range(19)])
        for index, q in enumerate(wanted):
            edge_ref[side, index] = base[q]
        for k in range(5):
            edge_shear[side, k] = shear[k]

    def plane(z, carry):
        for half in range(width // 16):
            rows = pl.ds(16 * half, 16)
            base, shear = relax_parts([pops[q, z, rows, :].astype(jnp.float32) for q in range(19)])
            for q in range(19):
                base_ref[q, z, rows, :] = base[q]
            for k in range(5):
                shear_ref[k, z, rows, :] = shear[k]
        return carry

    lax.fori_loop(0, depth, plane, 0)


def ready(populations, before, after, after_this):
    _, depth, width, lanes = populations.shape
    return pl.pallas_call(
        ready_kernel,
        out_shape=(
            full((19, depth, width, lanes), jnp.float32),
            full((5, depth, width, lanes), jnp.float32),
            full((2, 5, depth, lanes), jnp.float32),
            full((2, 5, depth, lanes), jnp.float32),
        ),
        in_specs=in_vmem(3) + [pl.BlockSpec(memory_space=pl.ANY)],
        out_specs=tuple(in_vmem(4)),
        compiler_params=params(),
        cost_estimate=cost(2.5),
        name="ready",
    )(populations, before, after, after_this)


def table_rows(table, at, flux):
    for dim in range(3):
        coarse, fine = split(flux[dim])
        table[0, at, dim * LANES : (dim + 1) * LANES] = coarse
        table[1, at, dim * LANES : (dim + 1) * LANES] = fine


def add_flux(flux, q, moved):
    for dim in range(3):
        sign = VELOCITIES[q][dim]
        if sign:
            flux[dim] = flux[dim] + moved if sign > 0 else flux[dim] - moved


def marker_force(table, start, rows, cells, weights):
    taps, markers = cells.shape
    row_of = lax.broadcasted_iota(jnp.int32, (rows, markers), 0) + start
    lane_of = lax.broadcasted_iota(jnp.int32, (LANES, markers), 0)
    contract = (((0,), (0,)), ((), ()))
    force = [jnp.zeros((1, markers), jnp.float32) for _ in range(3)]
    for tap in range(taps):
        cell = cells[tap : tap + 1, :]
        row, lane = lax.shift_right_logical(cell, 7), lax.bitwise_and(cell, LANES - 1)
        pick = jnp.where(row_of == row, 1.0, 0.0).astype(jnp.bfloat16)
        picked = lax.dot_general(
            table[0], pick, contract, preferred_element_type=jnp.float32
        ) + lax.dot_general(table[1], pick, contract, preferred_element_type=jnp.float32)
        weight = jnp.where(lane_of == lane, -weights[tap : tap + 1, :], 0.0)
        for dim in range(3):
            lanes = picked[dim * LANES : (dim + 1) * LANES, :]
            force[dim] = force[dim] + jnp.sum(lanes * weight, axis=0, keepdims=True)
    return jnp.concatenate(force + [jnp.zeros((5, markers), jnp.float32)], axis=0)


def step_kernel(
    base_ref,
    shear_ref,
    edge_ref,
    edge_shear,
    sums_ref,
    mag_in_ref,
    mag_out_ref,
    cell_ref,
    weight_ref,
    segment_ref,
    note_below,
    note_above,
    next_hbm,
    eddy_ref,
    partial_ref,
    rising_ref,
    falling_ref,
    post,
    nexts,
    table,
    face_table,
    eddy,
    line,
    out_sems,
):
    depth, width = shear_ref.shape[1:3]
    lines = width + 2
    part = depth // 4
    eddy[...] = jnp.zeros_like(eddy)
    eddy[pl.ds(OWN - TOP - 1, lines), :] = jnp.maximum(
        sums_ref[pl.ds(0, lines), :] / (sums_ref[pl.ds(lines, lines), :] + eps_sum), 0.0
    )
    eddy_ref[...] = eddy[pl.ds(OWN - TOP, width), :]

    for side, (wanted, row, place) in enumerate(
        ((BEFORE, OWN - TOP - 1, FIRST - 1), (AFTER, OWN - TOP + width, FIRST + width))
    ):
        for z in range(depth):
            if z == 0:
                size = mag_out_ref[1, pl.ds(row, 1), :]
            elif z == depth - 1:
                size = mag_out_ref[6, pl.ds(row, 1), :]
            else:
                size = mag_in_ref[z - 1, pl.ds(row, 1), :]
            line[pl.ds(z, 1), :] = size
        rate = relax_rate(eddy[pl.ds(row, 1), :], line[...])
        changes = shear_changes([edge_shear[side, k] for k in range(5)], rate)
        for index, q in enumerate(wanted):
            out = edge_ref[side, index] + changes[q]
            for z in range(depth):
                post[q, z, pl.ds(place, 1), :] = out[z : z + 1]

    def collide(z, size_ref, at):
        for half in range(width // 16):
            rows = pl.ds(16 * half, 16)
            around = pl.ds(OWN - TOP + 16 * half, 16)
            rate = relax_rate(eddy[around, :], size_ref[at, around, :])
            changes = shear_changes([shear_ref[k, z, rows, :] for k in range(5)], rate)
            for q in range(19):
                value = base_ref[q, z, rows, :]
                if q:
                    value = value + changes[q]
                post[q, z, pl.ds(FIRST + 16 * half, 16), :] = value

    def inner(z, carry):
        collide(z, mag_in_ref, z - 1)
        return carry

    collide(0, mag_out_ref, 1)
    collide(depth - 1, mag_out_ref, 6)
    lax.fori_loop(1, depth - 1, inner, 0)

    def shifted(q, z, half):
        shift_x, shift_y, _ = VELOCITIES[q]
        piece = post[q, z, pl.ds(FIRST + 16 * half - shift_y, 16), :]
        if shift_x:
            piece = minus(piece) if shift_x > 0 else plus(piece)
        return piece.astype(jnp.bfloat16)

    def run(z, leave_out=()):
        for half in range(width // 16):
            flux = [0.0, 0.0, 0.0]
            for q in range(19):
                if q in leave_out:
                    continue
                moved = shifted(q, z - VELOCITIES[q][2], half)
                nexts[q, z, pl.ds(16 * half, 16), :] = moved
                if q:
                    add_flux(flux, q, moved.astype(jnp.float32))
            table_rows(table, pl.ds(pl.multiple_of(z * width + 16 * half, 16), 16), flux)

    def run_inner(z, carry):
        run(z)
        return carry

    for side, (wanted, z, out) in enumerate(
        ((RISING, depth - 1, rising_ref), (FALLING, 0, falling_ref))
    ):
        for half in range(width // 16):
            rows = pl.ds(16 * half, 16)
            flux = [0.0, 0.0, 0.0]
            for index, q in enumerate(wanted):
                moved = shifted(q, z, half)
                out[index, rows, :] = moved
                add_flux(flux, q, moved.astype(jnp.float32))
            table_rows(face_table.at[side], rows, flux)

    outs = []
    for index in range(4):
        start, stop = index * part, (index + 1) * part
        if index == 0:
            run(0, RISING)
            start += 1
        if index == 3:
            run(depth - 1, FALLING)
            stop -= 1
        lax.fori_loop(start, stop, run_inner, 0)
        place = pl.ds(index * part, part)
        outs.append(
            pltpu.make_async_copy(nexts.at[:, place], next_hbm.at[:, place], out_sems.at[index])
        )
        outs[-1].start()

    owners = partial_ref.shape[0]
    taps, markers = cell_ref.shape
    segments = owners * SEG_DEV
    segment_of = lax.broadcasted_iota(jnp.int32, (segments, markers), 0)
    totals = jnp.zeros((8, segments), jnp.float32)
    groups = [
        (table, 0, depth * width, cell_ref[...], weight_ref[...], segment_ref[...]),
    ]
    for side, (note, start) in enumerate(((note_above, 0), (note_below, (depth - 1) * width))):
        groups.append(
            (
                face_table.at[side],
                start,
                width,
                note[pl.ds(NOTE, taps), :].astype(jnp.int32),
                note[pl.ds(NOTE + taps, taps), :],
                note[pl.ds(NOTE + 2 * taps, 1), :].astype(jnp.int32),
            )
        )
    for rows_table, start, rows, cells, weights, segment in groups:
        totals = totals + lax.dot_general(
            marker_force(rows_table, start, rows, cells, weights),
            jnp.where(segment_of == segment, 1.0, 0.0),
            (((1,), (1,)), ((), ())),
            precision=lax.Precision.HIGHEST,
            preferred_element_type=jnp.float32,
        )
    owner_of = lax.broadcasted_iota(jnp.int32, (owners, segments), 0)
    at_segment = lax.broadcasted_iota(jnp.int32, (owners, segments), 1)
    mine = lax.shift_right_logical(at_segment, 3) == owner_of
    spot = lax.broadcasted_iota(jnp.int32, (segments, LANES), 0)
    at_lane = lax.broadcasted_iota(jnp.int32, (segments, LANES), 1)
    packed = jnp.zeros((owners, LANES), jnp.float32)
    for dim in range(3):
        spread = jnp.where(mine, totals[dim : dim + 1, :], 0.0)
        to_lane = lax.bitwise_and(spot, SEG_DEV - 1) + dim * SEG_DEV == at_lane
        packed = packed + jnp.dot(
            spread,
            jnp.where(to_lane, 1.0, 0.0),
            precision=lax.Precision.HIGHEST,
            preferred_element_type=jnp.float32,
        )
    partial_ref[:, 0, :] = packed
    for copy in outs:
        copy.wait()


def step(parts, sums, mag_in, mag_out, cells, weights, segments, notes, owners):
    _, depth, width, lanes = parts[0].shape
    face = full((5, width, lanes), jnp.bfloat16)
    return pl.pallas_call(
        step_kernel,
        out_shape=(
            full((19, depth, width, lanes), jnp.bfloat16),
            full((width, lanes), jnp.float32),
            full((owners, 1, lanes), jnp.float32),
            face,
            face,
        ),
        in_specs=in_vmem(12),
        out_specs=(pl.BlockSpec(memory_space=pl.ANY),) + tuple(in_vmem(4)),
        scratch_shapes=[
            pltpu.VMEM((19, depth, FIRST + width + 8, lanes), jnp.float32),
            pltpu.VMEM((19, depth, width, lanes), jnp.bfloat16),
            pltpu.VMEM((2, depth * width, 3 * lanes), jnp.bfloat16),
            pltpu.VMEM((2, 2, width, 3 * lanes), jnp.bfloat16),
            pltpu.VMEM((EXT, lanes), jnp.float32),
            pltpu.VMEM((depth, lanes), jnp.float32),
            pltpu.SemaphoreType.DMA((4,)),
        ],
        compiler_params=params(),
        cost_estimate=cost(5),
        name="step",
    )(*parts, sums, mag_in, mag_out, cells, weights, segments, *notes)


def arrive_kernel(next_in, rising_ref, falling_ref, next_hbm, sems):
    depth = next_hbm.shape[1]
    copies = []
    for source, wanted, z in ((rising_ref, RISING, 0), (falling_ref, FALLING, depth - 1)):
        for index, q in enumerate(wanted):
            copies.append(
                pltpu.make_async_copy(source.at[index], next_hbm.at[q, z], sems.at[len(copies)])
            )
            copies[-1].start()
    for copy in copies:
        copy.wait()


def arrive(populations_next, rising, falling):
    hbm = pl.BlockSpec(memory_space=pl.ANY)
    return pl.pallas_call(
        arrive_kernel,
        out_shape=full(populations_next.shape, jnp.bfloat16),
        in_specs=[hbm] + in_vmem(2),
        out_specs=hbm,
        input_output_aliases={0: 0},
        scratch_shapes=[pltpu.SemaphoreType.DMA((10,))],
        compiler_params=params(),
        cost_estimate=cost(0.5),
        name="arrive",
    )(populations_next, rising, falling)


def finish_kernel(arrived_ref, out_ref):
    total = jnp.sum(arrived_ref[:, 0, :], axis=0, keepdims=True)
    for dim in range(3):
        out_ref[pl.ds(dim, 1), :] = total[:, dim * SEG_DEV : (dim + 1) * SEG_DEV]


def finish(arrived):
    return pl.pallas_call(
        finish_kernel,
        out_shape=full((3, SEG_DEV), jnp.float32),
        in_specs=in_vmem(1),
        out_specs=in_vmem(1)[0],
        name="finish",
    )(arrived)


def span_sum(values):
    count = lax.axis_size("span")
    if count & (count - 1):
        return lax.psum(values, "span")
    distance = 1
    while distance < count:
        pairs = [(i, i ^ distance) for i in range(count)]
        values = values + lax.ppermute(values, "span", pairs)
        distance *= 2
    return values


def local(populations, cell_index, marker_weight, segment_id):
    owners = lax.axis_size("span") * lax.axis_size("cross")
    cells, weights, segments = cell_index.T, marker_weight.T, segment_id[None, :]
    vel, y_first, y_last, z_first, z_last = block_moments(populations)
    low, high = exchange(y_first, y_last, "cross")
    below, above = exchange(z_first, z_last, "span")
    note_first, note_last = edge_notes(low, high, cells, weights, segments)
    notes = exchange(note_first, note_last, "span")
    partial, mag_in = inner_sums(vel, low, high)
    before, after = exchange(*face_rows(populations, partial), "cross")
    sums, mag_out = outer_sums(vel, low, high, below, above, *notes, partial)
    parts = ready(populations, before, after, sums)
    sums = span_sum(sums)
    moved, eddy_coeff, packed, rising, falling = step(
        parts, sums, mag_in, mag_out, cells, weights, segments, notes, owners
    )
    arrived = lax.all_to_all(packed, ("span", "cross"), 0, 0)
    populations_next = arrive(moved, *exchange(falling, rising, "span"))
    return (populations_next, eddy_coeff, finish(arrived))


def solution(mesh):
    in_specs = (
        P(None, "span", "cross", None),
        P(("span", "cross"), None),
        P(("span", "cross"), None),
        P(("span", "cross")),
    )
    out_specs = (P(None, "span", "cross", None), P("cross", None), P(None, ("span", "cross")))
    return jax.shard_map(local, mesh=mesh, in_specs=in_specs, out_specs=out_specs, check_vma=False)
```

```python
import functools

import jax
import jax.numpy as jnp
from jax import lax
from jax.experimental import pallas as pl
from jax.experimental.pallas import tpu as pltpu
from jax.sharding import PartitionSpec as P

SEG_DEV = 8
LANES = 128
HALO = 3
EXT = 40
PAD = 56
OWN = 10
TOP = 8
CHUNKS = (8, 16, 24, 32, 40)
VMEM = 28 * 1024 * 1024

eps_sum = 1e-06
base_visc = 0.005

VELOCITIES = [
    [0, 0, 0],
    [1, 0, 0],
    [-1, 0, 0],
    [0, 1, 0],
    [0, -1, 0],
    [0, 0, 1],
    [0, 0, -1],
    [1, 1, 0],
    [-1, -1, 0],
    [1, -1, 0],
    [-1, 1, 0],
    [1, 0, 1],
    [-1, 0, -1],
    [1, 0, -1],
    [-1, 0, 1],
    [0, 1, 1],
    [0, -1, -1],
    [0, 1, -1],
    [0, -1, 1],
]


def swap(first, second, axis):
    count = lax.axis_size(axis)
    near = [(i, i ^ 1) for i in range(count)]
    other = [(i, (i + 1 if i % 2 else i - 1) % count) for i in range(count)]
    return lax.ppermute(first, axis, near), lax.ppermute(second, axis, other)


def is_odd(axis):
    return lax.rem(lax.axis_index(axis), 2) == 1


def send_pair(axis, upwards, downwards, first, second):
    odd = is_odd(axis)

    @pl.when(odd)
    def _():
        first[...] = downwards
        second[...] = upwards

    @pl.when(jnp.logical_not(odd))
    def _():
        first[...] = upwards
        second[...] = downwards


def below_above(axis, first, second):
    odd = is_odd(axis)
    return jnp.where(odd, first, second), jnp.where(odd, second, first)


def full(shape, dtype):
    return jax.ShapeDtypeStruct(shape, dtype)


def in_vmem(count):
    return [pl.BlockSpec(memory_space=pltpu.VMEM)] * count


def params():
    return pltpu.CompilerParams(vmem_limit_bytes=VMEM)


def cost(micros):
    return pl.CostEstimate(flops=0, bytes_accessed=int(micros * 3.6e6), transcendentals=0)


def plus(array):
    return pltpu.roll(array, LANES - 1, 1)


def minus(array):
    return pltpu.roll(array, 1, 1)


STEP = 2.0**-15


def encode(value):
    return jnp.round(value * (1.0 / STEP)).astype(jnp.int32).astype(jnp.int16)


def decode(coded):
    return coded.astype(jnp.int32).astype(jnp.float32) * STEP


def split(value):
    high = value.astype(jnp.bfloat16)
    return high, (value - high.astype(jnp.float32)).astype(jnp.bfloat16)


def moments_kernel(pops, vel_ref, first, second, rows):
    depth, width = pops.shape[1:3]

    def plane(z, carry):
        for half in range(width // 16):
            at = pl.ds(16 * half, 16)
            f = [pops[q, z, at, :].astype(jnp.float32) for q in range(19)]
            flux = [0.0, 0.0, 0.0]
            density = f[0]
            for q in range(1, 19, 2):
                even, odd = f[q] + f[q + 1], f[q] - f[q + 1]
                density = density + even
                for dim in range(3):
                    sign = VELOCITIES[q][dim]
                    if sign:
                        flux[dim] = flux[dim] + odd if sign > 0 else flux[dim] - odd
            inverse = 1.0 / density
            for dim in range(3):
                speed = flux[dim] * inverse
                vel_ref[dim, z, at, :] = speed
                for k in range(HALO):
                    if half == 0:
                        rows[0, dim * HALO + k, pl.ds(z, 1), :] = speed[k : k + 1]
                    if half == width // 16 - 1:
                        rows[1, dim * HALO + k, pl.ds(z, 1), :] = speed[15 - k : 16 - k]
        return carry

    lax.fori_loop(0, depth, plane, 0)
    send_pair("cross", encode(rows[1]), encode(rows[0]), first, second)


def block_moments(populations):
    _, depth, width, lanes = populations.shape
    edge = full((3 * HALO, depth, lanes), jnp.int16)
    return pl.pallas_call(
        moments_kernel,
        out_shape=(full((3, depth, width, lanes), jnp.float32), edge, edge),
        in_specs=in_vmem(1),
        out_specs=tuple(in_vmem(3)),
        scratch_shapes=[pltpu.VMEM((2, 3 * HALO, depth, lanes), jnp.float32)],
        compiler_params=params(),
        cost_estimate=cost(1),
        name="moments",
    )(populations)


def decode_rows(first, second, rows):
    rows[0], rows[1] = below_above("cross", decode(first[...]), decode(second[...]))


def place_plane(ext, p, vel_ref, rows, z):
    width = vel_ref.shape[2]
    for dim in range(3):
        ext[dim, p, pl.ds(OWN, width), :] = vel_ref[dim, z]
        for k in range(HALO):
            line = pl.ds(z, 1)
            ext[dim, p, pl.ds(OWN - 1 - k, 1), :] = rows[0, dim * HALO + k, line, :]
            ext[dim, p, pl.ds(OWN + width + k, 1), :] = rows[1, dim * HALO + k, line, :]


TALL = 40


def edges_kernel(
    vel_ref,
    low_ref,
    high_ref,
    cell_ref,
    weight_ref,
    segment_ref,
    first,
    second,
    rows,
    planes,
    note,
    coded,
):
    depth, width = vel_ref.shape[1:3]
    taps = cell_ref.shape[0]
    decode_rows(low_ref, high_ref, rows)
    fixed = weight_ref[...] * 2.0**16
    coarse = jnp.round(fixed)
    note[...] = jnp.zeros_like(note)
    note[pl.ds(0, taps), :] = cell_ref[...].astype(jnp.float32) - 2.0**15
    note[pl.ds(taps, taps), :] = coarse
    note[pl.ds(2 * taps, taps), :] = jnp.round((fixed - coarse) * 2.0**15)
    note[pl.ds(3 * taps, 1), :] = segment_ref[...].astype(jnp.float32)
    for side, pair in enumerate(((0, 1), (depth - 1, depth - 2))):
        planes[...] = jnp.zeros_like(planes)
        for dim in range(3):
            for index, z in enumerate(pair):
                slot = 2 * dim + index
                planes[slot, pl.ds(HALO, width), :] = vel_ref[dim, z]
                for k in range(HALO):
                    line = pl.ds(z, 1)
                    planes[slot, pl.ds(HALO - 1 - k, 1), :] = rows[0, dim * HALO + k, line, :]
                    planes[slot, pl.ds(HALO + width + k, 1), :] = rows[1, dim * HALO + k, line, :]
        coded[side, pl.ds(0, 6)] = encode(planes[...])
        coded[side, 6] = note[...].astype(jnp.int32).astype(jnp.int16)
    send_pair("span", coded[1], coded[0], first, second)


def edge_planes(vel, low, high, cells, weights, segments):
    pair = full((7, TALL, LANES), jnp.int16)
    return pl.pallas_call(
        edges_kernel,
        out_shape=(pair, pair),
        in_specs=in_vmem(6),
        out_specs=tuple(in_vmem(2)),
        scratch_shapes=[
            pltpu.VMEM((2, 3 * HALO, vel.shape[1], LANES), jnp.float32),
            pltpu.VMEM((6, TALL, LANES), jnp.float32),
            pltpu.VMEM((TALL, LANES), jnp.float32),
            pltpu.VMEM((2, 7, TALL, LANES), jnp.int16),
        ],
        compiler_params=params(),
        cost_estimate=cost(0.2),
        name="edges",
    )(vel, low, high, cells, weights, segments)


def strain_parts(ref, p, row):
    grads = []
    for dim in range(3):
        here = ref[dim, p, pl.ds(row, 8), :]
        grads.append(
            (
                plus(here) - minus(here),
                ref[dim, p, pl.ds(row + 1, 8), :] - ref[dim, p, pl.ds(row - 1, 8), :],
                ref[dim, p + 1, pl.ds(row, 8), :] - ref[dim, p - 1, pl.ds(row, 8), :],
            )
        )
    parts = [
        grads[0][0],
        grads[1][1],
        grads[2][2],
        grads[0][1] + grads[1][0],
        grads[0][2] + grads[2][0],
        grads[1][2] + grads[2][1],
    ]
    straight = parts[0] * parts[0] + parts[1] * parts[1] + parts[2] * parts[2]
    mixed = parts[3] * parts[3] + parts[4] * parts[4] + parts[5] * parts[5]
    return parts, jnp.sqrt(0.5 * straight + 0.25 * mixed)


def weigh(low, middle, high):
    return (low + high) + (middle + middle)


PAIRS = ((0, 0), (1, 1), (2, 2), (0, 1), (0, 2), (1, 2))


def model_sums(planes, ext, hat, prods, zsum, acc_ref, store_mag):
    def first_pass(p, carry):
        for row in CHUNKS:
            rows = pl.ds(row, 8)
            parts, size = strain_parts(ext, p, row)
            store_mag(p, row, size)
            for k in range(6):
                prods[k, p, rows, :] = size * parts[k]
            for k, (i, j) in enumerate(PAIRS):
                prods[6 + k, p, rows, :] = ext[i, p, rows, :] * ext[j, p, rows, :]
            for dim in range(3):
                lines = []
                for shift in (-1, 0, 1):
                    at = pl.ds(row + shift, 8)
                    lines.append(
                        weigh(ext[dim, p - 1, at, :], ext[dim, p, at, :], ext[dim, p + 1, at, :])
                    )
                line = weigh(*lines)
                hat[dim, p, rows, :] = (1.0 / 64.0) * weigh(minus(line), line, plus(line))
        return carry

    lax.fori_loop(1, planes - 1, first_pass, 0)

    def second_pass(p, carry):
        for row in CHUNKS:
            rows = pl.ds(row, 8)
            for k in range(12):
                zsum[k, rows, :] = weigh(
                    prods[k, p - 1, rows, :], prods[k, p, rows, :], prods[k, p + 1, rows, :]
                )
        for row in CHUNKS:
            rows = pl.ds(row, 8)
            parts, size = strain_parts(hat, p, row)
            size = 256.0 * size
            here = [hat[dim, p, rows, :] for dim in range(3)]
            scaled = [64.0 * speed for speed in here]
            smooth = []
            for k in range(12):
                line = weigh(
                    zsum[k, pl.ds(row - 1, 8), :], zsum[k, rows, :], zsum[k, pl.ds(row + 1, 8), :]
                )
                smooth.append(weigh(minus(line), line, plus(line)))
            lm = 0.0
            squares = [0.0, 0.0]
            for k, (i, j) in enumerate(PAIRS):
                model = smooth[k] - size * parts[k]
                leonard = smooth[6 + k] - scaled[i] * here[j]
                lm = lm + leonard * model
                squares[k // 3] = squares[k // 3] + model * model
            out = pl.ds(row - TOP, 8)
            acc_ref[0, out, :] += (1.0 / 4096.0) * lm
            acc_ref[1, out, :] += (1.0 / 4096.0) * (squares[0] + 0.5 * squares[1])
        return carry

    lax.fori_loop(2, planes - 2, second_pass, 0)


def inner_kernel(vel_ref, low_ref, high_ref, acc_ref, mag_ref, ext, hat, prods, zsum, rows):
    depth = vel_ref.shape[1]
    decode_rows(low_ref, high_ref, rows)

    def assemble(p, carry):
        place_plane(ext, p, vel_ref, rows, p)
        return carry

    lax.fori_loop(0, depth, assemble, 0)
    acc_ref[...] = jnp.zeros_like(acc_ref)

    def store_mag(p, row, size):
        mag_ref[p - 1, pl.ds(row - TOP, 8), :] = size

    model_sums(depth, ext, hat, prods, zsum, acc_ref, store_mag)


def model_scratch(planes, depth):
    return [
        pltpu.VMEM((3, planes, PAD, LANES), jnp.float32),
        pltpu.VMEM((3, planes, PAD, LANES), jnp.float32),
        pltpu.VMEM((12, planes, PAD, LANES), jnp.float32),
        pltpu.VMEM((12, PAD, LANES), jnp.float32),
        pltpu.VMEM((2, 3 * HALO, depth, LANES), jnp.float32),
    ]


def inner_sums(vel, low, high):
    depth = vel.shape[1]
    return pl.pallas_call(
        inner_kernel,
        out_shape=(
            full((2, EXT, LANES), jnp.float32),
            full((depth - 2, EXT, LANES), jnp.float32),
        ),
        in_specs=in_vmem(3),
        out_specs=tuple(in_vmem(2)),
        scratch_shapes=model_scratch(depth, depth),
        compiler_params=params(),
        cost_estimate=cost(5),
        name="inner_sums",
    )(vel, low, high)


def outer_kernel(
    vel_ref,
    low_ref,
    high_ref,
    first_ref,
    second_ref,
    partial_ref,
    sums_ref,
    mag_ref,
    ext,
    hat,
    prods,
    zsum,
    rows,
    acc,
):
    depth, width = vel_ref.shape[1:3]
    decode_rows(low_ref, high_ref, rows)
    acc[...] = partial_ref[...]
    below, above = below_above(
        "span", decode(first_ref[pl.ds(0, 6)]), decode(second_ref[pl.ds(0, 6)])
    )
    for side, (message, places, start) in enumerate(
        ((below, (1, 0), 0), (above, (4, 5), depth - 4))
    ):
        for index in range(4):
            place_plane(ext, index + (2 if side == 0 else 0), vel_ref, rows, start + index)
        for dim in range(3):
            for index, p in enumerate(places):
                ext[dim, p, pl.ds(OWN - HALO, TALL), :] = message[2 * dim + index]

        def store_mag(p, row, size):
            mag_ref[4 * side + p - 1, pl.ds(row - TOP, 8), :] = size

        model_sums(6, ext, hat, prods, zsum, acc, store_mag)
    lines = width + 2
    sums_ref[...] = jnp.zeros_like(sums_ref)
    for index in range(2):
        sums_ref[pl.ds(index * lines, lines), :] = acc[index, pl.ds(OWN - TOP - 1, lines), :]


def outer_sums(vel, low, high, below, above, partial):
    depth, width = vel.shape[1:3]
    return pl.pallas_call(
        outer_kernel,
        out_shape=(
            full((-(-2 * (width + 2) // 8) * 8, LANES), jnp.float32),
            full((8, EXT, LANES), jnp.float32),
        ),
        in_specs=in_vmem(6),
        out_specs=tuple(in_vmem(2)),
        scratch_shapes=model_scratch(6, depth) + [pltpu.VMEM((2, EXT, LANES), jnp.float32)],
        compiler_params=params(),
        cost_estimate=cost(2),
        name="outer_sums",
    )(vel, low, high, below, above, partial)


def rows_kernel(pops, after_this, first, second, rows):
    depth, width = pops.shape[1:3]

    def plane(z, carry):
        for q in range(19):
            low = pops[q, z, pl.ds(0, 16), :].astype(jnp.float32)
            high = pops[q, z, pl.ds(width - 16, 16), :].astype(jnp.float32)
            rows[0, q, pl.ds(z, 1), :] = low[:1]
            rows[1, q, pl.ds(z, 1), :] = high[15:]
        return carry

    lax.fori_loop(0, depth, plane, 0)
    send_pair(
        "cross", rows[1].astype(jnp.bfloat16), rows[0].astype(jnp.bfloat16), first, second
    )


def face_rows(populations, after_this):
    _, depth, width, lanes = populations.shape
    edge = full((19, depth, lanes), jnp.bfloat16)
    return pl.pallas_call(
        rows_kernel,
        out_shape=(edge, edge),
        in_specs=in_vmem(1) + [pl.BlockSpec(memory_space=pl.ANY)],
        out_specs=tuple(in_vmem(2)),
        scratch_shapes=[pltpu.VMEM((2, 19, depth, lanes), jnp.float32)],
        compiler_params=params(),
        cost_estimate=cost(0.5),
        name="face_rows",
    )(populations, after_this)


def relax_parts(f):
    even = {q: f[q] + f[q + 1] for q in range(1, 19, 2)}
    odd = {q: f[q] - f[q + 1] for q in range(1, 19, 2)}
    x_xy, x_xz = odd[7] + odd[9], odd[11] + odd[13]
    y_yz, y_xy = odd[15] + odd[17], odd[7] - odd[9]
    z_xz, z_yz = odd[11] - odd[13], odd[15] - odd[17]
    flux, up, down, axis_odd = [], [], [], []
    for first, second, along in ((x_xy, x_xz, 1), (y_yz, y_xy, 3), (z_xz, z_yz, 5)):
        sides = first + second
        total = odd[along] + sides
        heat = 0.15 * (sides - (2.0 / 3.0) * total)
        twist = (1.98 / 8.0) * (first - second)
        flux.append(total)
        up.append(heat + twist)
        down.append(heat - twist)
        axis_odd.append(4.0 * heat)
    a, b, c = even[7] + even[9], even[11] + even[13], even[15] + even[17]
    axes = even[1] + even[3] + even[5]
    diagonals = a + b + c
    density = f[0] + axes + diagonals
    inverse = 1.0 / density
    speed = [total * inverse for total in flux]
    square = [total * part for total, part in zip(flux, speed)]
    energy = square[0] + square[1] + square[2]
    d_e = (1.19 / 126.0) * (diagonals - f[0] - energy)
    d_eps = (1.4 / 252.0) * (9.0 * f[0] - 7.0 * axes - 2.0 * diagonals + 5.5 * energy)
    ax_n, dg_n, eq_n = 3.0 * even[1] - axes, diagonals - 3.0 * c, 3.0 * square[0] - energy
    ax_w, dg_w, eq_w = even[3] - even[5], a - b, square[1] - square[2]
    d_pn = (1.4 / 72.0) * (dg_n - 2.0 * ax_n + 0.5 * eq_n)
    d_pw = (1.4 / 24.0) * (dg_w - 2.0 * ax_w + 0.5 * eq_w)
    shear = [
        (1.0 / 36.0) * (ax_n + dg_n - eq_n),
        (1.0 / 12.0) * (ax_w + dg_w - eq_w),
        0.25 * (even[7] - even[9] - flux[0] * speed[1]),
        0.25 * (even[11] - even[13] - flux[0] * speed[2]),
        0.25 * (even[15] - even[17] - flux[1] * speed[2]),
    ]
    base_axis = 11.0 * d_e + 4.0 * d_eps
    base_diag = -8.0 * d_e - d_eps
    base = [None] * 19
    base[0] = f[0] + (30.0 * d_e - 12.0 * d_eps)
    rest = base_axis - 2.0 * d_pn
    for q, change, skew in (
        (1, base_axis + 4.0 * d_pn, axis_odd[0]),
        (3, rest + 2.0 * d_pw, axis_odd[1]),
        (5, rest - 2.0 * d_pw, axis_odd[2]),
    ):
        base[q] = f[q] + (change + skew)
        base[q + 1] = f[q + 1] + (change - skew)
    rest = base_diag - d_pn
    for q, change, one, two in (
        (7, rest - d_pw, up[0], down[1]),
        (11, rest + d_pw, down[0], up[2]),
        (15, base_diag + 2.0 * d_pn, up[1], down[2]),
    ):
        same, other = one + two, one - two
        base[q] = f[q] + (change - same)
        base[q + 1] = f[q + 1] + (change + same)
        base[q + 2] = f[q + 2] + (change - other)
        base[q + 3] = f[q + 3] + (change + other)
    return base, shear


def shear_changes(shear, rate):
    n, w, xy, xz, yz = [rate * part for part in shear]
    lean = n + w
    tilt = n - w
    twice = n + n
    changes = [None] * 19
    changes[1] = changes[2] = -twice
    changes[3] = changes[4] = tilt
    changes[5] = changes[6] = lean
    changes[7] = changes[8] = -(lean + xy)
    changes[9] = changes[10] = xy - lean
    changes[11] = changes[12] = -(tilt + xz)
    changes[13] = changes[14] = xz - tilt
    changes[15] = changes[16] = twice - yz
    changes[17] = changes[18] = twice + yz
    return changes


def relax_rate(eddy, size):
    return 1.0 / (0.5 + 3.0 * (base_visc + eddy * size))


BEFORE = [q for q in range(19) if VELOCITIES[q][1] > 0]
AFTER = [q for q in range(19) if VELOCITIES[q][1] < 0]
RISING = [q for q in range(19) if VELOCITIES[q][2] > 0]
FALLING = [q for q in range(19) if VELOCITIES[q][2] < 0]
FIRST = 8


def ready_kernel(pops, first, second, after_this, base_ref, shear_ref, edge_ref, edge_shear):
    depth, width = pops.shape[1:3]
    rows = [
        below_above("cross", first[q].astype(jnp.float32), second[q].astype(jnp.float32))
        for q in range(19)
    ]
    for side, wanted in enumerate((BEFORE, AFTER)):
        base, shear = relax_parts([pair[side] for pair in rows])
        for index, q in enumerate(wanted):
            edge_ref[side, index] = base[q]
        for k in range(5):
            edge_shear[side, k] = shear[k]

    def plane(z, carry):
        for half in range(width // 16):
            rows = pl.ds(16 * half, 16)
            base, shear = relax_parts([pops[q, z, rows, :].astype(jnp.float32) for q in range(19)])
            for q in range(19):
                base_ref[q, z, rows, :] = base[q]
            for k in range(5):
                shear_ref[k, z, rows, :] = shear[k]
        return carry

    lax.fori_loop(0, depth, plane, 0)


def ready(populations, before, after, after_this):
    _, depth, width, lanes = populations.shape
    return pl.pallas_call(
        ready_kernel,
        out_shape=(
            full((19, depth, width, lanes), jnp.float32),
            full((5, depth, width, lanes), jnp.float32),
            full((2, 5, depth, lanes), jnp.float32),
            full((2, 5, depth, lanes), jnp.float32),
        ),
        in_specs=in_vmem(3) + [pl.BlockSpec(memory_space=pl.ANY)],
        out_specs=tuple(in_vmem(4)),
        compiler_params=params(),
        cost_estimate=cost(2.5),
        name="ready",
    )(populations, before, after, after_this)


def table_rows(table, at, flux):
    for dim in range(3):
        coarse, fine = split(flux[dim])
        table[0, at, dim * LANES : (dim + 1) * LANES] = coarse
        table[1, at, dim * LANES : (dim + 1) * LANES] = fine


def add_flux(flux, q, moved):
    for dim in range(3):
        sign = VELOCITIES[q][dim]
        if sign:
            flux[dim] = flux[dim] + moved if sign > 0 else flux[dim] - moved


def marker_force(table, start, rows, cells, weights):
    taps, markers = cells.shape
    row_of = lax.broadcasted_iota(jnp.int32, (rows, markers), 0) + start
    lane_of = lax.broadcasted_iota(jnp.int32, (LANES, markers), 0)
    row, lane = lax.shift_right_logical(cells, 7), lax.bitwise_and(cells, LANES - 1)
    pick = jnp.concatenate(
        [
            jnp.where(row_of == row[tap : tap + 1, :], 1.0, 0.0).astype(jnp.bfloat16)
            for tap in range(taps)
        ],
        axis=1,
    )
    contract = (((0,), (0,)), ((), ()))
    picked = lax.dot_general(
        table[0], pick, contract, preferred_element_type=jnp.float32
    ) + lax.dot_general(table[1], pick, contract, preferred_element_type=jnp.float32)
    force = [0.0, 0.0, 0.0]
    for tap in range(taps):
        weight = jnp.where(lane_of == lane[tap : tap + 1, :], -weights[tap : tap + 1, :], 0.0)
        at = slice(tap * markers, (tap + 1) * markers)
        for dim in range(3):
            force[dim] = force[dim] + picked[dim * LANES : (dim + 1) * LANES, at] * weight
    return [jnp.sum(part, axis=0, keepdims=True) for part in force]


def step_kernel(
    base_ref,
    shear_ref,
    edge_ref,
    edge_shear,
    sums_ref,
    mag_in_ref,
    mag_out_ref,
    cell_ref,
    weight_ref,
    segment_ref,
    note_first,
    note_second,
    next_hbm,
    eddy_ref,
    partial_ref,
    first_ref,
    second_ref,
    post,
    nexts,
    table,
    face_table,
    faces,
    eddy,
    line,
    out_sems,
):
    depth, width = shear_ref.shape[1:3]
    lines = width + 2
    part = depth // 4
    eddy[...] = jnp.zeros_like(eddy)
    eddy[pl.ds(OWN - TOP - 1, lines), :] = jnp.maximum(
        sums_ref[pl.ds(0, lines), :] / (sums_ref[pl.ds(lines, lines), :] + eps_sum), 0.0
    )
    eddy_ref[...] = eddy[pl.ds(OWN - TOP, width), :]

    for side, (wanted, row, place) in enumerate(
        ((BEFORE, OWN - TOP - 1, FIRST - 1), (AFTER, OWN - TOP + width, FIRST + width))
    ):
        for z in range(depth):
            if z == 0:
                size = mag_out_ref[1, pl.ds(row, 1), :]
            elif z == depth - 1:
                size = mag_out_ref[6, pl.ds(row, 1), :]
            else:
                size = mag_in_ref[z - 1, pl.ds(row, 1), :]
            line[pl.ds(z, 1), :] = size
        rate = relax_rate(eddy[pl.ds(row, 1), :], line[...])
        changes = shear_changes([edge_shear[side, k] for k in range(5)], rate)
        for index, q in enumerate(wanted):
            out = edge_ref[side, index] + changes[q]
            for z in range(depth):
                post[q, z, pl.ds(place, 1), :] = out[z : z + 1]

    def collide(z, size_ref, at):
        for half in range(width // 16):
            rows = pl.ds(16 * half, 16)
            around = pl.ds(OWN - TOP + 16 * half, 16)
            rate = relax_rate(eddy[around, :], size_ref[at, around, :])
            changes = shear_changes([shear_ref[k, z, rows, :] for k in range(5)], rate)
            for q in range(19):
                value = base_ref[q, z, rows, :]
                if q:
                    value = value + changes[q]
                post[q, z, pl.ds(FIRST + 16 * half, 16), :] = value

    def inner(z, carry):
        collide(z, mag_in_ref, z - 1)
        return carry

    collide(0, mag_out_ref, 1)
    collide(depth - 1, mag_out_ref, 6)
    lax.fori_loop(1, depth - 1, inner, 0)

    def shifted(q, z, half):
        shift_x, shift_y, _ = VELOCITIES[q]
        piece = post[q, z, pl.ds(FIRST + 16 * half - shift_y, 16), :]
        if shift_x:
            piece = minus(piece) if shift_x > 0 else plus(piece)
        return piece.astype(jnp.bfloat16)

    def run(z, leave_out=()):
        for half in range(width // 16):
            flux = [0.0, 0.0, 0.0]
            for q in range(19):
                if q in leave_out:
                    continue
                moved = shifted(q, z - VELOCITIES[q][2], half)
                nexts[q, z, pl.ds(16 * half, 16), :] = moved
                if q:
                    add_flux(flux, q, moved.astype(jnp.float32))
            table_rows(table, pl.ds(pl.multiple_of(z * width + 16 * half, 16), 16), flux)

    def run_inner(z, carry):
        run(z)
        return carry

    for side, (wanted, z) in enumerate(((RISING, depth - 1), (FALLING, 0))):
        for half in range(width // 16):
            rows = pl.ds(16 * half, 16)
            flux = [0.0, 0.0, 0.0]
            for index, q in enumerate(wanted):
                moved = shifted(q, z, half)
                faces[side, index, rows, :] = moved
                add_flux(flux, q, moved.astype(jnp.float32))
            table_rows(face_table.at[side], rows, flux)
    send_pair("span", faces[0], faces[1], first_ref, second_ref)

    outs = []
    for index in range(4):
        start, stop = index * part, (index + 1) * part
        if index == 0:
            run(0, RISING)
            start += 1
        if index == 3:
            run(depth - 1, FALLING)
            stop -= 1
        lax.fori_loop(start, stop, run_inner, 0)
        place = pl.ds(index * part, part)
        outs.append(
            pltpu.make_async_copy(nexts.at[:, place], next_hbm.at[:, place], out_sems.at[index])
        )
        outs[-1].start()

    owners = partial_ref.shape[0]
    taps, markers = cell_ref.shape
    owner_of = lax.broadcasted_iota(jnp.int32, (owners, markers), 0)
    place_of = lax.broadcasted_iota(jnp.int32, (SEG_DEV, markers), 0)
    totals = [jnp.zeros((owners, SEG_DEV), jnp.float32) for _ in range(3)]
    groups = [
        (table, 0, depth * width, cell_ref[...], weight_ref[...], segment_ref[...]),
    ]
    note_below, note_above = below_above(
        "span", note_first[6].astype(jnp.int32), note_second[6].astype(jnp.int32)
    )
    for side, (note, start) in enumerate(((note_above, 0), (note_below, (depth - 1) * width))):
        groups.append(
            (
                face_table.at[side],
                start,
                width,
                note[:taps] + 2**15,
                note[taps : 2 * taps].astype(jnp.float32) * 2.0**-16
                + note[2 * taps : 3 * taps].astype(jnp.float32) * 2.0**-31,
                note[3 * taps : 3 * taps + 1],
            )
        )
    for rows_table, start, rows, cells, weights, segment in groups:
        owner = jnp.where(owner_of == lax.shift_right_logical(segment, 3), 1.0, 0.0)
        owner = owner.astype(jnp.bfloat16)
        place = place_of == lax.bitwise_and(segment, SEG_DEV - 1)
        for dim, force in enumerate(marker_force(rows_table, start, rows, cells, weights)):
            rest = jnp.where(place, force, 0.0)
            for _ in range(3):
                coarse, _ = split(rest)
                rest = rest - coarse.astype(jnp.float32)
                totals[dim] = totals[dim] + lax.dot_general(
                    owner,
                    coarse,
                    (((1,), (1,)), ((), ())),
                    preferred_element_type=jnp.float32,
                )
    for dim in range(3):
        partial_ref[:, dim, :] = totals[dim]
    for copy in outs:
        copy.wait()


def step(parts, sums, mag_in, mag_out, cells, weights, segments, notes, owners):
    _, depth, width, lanes = parts[0].shape
    face = full((5, width, lanes), jnp.bfloat16)
    return pl.pallas_call(
        step_kernel,
        out_shape=(
            full((19, depth, width, lanes), jnp.bfloat16),
            full((width, lanes), jnp.float32),
            full((owners, 3, SEG_DEV), jnp.float32),
            face,
            face,
        ),
        in_specs=in_vmem(12),
        out_specs=(pl.BlockSpec(memory_space=pl.ANY),) + tuple(in_vmem(4)),
        scratch_shapes=[
            pltpu.VMEM((19, depth, FIRST + width + 8, lanes), jnp.float32),
            pltpu.VMEM((19, depth, width, lanes), jnp.bfloat16),
            pltpu.VMEM((2, depth * width, 3 * lanes), jnp.bfloat16),
            pltpu.VMEM((2, 2, width, 3 * lanes), jnp.bfloat16),
            pltpu.VMEM((2, 5, width, lanes), jnp.bfloat16),
            pltpu.VMEM((EXT, lanes), jnp.float32),
            pltpu.VMEM((depth, lanes), jnp.float32),
            pltpu.SemaphoreType.DMA((4,)),
        ],
        compiler_params=params(),
        cost_estimate=cost(5),
        name="step",
    )(*parts, sums, mag_in, mag_out, cells, weights, segments, *notes)


def arrive_kernel(next_in, first, second, next_hbm, sems):
    depth = next_hbm.shape[1]
    odd = is_odd("span")

    def place(below, above):
        copies = []
        for source, wanted, z in ((below, RISING, 0), (above, FALLING, depth - 1)):
            for index, q in enumerate(wanted):
                copies.append(
                    pltpu.make_async_copy(source.at[index], next_hbm.at[q, z], sems.at[len(copies)])
                )
                copies[-1].start()
        for copy in copies:
            copy.wait()

    @pl.when(odd)
    def _():
        place(first, second)

    @pl.when(jnp.logical_not(odd))
    def _():
        place(second, first)


def arrive(populations_next, first, second):
    hbm = pl.BlockSpec(memory_space=pl.ANY)
    return pl.pallas_call(
        arrive_kernel,
        out_shape=full(populations_next.shape, jnp.bfloat16),
        in_specs=[hbm] + in_vmem(2),
        out_specs=hbm,
        input_output_aliases={0: 0},
        scratch_shapes=[pltpu.SemaphoreType.DMA((10,))],
        compiler_params=params(),
        cost_estimate=cost(0.5),
        name="arrive",
    )(populations_next, first, second)


def local(populations, cell_index, marker_weight, segment_id):
    owners = lax.axis_size("span") * lax.axis_size("cross")
    cells, weights, segments = cell_index.T, marker_weight.T, segment_id[None, :]
    vel, *lines = block_moments(populations)
    lines = swap(*lines, "cross")
    planes = swap(*edge_planes(vel, *lines, cells, weights, segments), "span")
    partial, mag_in = inner_sums(vel, *lines)
    faces = swap(*face_rows(populations, partial), "cross")
    sums, mag_out = outer_sums(vel, *lines, *planes, partial)
    parts = ready(populations, *faces, sums)
    count = lax.axis_size("span")
    if count & (count - 1):
        sums = lax.psum(sums, "span")
    else:
        distance = 1
        while distance < count:
            pairs = [(i, i ^ distance) for i in range(count)]
            sums = sums + lax.ppermute(sums, "span", pairs)
            distance *= 2
    moved, eddy_coeff, packed, *leaving = step(
        parts, sums, mag_in, mag_out, cells, weights, segments, planes, owners
    )
    arrived = lax.all_to_all(packed, ("span", "cross"), 0, 0)
    populations_next = arrive(moved, *swap(*leaving, "span"))
    return (populations_next, eddy_coeff, jnp.sum(arrived, axis=0))


def solution(mesh):
    in_specs = (
        P(None, "span", "cross", None),
        P(("span", "cross"), None),
        P(("span", "cross"), None),
        P(("span", "cross")),
    )
    out_specs = (P(None, "span", "cross", None), P("cross", None), P(None, ("span", "cross")))
    return jax.shard_map(local, mesh=mesh, in_specs=in_specs, out_specs=out_specs, check_vma=False)
```

```python
import functools

import jax
import jax.numpy as jnp
from jax import lax
from jax.experimental import pallas as pl
from jax.experimental.pallas import tpu as pltpu
from jax.sharding import PartitionSpec as P

SEG_DEV = 8
LANES = 128
HALO = 3
EXT = 40
PAD = 56
OWN = 11
TOP = 8
CHUNKS = (8, 16, 24, 32, 40)
VMEM = 28 * 1024 * 1024

eps_sum = 1e-06
base_visc = 0.005

VELOCITIES = [
    [0, 0, 0],
    [1, 0, 0],
    [-1, 0, 0],
    [0, 1, 0],
    [0, -1, 0],
    [0, 0, 1],
    [0, 0, -1],
    [1, 1, 0],
    [-1, -1, 0],
    [1, -1, 0],
    [-1, 1, 0],
    [1, 0, 1],
    [-1, 0, -1],
    [1, 0, -1],
    [-1, 0, 1],
    [0, 1, 1],
    [0, -1, -1],
    [0, 1, -1],
    [0, -1, 1],
]


def swap(first, second, axis):
    count = lax.axis_size(axis)
    near = [(i, i ^ 1) for i in range(count)]
    other = [(i, (i + 1 if i % 2 else i - 1) % count) for i in range(count)]
    return lax.ppermute(first, axis, near), lax.ppermute(second, axis, other)


def is_odd(axis):
    return lax.rem(lax.axis_index(axis), 2) == 1


def send_pair(axis, upwards, downwards, first, second):
    odd = is_odd(axis)

    @pl.when(odd)
    def _():
        first[...] = downwards
        second[...] = upwards

    @pl.when(jnp.logical_not(odd))
    def _():
        first[...] = upwards
        second[...] = downwards


def below_above(axis, first, second):
    odd = is_odd(axis)
    return jnp.where(odd, first, second), jnp.where(odd, second, first)


def full(shape, dtype):
    return jax.ShapeDtypeStruct(shape, dtype)


def in_vmem(count):
    return [pl.BlockSpec(memory_space=pltpu.VMEM)] * count


def params():
    return pltpu.CompilerParams(vmem_limit_bytes=VMEM)


def cost(micros):
    return pl.CostEstimate(flops=0, bytes_accessed=int(micros * 3.6e6), transcendentals=0)


def plus(array):
    return pltpu.roll(array, LANES - 1, 1)


def minus(array):
    return pltpu.roll(array, 1, 1)


STEP = 2.0**-15


def encode(value):
    return jnp.round(value * (1.0 / STEP)).astype(jnp.int32).astype(jnp.int16)


def decode(coded):
    return coded.astype(jnp.int32).astype(jnp.float32) * STEP


def split(value):
    high = value.astype(jnp.bfloat16)
    return high, (value - high.astype(jnp.float32)).astype(jnp.bfloat16)


def moments_kernel(pops, vel_ref, first, second, rows):
    depth, width = pops.shape[1:3]

    def plane(z, carry):
        for half in range(width // 16):
            at = pl.ds(16 * half, 16)
            f = [pops[q, z, at, :].astype(jnp.float32) for q in range(19)]
            flux = [0.0, 0.0, 0.0]
            density = f[0]
            for q in range(1, 19, 2):
                even, odd = f[q] + f[q + 1], f[q] - f[q + 1]
                density = density + even
                for dim in range(3):
                    sign = VELOCITIES[q][dim]
                    if sign:
                        flux[dim] = flux[dim] + odd if sign > 0 else flux[dim] - odd
            inverse = 1.0 / density
            for dim in range(3):
                speed = flux[dim] * inverse
                vel_ref[dim, z, at, :] = speed
                for k in range(HALO):
                    if half == 0:
                        rows[0, dim * HALO + k, pl.ds(z, 1), :] = speed[k : k + 1]
                    if half == width // 16 - 1:
                        rows[1, dim * HALO + k, pl.ds(z, 1), :] = speed[15 - k : 16 - k]
        return carry

    lax.fori_loop(0, depth, plane, 0)
    send_pair("cross", encode(rows[1]), encode(rows[0]), first, second)


def block_moments(populations):
    _, depth, width, lanes = populations.shape
    edge = full((3 * HALO, depth, lanes), jnp.int16)
    return pl.pallas_call(
        moments_kernel,
        out_shape=(full((3, depth, width, lanes), jnp.float32), edge, edge),
        in_specs=in_vmem(1),
        out_specs=tuple(in_vmem(3)),
        scratch_shapes=[pltpu.VMEM((2, 3 * HALO, depth, lanes), jnp.float32)],
        compiler_params=params(),
        cost_estimate=cost(1),
        name="moments",
    )(populations)


def decode_rows(first, second, rows):
    rows[0], rows[1] = below_above("cross", decode(first[...]), decode(second[...]))


def place_plane(ext, p, vel_ref, rows, z):
    width = vel_ref.shape[2]
    for dim in range(3):
        ext[dim, p, pl.ds(OWN, width), :] = vel_ref[dim, z]
        for k in range(HALO):
            line = pl.ds(z, 1)
            ext[dim, p, pl.ds(OWN - 1 - k, 1), :] = rows[0, dim * HALO + k, line, :]
            ext[dim, p, pl.ds(OWN + width + k, 1), :] = rows[1, dim * HALO + k, line, :]


TALL = 40


def edges_kernel(
    vel_ref,
    low_ref,
    high_ref,
    cell_ref,
    weight_ref,
    segment_ref,
    first,
    second,
    rows,
    planes,
    note,
    coded,
):
    depth, width = vel_ref.shape[1:3]
    taps = cell_ref.shape[0]
    decode_rows(low_ref, high_ref, rows)
    fixed = weight_ref[...] * 2.0**16
    coarse = jnp.round(fixed)
    note[...] = jnp.zeros_like(note)
    note[pl.ds(0, taps), :] = cell_ref[...].astype(jnp.float32) - 2.0**15
    note[pl.ds(taps, taps), :] = coarse
    note[pl.ds(2 * taps, taps), :] = jnp.round((fixed - coarse) * 2.0**15)
    note[pl.ds(3 * taps, 1), :] = segment_ref[...].astype(jnp.float32)
    for side, pair in enumerate(((0, 1), (depth - 1, depth - 2))):
        planes[...] = jnp.zeros_like(planes)
        for dim in range(3):
            for index, z in enumerate(pair):
                slot = 2 * dim + index
                planes[slot, pl.ds(HALO, width), :] = vel_ref[dim, z]
                for k in range(HALO):
                    line = pl.ds(z, 1)
                    planes[slot, pl.ds(HALO - 1 - k, 1), :] = rows[0, dim * HALO + k, line, :]
                    planes[slot, pl.ds(HALO + width + k, 1), :] = rows[1, dim * HALO + k, line, :]
        coded[side, pl.ds(0, 6)] = encode(planes[...])
        coded[side, 6] = note[...].astype(jnp.int32).astype(jnp.int16)
    send_pair("span", coded[1], coded[0], first, second)


def edge_planes(vel, low, high, cells, weights, segments):
    pair = full((7, TALL, LANES), jnp.int16)
    return pl.pallas_call(
        edges_kernel,
        out_shape=(pair, pair),
        in_specs=in_vmem(6),
        out_specs=tuple(in_vmem(2)),
        scratch_shapes=[
            pltpu.VMEM((2, 3 * HALO, vel.shape[1], LANES), jnp.float32),
            pltpu.VMEM((6, TALL, LANES), jnp.float32),
            pltpu.VMEM((TALL, LANES), jnp.float32),
            pltpu.VMEM((2, 7, TALL, LANES), jnp.int16),
        ],
        compiler_params=params(),
        cost_estimate=cost(0.2),
        name="edges",
    )(vel, low, high, cells, weights, segments)


def plane_loop(start, stop, body, carry, most):
    count = stop - start
    step = max(size for size in range(1, most + 1) if count % size == 0)

    def block(index, carry):
        for shift in range(step):
            carry = body(start + index * step + shift, carry)
        return carry

    if count == step:
        return block(0, carry)
    return lax.fori_loop(0, count // step, block, carry)


def strain_parts(ref, p, row, before, here, after):
    grads = [
        (
            plus(here[dim]) - minus(here[dim]),
            ref[dim, p, pl.ds(row + 1, 8), :] - ref[dim, p, pl.ds(row - 1, 8), :],
            after[dim] - before[dim],
        )
        for dim in range(3)
    ]
    parts = [
        grads[0][0],
        grads[1][1],
        grads[2][2],
        grads[0][1] + grads[1][0],
        grads[0][2] + grads[2][0],
        grads[1][2] + grads[2][1],
    ]
    straight = parts[0] * parts[0] + parts[1] * parts[1] + parts[2] * parts[2]
    mixed = parts[3] * parts[3] + parts[4] * parts[4] + parts[5] * parts[5]
    return parts, jnp.sqrt(0.5 * straight + 0.25 * mixed)


def weigh(low, middle, high):
    return (low + high) + (middle + middle)


PAIRS = ((0, 0), (1, 1), (2, 2), (0, 1), (0, 2), (1, 2))


def three(ref, p, rows):
    return [ref[dim, p, rows, :] for dim in range(3)]


def model_sums(planes, ext, hat, zsum, zvel, acc_ref, store_mag):
    for row in CHUNKS:
        rows = pl.ds(row, 8)

        def first_pass(p, carry):
            before, here, lag, last = carry
            after = three(ext, p + 1, rows)
            parts, size = strain_parts(ext, p, row, before, here, after)
            store_mag(p, row, size)
            prods = [size * part for part in parts] + [here[i] * here[j] for i, j in PAIRS]
            for k in range(12):
                zsum[k, p - 1, rows, :] = lag[k] + prods[k]
            for dim in range(3):
                zvel[dim, p, rows, :] = weigh(before[dim], here[dim], after[dim])
            lag = [last[k] + (prods[k] + prods[k]) for k in range(12)]
            return here, after, lag, prods

        none = [jnp.zeros((8, LANES), jnp.float32)] * 12
        carry = (three(ext, 0, rows), three(ext, 1, rows), none, none)
        plane_loop(1, planes - 1, first_pass, carry, 7)

    def second_pass(p, carry):
        for row in CHUNKS:
            for dim in range(3):
                line = weigh(*[zvel[dim, p, pl.ds(row + shift, 8), :] for shift in (-1, 0, 1)])
                hat[dim, p, pl.ds(row, 8), :] = (1.0 / 64.0) * weigh(minus(line), line, plus(line))
        return carry

    plane_loop(1, planes - 1, second_pass, 0, 2)

    for row in CHUNKS:
        rows = pl.ds(row, 8)

        def third_pass(p, carry):
            before, here, lm, mm = carry
            after = three(hat, p + 1, rows)
            parts, size = strain_parts(hat, p, row, before, here, after)
            size = 256.0 * size
            scaled = [64.0 * speed for speed in here]
            squares = [0.0, 0.0]
            for k, (i, j) in enumerate(PAIRS):
                smooth = []
                for field in (k, 6 + k):
                    line = weigh(
                        *[zsum[field, p, pl.ds(row + shift, 8), :] for shift in (-1, 0, 1)]
                    )
                    smooth.append(weigh(minus(line), line, plus(line)))
                model = smooth[0] - size * parts[k]
                lm = lm + (smooth[1] - scaled[i] * here[j]) * model
                squares[k // 3] = squares[k // 3] + model * model
            return here, after, lm, mm + (squares[0] + 0.5 * squares[1])

        none = jnp.zeros((8, LANES), jnp.float32)
        carry = (three(hat, 1, rows), three(hat, 2, rows), none, none)
        _, _, lm, mm = plane_loop(2, planes - 2, third_pass, carry, 6)
        out = pl.ds(row - TOP, 8)
        acc_ref[0, out, :] += (1.0 / 4096.0) * lm
        acc_ref[1, out, :] += (1.0 / 4096.0) * mm


def inner_kernel(vel_ref, low_ref, high_ref, acc_ref, mag_ref, ext, hat, zsum, zvel, rows):
    depth = vel_ref.shape[1]
    decode_rows(low_ref, high_ref, rows)

    def assemble(p, carry):
        place_plane(ext, p, vel_ref, rows, p)
        return carry

    lax.fori_loop(0, depth, assemble, 0)
    acc_ref[...] = jnp.zeros_like(acc_ref)

    def store_mag(p, row, size):
        mag_ref[p - 1, pl.ds(row - TOP, 8), :] = size

    model_sums(depth, ext, hat, zsum, zvel, acc_ref, store_mag)


def model_scratch(planes, depth):
    return [
        pltpu.VMEM((3, planes, PAD, LANES), jnp.float32),
        pltpu.VMEM((3, planes, PAD, LANES), jnp.float32),
        pltpu.VMEM((12, planes, PAD, LANES), jnp.float32),
        pltpu.VMEM((3, planes, PAD, LANES), jnp.float32),
        pltpu.VMEM((2, 3 * HALO, depth, LANES), jnp.float32),
    ]


def inner_sums(vel, low, high):
    depth = vel.shape[1]
    return pl.pallas_call(
        inner_kernel,
        out_shape=(
            full((2, EXT, LANES), jnp.float32),
            full((depth - 2, EXT, LANES), jnp.float32),
        ),
        in_specs=in_vmem(3),
        out_specs=tuple(in_vmem(2)),
        scratch_shapes=model_scratch(depth, depth),
        compiler_params=params(),
        cost_estimate=cost(5),
        name="inner_sums",
    )(vel, low, high)


def outer_kernel(
    vel_ref,
    low_ref,
    high_ref,
    first_ref,
    second_ref,
    partial_ref,
    sums_ref,
    mag_ref,
    ext,
    hat,
    zsum,
    zvel,
    rows,
    acc,
):
    depth, width = vel_ref.shape[1:3]
    decode_rows(low_ref, high_ref, rows)
    acc[...] = partial_ref[...]
    below, above = below_above(
        "span", decode(first_ref[pl.ds(0, 6)]), decode(second_ref[pl.ds(0, 6)])
    )
    for side, (message, places, start) in enumerate(
        ((below, (1, 0), 0), (above, (4, 5), depth - 4))
    ):
        for index in range(4):
            place_plane(ext, index + (2 if side == 0 else 0), vel_ref, rows, start + index)
        for dim in range(3):
            for index, p in enumerate(places):
                ext[dim, p, pl.ds(OWN - HALO, TALL), :] = message[2 * dim + index]

        def store_mag(p, row, size):
            mag_ref[4 * side + p - 1, pl.ds(row - TOP, 8), :] = size

        model_sums(6, ext, hat, zsum, zvel, acc, store_mag)
    lines = width + 2
    sums_ref[...] = jnp.zeros_like(sums_ref)
    for index in range(2):
        sums_ref[pl.ds(index * lines, lines), :] = acc[index, pl.ds(OWN - TOP - 1, lines), :]


def outer_sums(vel, low, high, below, above, partial):
    depth, width = vel.shape[1:3]
    return pl.pallas_call(
        outer_kernel,
        out_shape=(
            full((-(-2 * (width + 2) // 8) * 8, LANES), jnp.float32),
            full((8, EXT, LANES), jnp.float32),
        ),
        in_specs=in_vmem(6),
        out_specs=tuple(in_vmem(2)),
        scratch_shapes=model_scratch(6, depth) + [pltpu.VMEM((2, EXT, LANES), jnp.float32)],
        compiler_params=params(),
        cost_estimate=cost(2),
        name="outer_sums",
    )(vel, low, high, below, above, partial)


def rows_kernel(pops, after_this, first, second, rows):
    depth, width = pops.shape[1:3]

    def plane(z, carry):
        for q in range(19):
            low = pops[q, z, pl.ds(0, 16), :].astype(jnp.float32)
            high = pops[q, z, pl.ds(width - 16, 16), :].astype(jnp.float32)
            rows[0, q, pl.ds(z, 1), :] = low[:1]
            rows[1, q, pl.ds(z, 1), :] = high[15:]
        return carry

    lax.fori_loop(0, depth, plane, 0)
    send_pair(
        "cross", rows[1].astype(jnp.bfloat16), rows[0].astype(jnp.bfloat16), first, second
    )


def face_rows(populations, after_this):
    _, depth, width, lanes = populations.shape
    edge = full((19, depth, lanes), jnp.bfloat16)
    return pl.pallas_call(
        rows_kernel,
        out_shape=(edge, edge),
        in_specs=in_vmem(1) + [pl.BlockSpec(memory_space=pl.ANY)],
        out_specs=tuple(in_vmem(2)),
        scratch_shapes=[pltpu.VMEM((2, 19, depth, lanes), jnp.float32)],
        compiler_params=params(),
        cost_estimate=cost(0.5),
        name="face_rows",
    )(populations, after_this)


def relax_parts(f):
    even = {q: f[q] + f[q + 1] for q in range(1, 19, 2)}
    odd = {q: f[q] - f[q + 1] for q in range(1, 19, 2)}
    x_xy, x_xz = odd[7] + odd[9], odd[11] + odd[13]
    y_yz, y_xy = odd[15] + odd[17], odd[7] - odd[9]
    z_xz, z_yz = odd[11] - odd[13], odd[15] - odd[17]
    flux, up, down, axis_odd = [], [], [], []
    for first, second, along in ((x_xy, x_xz, 1), (y_yz, y_xy, 3), (z_xz, z_yz, 5)):
        sides = first + second
        total = odd[along] + sides
        heat = 0.15 * (sides - (2.0 / 3.0) * total)
        twist = (1.98 / 8.0) * (first - second)
        flux.append(total)
        up.append(heat + twist)
        down.append(heat - twist)
        axis_odd.append(4.0 * heat)
    a, b, c = even[7] + even[9], even[11] + even[13], even[15] + even[17]
    axes = even[1] + even[3] + even[5]
    diagonals = a + b + c
    density = f[0] + axes + diagonals
    inverse = 1.0 / density
    speed = [total * inverse for total in flux]
    square = [total * part for total, part in zip(flux, speed)]
    energy = square[0] + square[1] + square[2]
    d_e = (1.19 / 126.0) * (diagonals - f[0] - energy)
    d_eps = (1.4 / 252.0) * (9.0 * f[0] - 7.0 * axes - 2.0 * diagonals + 5.5 * energy)
    ax_n, dg_n, eq_n = 3.0 * even[1] - axes, diagonals - 3.0 * c, 3.0 * square[0] - energy
    ax_w, dg_w, eq_w = even[3] - even[5], a - b, square[1] - square[2]
    d_pn = (1.4 / 72.0) * (dg_n - 2.0 * ax_n + 0.5 * eq_n)
    d_pw = (1.4 / 24.0) * (dg_w - 2.0 * ax_w + 0.5 * eq_w)
    shear = [
        (1.0 / 36.0) * (ax_n + dg_n - eq_n),
        (1.0 / 12.0) * (ax_w + dg_w - eq_w),
        0.25 * (even[7] - even[9] - flux[0] * speed[1]),
        0.25 * (even[11] - even[13] - flux[0] * speed[2]),
        0.25 * (even[15] - even[17] - flux[1] * speed[2]),
    ]
    base_axis = 11.0 * d_e + 4.0 * d_eps
    base_diag = -8.0 * d_e - d_eps
    base = [None] * 19
    base[0] = f[0] + (30.0 * d_e - 12.0 * d_eps)
    rest = base_axis - 2.0 * d_pn
    for q, change, skew in (
        (1, base_axis + 4.0 * d_pn, axis_odd[0]),
        (3, rest + 2.0 * d_pw, axis_odd[1]),
        (5, rest - 2.0 * d_pw, axis_odd[2]),
    ):
        base[q] = f[q] + (change + skew)
        base[q + 1] = f[q + 1] + (change - skew)
    rest = base_diag - d_pn
    for q, change, one, two in (
        (7, rest - d_pw, up[0], down[1]),
        (11, rest + d_pw, down[0], up[2]),
        (15, base_diag + 2.0 * d_pn, up[1], down[2]),
    ):
        same, other = one + two, one - two
        base[q] = f[q] + (change - same)
        base[q + 1] = f[q + 1] + (change + same)
        base[q + 2] = f[q + 2] + (change - other)
        base[q + 3] = f[q + 3] + (change + other)
    return base, shear


def shear_changes(shear, rate):
    n, w, xy, xz, yz = [rate * part for part in shear]
    lean = n + w
    tilt = n - w
    twice = n + n
    changes = [None] * 19
    changes[1] = changes[2] = -twice
    changes[3] = changes[4] = tilt
    changes[5] = changes[6] = lean
    changes[7] = changes[8] = -(lean + xy)
    changes[9] = changes[10] = xy - lean
    changes[11] = changes[12] = -(tilt + xz)
    changes[13] = changes[14] = xz - tilt
    changes[15] = changes[16] = twice - yz
    changes[17] = changes[18] = twice + yz
    return changes


def relax_rate(eddy, size):
    return 1.0 / (0.5 + 3.0 * (base_visc + eddy * size))


BEFORE = [q for q in range(19) if VELOCITIES[q][1] > 0]
AFTER = [q for q in range(19) if VELOCITIES[q][1] < 0]
RISING = [q for q in range(19) if VELOCITIES[q][2] > 0]
FALLING = [q for q in range(19) if VELOCITIES[q][2] < 0]
FIRST = 8


def ready_kernel(pops, first, second, after_this, base_ref, shear_ref, edge_ref, edge_shear):
    depth, width = pops.shape[1:3]
    rows = [
        below_above("cross", first[q].astype(jnp.float32), second[q].astype(jnp.float32))
        for q in range(19)
    ]
    for side, wanted in enumerate((BEFORE, AFTER)):
        base, shear = relax_parts([pair[side] for pair in rows])
        for index, q in enumerate(wanted):
            edge_ref[side, index] = base[q]
        for k in range(5):
            edge_shear[side, k] = shear[k]

    def plane(z, carry):
        for half in range(width // 16):
            rows = pl.ds(16 * half, 16)
            base, shear = relax_parts([pops[q, z, rows, :].astype(jnp.float32) for q in range(19)])
            for q in range(19):
                base_ref[q, z, rows, :] = base[q]
            for k in range(5):
                shear_ref[k, z, rows, :] = shear[k]
        return carry

    lax.fori_loop(0, depth, plane, 0)


def ready(populations, before, after, after_this):
    _, depth, width, lanes = populations.shape
    return pl.pallas_call(
        ready_kernel,
        out_shape=(
            full((19, depth, width, lanes), jnp.float32),
            full((5, depth, width, lanes), jnp.float32),
            full((2, 5, depth, lanes), jnp.float32),
            full((2, 5, depth, lanes), jnp.float32),
        ),
        in_specs=in_vmem(3) + [pl.BlockSpec(memory_space=pl.ANY)],
        out_specs=tuple(in_vmem(4)),
        compiler_params=params(),
        cost_estimate=cost(2.5),
        name="ready",
    )(populations, before, after, after_this)


def table_rows(table, at, flux):
    for dim in range(3):
        coarse, fine = split(flux[dim])
        table[0, at, dim * LANES : (dim + 1) * LANES] = coarse
        table[1, at, dim * LANES : (dim + 1) * LANES] = fine


def add_flux(flux, q, moved):
    for dim in range(3):
        sign = VELOCITIES[q][dim]
        if sign:
            flux[dim] = flux[dim] + moved if sign > 0 else flux[dim] - moved


def marker_force(table, start, rows, cells, weights):
    taps, markers = cells.shape
    row_of = lax.broadcasted_iota(jnp.int32, (rows, markers), 0) + start
    lane_of = lax.broadcasted_iota(jnp.int32, (LANES, markers), 0)
    row, lane = lax.shift_right_logical(cells, 7), lax.bitwise_and(cells, LANES - 1)
    pick = jnp.concatenate(
        [
            jnp.where(row_of == row[tap : tap + 1, :], 1.0, 0.0).astype(jnp.bfloat16)
            for tap in range(taps)
        ],
        axis=1,
    )
    contract = (((0,), (0,)), ((), ()))
    picked = lax.dot_general(
        table[0], pick, contract, preferred_element_type=jnp.float32
    ) + lax.dot_general(table[1], pick, contract, preferred_element_type=jnp.float32)
    force = [0.0, 0.0, 0.0]
    for tap in range(taps):
        weight = jnp.where(lane_of == lane[tap : tap + 1, :], -weights[tap : tap + 1, :], 0.0)
        at = slice(tap * markers, (tap + 1) * markers)
        for dim in range(3):
            force[dim] = force[dim] + picked[dim * LANES : (dim + 1) * LANES, at] * weight
    return [jnp.sum(part, axis=0, keepdims=True) for part in force]


def step_kernel(
    base_ref,
    shear_ref,
    edge_ref,
    edge_shear,
    sums_ref,
    mag_in_ref,
    mag_out_ref,
    cell_ref,
    weight_ref,
    segment_ref,
    note_first,
    note_second,
    next_hbm,
    eddy_ref,
    partial_ref,
    first_ref,
    second_ref,
    post,
    nexts,
    table,
    face_table,
    faces,
    eddy,
    line,
    out_sems,
):
    depth, width = shear_ref.shape[1:3]
    lines = width + 2
    part = depth // 4
    eddy[...] = jnp.zeros_like(eddy)
    eddy[pl.ds(OWN - TOP - 1, lines), :] = jnp.maximum(
        sums_ref[pl.ds(0, lines), :] / (sums_ref[pl.ds(lines, lines), :] + eps_sum), 0.0
    )
    eddy_ref[...] = eddy[pl.ds(OWN - TOP, width), :]

    for side, (wanted, row, place) in enumerate(
        ((BEFORE, OWN - TOP - 1, FIRST - 1), (AFTER, OWN - TOP + width, FIRST + width))
    ):
        for z in range(depth):
            if z == 0:
                size = mag_out_ref[1, pl.ds(row, 1), :]
            elif z == depth - 1:
                size = mag_out_ref[6, pl.ds(row, 1), :]
            else:
                size = mag_in_ref[z - 1, pl.ds(row, 1), :]
            line[pl.ds(z, 1), :] = size
        rate = relax_rate(eddy[pl.ds(row, 1), :], line[...])
        changes = shear_changes([edge_shear[side, k] for k in range(5)], rate)
        for index, q in enumerate(wanted):
            out = edge_ref[side, index] + changes[q]
            for z in range(depth):
                post[q, z, pl.ds(place, 1), :] = out[z : z + 1]

    def collide(z, size_ref, at):
        for half in range(width // 16):
            rows = pl.ds(16 * half, 16)
            around = pl.ds(OWN - TOP + 16 * half, 16)
            rate = relax_rate(eddy[around, :], size_ref[at, around, :])
            changes = shear_changes([shear_ref[k, z, rows, :] for k in range(5)], rate)
            for q in range(19):
                value = base_ref[q, z, rows, :]
                if q:
                    value = value + changes[q]
                post[q, z, pl.ds(FIRST + 16 * half, 16), :] = value

    def inner(z, carry):
        collide(z, mag_in_ref, z - 1)
        return carry

    collide(0, mag_out_ref, 1)
    collide(depth - 1, mag_out_ref, 6)
    lax.fori_loop(1, depth - 1, inner, 0)

    def shifted(q, z, half):
        shift_x, shift_y, _ = VELOCITIES[q]
        piece = post[q, z, pl.ds(FIRST + 16 * half - shift_y, 16), :]
        if shift_x:
            piece = minus(piece) if shift_x > 0 else plus(piece)
        return piece.astype(jnp.bfloat16)

    def run(z, leave_out=()):
        for half in range(width // 16):
            flux = [0.0, 0.0, 0.0]
            for q in range(19):
                if q in leave_out:
                    continue
                moved = shifted(q, z - VELOCITIES[q][2], half)
                nexts[q, z, pl.ds(16 * half, 16), :] = moved
                if q:
                    add_flux(flux, q, moved.astype(jnp.float32))
            table_rows(table, pl.ds(pl.multiple_of(z * width + 16 * half, 16), 16), flux)

    def run_inner(z, carry):
        run(z)
        return carry

    for side, (wanted, z) in enumerate(((RISING, depth - 1), (FALLING, 0))):
        for half in range(width // 16):
            rows = pl.ds(16 * half, 16)
            flux = [0.0, 0.0, 0.0]
            for index, q in enumerate(wanted):
                moved = shifted(q, z, half)
                faces[side, index, rows, :] = moved
                add_flux(flux, q, moved.astype(jnp.float32))
            table_rows(face_table.at[side], rows, flux)
    send_pair("span", faces[0], faces[1], first_ref, second_ref)

    outs = []
    for index in range(4):
        start, stop = index * part, (index + 1) * part
        if index == 0:
            run(0, RISING)
            start += 1
        if index == 3:
            run(depth - 1, FALLING)
            stop -= 1
        lax.fori_loop(start, stop, run_inner, 0)
        place = pl.ds(index * part, part)
        outs.append(
            pltpu.make_async_copy(nexts.at[:, place], next_hbm.at[:, place], out_sems.at[index])
        )
        outs[-1].start()

    owners = partial_ref.shape[0]
    taps, markers = cell_ref.shape
    owner_of = lax.broadcasted_iota(jnp.int32, (owners, markers), 0)
    place_of = lax.broadcasted_iota(jnp.int32, (SEG_DEV, markers), 0)
    totals = [jnp.zeros((owners, SEG_DEV), jnp.float32) for _ in range(3)]
    groups = [
        (table, 0, depth * width, cell_ref[...], weight_ref[...], segment_ref[...]),
    ]
    note_below, note_above = below_above(
        "span", note_first[6].astype(jnp.int32), note_second[6].astype(jnp.int32)
    )
    for side, (note, start) in enumerate(((note_above, 0), (note_below, (depth - 1) * width))):
        groups.append(
            (
                face_table.at[side],
                start,
                width,
                note[:taps] + 2**15,
                note[taps : 2 * taps].astype(jnp.float32) * 2.0**-16
                + note[2 * taps : 3 * taps].astype(jnp.float32) * 2.0**-31,
                note[3 * taps : 3 * taps + 1],
            )
        )
    for rows_table, start, rows, cells, weights, segment in groups:
        owner = jnp.where(owner_of == lax.shift_right_logical(segment, 3), 1.0, 0.0)
        owner = owner.astype(jnp.bfloat16)
        place = place_of == lax.bitwise_and(segment, SEG_DEV - 1)
        for dim, force in enumerate(marker_force(rows_table, start, rows, cells, weights)):
            rest = jnp.where(place, force, 0.0)
            for _ in range(3):
                coarse, _ = split(rest)
                rest = rest - coarse.astype(jnp.float32)
                totals[dim] = totals[dim] + lax.dot_general(
                    owner,
                    coarse,
                    (((1,), (1,)), ((), ())),
                    preferred_element_type=jnp.float32,
                )
    for dim in range(3):
        partial_ref[:, dim, :] = totals[dim]
    for copy in outs:
        copy.wait()


def step(parts, sums, mag_in, mag_out, cells, weights, segments, notes, owners):
    _, depth, width, lanes = parts[0].shape
    face = full((5, width, lanes), jnp.bfloat16)
    return pl.pallas_call(
        step_kernel,
        out_shape=(
            full((19, depth, width, lanes), jnp.bfloat16),
            full((width, lanes), jnp.float32),
            full((owners, 3, SEG_DEV), jnp.float32),
            face,
            face,
        ),
        in_specs=in_vmem(12),
        out_specs=(pl.BlockSpec(memory_space=pl.ANY),) + tuple(in_vmem(4)),
        scratch_shapes=[
            pltpu.VMEM((19, depth, FIRST + width + 8, lanes), jnp.float32),
            pltpu.VMEM((19, depth, width, lanes), jnp.bfloat16),
            pltpu.VMEM((2, depth * width, 3 * lanes), jnp.bfloat16),
            pltpu.VMEM((2, 2, width, 3 * lanes), jnp.bfloat16),
            pltpu.VMEM((2, 5, width, lanes), jnp.bfloat16),
            pltpu.VMEM((EXT, lanes), jnp.float32),
            pltpu.VMEM((depth, lanes), jnp.float32),
            pltpu.SemaphoreType.DMA((4,)),
        ],
        compiler_params=params(),
        cost_estimate=cost(5),
        name="step",
    )(*parts, sums, mag_in, mag_out, cells, weights, segments, *notes)


def arrive_kernel(next_in, first, second, arrived_hbm, next_hbm, force_ref, arrived, sems):
    depth = next_hbm.shape[1]
    odd = is_odd("span")
    shares = pltpu.make_async_copy(arrived_hbm, arrived, sems.at[10])
    shares.start()

    def place(below, above):
        copies = []
        for source, wanted, z in ((below, RISING, 0), (above, FALLING, depth - 1)):
            for index, q in enumerate(wanted):
                copies.append(
                    pltpu.make_async_copy(source.at[index], next_hbm.at[q, z], sems.at[len(copies)])
                )
                copies[-1].start()
        for copy in copies:
            copy.wait()

    @pl.when(odd)
    def _():
        place(first, second)

    @pl.when(jnp.logical_not(odd))
    def _():
        place(second, first)

    shares.wait()
    force_ref[...] = jnp.sum(arrived[...], axis=0)


def arrive(populations_next, first, second, arrived):
    hbm = pl.BlockSpec(memory_space=pl.ANY)
    return pl.pallas_call(
        arrive_kernel,
        out_shape=(
            full(populations_next.shape, jnp.bfloat16),
            full(arrived.shape[1:], jnp.float32),
        ),
        in_specs=[hbm] + in_vmem(2) + [hbm],
        out_specs=(hbm, in_vmem(1)[0]),
        input_output_aliases={0: 0},
        scratch_shapes=[
            pltpu.VMEM(arrived.shape, jnp.float32),
            pltpu.SemaphoreType.DMA((11,)),
        ],
        compiler_params=params(),
        cost_estimate=cost(0.5),
        name="arrive",
    )(populations_next, first, second, arrived)


def local(populations, cell_index, marker_weight, segment_id):
    owners = lax.axis_size("span") * lax.axis_size("cross")
    cells, weights, segments = cell_index.T, marker_weight.T, segment_id[None, :]
    vel, *lines = block_moments(populations)
    lines = swap(*lines, "cross")
    planes = swap(*edge_planes(vel, *lines, cells, weights, segments), "span")
    partial, mag_in = inner_sums(vel, *lines)
    faces = swap(*face_rows(populations, partial), "cross")
    sums, mag_out = outer_sums(vel, *lines, *planes, partial)
    parts = ready(populations, *faces, sums)
    count = lax.axis_size("span")
    if count & (count - 1):
        sums = lax.psum(sums, "span")
    else:
        distance = 1
        while distance < count:
            pairs = [(i, i ^ distance) for i in range(count)]
            sums = sums + lax.ppermute(sums, "span", pairs)
            distance *= 2
    moved, eddy_coeff, packed, *leaving = step(
        parts, sums, mag_in, mag_out, cells, weights, segments, planes, owners
    )
    arrived = lax.all_to_all(packed, ("span", "cross"), 0, 0)
    populations_next, segment_force = arrive(moved, *swap(*leaving, "span"), arrived)
    return (populations_next, eddy_coeff, segment_force)


def solution(mesh):
    in_specs = (
        P(None, "span", "cross", None),
        P(("span", "cross"), None),
        P(("span", "cross"), None),
        P(("span", "cross")),
    )
    out_specs = (P(None, "span", "cross", None), P("cross", None), P(None, ("span", "cross")))
    return jax.shard_map(local, mesh=mesh, in_specs=in_specs, out_specs=out_specs, check_vma=False)
```

```python
import functools

import jax
import jax.numpy as jnp
from jax import lax
from jax.experimental import pallas as pl
from jax.experimental.pallas import tpu as pltpu
from jax.sharding import PartitionSpec as P

SEG_DEV = 8
LANES = 128
HALO = 3
EXT = 40
PAD = 56
OWN = 11
TOP = 8
CHUNKS = (8, 16, 24, 32, 40)
VMEM = 28 * 1024 * 1024

eps_sum = 1e-06
base_visc = 0.005

VELOCITIES = [
    [0, 0, 0],
    [1, 0, 0],
    [-1, 0, 0],
    [0, 1, 0],
    [0, -1, 0],
    [0, 0, 1],
    [0, 0, -1],
    [1, 1, 0],
    [-1, -1, 0],
    [1, -1, 0],
    [-1, 1, 0],
    [1, 0, 1],
    [-1, 0, -1],
    [1, 0, -1],
    [-1, 0, 1],
    [0, 1, 1],
    [0, -1, -1],
    [0, 1, -1],
    [0, -1, 1],
]


def swap(first, second, axis):
    count = lax.axis_size(axis)
    near = [(i, i ^ 1) for i in range(count)]
    other = [(i, (i + 1 if i % 2 else i - 1) % count) for i in range(count)]
    return lax.ppermute(first, axis, near), lax.ppermute(second, axis, other)


def is_odd(axis):
    return lax.rem(lax.axis_index(axis), 2) == 1


def send_pair(axis, upwards, downwards, first, second):
    odd = is_odd(axis)

    @pl.when(odd)
    def _():
        first[...] = downwards
        second[...] = upwards

    @pl.when(jnp.logical_not(odd))
    def _():
        first[...] = upwards
        second[...] = downwards


def below_above(axis, first, second):
    odd = is_odd(axis)
    return jnp.where(odd, first, second), jnp.where(odd, second, first)


def full(shape, dtype):
    return jax.ShapeDtypeStruct(shape, dtype)


def in_vmem(count):
    return [pl.BlockSpec(memory_space=pltpu.VMEM)] * count


def params():
    return pltpu.CompilerParams(vmem_limit_bytes=VMEM)


def cost(micros):
    return pl.CostEstimate(flops=0, bytes_accessed=int(micros * 3.6e6), transcendentals=0)


def plus(array):
    return pltpu.roll(array, LANES - 1, 1)


def minus(array):
    return pltpu.roll(array, 1, 1)


STEP = 2.0**-15


def encode(value):
    return jnp.round(value * (1.0 / STEP)).astype(jnp.int32).astype(jnp.int16)


def decode(coded):
    return coded.astype(jnp.int32).astype(jnp.float32) * STEP


def split(value):
    high = value.astype(jnp.bfloat16)
    return high, (value - high.astype(jnp.float32)).astype(jnp.bfloat16)


def moments_kernel(pops, vel_ref, first, second, rows):
    depth, width = pops.shape[1:3]

    def plane(z, carry):
        for half in range(width // 16):
            at = pl.ds(16 * half, 16)
            f = [pops[q, z, at, :].astype(jnp.float32) for q in range(19)]
            flux = [0.0, 0.0, 0.0]
            density = f[0]
            for q in range(1, 19, 2):
                even, odd = f[q] + f[q + 1], f[q] - f[q + 1]
                density = density + even
                for dim in range(3):
                    sign = VELOCITIES[q][dim]
                    if sign:
                        flux[dim] = flux[dim] + odd if sign > 0 else flux[dim] - odd
            inverse = 1.0 / density
            for dim in range(3):
                speed = flux[dim] * inverse
                vel_ref[dim, z, at, :] = speed
                for k in range(HALO):
                    if half == 0:
                        rows[0, dim * HALO + k, pl.ds(z, 1), :] = speed[k : k + 1]
                    if half == width // 16 - 1:
                        rows[1, dim * HALO + k, pl.ds(z, 1), :] = speed[15 - k : 16 - k]
        return carry

    lax.fori_loop(0, depth, plane, 0)
    send_pair("cross", encode(rows[1]), encode(rows[0]), first, second)


def block_moments(populations):
    _, depth, width, lanes = populations.shape
    edge = full((3 * HALO, depth, lanes), jnp.int16)
    return pl.pallas_call(
        moments_kernel,
        out_shape=(full((3, depth, width, lanes), jnp.float32), edge, edge),
        in_specs=in_vmem(1),
        out_specs=tuple(in_vmem(3)),
        scratch_shapes=[
            pltpu.VMEM((2, 3 * HALO, depth, lanes), jnp.float32),
        ],
        compiler_params=params(),
        cost_estimate=cost(1),
        name="moments",
    )(populations)


def decode_rows(first, second, rows):
    rows[0], rows[1] = below_above("cross", decode(first[...]), decode(second[...]))


def place_plane(ext, p, vel_ref, rows, z):
    width = vel_ref.shape[2]
    for dim in range(3):
        ext[dim, p, pl.ds(OWN, width), :] = vel_ref[dim, z]
        for k in range(HALO):
            line = pl.ds(z, 1)
            ext[dim, p, pl.ds(OWN - 1 - k, 1), :] = rows[0, dim * HALO + k, line, :]
            ext[dim, p, pl.ds(OWN + width + k, 1), :] = rows[1, dim * HALO + k, line, :]


TALL = 40


def edges_kernel(
    vel_ref,
    low_ref,
    high_ref,
    cell_ref,
    weight_ref,
    segment_ref,
    first,
    second,
    rows,
    planes,
    note,
    coded,
):
    depth, width = vel_ref.shape[1:3]
    taps = cell_ref.shape[0]
    decode_rows(low_ref, high_ref, rows)
    fixed = weight_ref[...] * 2.0**16
    coarse = jnp.round(fixed)
    note[...] = jnp.zeros_like(note)
    note[pl.ds(0, taps), :] = cell_ref[...].astype(jnp.float32) - 2.0**15
    note[pl.ds(taps, taps), :] = coarse
    note[pl.ds(2 * taps, taps), :] = jnp.round((fixed - coarse) * 2.0**15)
    note[pl.ds(3 * taps, 1), :] = segment_ref[...].astype(jnp.float32)
    for side, pair in enumerate(((0, 1), (depth - 1, depth - 2))):
        planes[...] = jnp.zeros_like(planes)
        for dim in range(3):
            for index, z in enumerate(pair):
                slot = 2 * dim + index
                planes[slot, pl.ds(HALO, width), :] = vel_ref[dim, z]
                for k in range(HALO):
                    line = pl.ds(z, 1)
                    planes[slot, pl.ds(HALO - 1 - k, 1), :] = rows[0, dim * HALO + k, line, :]
                    planes[slot, pl.ds(HALO + width + k, 1), :] = rows[1, dim * HALO + k, line, :]
        coded[side, pl.ds(0, 6)] = encode(planes[...])
        coded[side, 6] = note[...].astype(jnp.int32).astype(jnp.int16)
    send_pair("span", coded[1], coded[0], first, second)


def edge_planes(vel, low, high, cells, weights, segments):
    pair = full((7, TALL, LANES), jnp.int16)
    return pl.pallas_call(
        edges_kernel,
        out_shape=(pair, pair),
        in_specs=in_vmem(6),
        out_specs=tuple(in_vmem(2)),
        scratch_shapes=[
            pltpu.VMEM((2, 3 * HALO, vel.shape[1], LANES), jnp.float32),
            pltpu.VMEM((6, TALL, LANES), jnp.float32),
            pltpu.VMEM((TALL, LANES), jnp.float32),
            pltpu.VMEM((2, 7, TALL, LANES), jnp.int16),
        ],
        compiler_params=params(),
        cost_estimate=cost(0.2),
        name="edges",
    )(vel, low, high, cells, weights, segments)


def plane_loop(start, stop, body, carry, most):
    count = stop - start
    step = max(size for size in range(1, most + 1) if count % size == 0)

    def block(index, carry):
        for shift in range(step):
            carry = body(start + index * step + shift, carry)
        return carry

    if count == step:
        return block(0, carry)
    return lax.fori_loop(0, count // step, block, carry)


def strain_parts(ref, p, row, before, here, after):
    grads = [
        (
            plus(here[dim]) - minus(here[dim]),
            ref[dim, p, pl.ds(row + 1, 8), :] - ref[dim, p, pl.ds(row - 1, 8), :],
            after[dim] - before[dim],
        )
        for dim in range(3)
    ]
    parts = [
        grads[0][0],
        grads[1][1],
        grads[2][2],
        grads[0][1] + grads[1][0],
        grads[0][2] + grads[2][0],
        grads[1][2] + grads[2][1],
    ]
    straight = parts[0] * parts[0] + parts[1] * parts[1] + parts[2] * parts[2]
    mixed = parts[3] * parts[3] + parts[4] * parts[4] + parts[5] * parts[5]
    return parts, jnp.sqrt(0.5 * straight + 0.25 * mixed)


def weigh(low, middle, high):
    return (low + high) + (middle + middle)


PAIRS = ((0, 0), (1, 1), (2, 2), (0, 1), (0, 2), (1, 2))


def three(ref, p, rows):
    return [ref[dim, p, rows, :] for dim in range(3)]


def model_sums(planes, ext, hat, zsum, zvel, acc_ref, store_mag):
    for row in CHUNKS:
        rows = pl.ds(row, 8)

        def first_pass(p, carry):
            before, here, lag, last = carry
            after = three(ext, p + 1, rows)
            parts, size = strain_parts(ext, p, row, before, here, after)
            store_mag(p, row, size)
            prods = [size * part for part in parts] + [here[i] * here[j] for i, j in PAIRS]
            for k in range(12):
                zsum[k, p - 1, rows, :] = lag[k] + prods[k]
            for dim in range(3):
                zvel[dim, p, rows, :] = weigh(before[dim], here[dim], after[dim])
            lag = [last[k] + (prods[k] + prods[k]) for k in range(12)]
            return here, after, lag, prods

        none = [jnp.zeros((8, LANES), jnp.float32)] * 12
        carry = (three(ext, 0, rows), three(ext, 1, rows), none, none)
        plane_loop(1, planes - 1, first_pass, carry, 7)

    def second_pass(p, carry):
        for row in CHUNKS:
            for dim in range(3):
                line = weigh(*[zvel[dim, p, pl.ds(row + shift, 8), :] for shift in (-1, 0, 1)])
                hat[dim, p, pl.ds(row, 8), :] = (1.0 / 64.0) * weigh(minus(line), line, plus(line))
        return carry

    plane_loop(1, planes - 1, second_pass, 0, 2)

    for row in CHUNKS:
        rows = pl.ds(row, 8)

        def third_pass(p, carry):
            before, here, lm, mm = carry
            after = three(hat, p + 1, rows)
            parts, size = strain_parts(hat, p, row, before, here, after)
            size = 256.0 * size
            scaled = [64.0 * speed for speed in here]
            squares = [0.0, 0.0]
            for k, (i, j) in enumerate(PAIRS):
                smooth = []
                for field in (k, 6 + k):
                    line = weigh(
                        *[zsum[field, p, pl.ds(row + shift, 8), :] for shift in (-1, 0, 1)]
                    )
                    smooth.append(weigh(minus(line), line, plus(line)))
                model = smooth[0] - size * parts[k]
                lm = lm + (smooth[1] - scaled[i] * here[j]) * model
                squares[k // 3] = squares[k // 3] + model * model
            return here, after, lm, mm + (squares[0] + 0.5 * squares[1])

        none = jnp.zeros((8, LANES), jnp.float32)
        carry = (three(hat, 1, rows), three(hat, 2, rows), none, none)
        _, _, lm, mm = plane_loop(2, planes - 2, third_pass, carry, 6)
        out = pl.ds(row - TOP, 8)
        acc_ref[0, out, :] += (1.0 / 4096.0) * lm
        acc_ref[1, out, :] += (1.0 / 4096.0) * mm


def inner_kernel(vel_ref, low_ref, high_ref, acc_ref, mag_ref, ext, hat, zsum, zvel, rows):
    depth = vel_ref.shape[1]
    decode_rows(low_ref, high_ref, rows)

    def assemble(p, carry):
        place_plane(ext, p, vel_ref, rows, p)
        return carry

    lax.fori_loop(0, depth, assemble, 0)
    acc_ref[...] = jnp.zeros_like(acc_ref)

    def store_mag(p, row, size):
        mag_ref[p - 1, pl.ds(row - TOP, 8), :] = size

    model_sums(depth, ext, hat, zsum, zvel, acc_ref, store_mag)


def model_scratch(planes, depth):
    return [
        pltpu.VMEM((3, planes, PAD, LANES), jnp.float32),
        pltpu.VMEM((3, planes, PAD, LANES), jnp.float32),
        pltpu.VMEM((12, planes, PAD, LANES), jnp.float32),
        pltpu.VMEM((3, planes, PAD, LANES), jnp.float32),
        pltpu.VMEM((2, 3 * HALO, depth, LANES), jnp.float32),
    ]


def inner_sums(vel, low, high):
    depth = vel.shape[1]
    return pl.pallas_call(
        inner_kernel,
        out_shape=(
            full((2, EXT, LANES), jnp.float32),
            full((depth - 2, EXT, LANES), jnp.float32),
        ),
        in_specs=in_vmem(3),
        out_specs=tuple(in_vmem(2)),
        scratch_shapes=model_scratch(depth, depth),
        compiler_params=params(),
        cost_estimate=cost(5),
        name="inner_sums",
    )(vel, low, high)


def outer_kernel(
    vel_ref,
    low_ref,
    high_ref,
    first_ref,
    second_ref,
    partial_ref,
    sums_ref,
    mag_ref,
    ext,
    hat,
    zsum,
    zvel,
    rows,
    acc,
):
    depth, width = vel_ref.shape[1:3]
    decode_rows(low_ref, high_ref, rows)
    acc[...] = partial_ref[...]
    below, above = below_above(
        "span", decode(first_ref[pl.ds(0, 6)]), decode(second_ref[pl.ds(0, 6)])
    )
    for side, (message, places, start) in enumerate(
        ((below, (1, 0), 0), (above, (4, 5), depth - 4))
    ):
        for index in range(4):
            place_plane(ext, index + (2 if side == 0 else 0), vel_ref, rows, start + index)
        for dim in range(3):
            for index, p in enumerate(places):
                ext[dim, p, pl.ds(OWN - HALO, TALL), :] = message[2 * dim + index]

        def store_mag(p, row, size):
            mag_ref[4 * side + p - 1, pl.ds(row - TOP, 8), :] = size

        model_sums(6, ext, hat, zsum, zvel, acc, store_mag)
    lines = width + 2
    sums_ref[...] = jnp.zeros_like(sums_ref)
    for index in range(2):
        sums_ref[pl.ds(index * lines, lines), :] = acc[index, pl.ds(OWN - TOP - 1, lines), :]


def outer_sums(vel, low, high, below, above, partial):
    depth, width = vel.shape[1:3]
    return pl.pallas_call(
        outer_kernel,
        out_shape=(
            full((-(-2 * (width + 2) // 8) * 8, LANES), jnp.float32),
            full((8, EXT, LANES), jnp.float32),
        ),
        in_specs=in_vmem(6),
        out_specs=tuple(in_vmem(2)),
        scratch_shapes=model_scratch(6, depth) + [pltpu.VMEM((2, EXT, LANES), jnp.float32)],
        compiler_params=params(),
        cost_estimate=cost(2),
        name="outer_sums",
    )(vel, low, high, below, above, partial)


def rows_kernel(pops, after_this, first, second, rows):
    depth, width = pops.shape[1:3]

    def plane(z, carry):
        for q in range(19):
            low = pops[q, z, pl.ds(0, 16), :].astype(jnp.float32)
            high = pops[q, z, pl.ds(width - 16, 16), :].astype(jnp.float32)
            rows[0, q, pl.ds(z, 1), :] = low[:1]
            rows[1, q, pl.ds(z, 1), :] = high[15:]
        return carry

    lax.fori_loop(0, depth, plane, 0)
    send_pair(
        "cross", rows[1].astype(jnp.bfloat16), rows[0].astype(jnp.bfloat16), first, second
    )


def face_rows(populations, after_this):
    _, depth, width, lanes = populations.shape
    edge = full((19, depth, lanes), jnp.bfloat16)
    return pl.pallas_call(
        rows_kernel,
        out_shape=(edge, edge),
        in_specs=in_vmem(1) + [pl.BlockSpec(memory_space=pl.ANY)],
        out_specs=tuple(in_vmem(2)),
        scratch_shapes=[pltpu.VMEM((2, 19, depth, lanes), jnp.float32)],
        compiler_params=params(),
        cost_estimate=cost(0.5),
        name="face_rows",
    )(populations, after_this)


def relax_parts(f):
    even = {q: f[q] + f[q + 1] for q in range(1, 19, 2)}
    odd = {q: f[q] - f[q + 1] for q in range(1, 19, 2)}
    x_xy, x_xz = odd[7] + odd[9], odd[11] + odd[13]
    y_yz, y_xy = odd[15] + odd[17], odd[7] - odd[9]
    z_xz, z_yz = odd[11] - odd[13], odd[15] - odd[17]
    flux, up, down, axis_odd = [], [], [], []
    for first, second, along in ((x_xy, x_xz, 1), (y_yz, y_xy, 3), (z_xz, z_yz, 5)):
        sides = first + second
        total = odd[along] + sides
        heat = 0.15 * (sides - (2.0 / 3.0) * total)
        twist = (1.98 / 8.0) * (first - second)
        flux.append(total)
        up.append(heat + twist)
        down.append(heat - twist)
        axis_odd.append(4.0 * heat)
    a, b, c = even[7] + even[9], even[11] + even[13], even[15] + even[17]
    axes = even[1] + even[3] + even[5]
    diagonals = a + b + c
    density = f[0] + axes + diagonals
    inverse = 1.0 / density
    speed = [total * inverse for total in flux]
    square = [total * part for total, part in zip(flux, speed)]
    energy = square[0] + square[1] + square[2]
    d_e = (1.19 / 126.0) * (diagonals - f[0] - energy)
    d_eps = (1.4 / 252.0) * (9.0 * f[0] - 7.0 * axes - 2.0 * diagonals + 5.5 * energy)
    ax_n, dg_n, eq_n = 3.0 * even[1] - axes, diagonals - 3.0 * c, 3.0 * square[0] - energy
    ax_w, dg_w, eq_w = even[3] - even[5], a - b, square[1] - square[2]
    d_pn = (1.4 / 72.0) * (dg_n - 2.0 * ax_n + 0.5 * eq_n)
    d_pw = (1.4 / 24.0) * (dg_w - 2.0 * ax_w + 0.5 * eq_w)
    shear = [
        (1.0 / 36.0) * (ax_n + dg_n - eq_n),
        (1.0 / 12.0) * (ax_w + dg_w - eq_w),
        0.25 * (even[7] - even[9] - flux[0] * speed[1]),
        0.25 * (even[11] - even[13] - flux[0] * speed[2]),
        0.25 * (even[15] - even[17] - flux[1] * speed[2]),
    ]
    base_axis = 11.0 * d_e + 4.0 * d_eps
    base_diag = -8.0 * d_e - d_eps
    base = [None] * 19
    base[0] = f[0] + (30.0 * d_e - 12.0 * d_eps)
    rest = base_axis - 2.0 * d_pn
    for q, change, skew in (
        (1, base_axis + 4.0 * d_pn, axis_odd[0]),
        (3, rest + 2.0 * d_pw, axis_odd[1]),
        (5, rest - 2.0 * d_pw, axis_odd[2]),
    ):
        base[q] = f[q] + (change + skew)
        base[q + 1] = f[q + 1] + (change - skew)
    rest = base_diag - d_pn
    for q, change, one, two in (
        (7, rest - d_pw, up[0], down[1]),
        (11, rest + d_pw, down[0], up[2]),
        (15, base_diag + 2.0 * d_pn, up[1], down[2]),
    ):
        same, other = one + two, one - two
        base[q] = f[q] + (change - same)
        base[q + 1] = f[q + 1] + (change + same)
        base[q + 2] = f[q + 2] + (change - other)
        base[q + 3] = f[q + 3] + (change + other)
    return base, shear


def shear_changes(shear, rate):
    n, w, xy, xz, yz = [rate * part for part in shear]
    lean = n + w
    tilt = n - w
    twice = n + n
    changes = [None] * 19
    changes[1] = changes[2] = -twice
    changes[3] = changes[4] = tilt
    changes[5] = changes[6] = lean
    changes[7] = changes[8] = -(lean + xy)
    changes[9] = changes[10] = xy - lean
    changes[11] = changes[12] = -(tilt + xz)
    changes[13] = changes[14] = xz - tilt
    changes[15] = changes[16] = twice - yz
    changes[17] = changes[18] = twice + yz
    return changes


def relax_rate(eddy, size):
    return 1.0 / (0.5 + 3.0 * (base_visc + eddy * size))


BEFORE = [q for q in range(19) if VELOCITIES[q][1] > 0]
AFTER = [q for q in range(19) if VELOCITIES[q][1] < 0]
RISING = [q for q in range(19) if VELOCITIES[q][2] > 0]
FALLING = [q for q in range(19) if VELOCITIES[q][2] < 0]
FIRST = 8


def ready_kernel(pops, first, second, after_this, base_ref, shear_ref, edge_ref, edge_shear):
    depth, width = pops.shape[1:3]
    rows = [
        below_above("cross", first[q].astype(jnp.float32), second[q].astype(jnp.float32))
        for q in range(19)
    ]
    for side, wanted in enumerate((BEFORE, AFTER)):
        base, shear = relax_parts([pair[side] for pair in rows])
        for index, q in enumerate(wanted):
            edge_ref[side, index] = base[q]
        for k in range(5):
            edge_shear[side, k] = shear[k]

    def plane(z, carry):
        for half in range(width // 16):
            rows = pl.ds(16 * half, 16)
            base, shear = relax_parts([pops[q, z, rows, :].astype(jnp.float32) for q in range(19)])
            for q in range(19):
                base_ref[q, z, rows, :] = base[q]
            for k in range(5):
                shear_ref[k, z, rows, :] = shear[k]
        return carry

    lax.fori_loop(0, depth, plane, 0)


def ready(populations, before, after, after_this):
    _, depth, width, lanes = populations.shape
    return pl.pallas_call(
        ready_kernel,
        out_shape=(
            full((19, depth, width, lanes), jnp.float32),
            full((5, depth, width, lanes), jnp.float32),
            full((2, 5, depth, lanes), jnp.float32),
            full((2, 5, depth, lanes), jnp.float32),
        ),
        in_specs=in_vmem(3) + [pl.BlockSpec(memory_space=pl.ANY)],
        out_specs=tuple(in_vmem(4)),
        compiler_params=params(),
        cost_estimate=cost(2.5),
        name="ready",
    )(populations, before, after, after_this)


def table_rows(table, at, flux):
    for dim in range(3):
        coarse, fine = split(flux[dim])
        table[0, at, dim * LANES : (dim + 1) * LANES] = coarse
        table[1, at, dim * LANES : (dim + 1) * LANES] = fine


def add_flux(flux, q, moved):
    for dim in range(3):
        sign = VELOCITIES[q][dim]
        if sign:
            flux[dim] = flux[dim] + moved if sign > 0 else flux[dim] - moved


def picks_kernel(
    cell_ref, weight_ref, segment_ref, note_first, note_second, after_this, own, faces, masks, owner
):
    taps, markers = cell_ref.shape
    cells_all, width = own.shape[1], faces.shape[2]
    owners = owner.shape[1]
    note_below, note_above = below_above(
        "span", note_first[6].astype(jnp.int32), note_second[6].astype(jnp.int32)
    )
    groups = [(cell_ref[...], weight_ref[...], segment_ref[...])]
    for note in (note_above, note_below):
        groups.append(
            (
                note[:taps] + 2**15,
                note[taps : 2 * taps].astype(jnp.float32) * 2.0**-16
                + note[2 * taps : 3 * taps].astype(jnp.float32) * 2.0**-31,
                note[3 * taps : 3 * taps + 1],
            )
        )
    owner_of = lax.broadcasted_iota(jnp.int32, (owners, markers), 0)
    for group, (cells, weights, segment) in enumerate(groups):
        row = lax.shift_right_logical(cells, 7).astype(jnp.float32).T.astype(jnp.int32)
        lane = lax.bitwise_and(cells, LANES - 1).astype(jnp.float32).T.astype(jnp.int32)
        weight = weights.T
        count = cells_all if group == 0 else width
        start = cells_all - width if group == 2 else 0
        row_of = lax.broadcasted_iota(jnp.int32, (markers, count), 1) + start
        lane_of = lax.broadcasted_iota(jnp.int32, (markers, LANES), 1)
        for tap in range(taps):
            at = pl.ds(tap * markers, markers)
            pick = jnp.where(row_of == row[:, tap : tap + 1], 1.0, 0.0).astype(jnp.bfloat16)
            if group == 0:
                own[at, :] = pick
            else:
                faces[group - 1, at, :] = pick
            masks[group, at, :] = jnp.where(
                lane_of == lane[:, tap : tap + 1], -weight[:, tap : tap + 1], 0.0
            )
        hit = jnp.where(owner_of == lax.shift_right_logical(segment, 3), 1.0, 0.0)
        owner[group] = hit.astype(jnp.bfloat16)


def marker_picks(cells, weights, segments, notes, after_this, rows, width, owners):
    taps, markers = cells.shape
    return pl.pallas_call(
        picks_kernel,
        out_shape=(
            full((taps * markers, rows), jnp.bfloat16),
            full((2, taps * markers, width), jnp.bfloat16),
            full((3, taps * markers, LANES), jnp.float32),
            full((3, owners, markers), jnp.bfloat16),
        ),
        in_specs=in_vmem(5) + [pl.BlockSpec(memory_space=pl.ANY)],
        out_specs=tuple(in_vmem(4)),
        compiler_params=params(),
        cost_estimate=cost(1),
        name="picks",
    )(cells, weights, segments, *notes, after_this)


def parts_of(value):
    coarse, _ = split(value)
    rest = value - coarse.astype(jnp.float32)
    middle, fine = split(rest)
    return coarse, middle, fine


def across(first, second):
    total = 0.0
    for part in parts_of(second):
        total = total + lax.dot_general(
            first, part, (((1,), (1,)), ((), ())), preferred_element_type=jnp.float32
        )
    return total


def marker_force(table, pick, mask_ref, group, taps):
    picked = jnp.dot(pick, table[0], preferred_element_type=jnp.float32) + jnp.dot(
        pick, table[1], preferred_element_type=jnp.float32
    )
    markers = picked.shape[0] // taps
    force = []
    for dim in range(3):
        total = 0.0
        for tap in range(taps):
            at = slice(tap * markers, (tap + 1) * markers)
            mask = mask_ref[group, pl.ds(tap * markers, markers), :]
            total = total + picked[at, dim * LANES : (dim + 1) * LANES] * mask
        force.append(total)
    ones = jnp.ones((8, LANES), jnp.bfloat16)
    return across(ones, jnp.concatenate(force, axis=0))[:1]


def step_kernel(
    base_ref,
    shear_ref,
    edge_ref,
    edge_shear,
    sums_ref,
    mag_in_ref,
    mag_out_ref,
    segment_ref,
    note_first,
    note_second,
    own_ref,
    face_ref,
    mask_ref,
    owner_ref,
    next_hbm,
    eddy_ref,
    partial_ref,
    first_ref,
    second_ref,
    post,
    nexts,
    table,
    face_table,
    faces,
    eddy,
    line,
    out_sems,
):
    depth, width = shear_ref.shape[1:3]
    lines = width + 2
    part = depth // 4
    eddy[...] = jnp.zeros_like(eddy)
    eddy[pl.ds(OWN - TOP - 1, lines), :] = jnp.maximum(
        sums_ref[pl.ds(0, lines), :] / (sums_ref[pl.ds(lines, lines), :] + eps_sum), 0.0
    )
    eddy_ref[...] = eddy[pl.ds(OWN - TOP, width), :]

    for side, (wanted, row, place) in enumerate(
        ((BEFORE, OWN - TOP - 1, FIRST - 1), (AFTER, OWN - TOP + width, FIRST + width))
    ):
        for z in range(depth):
            if z == 0:
                size = mag_out_ref[1, pl.ds(row, 1), :]
            elif z == depth - 1:
                size = mag_out_ref[6, pl.ds(row, 1), :]
            else:
                size = mag_in_ref[z - 1, pl.ds(row, 1), :]
            line[pl.ds(z, 1), :] = size
        rate = relax_rate(eddy[pl.ds(row, 1), :], line[...])
        changes = shear_changes([edge_shear[side, k] for k in range(5)], rate)
        for index, q in enumerate(wanted):
            out = edge_ref[side, index] + changes[q]
            for z in range(depth):
                post[q, z, pl.ds(place, 1), :] = out[z : z + 1]

    def collide(z, size_ref, at):
        for half in range(width // 16):
            rows = pl.ds(16 * half, 16)
            around = pl.ds(OWN - TOP + 16 * half, 16)
            rate = relax_rate(eddy[around, :], size_ref[at, around, :])
            changes = shear_changes([shear_ref[k, z, rows, :] for k in range(5)], rate)
            for q in range(19):
                value = base_ref[q, z, rows, :]
                if q:
                    value = value + changes[q]
                post[q, z, pl.ds(FIRST + 16 * half, 16), :] = value

    def inner(z, carry):
        collide(z, mag_in_ref, z - 1)
        return carry

    collide(0, mag_out_ref, 1)
    collide(depth - 1, mag_out_ref, 6)
    lax.fori_loop(1, depth - 1, inner, 0)

    def shifted(q, z, half):
        shift_x, shift_y, _ = VELOCITIES[q]
        piece = post[q, z, pl.ds(FIRST + 16 * half - shift_y, 16), :]
        if shift_x:
            piece = minus(piece) if shift_x > 0 else plus(piece)
        return piece.astype(jnp.bfloat16)

    def run(z, leave_out=()):
        for half in range(width // 16):
            flux = [0.0, 0.0, 0.0]
            for q in range(19):
                if q in leave_out:
                    continue
                moved = shifted(q, z - VELOCITIES[q][2], half)
                nexts[q, z, pl.ds(16 * half, 16), :] = moved
                if q:
                    add_flux(flux, q, moved.astype(jnp.float32))
            table_rows(table, pl.ds(pl.multiple_of(z * width + 16 * half, 16), 16), flux)

    def run_inner(z, carry):
        run(z)
        return carry

    for side, (wanted, z) in enumerate(((RISING, depth - 1), (FALLING, 0))):
        for half in range(width // 16):
            rows = pl.ds(16 * half, 16)
            flux = [0.0, 0.0, 0.0]
            for index, q in enumerate(wanted):
                moved = shifted(q, z, half)
                faces[side, index, rows, :] = moved
                add_flux(flux, q, moved.astype(jnp.float32))
            table_rows(face_table.at[side], rows, flux)
    send_pair("span", faces[0], faces[1], first_ref, second_ref)

    outs = []
    for index in range(4):
        start, stop = index * part, (index + 1) * part
        if index == 0:
            run(0, RISING)
            start += 1
        if index == 3:
            run(depth - 1, FALLING)
            stop -= 1
        lax.fori_loop(start, stop, run_inner, 0)
        place = pl.ds(index * part, part)
        outs.append(
            pltpu.make_async_copy(nexts.at[:, place], next_hbm.at[:, place], out_sems.at[index])
        )
        outs[-1].start()

    note_below, note_above = below_above(
        "span", note_first[6].astype(jnp.int32), note_second[6].astype(jnp.int32)
    )
    markers = segment_ref.shape[1]
    taps = own_ref.shape[0] // markers
    place_of = lax.broadcasted_iota(jnp.int32, (SEG_DEV, markers), 0)
    spread = []
    for group, (rows_table, pick, segment) in enumerate(
        (
            (table, own_ref[...], segment_ref[...]),
            (face_table.at[0], face_ref[0], note_above[3 * taps : 3 * taps + 1]),
            (face_table.at[1], face_ref[1], note_below[3 * taps : 3 * taps + 1]),
        )
    ):
        force = marker_force(rows_table, pick, mask_ref, group, taps)
        place = place_of == lax.bitwise_and(segment, SEG_DEV - 1)
        spread.append(
            jnp.concatenate(
                [
                    jnp.where(place, force[:, dim * markers : (dim + 1) * markers], 0.0)
                    for dim in range(3)
                ],
                axis=0,
            )
        )
    totals = 0.0
    for group in range(3):
        totals = totals + across(owner_ref[group], spread[group])
    for dim in range(3):
        partial_ref[:, dim, :] = totals[:, dim * SEG_DEV : (dim + 1) * SEG_DEV]
    for copy in outs:
        copy.wait()


def step(parts, sums, mag_in, mag_out, segments, notes, picks):
    _, depth, width, lanes = parts[0].shape
    owners = picks[3].shape[1]
    face = full((5, width, lanes), jnp.bfloat16)
    return pl.pallas_call(
        step_kernel,
        out_shape=(
            full((19, depth, width, lanes), jnp.bfloat16),
            full((width, lanes), jnp.float32),
            full((owners, 3, SEG_DEV), jnp.float32),
            face,
            face,
        ),
        in_specs=in_vmem(14),
        out_specs=(pl.BlockSpec(memory_space=pl.ANY),) + tuple(in_vmem(4)),
        scratch_shapes=[
            pltpu.VMEM((19, depth, FIRST + width + 8, lanes), jnp.float32),
            pltpu.VMEM((19, depth, width, lanes), jnp.bfloat16),
            pltpu.VMEM((2, depth * width, 3 * lanes), jnp.bfloat16),
            pltpu.VMEM((2, 2, width, 3 * lanes), jnp.bfloat16),
            pltpu.VMEM((2, 5, width, lanes), jnp.bfloat16),
            pltpu.VMEM((EXT, lanes), jnp.float32),
            pltpu.VMEM((depth, lanes), jnp.float32),
            pltpu.SemaphoreType.DMA((4,)),
        ],
        compiler_params=params(),
        cost_estimate=cost(5),
        name="step",
    )(*parts, sums, mag_in, mag_out, segments, *notes, *picks)


def arrive_kernel(next_in, first, second, arrived_hbm, next_hbm, force_ref, arrived, sems):
    depth = next_hbm.shape[1]
    odd = is_odd("span")
    shares = pltpu.make_async_copy(arrived_hbm, arrived, sems.at[10])
    shares.start()

    def place(below, above):
        copies = []
        for source, wanted, z in ((below, RISING, 0), (above, FALLING, depth - 1)):
            for index, q in enumerate(wanted):
                copies.append(
                    pltpu.make_async_copy(source.at[index], next_hbm.at[q, z], sems.at[len(copies)])
                )
                copies[-1].start()
        for copy in copies:
            copy.wait()

    @pl.when(odd)
    def _():
        place(first, second)

    @pl.when(jnp.logical_not(odd))
    def _():
        place(second, first)

    shares.wait()
    force_ref[...] = jnp.sum(arrived[...], axis=0)


def arrive(populations_next, first, second, arrived):
    hbm = pl.BlockSpec(memory_space=pl.ANY)
    return pl.pallas_call(
        arrive_kernel,
        out_shape=(
            full(populations_next.shape, jnp.bfloat16),
            full(arrived.shape[1:], jnp.float32),
        ),
        in_specs=[hbm] + in_vmem(2) + [hbm],
        out_specs=(hbm, in_vmem(1)[0]),
        input_output_aliases={0: 0},
        scratch_shapes=[
            pltpu.VMEM(arrived.shape, jnp.float32),
            pltpu.SemaphoreType.DMA((11,)),
        ],
        compiler_params=params(),
        cost_estimate=cost(0.5),
        name="arrive",
    )(populations_next, first, second, arrived)


def local(populations, cell_index, marker_weight, segment_id):
    owners = lax.axis_size("span") * lax.axis_size("cross")
    cells, weights, segments = cell_index.T, marker_weight.T, segment_id[None, :]
    vel, *lines = block_moments(populations)
    lines = swap(*lines, "cross")
    planes = swap(*edge_planes(vel, *lines, cells, weights, segments), "span")
    partial, mag_in = inner_sums(vel, *lines)
    sums, mag_out = outer_sums(vel, *lines, *planes, partial)
    faces = swap(*face_rows(populations, partial), "cross")
    parts = ready(populations, *faces, sums)
    rows, width = populations.shape[1] * populations.shape[2], populations.shape[2]
    count = lax.axis_size("span")
    if count & (count - 1):
        sums = lax.psum(sums, "span")
        picks = marker_picks(cells, weights, segments, planes, sums, rows, width, owners)
    else:
        distance = 1
        while distance < count:
            pairs = [(i, i ^ distance) for i in range(count)]
            other = lax.ppermute(sums, "span", pairs)
            if distance == 2:
                picks = marker_picks(cells, weights, segments, planes, sums, rows, width, owners)
                sums, picks = lax.optimization_barrier((sums + other, picks))
            else:
                sums = sums + other
            distance *= 2
    moved, eddy_coeff, packed, *leaving = step(
        parts, sums, mag_in, mag_out, segments, planes, picks
    )
    arrived = lax.all_to_all(packed, ("span", "cross"), 0, 0)
    populations_next, segment_force = arrive(moved, *swap(*leaving, "span"), arrived)
    return (populations_next, eddy_coeff, segment_force)


def solution(mesh):
    in_specs = (
        P(None, "span", "cross", None),
        P(("span", "cross"), None),
        P(("span", "cross"), None),
        P(("span", "cross")),
    )
    out_specs = (P(None, "span", "cross", None), P("cross", None), P(None, ("span", "cross")))
    return jax.shard_map(local, mesh=mesh, in_specs=in_specs, out_specs=out_specs, check_vma=False)
```

```python
import functools

import jax
import jax.numpy as jnp
from jax import lax
from jax.experimental import pallas as pl
from jax.experimental.pallas import tpu as pltpu
from jax.sharding import PartitionSpec as P

SEG_DEV = 8
LANES = 128
HALO = 3
EXT = 40
PAD = 56
OWN = 11
TOP = 8
CHUNKS = (8, 16, 24, 32, 40)
VMEM = 28 * 1024 * 1024

eps_sum = 1e-06
base_visc = 0.005

VELOCITIES = [
    [0, 0, 0],
    [1, 0, 0],
    [-1, 0, 0],
    [0, 1, 0],
    [0, -1, 0],
    [0, 0, 1],
    [0, 0, -1],
    [1, 1, 0],
    [-1, -1, 0],
    [1, -1, 0],
    [-1, 1, 0],
    [1, 0, 1],
    [-1, 0, -1],
    [1, 0, -1],
    [-1, 0, 1],
    [0, 1, 1],
    [0, -1, -1],
    [0, 1, -1],
    [0, -1, 1],
]


def swap(first, second, axis):
    count = lax.axis_size(axis)
    near = [(i, i ^ 1) for i in range(count)]
    other = [(i, (i + 1 if i % 2 else i - 1) % count) for i in range(count)]
    return lax.ppermute(first, axis, near), lax.ppermute(second, axis, other)


def is_odd(axis):
    return lax.rem(lax.axis_index(axis), 2) == 1


def send_pair(axis, upwards, downwards, first, second):
    odd = is_odd(axis)

    @pl.when(odd)
    def _():
        first[...] = downwards
        second[...] = upwards

    @pl.when(jnp.logical_not(odd))
    def _():
        first[...] = upwards
        second[...] = downwards


def below_above(axis, first, second):
    odd = is_odd(axis)
    return jnp.where(odd, first, second), jnp.where(odd, second, first)


def full(shape, dtype):
    return jax.ShapeDtypeStruct(shape, dtype)


def in_vmem(count):
    return [pl.BlockSpec(memory_space=pltpu.VMEM)] * count


def params():
    return pltpu.CompilerParams(vmem_limit_bytes=VMEM)


def cost(micros):
    return pl.CostEstimate(flops=0, bytes_accessed=int(micros * 3.6e6), transcendentals=0)


def plus(array):
    return pltpu.roll(array, LANES - 1, 1)


def minus(array):
    return pltpu.roll(array, 1, 1)


STEP = 2.0**-15


def encode(value):
    return jnp.round(value * (1.0 / STEP)).astype(jnp.int32).astype(jnp.int16)


def decode(coded):
    return coded.astype(jnp.int32).astype(jnp.float32) * STEP


def split(value):
    high = value.astype(jnp.bfloat16)
    return high, (value - high.astype(jnp.float32)).astype(jnp.bfloat16)


def moments_kernel(pops, vel_ref, first, second, rows):
    depth, width = pops.shape[1:3]

    def plane(z, carry):
        for half in range(width // 16):
            at = pl.ds(16 * half, 16)
            f = [pops[q, z, at, :].astype(jnp.float32) for q in range(19)]
            flux = [0.0, 0.0, 0.0]
            density = f[0]
            for q in range(1, 19, 2):
                even, odd = f[q] + f[q + 1], f[q] - f[q + 1]
                density = density + even
                for dim in range(3):
                    sign = VELOCITIES[q][dim]
                    if sign:
                        flux[dim] = flux[dim] + odd if sign > 0 else flux[dim] - odd
            inverse = 1.0 / density
            for dim in range(3):
                speed = flux[dim] * inverse
                vel_ref[dim, z, at, :] = speed
                for k in range(HALO):
                    if half == 0:
                        rows[0, dim * HALO + k, pl.ds(z, 1), :] = speed[k : k + 1]
                    if half == width // 16 - 1:
                        rows[1, dim * HALO + k, pl.ds(z, 1), :] = speed[15 - k : 16 - k]
        return carry

    lax.fori_loop(0, depth, plane, 0)
    send_pair("cross", encode(rows[1]), encode(rows[0]), first, second)


def block_moments(populations):
    _, depth, width, lanes = populations.shape
    edge = full((3 * HALO, depth, lanes), jnp.int16)
    return pl.pallas_call(
        moments_kernel,
        out_shape=(full((3, depth, width, lanes), jnp.float32), edge, edge),
        in_specs=in_vmem(1),
        out_specs=tuple(in_vmem(3)),
        scratch_shapes=[pltpu.VMEM((2, 3 * HALO, depth, lanes), jnp.float32)],
        compiler_params=params(),
        cost_estimate=cost(1),
        name="moments",
    )(populations)


def decode_rows(first, second, rows):
    rows[0], rows[1] = below_above("cross", decode(first[...]), decode(second[...]))


def place_plane(ext, p, vel_ref, rows, z):
    width = vel_ref.shape[2]
    for dim in range(3):
        ext[dim, p, pl.ds(OWN, width), :] = vel_ref[dim, z]
        for k in range(HALO):
            line = pl.ds(z, 1)
            ext[dim, p, pl.ds(OWN - 1 - k, 1), :] = rows[0, dim * HALO + k, line, :]
            ext[dim, p, pl.ds(OWN + width + k, 1), :] = rows[1, dim * HALO + k, line, :]


TALL = 40


def edges_kernel(
    vel_ref,
    low_ref,
    high_ref,
    cell_ref,
    weight_ref,
    segment_ref,
    first,
    second,
    rows,
    planes,
    note,
    coded,
):
    depth, width = vel_ref.shape[1:3]
    taps = cell_ref.shape[0]
    decode_rows(low_ref, high_ref, rows)
    fixed = weight_ref[...] * 2.0**16
    coarse = jnp.round(fixed)
    note[...] = jnp.zeros_like(note)
    note[pl.ds(0, taps), :] = cell_ref[...].astype(jnp.float32) - 2.0**15
    note[pl.ds(taps, taps), :] = coarse
    note[pl.ds(2 * taps, taps), :] = jnp.round((fixed - coarse) * 2.0**15)
    note[pl.ds(3 * taps, 1), :] = segment_ref[...].astype(jnp.float32)
    for side, pair in enumerate(((0, 1), (depth - 1, depth - 2))):
        planes[...] = jnp.zeros_like(planes)
        for dim in range(3):
            for index, z in enumerate(pair):
                slot = 2 * dim + index
                planes[slot, pl.ds(HALO, width), :] = vel_ref[dim, z]
                for k in range(HALO):
                    line = pl.ds(z, 1)
                    planes[slot, pl.ds(HALO - 1 - k, 1), :] = rows[0, dim * HALO + k, line, :]
                    planes[slot, pl.ds(HALO + width + k, 1), :] = rows[1, dim * HALO + k, line, :]
        coded[side, pl.ds(0, 6)] = encode(planes[...])
        coded[side, 6] = note[...].astype(jnp.int32).astype(jnp.int16)
    send_pair("span", coded[1], coded[0], first, second)


def edge_planes(vel, low, high, cells, weights, segments):
    pair = full((7, TALL, LANES), jnp.int16)
    return pl.pallas_call(
        edges_kernel,
        out_shape=(pair, pair),
        in_specs=in_vmem(6),
        out_specs=tuple(in_vmem(2)),
        scratch_shapes=[
            pltpu.VMEM((2, 3 * HALO, vel.shape[1], LANES), jnp.float32),
            pltpu.VMEM((6, TALL, LANES), jnp.float32),
            pltpu.VMEM((TALL, LANES), jnp.float32),
            pltpu.VMEM((2, 7, TALL, LANES), jnp.int16),
        ],
        compiler_params=params(),
        cost_estimate=cost(0.2),
        name="edges",
    )(vel, low, high, cells, weights, segments)


def plane_loop(start, stop, body, carry, most):
    count = stop - start
    step = max(size for size in range(1, most + 1) if count % size == 0)

    def block(index, carry):
        for shift in range(step):
            carry = body(start + index * step + shift, carry)
        return carry

    if count == step:
        return block(0, carry)
    return lax.fori_loop(0, count // step, block, carry)


def strain_parts(ref, p, row, before, here, after):
    grads = [
        (
            plus(here[dim]) - minus(here[dim]),
            ref[dim, p, pl.ds(row + 1, 8), :] - ref[dim, p, pl.ds(row - 1, 8), :],
            after[dim] - before[dim],
        )
        for dim in range(3)
    ]
    parts = [
        grads[0][0],
        grads[1][1],
        grads[2][2],
        grads[0][1] + grads[1][0],
        grads[0][2] + grads[2][0],
        grads[1][2] + grads[2][1],
    ]
    straight = parts[0] * parts[0] + parts[1] * parts[1] + parts[2] * parts[2]
    mixed = parts[3] * parts[3] + parts[4] * parts[4] + parts[5] * parts[5]
    return parts, jnp.sqrt(0.5 * straight + 0.25 * mixed)


def weigh(low, middle, high):
    return (low + high) + (middle + middle)


PAIRS = ((0, 0), (1, 1), (2, 2), (0, 1), (0, 2), (1, 2))


def three(ref, p, rows):
    return [ref[dim, p, rows, :] for dim in range(3)]


def model_sums(planes, ext, hat, zsum, zvel, acc_ref, store_mag):
    for row in CHUNKS:
        rows = pl.ds(row, 8)

        def first_pass(p, carry):
            before, here, lag, last = carry
            after = three(ext, p + 1, rows)
            parts, size = strain_parts(ext, p, row, before, here, after)
            store_mag(p, row, size)
            prods = [size * part for part in parts] + [here[i] * here[j] for i, j in PAIRS]
            for k in range(12):
                zsum[k, p - 1, rows, :] = lag[k] + prods[k]
            for dim in range(3):
                zvel[dim, p, rows, :] = weigh(before[dim], here[dim], after[dim])
            lag = [last[k] + (prods[k] + prods[k]) for k in range(12)]
            return here, after, lag, prods

        none = [jnp.zeros((8, LANES), jnp.float32)] * 12
        carry = (three(ext, 0, rows), three(ext, 1, rows), none, none)
        plane_loop(1, planes - 1, first_pass, carry, 7)

    def second_pass(p, carry):
        for row in CHUNKS:
            for dim in range(3):
                line = weigh(*[zvel[dim, p, pl.ds(row + shift, 8), :] for shift in (-1, 0, 1)])
                hat[dim, p, pl.ds(row, 8), :] = (1.0 / 64.0) * weigh(minus(line), line, plus(line))
        return carry

    plane_loop(1, planes - 1, second_pass, 0, 2)

    for row in CHUNKS:
        rows = pl.ds(row, 8)

        def third_pass(p, carry):
            before, here, lm, mm = carry
            after = three(hat, p + 1, rows)
            parts, size = strain_parts(hat, p, row, before, here, after)
            size = 256.0 * size
            scaled = [64.0 * speed for speed in here]
            squares = [0.0, 0.0]
            for k, (i, j) in enumerate(PAIRS):
                smooth = []
                for field in (k, 6 + k):
                    line = weigh(
                        *[zsum[field, p, pl.ds(row + shift, 8), :] for shift in (-1, 0, 1)]
                    )
                    smooth.append(weigh(minus(line), line, plus(line)))
                model = smooth[0] - size * parts[k]
                lm = lm + (smooth[1] - scaled[i] * here[j]) * model
                squares[k // 3] = squares[k // 3] + model * model
            return here, after, lm, mm + (squares[0] + 0.5 * squares[1])

        none = jnp.zeros((8, LANES), jnp.float32)
        carry = (three(hat, 1, rows), three(hat, 2, rows), none, none)
        _, _, lm, mm = plane_loop(2, planes - 2, third_pass, carry, 6)
        out = pl.ds(row - TOP, 8)
        acc_ref[0, out, :] += (1.0 / 4096.0) * lm
        acc_ref[1, out, :] += (1.0 / 4096.0) * mm


def inner_kernel(vel_ref, low_ref, high_ref, acc_ref, mag_ref, ext, hat, zsum, zvel, rows):
    depth = vel_ref.shape[1]
    decode_rows(low_ref, high_ref, rows)

    def assemble(p, carry):
        place_plane(ext, p, vel_ref, rows, p)
        return carry

    lax.fori_loop(0, depth, assemble, 0)
    acc_ref[...] = jnp.zeros_like(acc_ref)

    def store_mag(p, row, size):
        mag_ref[p - 1, pl.ds(row - TOP, 8), :] = size

    model_sums(depth, ext, hat, zsum, zvel, acc_ref, store_mag)


def model_scratch(planes, depth):
    return [
        pltpu.VMEM((3, planes, PAD, LANES), jnp.float32),
        pltpu.VMEM((3, planes, PAD, LANES), jnp.float32),
        pltpu.VMEM((12, planes, PAD, LANES), jnp.float32),
        pltpu.VMEM((3, planes, PAD, LANES), jnp.float32),
        pltpu.VMEM((2, 3 * HALO, depth, LANES), jnp.float32),
    ]


def inner_sums(vel, low, high):
    depth = vel.shape[1]
    return pl.pallas_call(
        inner_kernel,
        out_shape=(
            full((2, EXT, LANES), jnp.float32),
            full((depth - 2, EXT, LANES), jnp.float32),
        ),
        in_specs=in_vmem(3),
        out_specs=tuple(in_vmem(2)),
        scratch_shapes=model_scratch(depth, depth),
        compiler_params=params(),
        cost_estimate=cost(5),
        name="inner_sums",
    )(vel, low, high)


def outer_kernel(
    vel_ref,
    low_ref,
    high_ref,
    first_ref,
    second_ref,
    partial_ref,
    sums_ref,
    mag_ref,
    ext,
    hat,
    zsum,
    zvel,
    rows,
    acc,
):
    depth, width = vel_ref.shape[1:3]
    decode_rows(low_ref, high_ref, rows)
    acc[...] = partial_ref[...]
    below, above = below_above(
        "span", decode(first_ref[pl.ds(0, 6)]), decode(second_ref[pl.ds(0, 6)])
    )
    for side, (message, places, start) in enumerate(
        ((below, (1, 0), 0), (above, (4, 5), depth - 4))
    ):
        for index in range(4):
            place_plane(ext, index + (2 if side == 0 else 0), vel_ref, rows, start + index)
        for dim in range(3):
            for index, p in enumerate(places):
                ext[dim, p, pl.ds(OWN - HALO, TALL), :] = message[2 * dim + index]

        def store_mag(p, row, size):
            mag_ref[4 * side + p - 1, pl.ds(row - TOP, 8), :] = size

        model_sums(6, ext, hat, zsum, zvel, acc, store_mag)
    lines = width + 2
    sums_ref[...] = jnp.zeros_like(sums_ref)
    for index in range(2):
        sums_ref[pl.ds(index * lines, lines), :] = acc[index, pl.ds(OWN - TOP - 1, lines), :]


def outer_sums(vel, low, high, below, above, partial):
    depth, width = vel.shape[1:3]
    return pl.pallas_call(
        outer_kernel,
        out_shape=(
            full((-(-2 * (width + 2) // 8) * 8, LANES), jnp.float32),
            full((8, EXT, LANES), jnp.float32),
        ),
        in_specs=in_vmem(6),
        out_specs=tuple(in_vmem(2)),
        scratch_shapes=model_scratch(6, depth) + [pltpu.VMEM((2, EXT, LANES), jnp.float32)],
        compiler_params=params(),
        cost_estimate=cost(2),
        name="outer_sums",
    )(vel, low, high, below, above, partial)


def rows_kernel(pops, after_this, first, second, rows):
    depth, width = pops.shape[1:3]

    def plane(z, carry):
        for q in range(19):
            low = pops[q, z, pl.ds(0, 16), :].astype(jnp.float32)
            high = pops[q, z, pl.ds(width - 16, 16), :].astype(jnp.float32)
            rows[0, q, pl.ds(z, 1), :] = low[:1]
            rows[1, q, pl.ds(z, 1), :] = high[15:]
        return carry

    lax.fori_loop(0, depth, plane, 0)
    send_pair(
        "cross", rows[1].astype(jnp.bfloat16), rows[0].astype(jnp.bfloat16), first, second
    )


def face_rows(populations, after_this):
    _, depth, width, lanes = populations.shape
    edge = full((19, depth, lanes), jnp.bfloat16)
    return pl.pallas_call(
        rows_kernel,
        out_shape=(edge, edge),
        in_specs=in_vmem(1) + [pl.BlockSpec(memory_space=pl.ANY)],
        out_specs=tuple(in_vmem(2)),
        scratch_shapes=[pltpu.VMEM((2, 19, depth, lanes), jnp.float32)],
        compiler_params=params(),
        cost_estimate=cost(0.5),
        name="face_rows",
    )(populations, after_this)


def relax_parts(f):
    even = {q: f[q] + f[q + 1] for q in range(1, 19, 2)}
    odd = {q: f[q] - f[q + 1] for q in range(1, 19, 2)}
    x_xy, x_xz = odd[7] + odd[9], odd[11] + odd[13]
    y_yz, y_xy = odd[15] + odd[17], odd[7] - odd[9]
    z_xz, z_yz = odd[11] - odd[13], odd[15] - odd[17]
    flux, up, down, axis_odd = [], [], [], []
    for first, second, along in ((x_xy, x_xz, 1), (y_yz, y_xy, 3), (z_xz, z_yz, 5)):
        sides = first + second
        total = odd[along] + sides
        heat = 0.15 * (sides - (2.0 / 3.0) * total)
        twist = (1.98 / 8.0) * (first - second)
        flux.append(total)
        up.append(heat + twist)
        down.append(heat - twist)
        axis_odd.append(4.0 * heat)
    a, b, c = even[7] + even[9], even[11] + even[13], even[15] + even[17]
    axes = even[1] + even[3] + even[5]
    diagonals = a + b + c
    density = f[0] + axes + diagonals
    inverse = 1.0 / density
    speed = [total * inverse for total in flux]
    square = [total * part for total, part in zip(flux, speed)]
    energy = square[0] + square[1] + square[2]
    d_e = (1.19 / 126.0) * (diagonals - f[0] - energy)
    d_eps = (1.4 / 252.0) * (9.0 * f[0] - 7.0 * axes - 2.0 * diagonals + 5.5 * energy)
    ax_n, dg_n, eq_n = 3.0 * even[1] - axes, diagonals - 3.0 * c, 3.0 * square[0] - energy
    ax_w, dg_w, eq_w = even[3] - even[5], a - b, square[1] - square[2]
    d_pn = (1.4 / 72.0) * (dg_n - 2.0 * ax_n + 0.5 * eq_n)
    d_pw = (1.4 / 24.0) * (dg_w - 2.0 * ax_w + 0.5 * eq_w)
    shear = [
        (1.0 / 36.0) * (ax_n + dg_n - eq_n),
        (1.0 / 12.0) * (ax_w + dg_w - eq_w),
        0.25 * (even[7] - even[9] - flux[0] * speed[1]),
        0.25 * (even[11] - even[13] - flux[0] * speed[2]),
        0.25 * (even[15] - even[17] - flux[1] * speed[2]),
    ]
    base_axis = 11.0 * d_e + 4.0 * d_eps
    base_diag = -8.0 * d_e - d_eps
    base = [None] * 19
    base[0] = f[0] + (30.0 * d_e - 12.0 * d_eps)
    rest = base_axis - 2.0 * d_pn
    for q, change, skew in (
        (1, base_axis + 4.0 * d_pn, axis_odd[0]),
        (3, rest + 2.0 * d_pw, axis_odd[1]),
        (5, rest - 2.0 * d_pw, axis_odd[2]),
    ):
        base[q] = f[q] + (change + skew)
        base[q + 1] = f[q + 1] + (change - skew)
    rest = base_diag - d_pn
    for q, change, one, two in (
        (7, rest - d_pw, up[0], down[1]),
        (11, rest + d_pw, down[0], up[2]),
        (15, base_diag + 2.0 * d_pn, up[1], down[2]),
    ):
        same, other = one + two, one - two
        base[q] = f[q] + (change - same)
        base[q + 1] = f[q + 1] + (change + same)
        base[q + 2] = f[q + 2] + (change - other)
        base[q + 3] = f[q + 3] + (change + other)
    return base, shear


def shear_changes(shear, rate):
    n, w, xy, xz, yz = [rate * part for part in shear]
    lean = n + w
    tilt = n - w
    twice = n + n
    changes = [None] * 19
    changes[1] = changes[2] = -twice
    changes[3] = changes[4] = tilt
    changes[5] = changes[6] = lean
    changes[7] = changes[8] = -(lean + xy)
    changes[9] = changes[10] = xy - lean
    changes[11] = changes[12] = -(tilt + xz)
    changes[13] = changes[14] = xz - tilt
    changes[15] = changes[16] = twice - yz
    changes[17] = changes[18] = twice + yz
    return changes


def relax_rate(eddy, size):
    return 1.0 / (0.5 + 3.0 * (base_visc + eddy * size))


BEFORE = [q for q in range(19) if VELOCITIES[q][1] > 0]
AFTER = [q for q in range(19) if VELOCITIES[q][1] < 0]
RISING = [q for q in range(19) if VELOCITIES[q][2] > 0]
FALLING = [q for q in range(19) if VELOCITIES[q][2] < 0]
FIRST = 8


def ready_kernel(pops, first, second, after_this, base_ref, shear_ref, edge_ref, edge_shear):
    depth, width = pops.shape[1:3]
    rows = [
        below_above("cross", first[q].astype(jnp.float32), second[q].astype(jnp.float32))
        for q in range(19)
    ]
    for side, wanted in enumerate((BEFORE, AFTER)):
        base, shear = relax_parts([pair[side] for pair in rows])
        for index, q in enumerate(wanted):
            edge_ref[side, index] = base[q]
        for k in range(5):
            edge_shear[side, k] = shear[k]

    def plane(z, carry):
        for half in range(width // 16):
            rows = pl.ds(16 * half, 16)
            base, shear = relax_parts([pops[q, z, rows, :].astype(jnp.float32) for q in range(19)])
            for q in range(19):
                base_ref[q, z, rows, :] = base[q]
            for k in range(5):
                shear_ref[k, z, rows, :] = shear[k]
        return carry

    lax.fori_loop(0, depth, plane, 0)


def ready(populations, before, after, after_this):
    _, depth, width, lanes = populations.shape
    return pl.pallas_call(
        ready_kernel,
        out_shape=(
            full((19, depth, width, lanes), jnp.float32),
            full((5, depth, width, lanes), jnp.float32),
            full((2, 5, depth, lanes), jnp.float32),
            full((2, 5, depth, lanes), jnp.float32),
        ),
        in_specs=in_vmem(3) + [pl.BlockSpec(memory_space=pl.ANY)],
        out_specs=tuple(in_vmem(4)),
        compiler_params=params(),
        cost_estimate=cost(2.5),
        name="ready",
    )(populations, before, after, after_this)


def table_rows(table, at, low_at, flux):
    for dim in range(3):
        coarse, fine = split(flux[dim])
        table[at, dim * LANES : (dim + 1) * LANES] = coarse
        table[low_at, dim * LANES : (dim + 1) * LANES] = fine


def add_flux(flux, q, moved):
    for dim in range(3):
        sign = VELOCITIES[q][dim]
        if sign:
            flux[dim] = flux[dim] + moved if sign > 0 else flux[dim] - moved


def marker_force(table, picks, lanes, weights, taps):
    lane_of = lax.broadcasted_iota(jnp.int32, (LANES, lanes[0].shape[1]), 0)
    picked = lax.dot_general(
        table,
        jnp.concatenate(picks, axis=1),
        (((0,), (0,)), ((), ())),
        preferred_element_type=jnp.float32,
    )
    markers = lanes[0].shape[1]
    force = [0.0, 0.0, 0.0]
    for tap, (lane, weight) in enumerate(zip(lanes, weights)):
        mask = jnp.where(lane_of == lane, -weight, 0.0)
        at = slice(tap * markers, (tap + 1) * markers)
        for dim in range(3):
            force[dim] = force[dim] + picked[dim * LANES : (dim + 1) * LANES, at] * mask
        if (tap + 1) % taps == 0:
            yield [jnp.sum(part, axis=0, keepdims=True) for part in force]
            force = [0.0, 0.0, 0.0]


def step_kernel(
    base_ref,
    shear_ref,
    edge_ref,
    edge_shear,
    sums_ref,
    mag_in_ref,
    mag_out_ref,
    cell_ref,
    weight_ref,
    segment_ref,
    note_first,
    note_second,
    next_hbm,
    eddy_ref,
    partial_ref,
    first_ref,
    second_ref,
    post,
    nexts,
    table,
    face_table,
    faces,
    eddy,
    line,
    out_sems,
):
    depth, width = shear_ref.shape[1:3]
    lines = width + 2
    part = depth // 4
    eddy[...] = jnp.zeros_like(eddy)
    eddy[pl.ds(OWN - TOP - 1, lines), :] = jnp.maximum(
        sums_ref[pl.ds(0, lines), :] / (sums_ref[pl.ds(lines, lines), :] + eps_sum), 0.0
    )
    eddy_ref[...] = eddy[pl.ds(OWN - TOP, width), :]

    for side, (wanted, row, place) in enumerate(
        ((BEFORE, OWN - TOP - 1, FIRST - 1), (AFTER, OWN - TOP + width, FIRST + width))
    ):
        for z in range(depth):
            if z == 0:
                size = mag_out_ref[1, pl.ds(row, 1), :]
            elif z == depth - 1:
                size = mag_out_ref[6, pl.ds(row, 1), :]
            else:
                size = mag_in_ref[z - 1, pl.ds(row, 1), :]
            line[pl.ds(z, 1), :] = size
        rate = relax_rate(eddy[pl.ds(row, 1), :], line[...])
        changes = shear_changes([edge_shear[side, k] for k in range(5)], rate)
        for index, q in enumerate(wanted):
            out = edge_ref[side, index] + changes[q]
            for z in range(depth):
                post[q, z, pl.ds(place, 1), :] = out[z : z + 1]

    def collide(z, size_ref, at):
        for half in range(width // 16):
            rows = pl.ds(16 * half, 16)
            around = pl.ds(OWN - TOP + 16 * half, 16)
            rate = relax_rate(eddy[around, :], size_ref[at, around, :])
            changes = shear_changes([shear_ref[k, z, rows, :] for k in range(5)], rate)
            for q in range(19):
                value = base_ref[q, z, rows, :]
                if q:
                    value = value + changes[q]
                post[q, z, pl.ds(FIRST + 16 * half, 16), :] = value

    def inner(z, carry):
        collide(z, mag_in_ref, z - 1)
        return carry

    collide(0, mag_out_ref, 1)
    collide(depth - 1, mag_out_ref, 6)
    lax.fori_loop(1, depth - 1, inner, 0)

    def shifted(q, z, half):
        shift_x, shift_y, _ = VELOCITIES[q]
        piece = post[q, z, pl.ds(FIRST + 16 * half - shift_y, 16), :]
        if shift_x:
            piece = minus(piece) if shift_x > 0 else plus(piece)
        return piece.astype(jnp.bfloat16)

    def run(z, leave_out=()):
        for half in range(width // 16):
            flux = [0.0, 0.0, 0.0]
            for q in range(19):
                if q in leave_out:
                    continue
                moved = shifted(q, z - VELOCITIES[q][2], half)
                nexts[q, z, pl.ds(16 * half, 16), :] = moved
                if q:
                    add_flux(flux, q, moved.astype(jnp.float32))
            row = pl.multiple_of(z * width + 16 * half, 16)
            low_row = pl.multiple_of((depth + z) * width + 16 * half, 16)
            table_rows(table, pl.ds(row, 16), pl.ds(low_row, 16), flux)

    def run_inner(z, carry):
        run(z)
        return carry

    for side, (wanted, z) in enumerate(((RISING, depth - 1), (FALLING, 0))):
        for half in range(width // 16):
            rows = pl.ds(16 * half, 16)
            flux = [0.0, 0.0, 0.0]
            for index, q in enumerate(wanted):
                moved = shifted(q, z, half)
                faces[side, index, rows, :] = moved
                add_flux(flux, q, moved.astype(jnp.float32))
            row = side * width + 16 * half
            table_rows(face_table, pl.ds(row, 16), pl.ds(2 * width + row, 16), flux)
    send_pair("span", faces[0], faces[1], first_ref, second_ref)

    outs = []
    for index in range(4):
        start, stop = index * part, (index + 1) * part
        if index == 0:
            run(0, RISING)
            start += 1
        if index == 3:
            run(depth - 1, FALLING)
            stop -= 1
        lax.fori_loop(start, stop, run_inner, 0)
        place = pl.ds(index * part, part)
        outs.append(
            pltpu.make_async_copy(nexts.at[:, place], next_hbm.at[:, place], out_sems.at[index])
        )
        outs[-1].start()

    owners = partial_ref.shape[0]
    taps, markers = cell_ref.shape
    cells_all = depth * width
    note_below, note_above = below_above(
        "span", note_first[6].astype(jnp.int32), note_second[6].astype(jnp.int32)
    )

    def one_hot(rows, period, wanted):
        row_of = lax.broadcasted_iota(jnp.int32, (period, markers), 0)
        picks = []
        for tap in range(taps):
            hit = jnp.where(row_of == wanted[tap : tap + 1, :], 1.0, 0.0).astype(jnp.bfloat16)
            picks.append(jnp.concatenate([hit] * (rows // period), axis=0))
        return picks

    def row_lane(cells):
        return lax.shift_right_logical(cells, 7), lax.bitwise_and(cells, LANES - 1)

    def each(array):
        return [array[tap : tap + 1, :] for tap in range(taps)]

    row, lane = row_lane(cell_ref[...])
    forces = list(
        marker_force(
            table[...],
            one_hot(2 * cells_all, cells_all, row),
            each(lane),
            each(weight_ref[...]),
            taps,
        )
    )
    segments = [segment_ref[...]]
    picks, lanes, weights = [], [], []
    for side, note in enumerate((note_above, note_below)):
        row, lane = row_lane(note[:taps] + 2**15)
        row = row - side * (cells_all - width)
        inside = jnp.logical_and(row >= 0, row < width)
        picks += one_hot(4 * width, 2 * width, jnp.where(inside, row + side * width, -1))
        lanes += each(lane)
        weights += each(
            note[taps : 2 * taps].astype(jnp.float32) * 2.0**-16
            + note[2 * taps : 3 * taps].astype(jnp.float32) * 2.0**-31
        )
        segments.append(note[3 * taps : 3 * taps + 1])
    forces += list(marker_force(face_table[...], picks, lanes, weights, taps))

    owner_of = lax.broadcasted_iota(jnp.int32, (owners, markers), 0)
    place_of = lax.broadcasted_iota(jnp.int32, (SEG_DEV, markers), 0)
    mine, spread = [], []
    for force, segment in zip(forces, segments):
        hit = jnp.where(owner_of == lax.shift_right_logical(segment, 3), 1.0, 0.0)
        mine.append(hit.astype(jnp.bfloat16))
        place = place_of == lax.bitwise_and(segment, SEG_DEV - 1)
        spread.append(
            jnp.concatenate([jnp.where(place, part, 0.0) for part in force], axis=0)
        )
    mine, rest = jnp.concatenate(mine, axis=1), jnp.concatenate(spread, axis=1)
    rest = jnp.concatenate([rest, jnp.zeros((LANES - 3 * SEG_DEV, 3 * markers), jnp.float32)], axis=0)
    totals = 0.0
    for _ in range(3):
        coarse = rest.astype(jnp.bfloat16)
        rest = rest - coarse.astype(jnp.float32)
        totals = totals + lax.dot_general(
            mine, coarse, (((1,), (1,)), ((), ())), preferred_element_type=jnp.float32
        )
    partial_ref[:, 0, :] = totals
    for copy in outs:
        copy.wait()


def step(parts, sums, mag_in, mag_out, cells, weights, segments, notes, owners):
    _, depth, width, lanes = parts[0].shape
    face = full((5, width, lanes), jnp.bfloat16)
    return pl.pallas_call(
        step_kernel,
        out_shape=(
            full((19, depth, width, lanes), jnp.bfloat16),
            full((width, lanes), jnp.float32),
            full((owners, 1, lanes), jnp.float32),
            face,
            face,
        ),
        in_specs=in_vmem(12),
        out_specs=(pl.BlockSpec(memory_space=pl.ANY),) + tuple(in_vmem(4)),
        scratch_shapes=[
            pltpu.VMEM((19, depth, FIRST + width + 8, lanes), jnp.float32),
            pltpu.VMEM((19, depth, width, lanes), jnp.bfloat16),
            pltpu.VMEM((2 * depth * width, 3 * lanes), jnp.bfloat16),
            pltpu.VMEM((4 * width, 3 * lanes), jnp.bfloat16),
            pltpu.VMEM((2, 5, width, lanes), jnp.bfloat16),
            pltpu.VMEM((EXT, lanes), jnp.float32),
            pltpu.VMEM((depth, lanes), jnp.float32),
            pltpu.SemaphoreType.DMA((4,)),
        ],
        compiler_params=params(),
        cost_estimate=cost(5),
        name="step",
    )(*parts, sums, mag_in, mag_out, cells, weights, segments, *notes)


def arrive_kernel(next_in, first, second, arrived_hbm, next_hbm, force_ref, arrived, sems):
    depth = next_hbm.shape[1]
    odd = is_odd("span")
    shares = pltpu.make_async_copy(arrived_hbm, arrived, sems.at[10])
    shares.start()

    def place(below, above):
        copies = []
        for source, wanted, z in ((below, RISING, 0), (above, FALLING, depth - 1)):
            for index, q in enumerate(wanted):
                copies.append(
                    pltpu.make_async_copy(source.at[index], next_hbm.at[q, z], sems.at[len(copies)])
                )
                copies[-1].start()
        for copy in copies:
            copy.wait()

    @pl.when(odd)
    def _():
        place(first, second)

    @pl.when(jnp.logical_not(odd))
    def _():
        place(second, first)

    shares.wait()
    total = jnp.sum(arrived[:, 0, :], axis=0, keepdims=True)
    for dim in range(3):
        force_ref[pl.ds(dim, 1), :] = total[:, dim * SEG_DEV : (dim + 1) * SEG_DEV]


def arrive(populations_next, first, second, arrived):
    hbm = pl.BlockSpec(memory_space=pl.ANY)
    return pl.pallas_call(
        arrive_kernel,
        out_shape=(
            full(populations_next.shape, jnp.bfloat16),
            full((3, SEG_DEV), jnp.float32),
        ),
        in_specs=[hbm] + in_vmem(2) + [hbm],
        out_specs=(hbm, in_vmem(1)[0]),
        input_output_aliases={0: 0},
        scratch_shapes=[
            pltpu.VMEM(arrived.shape, jnp.float32),
            pltpu.SemaphoreType.DMA((11,)),
        ],
        compiler_params=params(),
        cost_estimate=cost(0.5),
        name="arrive",
    )(populations_next, first, second, arrived)


def local(populations, cell_index, marker_weight, segment_id):
    owners = lax.axis_size("span") * lax.axis_size("cross")
    cells, weights, segments = cell_index.T, marker_weight.T, segment_id[None, :]
    vel, *lines = block_moments(populations)
    lines = swap(*lines, "cross")
    planes = swap(*edge_planes(vel, *lines, cells, weights, segments), "span")
    partial, mag_in = inner_sums(vel, *lines)
    faces = swap(*face_rows(populations, partial), "cross")
    sums, mag_out = outer_sums(vel, *lines, *planes, partial)
    parts = ready(populations, *faces, sums)
    count = lax.axis_size("span")
    if count & (count - 1):
        sums = lax.psum(sums, "span")
    else:
        distance = 1
        while distance < count:
            pairs = [(i, i ^ distance) for i in range(count)]
            sums = sums + lax.ppermute(sums, "span", pairs)
            distance *= 2
    moved, eddy_coeff, packed, *leaving = step(
        parts, sums, mag_in, mag_out, cells, weights, segments, planes, owners
    )
    arrived = lax.all_to_all(packed, ("span", "cross"), 0, 0)
    populations_next, segment_force = arrive(moved, *swap(*leaving, "span"), arrived)
    return (populations_next, eddy_coeff, segment_force)


def solution(mesh):
    in_specs = (
        P(None, "span", "cross", None),
        P(("span", "cross"), None),
        P(("span", "cross"), None),
        P(("span", "cross")),
    )
    out_specs = (P(None, "span", "cross", None), P("cross", None), P(None, ("span", "cross")))
    return jax.shard_map(local, mesh=mesh, in_specs=in_specs, out_specs=out_specs, check_vma=False)
```

```python
import functools

import jax
import jax.numpy as jnp
from jax import lax
from jax.experimental import pallas as pl
from jax.experimental.pallas import tpu as pltpu
from jax.sharding import PartitionSpec as P

SEG_DEV = 8
LANES = 128
HALO = 3
EXT = 40
PAD = 56
OWN = 11
TOP = 8
CHUNKS = (8, 16, 24, 32, 40)
VMEM = 28 * 1024 * 1024

eps_sum = 1e-06
base_visc = 0.005

VELOCITIES = [
    [0, 0, 0],
    [1, 0, 0],
    [-1, 0, 0],
    [0, 1, 0],
    [0, -1, 0],
    [0, 0, 1],
    [0, 0, -1],
    [1, 1, 0],
    [-1, -1, 0],
    [1, -1, 0],
    [-1, 1, 0],
    [1, 0, 1],
    [-1, 0, -1],
    [1, 0, -1],
    [-1, 0, 1],
    [0, 1, 1],
    [0, -1, -1],
    [0, 1, -1],
    [0, -1, 1],
]


def swap(first, second, axis):
    count = lax.axis_size(axis)
    near = [(i, i ^ 1) for i in range(count)]
    other = [(i, (i + 1 if i % 2 else i - 1) % count) for i in range(count)]
    return lax.ppermute(first, axis, near), lax.ppermute(second, axis, other)


def is_odd(axis):
    return lax.rem(lax.axis_index(axis), 2) == 1


def send_pair(axis, upwards, downwards, first, second):
    odd = is_odd(axis)

    @pl.when(odd)
    def _():
        first[...] = downwards
        second[...] = upwards

    @pl.when(jnp.logical_not(odd))
    def _():
        first[...] = upwards
        second[...] = downwards


def below_above(axis, first, second):
    odd = is_odd(axis)
    return jnp.where(odd, first, second), jnp.where(odd, second, first)


def full(shape, dtype):
    return jax.ShapeDtypeStruct(shape, dtype)


def in_vmem(count):
    return [pl.BlockSpec(memory_space=pltpu.VMEM)] * count


def params():
    return pltpu.CompilerParams(vmem_limit_bytes=VMEM)


def cost(micros):
    return pl.CostEstimate(flops=0, bytes_accessed=int(micros * 3.6e6), transcendentals=0)


def plus(array):
    return pltpu.roll(array, LANES - 1, 1)


def minus(array):
    return pltpu.roll(array, 1, 1)


STEP = 2.0**-15


def encode(value):
    return jnp.round(value * (1.0 / STEP)).astype(jnp.int32).astype(jnp.int16)


def decode(coded):
    return coded.astype(jnp.int32).astype(jnp.float32) * STEP


def split(value):
    high = value.astype(jnp.bfloat16)
    return high, (value - high.astype(jnp.float32)).astype(jnp.bfloat16)


def moments_kernel(pops, vel_ref, first, second, rows):
    depth, width = pops.shape[1:3]

    def plane(z, carry):
        for half in range(width // 16):
            at = pl.ds(16 * half, 16)
            f = [pops[q, z, at, :].astype(jnp.float32) for q in range(19)]
            flux = [0.0, 0.0, 0.0]
            density = f[0]
            for q in range(1, 19, 2):
                even, odd = f[q] + f[q + 1], f[q] - f[q + 1]
                density = density + even
                for dim in range(3):
                    sign = VELOCITIES[q][dim]
                    if sign:
                        flux[dim] = flux[dim] + odd if sign > 0 else flux[dim] - odd
            inverse = 1.0 / density
            for dim in range(3):
                speed = flux[dim] * inverse
                vel_ref[dim, z, at, :] = speed
                for k in range(HALO):
                    if half == 0:
                        rows[0, dim * HALO + k, pl.ds(z, 1), :] = speed[k : k + 1]
                    if half == width // 16 - 1:
                        rows[1, dim * HALO + k, pl.ds(z, 1), :] = speed[15 - k : 16 - k]
        return carry

    lax.fori_loop(0, depth, plane, 0)
    send_pair("cross", encode(rows[1]), encode(rows[0]), first, second)


def block_moments(populations):
    _, depth, width, lanes = populations.shape
    edge = full((3 * HALO, depth, lanes), jnp.int16)
    return pl.pallas_call(
        moments_kernel,
        out_shape=(full((3, depth, width, lanes), jnp.float32), edge, edge),
        in_specs=in_vmem(1),
        out_specs=tuple(in_vmem(3)),
        scratch_shapes=[pltpu.VMEM((2, 3 * HALO, depth, lanes), jnp.float32)],
        compiler_params=params(),
        cost_estimate=cost(1),
        name="moments",
    )(populations)


def decode_rows(first, second, rows):
    rows[0], rows[1] = below_above("cross", decode(first[...]), decode(second[...]))


def place_plane(ext, p, vel_ref, rows, z):
    width = vel_ref.shape[2]
    for dim in range(3):
        ext[dim, p, pl.ds(OWN, width), :] = vel_ref[dim, z]
        for k in range(HALO):
            line = pl.ds(z, 1)
            ext[dim, p, pl.ds(OWN - 1 - k, 1), :] = rows[0, dim * HALO + k, line, :]
            ext[dim, p, pl.ds(OWN + width + k, 1), :] = rows[1, dim * HALO + k, line, :]


TALL = 40


def edges_kernel(
    vel_ref,
    low_ref,
    high_ref,
    cell_ref,
    weight_ref,
    segment_ref,
    first,
    second,
    rows,
    planes,
    note,
    coded,
):
    depth, width = vel_ref.shape[1:3]
    taps = cell_ref.shape[0]
    decode_rows(low_ref, high_ref, rows)
    fixed = weight_ref[...] * 2.0**16
    coarse = jnp.round(fixed)
    note[...] = jnp.zeros_like(note)
    note[pl.ds(0, taps), :] = cell_ref[...].astype(jnp.float32) - 2.0**15
    note[pl.ds(taps, taps), :] = coarse
    note[pl.ds(2 * taps, taps), :] = jnp.round((fixed - coarse) * 2.0**15)
    note[pl.ds(3 * taps, 1), :] = segment_ref[...].astype(jnp.float32)
    for side, pair in enumerate(((0, 1), (depth - 1, depth - 2))):
        planes[...] = jnp.zeros_like(planes)
        for dim in range(3):
            for index, z in enumerate(pair):
                slot = 2 * dim + index
                planes[slot, pl.ds(HALO, width), :] = vel_ref[dim, z]
                for k in range(HALO):
                    line = pl.ds(z, 1)
                    planes[slot, pl.ds(HALO - 1 - k, 1), :] = rows[0, dim * HALO + k, line, :]
                    planes[slot, pl.ds(HALO + width + k, 1), :] = rows[1, dim * HALO + k, line, :]
        coded[side, pl.ds(0, 6)] = encode(planes[...])
        coded[side, 6] = note[...].astype(jnp.int32).astype(jnp.int16)
    send_pair("span", coded[1], coded[0], first, second)


def edge_planes(vel, low, high, cells, weights, segments):
    pair = full((7, TALL, LANES), jnp.int16)
    return pl.pallas_call(
        edges_kernel,
        out_shape=(pair, pair),
        in_specs=in_vmem(6),
        out_specs=tuple(in_vmem(2)),
        scratch_shapes=[
            pltpu.VMEM((2, 3 * HALO, vel.shape[1], LANES), jnp.float32),
            pltpu.VMEM((6, TALL, LANES), jnp.float32),
            pltpu.VMEM((TALL, LANES), jnp.float32),
            pltpu.VMEM((2, 7, TALL, LANES), jnp.int16),
        ],
        compiler_params=params(),
        cost_estimate=cost(0.2),
        name="edges",
    )(vel, low, high, cells, weights, segments)


def plane_loop(start, stop, body, carry, most):
    count = stop - start
    step = max(size for size in range(1, most + 1) if count % size == 0)

    def block(index, carry):
        for shift in range(step):
            carry = body(start + index * step + shift, carry)
        return carry

    if count == step:
        return block(0, carry)
    return lax.fori_loop(0, count // step, block, carry)


def strain_parts(ref, p, row, before, here, after):
    grads = [
        (
            plus(here[dim]) - minus(here[dim]),
            ref[dim, p, pl.ds(row + 1, 8), :] - ref[dim, p, pl.ds(row - 1, 8), :],
            after[dim] - before[dim],
        )
        for dim in range(3)
    ]
    parts = [
        grads[0][0],
        grads[1][1],
        grads[2][2],
        grads[0][1] + grads[1][0],
        grads[0][2] + grads[2][0],
        grads[1][2] + grads[2][1],
    ]
    straight = parts[0] * parts[0] + parts[1] * parts[1] + parts[2] * parts[2]
    mixed = parts[3] * parts[3] + parts[4] * parts[4] + parts[5] * parts[5]
    return parts, jnp.sqrt(0.5 * straight + 0.25 * mixed)


def weigh(low, middle, high):
    return (low + high) + (middle + middle)


PAIRS = ((0, 0), (1, 1), (2, 2), (0, 1), (0, 2), (1, 2))


def three(ref, p, rows):
    return [ref[dim, p, rows, :] for dim in range(3)]


def model_sums(planes, ext, hat, zsum, zvel, acc_ref, store_mag):
    for row in CHUNKS:
        rows = pl.ds(row, 8)

        def first_pass(p, carry):
            before, here, lag, last = carry
            after = three(ext, p + 1, rows)
            parts, size = strain_parts(ext, p, row, before, here, after)
            store_mag(p, row, size)
            prods = [size * part for part in parts] + [here[i] * here[j] for i, j in PAIRS]
            for k in range(12):
                zsum[k, p - 1, rows, :] = lag[k] + prods[k]
            for dim in range(3):
                zvel[dim, p, rows, :] = weigh(before[dim], here[dim], after[dim])
            lag = [last[k] + (prods[k] + prods[k]) for k in range(12)]
            return here, after, lag, prods

        none = [jnp.zeros((8, LANES), jnp.float32)] * 12
        carry = (three(ext, 0, rows), three(ext, 1, rows), none, none)
        plane_loop(1, planes - 1, first_pass, carry, 2)

    def second_pass(p, carry):
        for row in CHUNKS:
            for dim in range(3):
                line = weigh(*[zvel[dim, p, pl.ds(row + shift, 8), :] for shift in (-1, 0, 1)])
                hat[dim, p, pl.ds(row, 8), :] = (1.0 / 64.0) * weigh(minus(line), line, plus(line))
        return carry

    plane_loop(1, planes - 1, second_pass, 0, 2)

    for row in CHUNKS:
        rows = pl.ds(row, 8)

        def third_pass(p, carry):
            before, here, lm, mm = carry
            after = three(hat, p + 1, rows)
            parts, size = strain_parts(hat, p, row, before, here, after)
            size = 256.0 * size
            scaled = [64.0 * speed for speed in here]
            squares = [0.0, 0.0]
            for k, (i, j) in enumerate(PAIRS):
                smooth = []
                for field in (k, 6 + k):
                    line = weigh(
                        *[zsum[field, p, pl.ds(row + shift, 8), :] for shift in (-1, 0, 1)]
                    )
                    smooth.append(weigh(minus(line), line, plus(line)))
                model = smooth[0] - size * parts[k]
                lm = lm + (smooth[1] - scaled[i] * here[j]) * model
                squares[k // 3] = squares[k // 3] + model * model
            return here, after, lm, mm + (squares[0] + 0.5 * squares[1])

        none = jnp.zeros((8, LANES), jnp.float32)
        carry = (three(hat, 1, rows), three(hat, 2, rows), none, none)
        _, _, lm, mm = plane_loop(2, planes - 2, third_pass, carry, 2)
        out = pl.ds(row - TOP, 8)
        acc_ref[0, out, :] += (1.0 / 4096.0) * lm
        acc_ref[1, out, :] += (1.0 / 4096.0) * mm


def inner_kernel(vel_ref, low_ref, high_ref, acc_ref, mag_ref, ext, hat, zsum, zvel, rows):
    depth = vel_ref.shape[1]
    decode_rows(low_ref, high_ref, rows)

    def assemble(p, carry):
        place_plane(ext, p, vel_ref, rows, p)
        return carry

    lax.fori_loop(0, depth, assemble, 0)
    acc_ref[...] = jnp.zeros_like(acc_ref)

    def store_mag(p, row, size):
        mag_ref[p - 1, pl.ds(row - TOP, 8), :] = size

    model_sums(depth, ext, hat, zsum, zvel, acc_ref, store_mag)


def model_scratch(planes, depth):
    return [
        pltpu.VMEM((3, planes, PAD, LANES), jnp.float32),
        pltpu.VMEM((3, planes, PAD, LANES), jnp.float32),
        pltpu.VMEM((12, planes, PAD, LANES), jnp.float32),
        pltpu.VMEM((3, planes, PAD, LANES), jnp.float32),
        pltpu.VMEM((2, 3 * HALO, depth, LANES), jnp.float32),
    ]


def inner_sums(vel, low, high):
    depth = vel.shape[1]
    return pl.pallas_call(
        inner_kernel,
        out_shape=(
            full((2, EXT, LANES), jnp.float32),
            full((depth - 2, EXT, LANES), jnp.float32),
        ),
        in_specs=in_vmem(3),
        out_specs=tuple(in_vmem(2)),
        scratch_shapes=model_scratch(depth, depth),
        compiler_params=params(),
        cost_estimate=cost(5),
        name="inner_sums",
    )(vel, low, high)


def outer_kernel(
    vel_ref,
    low_ref,
    high_ref,
    first_ref,
    second_ref,
    partial_ref,
    sums_ref,
    mag_ref,
    ext,
    hat,
    zsum,
    zvel,
    rows,
    acc,
):
    depth, width = vel_ref.shape[1:3]
    decode_rows(low_ref, high_ref, rows)
    acc[...] = partial_ref[...]
    below, above = below_above(
        "span", decode(first_ref[pl.ds(0, 6)]), decode(second_ref[pl.ds(0, 6)])
    )
    for side, (message, places, start) in enumerate(
        ((below, (1, 0), 0), (above, (4, 5), depth - 4))
    ):
        for index in range(4):
            place_plane(ext, index + (2 if side == 0 else 0), vel_ref, rows, start + index)
        for dim in range(3):
            for index, p in enumerate(places):
                ext[dim, p, pl.ds(OWN - HALO, TALL), :] = message[2 * dim + index]

        def store_mag(p, row, size):
            mag_ref[4 * side + p - 1, pl.ds(row - TOP, 8), :] = size

        model_sums(6, ext, hat, zsum, zvel, acc, store_mag)
    lines = width + 2
    sums_ref[...] = jnp.zeros_like(sums_ref)
    for index in range(2):
        sums_ref[pl.ds(index * lines, lines), :] = acc[index, pl.ds(OWN - TOP - 1, lines), :]


def outer_sums(vel, low, high, below, above, partial):
    depth, width = vel.shape[1:3]
    return pl.pallas_call(
        outer_kernel,
        out_shape=(
            full((-(-2 * (width + 2) // 8) * 8, LANES), jnp.float32),
            full((8, EXT, LANES), jnp.float32),
        ),
        in_specs=in_vmem(6),
        out_specs=tuple(in_vmem(2)),
        scratch_shapes=model_scratch(6, depth) + [pltpu.VMEM((2, EXT, LANES), jnp.float32)],
        compiler_params=params(),
        cost_estimate=cost(2),
        name="outer_sums",
    )(vel, low, high, below, above, partial)


def rows_kernel(pops, after_this, first, second, rows):
    depth, width = pops.shape[1:3]

    def plane(z, carry):
        for q in range(19):
            low = pops[q, z, pl.ds(0, 16), :].astype(jnp.float32)
            high = pops[q, z, pl.ds(width - 16, 16), :].astype(jnp.float32)
            rows[0, q, pl.ds(z, 1), :] = low[:1]
            rows[1, q, pl.ds(z, 1), :] = high[15:]
        return carry

    lax.fori_loop(0, depth, plane, 0)
    send_pair(
        "cross", rows[1].astype(jnp.bfloat16), rows[0].astype(jnp.bfloat16), first, second
    )


def face_rows(populations, after_this):
    _, depth, width, lanes = populations.shape
    edge = full((19, depth, lanes), jnp.bfloat16)
    return pl.pallas_call(
        rows_kernel,
        out_shape=(edge, edge),
        in_specs=in_vmem(1) + [pl.BlockSpec(memory_space=pl.ANY)],
        out_specs=tuple(in_vmem(2)),
        scratch_shapes=[pltpu.VMEM((2, 19, depth, lanes), jnp.float32)],
        compiler_params=params(),
        cost_estimate=cost(0.5),
        name="face_rows",
    )(populations, after_this)


def relax_parts(f):
    even = {q: f[q] + f[q + 1] for q in range(1, 19, 2)}
    odd = {q: f[q] - f[q + 1] for q in range(1, 19, 2)}
    x_xy, x_xz = odd[7] + odd[9], odd[11] + odd[13]
    y_yz, y_xy = odd[15] + odd[17], odd[7] - odd[9]
    z_xz, z_yz = odd[11] - odd[13], odd[15] - odd[17]
    flux, up, down, axis_odd = [], [], [], []
    for first, second, along in ((x_xy, x_xz, 1), (y_yz, y_xy, 3), (z_xz, z_yz, 5)):
        sides = first + second
        total = odd[along] + sides
        heat = 0.15 * (sides - (2.0 / 3.0) * total)
        twist = (1.98 / 8.0) * (first - second)
        flux.append(total)
        up.append(heat + twist)
        down.append(heat - twist)
        axis_odd.append(4.0 * heat)
    a, b, c = even[7] + even[9], even[11] + even[13], even[15] + even[17]
    axes = even[1] + even[3] + even[5]
    diagonals = a + b + c
    density = f[0] + axes + diagonals
    inverse = 1.0 / density
    speed = [total * inverse for total in flux]
    square = [total * part for total, part in zip(flux, speed)]
    energy = square[0] + square[1] + square[2]
    d_e = (1.19 / 126.0) * (diagonals - f[0] - energy)
    d_eps = (1.4 / 252.0) * (9.0 * f[0] - 7.0 * axes - 2.0 * diagonals + 5.5 * energy)
    ax_n, dg_n, eq_n = 3.0 * even[1] - axes, diagonals - 3.0 * c, 3.0 * square[0] - energy
    ax_w, dg_w, eq_w = even[3] - even[5], a - b, square[1] - square[2]
    d_pn = (1.4 / 72.0) * (dg_n - 2.0 * ax_n + 0.5 * eq_n)
    d_pw = (1.4 / 24.0) * (dg_w - 2.0 * ax_w + 0.5 * eq_w)
    shear = [
        (1.0 / 36.0) * (ax_n + dg_n - eq_n),
        (1.0 / 12.0) * (ax_w + dg_w - eq_w),
        0.25 * (even[7] - even[9] - flux[0] * speed[1]),
        0.25 * (even[11] - even[13] - flux[0] * speed[2]),
        0.25 * (even[15] - even[17] - flux[1] * speed[2]),
    ]
    base_axis = 11.0 * d_e + 4.0 * d_eps
    base_diag = -8.0 * d_e - d_eps
    base = [None] * 19
    base[0] = f[0] + (30.0 * d_e - 12.0 * d_eps)
    rest = base_axis - 2.0 * d_pn
    for q, change, skew in (
        (1, base_axis + 4.0 * d_pn, axis_odd[0]),
        (3, rest + 2.0 * d_pw, axis_odd[1]),
        (5, rest - 2.0 * d_pw, axis_odd[2]),
    ):
        base[q] = f[q] + (change + skew)
        base[q + 1] = f[q + 1] + (change - skew)
    rest = base_diag - d_pn
    for q, change, one, two in (
        (7, rest - d_pw, up[0], down[1]),
        (11, rest + d_pw, down[0], up[2]),
        (15, base_diag + 2.0 * d_pn, up[1], down[2]),
    ):
        same, other = one + two, one - two
        base[q] = f[q] + (change - same)
        base[q + 1] = f[q + 1] + (change + same)
        base[q + 2] = f[q + 2] + (change - other)
        base[q + 3] = f[q + 3] + (change + other)
    return base, shear


def shear_changes(shear, rate):
    n, w, xy, xz, yz = [rate * part for part in shear]
    lean = n + w
    tilt = n - w
    twice = n + n
    changes = [None] * 19
    changes[1] = changes[2] = -twice
    changes[3] = changes[4] = tilt
    changes[5] = changes[6] = lean
    changes[7] = changes[8] = -(lean + xy)
    changes[9] = changes[10] = xy - lean
    changes[11] = changes[12] = -(tilt + xz)
    changes[13] = changes[14] = xz - tilt
    changes[15] = changes[16] = twice - yz
    changes[17] = changes[18] = twice + yz
    return changes


def relax_rate(eddy, size):
    return 1.0 / (0.5 + 3.0 * (base_visc + eddy * size))


BEFORE = [q for q in range(19) if VELOCITIES[q][1] > 0]
AFTER = [q for q in range(19) if VELOCITIES[q][1] < 0]
RISING = [q for q in range(19) if VELOCITIES[q][2] > 0]
FALLING = [q for q in range(19) if VELOCITIES[q][2] < 0]
FIRST = 8


def ready_kernel(pops, first, second, after_this, base_ref, shear_ref, edge_ref, edge_shear):
    depth, width = pops.shape[1:3]
    rows = [
        below_above("cross", first[q].astype(jnp.float32), second[q].astype(jnp.float32))
        for q in range(19)
    ]
    for side, wanted in enumerate((BEFORE, AFTER)):
        base, shear = relax_parts([pair[side] for pair in rows])
        for index, q in enumerate(wanted):
            edge_ref[side, index] = base[q]
        for k in range(5):
            edge_shear[side, k] = shear[k]

    def plane(z, carry):
        for half in range(width // 16):
            rows = pl.ds(16 * half, 16)
            base, shear = relax_parts([pops[q, z, rows, :].astype(jnp.float32) for q in range(19)])
            for q in range(19):
                base_ref[q, z, rows, :] = base[q]
            for k in range(5):
                shear_ref[k, z, rows, :] = shear[k]
        return carry

    lax.fori_loop(0, depth, plane, 0)


def ready(populations, before, after, after_this):
    _, depth, width, lanes = populations.shape
    return pl.pallas_call(
        ready_kernel,
        out_shape=(
            full((19, depth, width, lanes), jnp.float32),
            full((5, depth, width, lanes), jnp.float32),
            full((2, 5, depth, lanes), jnp.float32),
            full((2, 5, depth, lanes), jnp.float32),
        ),
        in_specs=in_vmem(3) + [pl.BlockSpec(memory_space=pl.ANY)],
        out_specs=tuple(in_vmem(4)),
        compiler_params=params(),
        cost_estimate=cost(2.5),
        name="ready",
    )(populations, before, after, after_this)


def table_rows(table, at, low_at, flux):
    for dim in range(3):
        coarse, fine = split(flux[dim])
        table[at, dim * LANES : (dim + 1) * LANES] = coarse
        table[low_at, dim * LANES : (dim + 1) * LANES] = fine


def add_flux(flux, q, moved):
    for dim in range(3):
        sign = VELOCITIES[q][dim]
        if sign:
            flux[dim] = flux[dim] + moved if sign > 0 else flux[dim] - moved


def marker_force(table, picks, lanes, weights, taps):
    lane_of = lax.broadcasted_iota(jnp.int32, (LANES, lanes[0].shape[1]), 0)
    picked = lax.dot_general(
        table,
        jnp.concatenate(picks, axis=1),
        (((0,), (0,)), ((), ())),
        preferred_element_type=jnp.float32,
    )
    markers = lanes[0].shape[1]
    force = [0.0, 0.0, 0.0]
    for tap, (lane, weight) in enumerate(zip(lanes, weights)):
        mask = jnp.where(lane_of == lane, -weight, 0.0)
        at = slice(tap * markers, (tap + 1) * markers)
        for dim in range(3):
            force[dim] = force[dim] + picked[dim * LANES : (dim + 1) * LANES, at] * mask
        if (tap + 1) % taps == 0:
            yield [jnp.sum(part, axis=0, keepdims=True) for part in force]
            force = [0.0, 0.0, 0.0]


def step_kernel(
    base_ref,
    shear_ref,
    edge_ref,
    edge_shear,
    sums_ref,
    mag_in_ref,
    mag_out_ref,
    cell_ref,
    weight_ref,
    segment_ref,
    note_first,
    note_second,
    next_hbm,
    eddy_ref,
    partial_ref,
    first_ref,
    second_ref,
    post,
    nexts,
    table,
    face_table,
    faces,
    eddy,
    line,
    out_sems,
):
    depth, width = shear_ref.shape[1:3]
    lines = width + 2
    part = depth // 4
    eddy[...] = jnp.zeros_like(eddy)
    eddy[pl.ds(OWN - TOP - 1, lines), :] = jnp.maximum(
        sums_ref[pl.ds(0, lines), :] / (sums_ref[pl.ds(lines, lines), :] + eps_sum), 0.0
    )
    eddy_ref[...] = eddy[pl.ds(OWN - TOP, width), :]

    for side, (wanted, row, place) in enumerate(
        ((BEFORE, OWN - TOP - 1, FIRST - 1), (AFTER, OWN - TOP + width, FIRST + width))
    ):
        for z in range(depth):
            if z == 0:
                size = mag_out_ref[1, pl.ds(row, 1), :]
            elif z == depth - 1:
                size = mag_out_ref[6, pl.ds(row, 1), :]
            else:
                size = mag_in_ref[z - 1, pl.ds(row, 1), :]
            line[pl.ds(z, 1), :] = size
        rate = relax_rate(eddy[pl.ds(row, 1), :], line[...])
        changes = shear_changes([edge_shear[side, k] for k in range(5)], rate)
        for index, q in enumerate(wanted):
            out = edge_ref[side, index] + changes[q]
            for z in range(depth):
                post[q, z, pl.ds(place, 1), :] = out[z : z + 1]

    def collide(z, size_ref, at):
        for half in range(width // 16):
            rows = pl.ds(16 * half, 16)
            around = pl.ds(OWN - TOP + 16 * half, 16)
            rate = relax_rate(eddy[around, :], size_ref[at, around, :])
            changes = shear_changes([shear_ref[k, z, rows, :] for k in range(5)], rate)
            for q in range(19):
                value = base_ref[q, z, rows, :]
                if q:
                    value = value + changes[q]
                post[q, z, pl.ds(FIRST + 16 * half, 16), :] = value

    def inner(z, carry):
        collide(z, mag_in_ref, z - 1)
        return carry

    collide(0, mag_out_ref, 1)
    collide(depth - 1, mag_out_ref, 6)
    lax.fori_loop(1, depth - 1, inner, 0)

    def shifted(q, z, half):
        shift_x, shift_y, _ = VELOCITIES[q]
        piece = post[q, z, pl.ds(FIRST + 16 * half - shift_y, 16), :]
        if shift_x:
            piece = minus(piece) if shift_x > 0 else plus(piece)
        return piece.astype(jnp.bfloat16)

    def run(z, leave_out=()):
        for half in range(width // 16):
            flux = [0.0, 0.0, 0.0]
            for q in range(19):
                if q in leave_out:
                    continue
                moved = shifted(q, z - VELOCITIES[q][2], half)
                nexts[q, z, pl.ds(16 * half, 16), :] = moved
                if q:
                    add_flux(flux, q, moved.astype(jnp.float32))
            row = pl.multiple_of(z * width + 16 * half, 16)
            low_row = pl.multiple_of((depth + z) * width + 16 * half, 16)
            table_rows(table, pl.ds(row, 16), pl.ds(low_row, 16), flux)

    def run_inner(z, carry):
        run(z)
        return carry

    for side, (wanted, z) in enumerate(((RISING, depth - 1), (FALLING, 0))):
        for half in range(width // 16):
            rows = pl.ds(16 * half, 16)
            flux = [0.0, 0.0, 0.0]
            for index, q in enumerate(wanted):
                moved = shifted(q, z, half)
                faces[side, index, rows, :] = moved
                add_flux(flux, q, moved.astype(jnp.float32))
            row = side * width + 16 * half
            table_rows(face_table, pl.ds(row, 16), pl.ds(2 * width + row, 16), flux)
    send_pair("span", faces[0], faces[1], first_ref, second_ref)

    outs = []
    for index in range(4):
        start, stop = index * part, (index + 1) * part
        if index == 0:
            run(0, RISING)
            start += 1
        if index == 3:
            run(depth - 1, FALLING)
            stop -= 1
        lax.fori_loop(start, stop, run_inner, 0)
        place = pl.ds(index * part, part)
        outs.append(
            pltpu.make_async_copy(nexts.at[:, place], next_hbm.at[:, place], out_sems.at[index])
        )
        outs[-1].start()

    owners = partial_ref.shape[0]
    taps, markers = cell_ref.shape
    cells_all = depth * width
    note_below, note_above = below_above(
        "span", note_first[6].astype(jnp.int32), note_second[6].astype(jnp.int32)
    )

    def one_hot(rows, period, wanted):
        row_of = lax.broadcasted_iota(jnp.int32, (period, markers), 0)
        picks = []
        for tap in range(taps):
            hit = jnp.where(row_of == wanted[tap : tap + 1, :], 1.0, 0.0).astype(jnp.bfloat16)
            picks.append(jnp.concatenate([hit] * (rows // period), axis=0))
        return picks

    def row_lane(cells):
        return lax.shift_right_logical(cells, 7), lax.bitwise_and(cells, LANES - 1)

    def each(array):
        return [array[tap : tap + 1, :] for tap in range(taps)]

    row, lane = row_lane(cell_ref[...])
    forces = list(
        marker_force(
            table[...],
            one_hot(2 * cells_all, cells_all, row),
            each(lane),
            each(weight_ref[...]),
            taps,
        )
    )
    segments = [segment_ref[...]]
    picks, lanes, weights = [], [], []
    for side, note in enumerate((note_above, note_below)):
        row, lane = row_lane(note[:taps] + 2**15)
        row = row - side * (cells_all - width)
        inside = jnp.logical_and(row >= 0, row < width)
        picks += one_hot(4 * width, 2 * width, jnp.where(inside, row + side * width, -1))
        lanes += each(lane)
        weights += each(
            note[taps : 2 * taps].astype(jnp.float32) * 2.0**-16
            + note[2 * taps : 3 * taps].astype(jnp.float32) * 2.0**-31
        )
        segments.append(note[3 * taps : 3 * taps + 1])
    forces += list(marker_force(face_table[...], picks, lanes, weights, taps))

    owner_of = lax.broadcasted_iota(jnp.int32, (owners, markers), 0)
    place_of = lax.broadcasted_iota(jnp.int32, (SEG_DEV, markers), 0)
    mine, spread = [], []
    for force, segment in zip(forces, segments):
        hit = jnp.where(owner_of == lax.shift_right_logical(segment, 3), 1.0, 0.0)
        mine.append(hit.astype(jnp.bfloat16))
        place = place_of == lax.bitwise_and(segment, SEG_DEV - 1)
        spread.append(
            jnp.concatenate([jnp.where(place, part, 0.0) for part in force], axis=0)
        )
    mine, rest = jnp.concatenate(mine, axis=1), jnp.concatenate(spread, axis=1)
    rest = jnp.concatenate([rest, jnp.zeros((LANES - 3 * SEG_DEV, 3 * markers), jnp.float32)], axis=0)
    totals = 0.0
    for _ in range(3):
        coarse = rest.astype(jnp.bfloat16)
        rest = rest - coarse.astype(jnp.float32)
        totals = totals + lax.dot_general(
            mine, coarse, (((1,), (1,)), ((), ())), preferred_element_type=jnp.float32
        )
    partial_ref[:, 0, :] = totals
    for copy in outs:
        copy.wait()


def step(parts, sums, mag_in, mag_out, cells, weights, segments, notes, owners):
    _, depth, width, lanes = parts[0].shape
    face = full((5, width, lanes), jnp.bfloat16)
    return pl.pallas_call(
        step_kernel,
        out_shape=(
            full((19, depth, width, lanes), jnp.bfloat16),
            full((width, lanes), jnp.float32),
            full((owners, 1, lanes), jnp.float32),
            face,
            face,
        ),
        in_specs=in_vmem(12),
        out_specs=(pl.BlockSpec(memory_space=pl.ANY),) + tuple(in_vmem(4)),
        scratch_shapes=[
            pltpu.VMEM((19, depth, FIRST + width + 8, lanes), jnp.float32),
            pltpu.VMEM((19, depth, width, lanes), jnp.bfloat16),
            pltpu.VMEM((2 * depth * width, 3 * lanes), jnp.bfloat16),
            pltpu.VMEM((4 * width, 3 * lanes), jnp.bfloat16),
            pltpu.VMEM((2, 5, width, lanes), jnp.bfloat16),
            pltpu.VMEM((EXT, lanes), jnp.float32),
            pltpu.VMEM((depth, lanes), jnp.float32),
            pltpu.SemaphoreType.DMA((4,)),
        ],
        compiler_params=params(),
        cost_estimate=cost(5),
        name="step",
    )(*parts, sums, mag_in, mag_out, cells, weights, segments, *notes)


def arrive_kernel(next_in, first, second, arrived_hbm, next_hbm, force_ref, arrived, sems):
    depth = next_hbm.shape[1]
    odd = is_odd("span")
    shares = pltpu.make_async_copy(arrived_hbm, arrived, sems.at[10])
    shares.start()

    def place(below, above):
        copies = []
        for source, wanted, z in ((below, RISING, 0), (above, FALLING, depth - 1)):
            for index, q in enumerate(wanted):
                copies.append(
                    pltpu.make_async_copy(source.at[index], next_hbm.at[q, z], sems.at[len(copies)])
                )
                copies[-1].start()
        for copy in copies:
            copy.wait()

    @pl.when(odd)
    def _():
        place(first, second)

    @pl.when(jnp.logical_not(odd))
    def _():
        place(second, first)

    shares.wait()
    total = jnp.sum(arrived[:, 0, :], axis=0, keepdims=True)
    for dim in range(3):
        force_ref[pl.ds(dim, 1), :] = total[:, dim * SEG_DEV : (dim + 1) * SEG_DEV]


def arrive(populations_next, first, second, arrived):
    hbm = pl.BlockSpec(memory_space=pl.ANY)
    return pl.pallas_call(
        arrive_kernel,
        out_shape=(
            full(populations_next.shape, jnp.bfloat16),
            full((3, SEG_DEV), jnp.float32),
        ),
        in_specs=[hbm] + in_vmem(2) + [hbm],
        out_specs=(hbm, in_vmem(1)[0]),
        input_output_aliases={0: 0},
        scratch_shapes=[
            pltpu.VMEM(arrived.shape, jnp.float32),
            pltpu.SemaphoreType.DMA((11,)),
        ],
        compiler_params=params(),
        cost_estimate=cost(0.5),
        name="arrive",
    )(populations_next, first, second, arrived)


def local(populations, cell_index, marker_weight, segment_id):
    owners = lax.axis_size("span") * lax.axis_size("cross")
    cells, weights, segments = cell_index.T, marker_weight.T, segment_id[None, :]
    vel, *lines = block_moments(populations)
    lines = swap(*lines, "cross")
    planes = swap(*edge_planes(vel, *lines, cells, weights, segments), "span")
    partial, mag_in = inner_sums(vel, *lines)
    faces = swap(*face_rows(populations, partial), "cross")
    sums, mag_out = outer_sums(vel, *lines, *planes, partial)
    parts = ready(populations, *faces, sums)
    count = lax.axis_size("span")
    if count & (count - 1):
        sums = lax.psum(sums, "span")
    else:
        distance = 1
        while distance < count:
            pairs = [(i, i ^ distance) for i in range(count)]
            sums = sums + lax.ppermute(sums, "span", pairs)
            distance *= 2
    moved, eddy_coeff, packed, *leaving = step(
        parts, sums, mag_in, mag_out, cells, weights, segments, planes, owners
    )
    arrived = lax.all_to_all(packed, ("span", "cross"), 0, 0)
    populations_next, segment_force = arrive(moved, *swap(*leaving, "span"), arrived)
    return (populations_next, eddy_coeff, segment_force)


def solution(mesh):
    in_specs = (
        P(None, "span", "cross", None),
        P(("span", "cross"), None),
        P(("span", "cross"), None),
        P(("span", "cross")),
    )
    out_specs = (P(None, "span", "cross", None), P("cross", None), P(None, ("span", "cross")))
    return jax.shard_map(local, mesh=mesh, in_specs=in_specs, out_specs=out_specs, check_vma=False)
```

```python
import functools

import jax
import jax.numpy as jnp
from jax import lax
from jax.experimental import pallas as pl
from jax.experimental.pallas import tpu as pltpu
from jax.sharding import PartitionSpec as P

SEG_DEV = 8
LANES = 128
HALO = 3
EXT = 40
PAD = 56
OWN = 11
TOP = 8
CHUNKS = (8, 16, 24, 32, 40)
VMEM = 28 * 1024 * 1024

eps_sum = 1e-06
base_visc = 0.005

VELOCITIES = [
    [0, 0, 0],
    [1, 0, 0],
    [-1, 0, 0],
    [0, 1, 0],
    [0, -1, 0],
    [0, 0, 1],
    [0, 0, -1],
    [1, 1, 0],
    [-1, -1, 0],
    [1, -1, 0],
    [-1, 1, 0],
    [1, 0, 1],
    [-1, 0, -1],
    [1, 0, -1],
    [-1, 0, 1],
    [0, 1, 1],
    [0, -1, -1],
    [0, 1, -1],
    [0, -1, 1],
]


def swap(first, second, axis):
    count = lax.axis_size(axis)
    near = [(i, i ^ 1) for i in range(count)]
    other = [(i, (i + 1 if i % 2 else i - 1) % count) for i in range(count)]
    return lax.ppermute(first, axis, near), lax.ppermute(second, axis, other)


def is_odd(axis):
    return lax.rem(lax.axis_index(axis), 2) == 1


def send_pair(axis, upwards, downwards, first, second):
    odd = is_odd(axis)

    @pl.when(odd)
    def _():
        first[...] = downwards
        second[...] = upwards

    @pl.when(jnp.logical_not(odd))
    def _():
        first[...] = upwards
        second[...] = downwards


def below_above(axis, first, second):
    odd = is_odd(axis)
    return jnp.where(odd, first, second), jnp.where(odd, second, first)


def full(shape, dtype):
    return jax.ShapeDtypeStruct(shape, dtype)


def in_vmem(count):
    return [pl.BlockSpec(memory_space=pltpu.VMEM)] * count


def params():
    return pltpu.CompilerParams(vmem_limit_bytes=VMEM)


def cost(micros):
    return pl.CostEstimate(flops=0, bytes_accessed=int(micros * 3.6e6), transcendentals=0)


def plus(array):
    return pltpu.roll(array, LANES - 1, 1)


def minus(array):
    return pltpu.roll(array, 1, 1)


STEP = 2.0**-15


def encode(value):
    return jnp.round(value * (1.0 / STEP)).astype(jnp.int32).astype(jnp.int16)


def decode(coded):
    return coded.astype(jnp.int32).astype(jnp.float32) * STEP


def split(value):
    high = value.astype(jnp.bfloat16)
    return high, (value - high.astype(jnp.float32)).astype(jnp.bfloat16)


def moments_kernel(pops, vel_ref, first, second, rows):
    depth, width = pops.shape[1:3]

    def plane(z, carry):
        for half in range(width // 16):
            at = pl.ds(16 * half, 16)
            f = [pops[q, z, at, :].astype(jnp.float32) for q in range(19)]
            flux = [0.0, 0.0, 0.0]
            density = f[0]
            for q in range(1, 19, 2):
                even, odd = f[q] + f[q + 1], f[q] - f[q + 1]
                density = density + even
                for dim in range(3):
                    sign = VELOCITIES[q][dim]
                    if sign:
                        flux[dim] = flux[dim] + odd if sign > 0 else flux[dim] - odd
            inverse = 1.0 / density
            for dim in range(3):
                speed = flux[dim] * inverse
                vel_ref[dim, z, at, :] = speed
                for k in range(HALO):
                    if half == 0:
                        rows[0, dim * HALO + k, pl.ds(z, 1), :] = speed[k : k + 1]
                    if half == width // 16 - 1:
                        rows[1, dim * HALO + k, pl.ds(z, 1), :] = speed[15 - k : 16 - k]
        return carry

    lax.fori_loop(0, depth, plane, 0)
    send_pair("cross", encode(rows[1]), encode(rows[0]), first, second)


def block_moments(populations):
    _, depth, width, lanes = populations.shape
    edge = full((3 * HALO, depth, lanes), jnp.int16)
    return pl.pallas_call(
        moments_kernel,
        out_shape=(full((3, depth, width, lanes), jnp.float32), edge, edge),
        in_specs=in_vmem(1),
        out_specs=tuple(in_vmem(3)),
        scratch_shapes=[pltpu.VMEM((2, 3 * HALO, depth, lanes), jnp.float32)],
        compiler_params=params(),
        cost_estimate=cost(1),
        name="moments",
    )(populations)


def decode_rows(first, second, rows):
    rows[0], rows[1] = below_above("cross", decode(first[...]), decode(second[...]))


def place_plane(ext, p, vel_ref, rows, z):
    width = vel_ref.shape[2]
    for dim in range(3):
        ext[dim, p, pl.ds(OWN, width), :] = vel_ref[dim, z]
        for k in range(HALO):
            line = pl.ds(z, 1)
            ext[dim, p, pl.ds(OWN - 1 - k, 1), :] = rows[0, dim * HALO + k, line, :]
            ext[dim, p, pl.ds(OWN + width + k, 1), :] = rows[1, dim * HALO + k, line, :]


TALL = 40


def edges_kernel(
    vel_ref,
    low_ref,
    high_ref,
    cell_ref,
    weight_ref,
    segment_ref,
    first,
    second,
    rows,
    planes,
    note,
    coded,
):
    depth, width = vel_ref.shape[1:3]
    taps = cell_ref.shape[0]
    decode_rows(low_ref, high_ref, rows)
    fixed = weight_ref[...] * 2.0**16
    coarse = jnp.round(fixed)
    note[...] = jnp.zeros_like(note)
    note[pl.ds(0, taps), :] = cell_ref[...].astype(jnp.float32) - 2.0**15
    note[pl.ds(taps, taps), :] = coarse
    note[pl.ds(2 * taps, taps), :] = jnp.round((fixed - coarse) * 2.0**15)
    note[pl.ds(3 * taps, 1), :] = segment_ref[...].astype(jnp.float32)
    for side, pair in enumerate(((0, 1), (depth - 1, depth - 2))):
        planes[...] = jnp.zeros_like(planes)
        for dim in range(3):
            for index, z in enumerate(pair):
                slot = 2 * dim + index
                planes[slot, pl.ds(HALO, width), :] = vel_ref[dim, z]
                for k in range(HALO):
                    line = pl.ds(z, 1)
                    planes[slot, pl.ds(HALO - 1 - k, 1), :] = rows[0, dim * HALO + k, line, :]
                    planes[slot, pl.ds(HALO + width + k, 1), :] = rows[1, dim * HALO + k, line, :]
        coded[side, pl.ds(0, 6)] = encode(planes[...])
        coded[side, 6] = note[...].astype(jnp.int32).astype(jnp.int16)
    send_pair("span", coded[1], coded[0], first, second)


def edge_planes(vel, low, high, cells, weights, segments):
    pair = full((7, TALL, LANES), jnp.int16)
    return pl.pallas_call(
        edges_kernel,
        out_shape=(pair, pair),
        in_specs=in_vmem(6),
        out_specs=tuple(in_vmem(2)),
        scratch_shapes=[
            pltpu.VMEM((2, 3 * HALO, vel.shape[1], LANES), jnp.float32),
            pltpu.VMEM((6, TALL, LANES), jnp.float32),
            pltpu.VMEM((TALL, LANES), jnp.float32),
            pltpu.VMEM((2, 7, TALL, LANES), jnp.int16),
        ],
        compiler_params=params(),
        cost_estimate=cost(0.2),
        name="edges",
    )(vel, low, high, cells, weights, segments)


def plane_loop(start, stop, body, carry, most):
    count = stop - start
    step = max(size for size in range(1, most + 1) if count % size == 0)

    def block(index, carry):
        for shift in range(step):
            carry = body(start + index * step + shift, carry)
        return carry

    if count == step:
        return block(0, carry)
    return lax.fori_loop(0, count // step, block, carry)


def strain_parts(ref, p, row, before, here, after):
    grads = [
        (
            plus(here[dim]) - minus(here[dim]),
            ref[dim, p, pl.ds(row + 1, 8), :] - ref[dim, p, pl.ds(row - 1, 8), :],
            after[dim] - before[dim],
        )
        for dim in range(3)
    ]
    parts = [
        grads[0][0],
        grads[1][1],
        grads[2][2],
        grads[0][1] + grads[1][0],
        grads[0][2] + grads[2][0],
        grads[1][2] + grads[2][1],
    ]
    straight = parts[0] * parts[0] + parts[1] * parts[1] + parts[2] * parts[2]
    mixed = parts[3] * parts[3] + parts[4] * parts[4] + parts[5] * parts[5]
    return parts, jnp.sqrt(0.5 * straight + 0.25 * mixed)


def weigh(low, middle, high):
    return (low + high) + (middle + middle)


PAIRS = ((0, 0), (1, 1), (2, 2), (0, 1), (0, 2), (1, 2))


def three(ref, p, rows):
    return [ref[dim, p, rows, :] for dim in range(3)]


def model_sums(planes, ext, hat, zsum, zvel, acc_ref, store_mag):
    for row in CHUNKS:
        rows = pl.ds(row, 8)

        def first_pass(p, carry):
            before, here, lag, last = carry
            after = three(ext, p + 1, rows)
            parts, size = strain_parts(ext, p, row, before, here, after)
            store_mag(p, row, size)
            prods = [size * part for part in parts] + [here[i] * here[j] for i, j in PAIRS]
            for k in range(12):
                zsum[k, p - 1, rows, :] = lag[k] + prods[k]
            for dim in range(3):
                zvel[dim, p, rows, :] = weigh(before[dim], here[dim], after[dim])
            lag = [last[k] + (prods[k] + prods[k]) for k in range(12)]
            return here, after, lag, prods

        none = [jnp.zeros((8, LANES), jnp.float32)] * 12
        carry = (three(ext, 0, rows), three(ext, 1, rows), none, none)
        plane_loop(1, planes - 1, first_pass, carry, 14)

    def second_pass(p, carry):
        for row in CHUNKS:
            for dim in range(3):
                line = weigh(*[zvel[dim, p, pl.ds(row + shift, 8), :] for shift in (-1, 0, 1)])
                hat[dim, p, pl.ds(row, 8), :] = (1.0 / 64.0) * weigh(minus(line), line, plus(line))
        return carry

    plane_loop(1, planes - 1, second_pass, 0, 14)

    for row in CHUNKS:
        rows = pl.ds(row, 8)

        def third_pass(p, carry):
            before, here, lm, mm = carry
            after = three(hat, p + 1, rows)
            parts, size = strain_parts(hat, p, row, before, here, after)
            size = 256.0 * size
            scaled = [64.0 * speed for speed in here]
            squares = [0.0, 0.0]
            for k, (i, j) in enumerate(PAIRS):
                smooth = []
                for field in (k, 6 + k):
                    line = weigh(
                        *[zsum[field, p, pl.ds(row + shift, 8), :] for shift in (-1, 0, 1)]
                    )
                    smooth.append(weigh(minus(line), line, plus(line)))
                model = smooth[0] - size * parts[k]
                lm = lm + (smooth[1] - scaled[i] * here[j]) * model
                squares[k // 3] = squares[k // 3] + model * model
            return here, after, lm, mm + (squares[0] + 0.5 * squares[1])

        none = jnp.zeros((8, LANES), jnp.float32)
        carry = (three(hat, 1, rows), three(hat, 2, rows), none, none)
        _, _, lm, mm = plane_loop(2, planes - 2, third_pass, carry, 12)
        out = pl.ds(row - TOP, 8)
        acc_ref[0, out, :] += (1.0 / 4096.0) * lm
        acc_ref[1, out, :] += (1.0 / 4096.0) * mm


def inner_kernel(vel_ref, low_ref, high_ref, acc_ref, mag_ref, ext, hat, zsum, zvel, rows):
    depth = vel_ref.shape[1]
    decode_rows(low_ref, high_ref, rows)

    def assemble(p, carry):
        place_plane(ext, p, vel_ref, rows, p)
        return carry

    lax.fori_loop(0, depth, assemble, 0)
    acc_ref[...] = jnp.zeros_like(acc_ref)

    def store_mag(p, row, size):
        mag_ref[p - 1, pl.ds(row - TOP, 8), :] = size

    model_sums(depth, ext, hat, zsum, zvel, acc_ref, store_mag)


def model_scratch(planes, depth):
    return [
        pltpu.VMEM((3, planes, PAD, LANES), jnp.float32),
        pltpu.VMEM((3, planes, PAD, LANES), jnp.float32),
        pltpu.VMEM((12, planes, PAD, LANES), jnp.float32),
        pltpu.VMEM((3, planes, PAD, LANES), jnp.float32),
        pltpu.VMEM((2, 3 * HALO, depth, LANES), jnp.float32),
    ]


def inner_sums(vel, low, high):
    depth = vel.shape[1]
    return pl.pallas_call(
        inner_kernel,
        out_shape=(
            full((2, EXT, LANES), jnp.float32),
            full((depth - 2, EXT, LANES), jnp.float32),
        ),
        in_specs=in_vmem(3),
        out_specs=tuple(in_vmem(2)),
        scratch_shapes=model_scratch(depth, depth),
        compiler_params=params(),
        cost_estimate=cost(5),
        name="inner_sums",
    )(vel, low, high)


def outer_kernel(
    vel_ref,
    low_ref,
    high_ref,
    first_ref,
    second_ref,
    partial_ref,
    sums_ref,
    mag_ref,
    ext,
    hat,
    zsum,
    zvel,
    rows,
    acc,
):
    depth, width = vel_ref.shape[1:3]
    decode_rows(low_ref, high_ref, rows)
    acc[...] = partial_ref[...]
    below, above = below_above(
        "span", decode(first_ref[pl.ds(0, 6)]), decode(second_ref[pl.ds(0, 6)])
    )
    for side, (message, places, start) in enumerate(
        ((below, (1, 0), 0), (above, (4, 5), depth - 4))
    ):
        for index in range(4):
            place_plane(ext, index + (2 if side == 0 else 0), vel_ref, rows, start + index)
        for dim in range(3):
            for index, p in enumerate(places):
                ext[dim, p, pl.ds(OWN - HALO, TALL), :] = message[2 * dim + index]

        def store_mag(p, row, size):
            mag_ref[4 * side + p - 1, pl.ds(row - TOP, 8), :] = size

        model_sums(6, ext, hat, zsum, zvel, acc, store_mag)
    lines = width + 2
    sums_ref[...] = jnp.zeros_like(sums_ref)
    for index in range(2):
        sums_ref[pl.ds(index * lines, lines), :] = acc[index, pl.ds(OWN - TOP - 1, lines), :]


def outer_sums(vel, low, high, below, above, partial):
    depth, width = vel.shape[1:3]
    return pl.pallas_call(
        outer_kernel,
        out_shape=(
            full((-(-2 * (width + 2) // 8) * 8, LANES), jnp.float32),
            full((8, EXT, LANES), jnp.float32),
        ),
        in_specs=in_vmem(6),
        out_specs=tuple(in_vmem(2)),
        scratch_shapes=model_scratch(6, depth) + [pltpu.VMEM((2, EXT, LANES), jnp.float32)],
        compiler_params=params(),
        cost_estimate=cost(2),
        name="outer_sums",
    )(vel, low, high, below, above, partial)


def rows_kernel(pops, after_this, first, second, rows):
    depth, width = pops.shape[1:3]

    def plane(z, carry):
        for q in range(19):
            low = pops[q, z, pl.ds(0, 16), :].astype(jnp.float32)
            high = pops[q, z, pl.ds(width - 16, 16), :].astype(jnp.float32)
            rows[0, q, pl.ds(z, 1), :] = low[:1]
            rows[1, q, pl.ds(z, 1), :] = high[15:]
        return carry

    lax.fori_loop(0, depth, plane, 0)
    send_pair(
        "cross", rows[1].astype(jnp.bfloat16), rows[0].astype(jnp.bfloat16), first, second
    )


def face_rows(populations, after_this):
    _, depth, width, lanes = populations.shape
    edge = full((19, depth, lanes), jnp.bfloat16)
    return pl.pallas_call(
        rows_kernel,
        out_shape=(edge, edge),
        in_specs=in_vmem(1) + [pl.BlockSpec(memory_space=pl.ANY)],
        out_specs=tuple(in_vmem(2)),
        scratch_shapes=[pltpu.VMEM((2, 19, depth, lanes), jnp.float32)],
        compiler_params=params(),
        cost_estimate=cost(0.5),
        name="face_rows",
    )(populations, after_this)


def relax_parts(f):
    even = {q: f[q] + f[q + 1] for q in range(1, 19, 2)}
    odd = {q: f[q] - f[q + 1] for q in range(1, 19, 2)}
    x_xy, x_xz = odd[7] + odd[9], odd[11] + odd[13]
    y_yz, y_xy = odd[15] + odd[17], odd[7] - odd[9]
    z_xz, z_yz = odd[11] - odd[13], odd[15] - odd[17]
    flux, up, down, axis_odd = [], [], [], []
    for first, second, along in ((x_xy, x_xz, 1), (y_yz, y_xy, 3), (z_xz, z_yz, 5)):
        sides = first + second
        total = odd[along] + sides
        heat = 0.15 * (sides - (2.0 / 3.0) * total)
        twist = (1.98 / 8.0) * (first - second)
        flux.append(total)
        up.append(heat + twist)
        down.append(heat - twist)
        axis_odd.append(4.0 * heat)
    a, b, c = even[7] + even[9], even[11] + even[13], even[15] + even[17]
    axes = even[1] + even[3] + even[5]
    diagonals = a + b + c
    density = f[0] + axes + diagonals
    inverse = 1.0 / density
    speed = [total * inverse for total in flux]
    square = [total * part for total, part in zip(flux, speed)]
    energy = square[0] + square[1] + square[2]
    d_e = (1.19 / 126.0) * (diagonals - f[0] - energy)
    d_eps = (1.4 / 252.0) * (9.0 * f[0] - 7.0 * axes - 2.0 * diagonals + 5.5 * energy)
    ax_n, dg_n, eq_n = 3.0 * even[1] - axes, diagonals - 3.0 * c, 3.0 * square[0] - energy
    ax_w, dg_w, eq_w = even[3] - even[5], a - b, square[1] - square[2]
    d_pn = (1.4 / 72.0) * (dg_n - 2.0 * ax_n + 0.5 * eq_n)
    d_pw = (1.4 / 24.0) * (dg_w - 2.0 * ax_w + 0.5 * eq_w)
    shear = [
        (1.0 / 36.0) * (ax_n + dg_n - eq_n),
        (1.0 / 12.0) * (ax_w + dg_w - eq_w),
        0.25 * (even[7] - even[9] - flux[0] * speed[1]),
        0.25 * (even[11] - even[13] - flux[0] * speed[2]),
        0.25 * (even[15] - even[17] - flux[1] * speed[2]),
    ]
    base_axis = 11.0 * d_e + 4.0 * d_eps
    base_diag = -8.0 * d_e - d_eps
    base = [None] * 19
    base[0] = f[0] + (30.0 * d_e - 12.0 * d_eps)
    rest = base_axis - 2.0 * d_pn
    for q, change, skew in (
        (1, base_axis + 4.0 * d_pn, axis_odd[0]),
        (3, rest + 2.0 * d_pw, axis_odd[1]),
        (5, rest - 2.0 * d_pw, axis_odd[2]),
    ):
        base[q] = f[q] + (change + skew)
        base[q + 1] = f[q + 1] + (change - skew)
    rest = base_diag - d_pn
    for q, change, one, two in (
        (7, rest - d_pw, up[0], down[1]),
        (11, rest + d_pw, down[0], up[2]),
        (15, base_diag + 2.0 * d_pn, up[1], down[2]),
    ):
        same, other = one + two, one - two
        base[q] = f[q] + (change - same)
        base[q + 1] = f[q + 1] + (change + same)
        base[q + 2] = f[q + 2] + (change - other)
        base[q + 3] = f[q + 3] + (change + other)
    return base, shear


def shear_changes(shear, rate):
    n, w, xy, xz, yz = [rate * part for part in shear]
    lean = n + w
    tilt = n - w
    twice = n + n
    changes = [None] * 19
    changes[1] = changes[2] = -twice
    changes[3] = changes[4] = tilt
    changes[5] = changes[6] = lean
    changes[7] = changes[8] = -(lean + xy)
    changes[9] = changes[10] = xy - lean
    changes[11] = changes[12] = -(tilt + xz)
    changes[13] = changes[14] = xz - tilt
    changes[15] = changes[16] = twice - yz
    changes[17] = changes[18] = twice + yz
    return changes


def relax_rate(eddy, size):
    return 1.0 / (0.5 + 3.0 * (base_visc + eddy * size))


BEFORE = [q for q in range(19) if VELOCITIES[q][1] > 0]
AFTER = [q for q in range(19) if VELOCITIES[q][1] < 0]
RISING = [q for q in range(19) if VELOCITIES[q][2] > 0]
FALLING = [q for q in range(19) if VELOCITIES[q][2] < 0]
FIRST = 8


def ready_kernel(pops, first, second, after_this, base_ref, shear_ref, edge_ref, edge_shear):
    depth, width = pops.shape[1:3]
    rows = [
        below_above("cross", first[q].astype(jnp.float32), second[q].astype(jnp.float32))
        for q in range(19)
    ]
    for side, wanted in enumerate((BEFORE, AFTER)):
        base, shear = relax_parts([pair[side] for pair in rows])
        for index, q in enumerate(wanted):
            edge_ref[side, index] = base[q]
        for k in range(5):
            edge_shear[side, k] = shear[k]

    def plane(z, carry):
        for half in range(width // 16):
            rows = pl.ds(16 * half, 16)
            base, shear = relax_parts([pops[q, z, rows, :].astype(jnp.float32) for q in range(19)])
            for q in range(19):
                base_ref[q, z, rows, :] = base[q]
            for k in range(5):
                shear_ref[k, z, rows, :] = shear[k]
        return carry

    lax.fori_loop(0, depth, plane, 0)


def ready(populations, before, after, after_this):
    _, depth, width, lanes = populations.shape
    return pl.pallas_call(
        ready_kernel,
        out_shape=(
            full((19, depth, width, lanes), jnp.float32),
            full((5, depth, width, lanes), jnp.float32),
            full((2, 5, depth, lanes), jnp.float32),
            full((2, 5, depth, lanes), jnp.float32),
        ),
        in_specs=in_vmem(3) + [pl.BlockSpec(memory_space=pl.ANY)],
        out_specs=tuple(in_vmem(4)),
        compiler_params=params(),
        cost_estimate=cost(2.5),
        name="ready",
    )(populations, before, after, after_this)


def table_rows(table, at, low_at, flux):
    for dim in range(3):
        coarse, fine = split(flux[dim])
        table[at, dim * LANES : (dim + 1) * LANES] = coarse
        table[low_at, dim * LANES : (dim + 1) * LANES] = fine


def add_flux(flux, q, moved):
    for dim in range(3):
        sign = VELOCITIES[q][dim]
        if sign:
            flux[dim] = flux[dim] + moved if sign > 0 else flux[dim] - moved


def marker_force(table, picks, lanes, weights, taps):
    lane_of = lax.broadcasted_iota(jnp.int32, (LANES, lanes[0].shape[1]), 0)
    picked = lax.dot_general(
        table,
        jnp.concatenate(picks, axis=1),
        (((0,), (0,)), ((), ())),
        preferred_element_type=jnp.float32,
    )
    markers = lanes[0].shape[1]
    force = [0.0, 0.0, 0.0]
    for tap, (lane, weight) in enumerate(zip(lanes, weights)):
        mask = jnp.where(lane_of == lane, -weight, 0.0)
        at = slice(tap * markers, (tap + 1) * markers)
        for dim in range(3):
            force[dim] = force[dim] + picked[dim * LANES : (dim + 1) * LANES, at] * mask
        if (tap + 1) % taps == 0:
            yield [jnp.sum(part, axis=0, keepdims=True) for part in force]
            force = [0.0, 0.0, 0.0]


def step_kernel(
    base_ref,
    shear_ref,
    edge_ref,
    edge_shear,
    sums_ref,
    mag_in_ref,
    mag_out_ref,
    cell_ref,
    weight_ref,
    segment_ref,
    note_first,
    note_second,
    next_hbm,
    eddy_ref,
    partial_ref,
    first_ref,
    second_ref,
    post,
    nexts,
    table,
    face_table,
    faces,
    eddy,
    line,
    out_sems,
):
    depth, width = shear_ref.shape[1:3]
    lines = width + 2
    part = depth // 4
    eddy[...] = jnp.zeros_like(eddy)
    eddy[pl.ds(OWN - TOP - 1, lines), :] = jnp.maximum(
        sums_ref[pl.ds(0, lines), :] / (sums_ref[pl.ds(lines, lines), :] + eps_sum), 0.0
    )
    eddy_ref[...] = eddy[pl.ds(OWN - TOP, width), :]

    for side, (wanted, row, place) in enumerate(
        ((BEFORE, OWN - TOP - 1, FIRST - 1), (AFTER, OWN - TOP + width, FIRST + width))
    ):
        for z in range(depth):
            if z == 0:
                size = mag_out_ref[1, pl.ds(row, 1), :]
            elif z == depth - 1:
                size = mag_out_ref[6, pl.ds(row, 1), :]
            else:
                size = mag_in_ref[z - 1, pl.ds(row, 1), :]
            line[pl.ds(z, 1), :] = size
        rate = relax_rate(eddy[pl.ds(row, 1), :], line[...])
        changes = shear_changes([edge_shear[side, k] for k in range(5)], rate)
        for index, q in enumerate(wanted):
            out = edge_ref[side, index] + changes[q]
            for z in range(depth):
                post[q, z, pl.ds(place, 1), :] = out[z : z + 1]

    def collide(z, size_ref, at):
        for half in range(width // 16):
            rows = pl.ds(16 * half, 16)
            around = pl.ds(OWN - TOP + 16 * half, 16)
            rate = relax_rate(eddy[around, :], size_ref[at, around, :])
            changes = shear_changes([shear_ref[k, z, rows, :] for k in range(5)], rate)
            for q in range(19):
                value = base_ref[q, z, rows, :]
                if q:
                    value = value + changes[q]
                post[q, z, pl.ds(FIRST + 16 * half, 16), :] = value

    def inner(z, carry):
        collide(z, mag_in_ref, z - 1)
        return carry

    collide(0, mag_out_ref, 1)
    collide(depth - 1, mag_out_ref, 6)
    lax.fori_loop(1, depth - 1, inner, 0)

    def shifted(q, z, half):
        shift_x, shift_y, _ = VELOCITIES[q]
        piece = post[q, z, pl.ds(FIRST + 16 * half - shift_y, 16), :]
        if shift_x:
            piece = minus(piece) if shift_x > 0 else plus(piece)
        return piece.astype(jnp.bfloat16)

    def run(z, leave_out=()):
        for half in range(width // 16):
            flux = [0.0, 0.0, 0.0]
            for q in range(19):
                if q in leave_out:
                    continue
                moved = shifted(q, z - VELOCITIES[q][2], half)
                nexts[q, z, pl.ds(16 * half, 16), :] = moved
                if q:
                    add_flux(flux, q, moved.astype(jnp.float32))
            row = pl.multiple_of(z * width + 16 * half, 16)
            low_row = pl.multiple_of((depth + z) * width + 16 * half, 16)
            table_rows(table, pl.ds(row, 16), pl.ds(low_row, 16), flux)

    def run_inner(z, carry):
        run(z)
        return carry

    for side, (wanted, z) in enumerate(((RISING, depth - 1), (FALLING, 0))):
        for half in range(width // 16):
            rows = pl.ds(16 * half, 16)
            flux = [0.0, 0.0, 0.0]
            for index, q in enumerate(wanted):
                moved = shifted(q, z, half)
                faces[side, index, rows, :] = moved
                add_flux(flux, q, moved.astype(jnp.float32))
            row = side * width + 16 * half
            table_rows(face_table, pl.ds(row, 16), pl.ds(2 * width + row, 16), flux)
    send_pair("span", faces[0], faces[1], first_ref, second_ref)

    outs = []
    for index in range(4):
        start, stop = index * part, (index + 1) * part
        if index == 0:
            run(0, RISING)
            start += 1
        if index == 3:
            run(depth - 1, FALLING)
            stop -= 1
        lax.fori_loop(start, stop, run_inner, 0)
        place = pl.ds(index * part, part)
        outs.append(
            pltpu.make_async_copy(nexts.at[:, place], next_hbm.at[:, place], out_sems.at[index])
        )
        outs[-1].start()

    owners = partial_ref.shape[0]
    taps, markers = cell_ref.shape
    cells_all = depth * width
    note_below, note_above = below_above(
        "span", note_first[6].astype(jnp.int32), note_second[6].astype(jnp.int32)
    )

    def one_hot(rows, period, wanted):
        row_of = lax.broadcasted_iota(jnp.int32, (period, markers), 0)
        picks = []
        for tap in range(taps):
            hit = jnp.where(row_of == wanted[tap : tap + 1, :], 1.0, 0.0).astype(jnp.bfloat16)
            picks.append(jnp.concatenate([hit] * (rows // period), axis=0))
        return picks

    def row_lane(cells):
        return lax.shift_right_logical(cells, 7), lax.bitwise_and(cells, LANES - 1)

    def each(array):
        return [array[tap : tap + 1, :] for tap in range(taps)]

    row, lane = row_lane(cell_ref[...])
    forces = list(
        marker_force(
            table[...],
            one_hot(2 * cells_all, cells_all, row),
            each(lane),
            each(weight_ref[...]),
            taps,
        )
    )
    segments = [segment_ref[...]]
    picks, lanes, weights = [], [], []
    for side, note in enumerate((note_above, note_below)):
        row, lane = row_lane(note[:taps] + 2**15)
        row = row - side * (cells_all - width)
        inside = jnp.logical_and(row >= 0, row < width)
        picks += one_hot(4 * width, 2 * width, jnp.where(inside, row + side * width, -1))
        lanes += each(lane)
        weights += each(
            note[taps : 2 * taps].astype(jnp.float32) * 2.0**-16
            + note[2 * taps : 3 * taps].astype(jnp.float32) * 2.0**-31
        )
        segments.append(note[3 * taps : 3 * taps + 1])
    forces += list(marker_force(face_table[...], picks, lanes, weights, taps))

    owner_of = lax.broadcasted_iota(jnp.int32, (owners, markers), 0)
    place_of = lax.broadcasted_iota(jnp.int32, (SEG_DEV, markers), 0)
    mine, spread = [], []
    for force, segment in zip(forces, segments):
        hit = jnp.where(owner_of == lax.shift_right_logical(segment, 3), 1.0, 0.0)
        mine.append(hit.astype(jnp.bfloat16))
        place = place_of == lax.bitwise_and(segment, SEG_DEV - 1)
        spread.append(
            jnp.concatenate([jnp.where(place, part, 0.0) for part in force], axis=0)
        )
    mine, rest = jnp.concatenate(mine, axis=1), jnp.concatenate(spread, axis=1)
    rest = jnp.concatenate([rest, jnp.zeros((LANES - 3 * SEG_DEV, 3 * markers), jnp.float32)], axis=0)
    totals = 0.0
    for _ in range(3):
        coarse = rest.astype(jnp.bfloat16)
        rest = rest - coarse.astype(jnp.float32)
        totals = totals + lax.dot_general(
            mine, coarse, (((1,), (1,)), ((), ())), preferred_element_type=jnp.float32
        )
    partial_ref[:, 0, :] = totals
    for copy in outs:
        copy.wait()


def step(parts, sums, mag_in, mag_out, cells, weights, segments, notes, owners):
    _, depth, width, lanes = parts[0].shape
    face = full((5, width, lanes), jnp.bfloat16)
    return pl.pallas_call(
        step_kernel,
        out_shape=(
            full((19, depth, width, lanes), jnp.bfloat16),
            full((width, lanes), jnp.float32),
            full((owners, 1, lanes), jnp.float32),
            face,
            face,
        ),
        in_specs=in_vmem(12),
        out_specs=(pl.BlockSpec(memory_space=pl.ANY),) + tuple(in_vmem(4)),
        scratch_shapes=[
            pltpu.VMEM((19, depth, FIRST + width + 8, lanes), jnp.float32),
            pltpu.VMEM((19, depth, width, lanes), jnp.bfloat16),
            pltpu.VMEM((2 * depth * width, 3 * lanes), jnp.bfloat16),
            pltpu.VMEM((4 * width, 3 * lanes), jnp.bfloat16),
            pltpu.VMEM((2, 5, width, lanes), jnp.bfloat16),
            pltpu.VMEM((EXT, lanes), jnp.float32),
            pltpu.VMEM((depth, lanes), jnp.float32),
            pltpu.SemaphoreType.DMA((4,)),
        ],
        compiler_params=params(),
        cost_estimate=cost(5),
        name="step",
    )(*parts, sums, mag_in, mag_out, cells, weights, segments, *notes)


def arrive_kernel(next_in, first, second, arrived_hbm, next_hbm, force_ref, arrived, sems):
    depth = next_hbm.shape[1]
    odd = is_odd("span")
    shares = pltpu.make_async_copy(arrived_hbm, arrived, sems.at[10])
    shares.start()

    def place(below, above):
        copies = []
        for source, wanted, z in ((below, RISING, 0), (above, FALLING, depth - 1)):
            for index, q in enumerate(wanted):
                copies.append(
                    pltpu.make_async_copy(source.at[index], next_hbm.at[q, z], sems.at[len(copies)])
                )
                copies[-1].start()
        for copy in copies:
            copy.wait()

    @pl.when(odd)
    def _():
        place(first, second)

    @pl.when(jnp.logical_not(odd))
    def _():
        place(second, first)

    shares.wait()
    total = jnp.sum(arrived[:, 0, :], axis=0, keepdims=True)
    for dim in range(3):
        force_ref[pl.ds(dim, 1), :] = total[:, dim * SEG_DEV : (dim + 1) * SEG_DEV]


def arrive(populations_next, first, second, arrived):
    hbm = pl.BlockSpec(memory_space=pl.ANY)
    return pl.pallas_call(
        arrive_kernel,
        out_shape=(
            full(populations_next.shape, jnp.bfloat16),
            full((3, SEG_DEV), jnp.float32),
        ),
        in_specs=[hbm] + in_vmem(2) + [hbm],
        out_specs=(hbm, in_vmem(1)[0]),
        input_output_aliases={0: 0},
        scratch_shapes=[
            pltpu.VMEM(arrived.shape, jnp.float32),
            pltpu.SemaphoreType.DMA((11,)),
        ],
        compiler_params=params(),
        cost_estimate=cost(0.5),
        name="arrive",
    )(populations_next, first, second, arrived)


def local(populations, cell_index, marker_weight, segment_id):
    owners = lax.axis_size("span") * lax.axis_size("cross")
    cells, weights, segments = cell_index.T, marker_weight.T, segment_id[None, :]
    vel, *lines = block_moments(populations)
    lines = swap(*lines, "cross")
    planes = swap(*edge_planes(vel, *lines, cells, weights, segments), "span")
    partial, mag_in = inner_sums(vel, *lines)
    faces = swap(*face_rows(populations, partial), "cross")
    sums, mag_out = outer_sums(vel, *lines, *planes, partial)
    parts = ready(populations, *faces, sums)
    count = lax.axis_size("span")
    if count & (count - 1):
        sums = lax.psum(sums, "span")
    else:
        distance = 1
        while distance < count:
            pairs = [(i, i ^ distance) for i in range(count)]
            sums = sums + lax.ppermute(sums, "span", pairs)
            distance *= 2
    moved, eddy_coeff, packed, *leaving = step(
        parts, sums, mag_in, mag_out, cells, weights, segments, planes, owners
    )
    arrived = lax.all_to_all(packed, ("span", "cross"), 0, 0)
    populations_next, segment_force = arrive(moved, *swap(*leaving, "span"), arrived)
    return (populations_next, eddy_coeff, segment_force)


def solution(mesh):
    in_specs = (
        P(None, "span", "cross", None),
        P(("span", "cross"), None),
        P(("span", "cross"), None),
        P(("span", "cross")),
    )
    out_specs = (P(None, "span", "cross", None), P("cross", None), P(None, ("span", "cross")))
    return jax.shard_map(local, mesh=mesh, in_specs=in_specs, out_specs=out_specs, check_vma=False)
```

```python
import functools

import jax
import jax.numpy as jnp
from jax import lax
from jax.experimental import pallas as pl
from jax.experimental.pallas import tpu as pltpu
from jax.sharding import PartitionSpec as P

SEG_DEV = 8
LANES = 128
HALO = 3
EXT = 40
PAD = 56
OWN = 11
TOP = 8
CHUNKS = (8, 16, 24, 32, 40)
VMEM = 28 * 1024 * 1024

eps_sum = 1e-06
base_visc = 0.005

VELOCITIES = [
    [0, 0, 0],
    [1, 0, 0],
    [-1, 0, 0],
    [0, 1, 0],
    [0, -1, 0],
    [0, 0, 1],
    [0, 0, -1],
    [1, 1, 0],
    [-1, -1, 0],
    [1, -1, 0],
    [-1, 1, 0],
    [1, 0, 1],
    [-1, 0, -1],
    [1, 0, -1],
    [-1, 0, 1],
    [0, 1, 1],
    [0, -1, -1],
    [0, 1, -1],
    [0, -1, 1],
]


def swap(first, second, axis):
    count = lax.axis_size(axis)
    near = [(i, i ^ 1) for i in range(count)]
    other = [(i, (i + 1 if i % 2 else i - 1) % count) for i in range(count)]
    return lax.ppermute(first, axis, near), lax.ppermute(second, axis, other)


def is_odd(axis):
    return lax.rem(lax.axis_index(axis), 2) == 1


def send_pair(axis, upwards, downwards, first, second):
    odd = is_odd(axis)

    @pl.when(odd)
    def _():
        first[...] = downwards
        second[...] = upwards

    @pl.when(jnp.logical_not(odd))
    def _():
        first[...] = upwards
        second[...] = downwards


def below_above(axis, first, second):
    odd = is_odd(axis)
    return jnp.where(odd, first, second), jnp.where(odd, second, first)


def full(shape, dtype):
    return jax.ShapeDtypeStruct(shape, dtype)


def in_vmem(count):
    return [pl.BlockSpec(memory_space=pltpu.VMEM)] * count


def params():
    return pltpu.CompilerParams(vmem_limit_bytes=VMEM)


def cost(micros):
    return pl.CostEstimate(flops=0, bytes_accessed=int(micros * 3.6e6), transcendentals=0)


def plus(array):
    return pltpu.roll(array, LANES - 1, 1)


def minus(array):
    return pltpu.roll(array, 1, 1)


STEP = 2.0**-15


def encode(value):
    return jnp.round(value * (1.0 / STEP)).astype(jnp.int32).astype(jnp.int16)


def decode(coded):
    return coded.astype(jnp.int32).astype(jnp.float32) * STEP


def split(value):
    high = value.astype(jnp.bfloat16)
    return high, (value - high.astype(jnp.float32)).astype(jnp.bfloat16)


def plane_loop(start, stop, body, carry, most):
    count = stop - start
    step = max(size for size in range(1, most + 1) if count % size == 0)

    def block(index, carry):
        for shift in range(step):
            carry = body(start + index * step + shift, carry)
        return carry

    if count == step:
        return block(0, carry)
    return lax.fori_loop(0, count // step, block, carry)


def moments_kernel(pops, vel_ref, first, second, rows):
    depth, width = pops.shape[1:3]

    def plane(z, carry):
        for half in range(width // 16):
            at = pl.ds(16 * half, 16)
            f = [pops[q, z, at, :].astype(jnp.float32) for q in range(19)]
            flux = [0.0, 0.0, 0.0]
            density = f[0]
            for q in range(1, 19, 2):
                even, odd = f[q] + f[q + 1], f[q] - f[q + 1]
                density = density + even
                for dim in range(3):
                    sign = VELOCITIES[q][dim]
                    if sign:
                        flux[dim] = flux[dim] + odd if sign > 0 else flux[dim] - odd
            inverse = 1.0 / density
            for dim in range(3):
                speed = flux[dim] * inverse
                vel_ref[dim, z, at, :] = speed
                for k in range(HALO):
                    if half == 0:
                        rows[0, dim * HALO + k, pl.ds(z, 1), :] = speed[k : k + 1]
                    if half == width // 16 - 1:
                        rows[1, dim * HALO + k, pl.ds(z, 1), :] = speed[15 - k : 16 - k]
        return carry

    plane_loop(0, depth, plane, 0, 4)
    send_pair("cross", encode(rows[1]), encode(rows[0]), first, second)


def block_moments(populations):
    _, depth, width, lanes = populations.shape
    edge = full((3 * HALO, depth, lanes), jnp.int16)
    return pl.pallas_call(
        moments_kernel,
        out_shape=(full((3, depth, width, lanes), jnp.float32), edge, edge),
        in_specs=in_vmem(1),
        out_specs=tuple(in_vmem(3)),
        scratch_shapes=[pltpu.VMEM((2, 3 * HALO, depth, lanes), jnp.float32)],
        compiler_params=params(),
        cost_estimate=cost(1),
        name="moments",
    )(populations)


def decode_rows(first, second, rows):
    rows[0], rows[1] = below_above("cross", decode(first[...]), decode(second[...]))


def place_plane(ext, p, vel_ref, rows, z):
    width = vel_ref.shape[2]
    for dim in range(3):
        ext[dim, p, pl.ds(OWN, width), :] = vel_ref[dim, z]
        for k in range(HALO):
            line = pl.ds(z, 1)
            ext[dim, p, pl.ds(OWN - 1 - k, 1), :] = rows[0, dim * HALO + k, line, :]
            ext[dim, p, pl.ds(OWN + width + k, 1), :] = rows[1, dim * HALO + k, line, :]


TALL = 40
FREE = [(slot, row) for slot in (1, 3, 5) for row in (0, 37, 38, 39)]
FREE += [(slot, row) for slot in (0, 2, 4) for row in (38, 39)]


def edges_kernel(
    vel_ref,
    low_ref,
    high_ref,
    cell_ref,
    weight_ref,
    segment_ref,
    first,
    second,
    rows,
    planes,
    note,
):
    depth, width = vel_ref.shape[1:3]
    taps = cell_ref.shape[0]
    decode_rows(low_ref, high_ref, rows)
    note[pl.ds(0, taps), :] = cell_ref[...].astype(jnp.float32) - 2.0**15
    note[pl.ds(taps, taps), :] = weight_ref[...] * 2.0**17 - 2.0**14
    note[pl.ds(2 * taps, 1), :] = segment_ref[...].astype(jnp.float32)
    coded = []
    for pair in ((0, 1), (depth - 1, depth - 2)):
        planes[...] = jnp.zeros_like(planes)
        for dim in range(3):
            for index, z in enumerate(pair):
                slot = 2 * dim + index
                planes[slot, pl.ds(HALO, width), :] = vel_ref[dim, z]
                for k in range(HALO):
                    line = pl.ds(z, 1)
                    planes[slot, pl.ds(HALO - 1 - k, 1), :] = rows[0, dim * HALO + k, line, :]
                    planes[slot, pl.ds(HALO + width + k, 1), :] = rows[1, dim * HALO + k, line, :]
        for index in range(2 * taps + 1):
            slot, row = FREE[index]
            planes[slot, pl.ds(row, 1), :] = note[pl.ds(index, 1), :] * STEP
        coded.append(encode(planes[...]))
    send_pair("span", coded[1], coded[0], first, second)


def free_rows(first, second, start, count):
    picked = []
    for message in (first, second):
        picked.append(
            jnp.concatenate(
                [
                    message[slot].astype(jnp.int32)[row : row + 1]
                    for slot, row in FREE[start : start + count]
                ],
                axis=0,
            )
        )
    return below_above("span", *picked)


def edge_planes(vel, low, high, cells, weights, segments):
    pair = full((6, TALL, LANES), jnp.int16)
    return pl.pallas_call(
        edges_kernel,
        out_shape=(pair, pair),
        in_specs=in_vmem(6),
        out_specs=tuple(in_vmem(2)),
        scratch_shapes=[
            pltpu.VMEM((2, 3 * HALO, vel.shape[1], LANES), jnp.float32),
            pltpu.VMEM((6, TALL, LANES), jnp.float32),
            pltpu.VMEM((2 * cells.shape[0] + 8, LANES), jnp.float32),
        ],
        compiler_params=params(),
        cost_estimate=cost(0.2),
        name="edges",
    )(vel, low, high, cells, weights, segments)


def strain_parts(ref, p, row, before, here, after):
    grads = [
        (
            plus(here[dim]) - minus(here[dim]),
            ref[dim, p, pl.ds(row + 1, 8), :] - ref[dim, p, pl.ds(row - 1, 8), :],
            after[dim] - before[dim],
        )
        for dim in range(3)
    ]
    parts = [
        grads[0][0],
        grads[1][1],
        grads[2][2],
        grads[0][1] + grads[1][0],
        grads[0][2] + grads[2][0],
        grads[1][2] + grads[2][1],
    ]
    straight = parts[0] * parts[0] + parts[1] * parts[1] + parts[2] * parts[2]
    mixed = parts[3] * parts[3] + parts[4] * parts[4] + parts[5] * parts[5]
    return parts, jnp.sqrt(0.5 * straight + 0.25 * mixed)


def weigh(low, middle, high):
    return (low + high) + (middle + middle)


PAIRS = ((0, 0), (1, 1), (2, 2), (0, 1), (0, 2), (1, 2))


def three(ref, p, rows):
    return [ref[dim, p, rows, :] for dim in range(3)]


def model_sums(planes, ext, hat, zsum, zvel, acc_ref, store_mag):
    for row in CHUNKS:
        rows = pl.ds(row, 8)

        def first_pass(p, carry):
            before, here, lag, last = carry
            after = three(ext, p + 1, rows)
            parts, size = strain_parts(ext, p, row, before, here, after)
            store_mag(p, row, size)
            prods = [size * part for part in parts] + [here[i] * here[j] for i, j in PAIRS]
            for k in range(12):
                zsum[k, p - 1, rows, :] = lag[k] + prods[k]
            for dim in range(3):
                zvel[dim, p, rows, :] = weigh(before[dim], here[dim], after[dim])
            lag = [last[k] + (prods[k] + prods[k]) for k in range(12)]
            return here, after, lag, prods

        none = [jnp.zeros((8, LANES), jnp.float32)] * 12
        carry = (three(ext, 0, rows), three(ext, 1, rows), none, none)
        plane_loop(1, planes - 1, first_pass, carry, 14)

    def second_pass(p, carry):
        for row in CHUNKS:
            for dim in range(3):
                line = weigh(*[zvel[dim, p, pl.ds(row + shift, 8), :] for shift in (-1, 0, 1)])
                hat[dim, p, pl.ds(row, 8), :] = (1.0 / 64.0) * weigh(minus(line), line, plus(line))
        return carry

    plane_loop(1, planes - 1, second_pass, 0, 14)

    for row in CHUNKS:
        rows = pl.ds(row, 8)

        def third_pass(p, carry):
            before, here, lm, mm = carry
            after = three(hat, p + 1, rows)
            parts, size = strain_parts(hat, p, row, before, here, after)
            size = 256.0 * size
            scaled = [64.0 * speed for speed in here]
            squares = [0.0, 0.0]
            for k, (i, j) in enumerate(PAIRS):
                smooth = []
                for field in (k, 6 + k):
                    line = weigh(
                        *[zsum[field, p, pl.ds(row + shift, 8), :] for shift in (-1, 0, 1)]
                    )
                    smooth.append(weigh(minus(line), line, plus(line)))
                model = smooth[0] - size * parts[k]
                lm = lm + (smooth[1] - scaled[i] * here[j]) * model
                squares[k // 3] = squares[k // 3] + model * model
            return here, after, lm, mm + (squares[0] + 0.5 * squares[1])

        none = jnp.zeros((8, LANES), jnp.float32)
        carry = (three(hat, 1, rows), three(hat, 2, rows), none, none)
        _, _, lm, mm = plane_loop(2, planes - 2, third_pass, carry, 12)
        out = pl.ds(row - TOP, 8)
        acc_ref[0, out, :] += (1.0 / 4096.0) * lm
        acc_ref[1, out, :] += (1.0 / 4096.0) * mm


def inner_kernel(vel_ref, low_ref, high_ref, acc_ref, mag_ref, ext, hat, zsum, zvel, rows):
    depth = vel_ref.shape[1]
    decode_rows(low_ref, high_ref, rows)

    def assemble(p, carry):
        place_plane(ext, p, vel_ref, rows, p)
        return carry

    plane_loop(0, depth, assemble, 0, 4)
    acc_ref[...] = jnp.zeros_like(acc_ref)

    def store_mag(p, row, size):
        mag_ref[p - 1, pl.ds(row - TOP, 8), :] = size

    model_sums(depth, ext, hat, zsum, zvel, acc_ref, store_mag)


def model_scratch(planes, depth):
    return [
        pltpu.VMEM((3, planes, PAD, LANES), jnp.float32),
        pltpu.VMEM((3, planes, PAD, LANES), jnp.float32),
        pltpu.VMEM((12, planes, PAD, LANES), jnp.float32),
        pltpu.VMEM((3, planes, PAD, LANES), jnp.float32),
        pltpu.VMEM((2, 3 * HALO, depth, LANES), jnp.float32),
    ]


def inner_sums(vel, low, high):
    depth = vel.shape[1]
    return pl.pallas_call(
        inner_kernel,
        out_shape=(
            full((2, EXT, LANES), jnp.float32),
            full((depth - 2, EXT, LANES), jnp.float32),
        ),
        in_specs=in_vmem(3),
        out_specs=tuple(in_vmem(2)),
        scratch_shapes=model_scratch(depth, depth),
        compiler_params=params(),
        cost_estimate=cost(5),
        name="inner_sums",
    )(vel, low, high)


def outer_kernel(
    vel_ref,
    low_ref,
    high_ref,
    first_ref,
    second_ref,
    partial_ref,
    sums_ref,
    mag_ref,
    ext,
    hat,
    zsum,
    zvel,
    rows,
    acc,
):
    depth, width = vel_ref.shape[1:3]
    decode_rows(low_ref, high_ref, rows)
    acc[...] = partial_ref[...]
    below, above = below_above("span", decode(first_ref[...]), decode(second_ref[...]))
    for side, (message, places, start) in enumerate(
        ((below, (1, 0), 0), (above, (4, 5), depth - 4))
    ):
        for index in range(4):
            place_plane(ext, index + (2 if side == 0 else 0), vel_ref, rows, start + index)
        for dim in range(3):
            for index, p in enumerate(places):
                ext[dim, p, pl.ds(OWN - HALO, TALL), :] = message[2 * dim + index]

        def store_mag(p, row, size):
            mag_ref[4 * side + p - 1, pl.ds(row - TOP, 8), :] = size

        model_sums(6, ext, hat, zsum, zvel, acc, store_mag)
    lines = width + 2
    sums_ref[...] = jnp.zeros_like(sums_ref)
    for index in range(2):
        sums_ref[pl.ds(index * lines, lines), :] = acc[index, pl.ds(OWN - TOP - 1, lines), :]


def outer_sums(vel, low, high, below, above, partial):
    depth, width = vel.shape[1:3]
    return pl.pallas_call(
        outer_kernel,
        out_shape=(
            full((-(-2 * (width + 2) // 8) * 8, LANES), jnp.float32),
            full((8, EXT, LANES), jnp.float32),
        ),
        in_specs=in_vmem(6),
        out_specs=tuple(in_vmem(2)),
        scratch_shapes=model_scratch(6, depth) + [pltpu.VMEM((2, EXT, LANES), jnp.float32)],
        compiler_params=params(),
        cost_estimate=cost(2),
        name="outer_sums",
    )(vel, low, high, below, above, partial)


def rows_kernel(pops, after_this, first, second, rows):
    depth, width = pops.shape[1:3]

    def plane(z, carry):
        for q in range(19):
            low = pops[q, z, pl.ds(0, 16), :].astype(jnp.float32)
            high = pops[q, z, pl.ds(width - 16, 16), :].astype(jnp.float32)
            rows[0, q, pl.ds(z, 1), :] = low[:1]
            rows[1, q, pl.ds(z, 1), :] = high[15:]
        return carry

    plane_loop(0, depth, plane, 0, 4)
    send_pair(
        "cross", rows[1].astype(jnp.bfloat16), rows[0].astype(jnp.bfloat16), first, second
    )


def face_rows(populations, after_this):
    _, depth, width, lanes = populations.shape
    edge = full((19, depth, lanes), jnp.bfloat16)
    return pl.pallas_call(
        rows_kernel,
        out_shape=(edge, edge),
        in_specs=in_vmem(1) + [pl.BlockSpec(memory_space=pl.ANY)],
        out_specs=tuple(in_vmem(2)),
        scratch_shapes=[pltpu.VMEM((2, 19, depth, lanes), jnp.float32)],
        compiler_params=params(),
        cost_estimate=cost(0.5),
        name="face_rows",
    )(populations, after_this)


def relax_parts(f):
    even = {q: f[q] + f[q + 1] for q in range(1, 19, 2)}
    odd = {q: f[q] - f[q + 1] for q in range(1, 19, 2)}
    x_xy, x_xz = odd[7] + odd[9], odd[11] + odd[13]
    y_yz, y_xy = odd[15] + odd[17], odd[7] - odd[9]
    z_xz, z_yz = odd[11] - odd[13], odd[15] - odd[17]
    flux, up, down, axis_odd = [], [], [], []
    for first, second, along in ((x_xy, x_xz, 1), (y_yz, y_xy, 3), (z_xz, z_yz, 5)):
        sides = first + second
        total = odd[along] + sides
        heat = 0.15 * (sides - (2.0 / 3.0) * total)
        twist = (1.98 / 8.0) * (first - second)
        flux.append(total)
        up.append(heat + twist)
        down.append(heat - twist)
        axis_odd.append(4.0 * heat)
    a, b, c = even[7] + even[9], even[11] + even[13], even[15] + even[17]
    axes = even[1] + even[3] + even[5]
    diagonals = a + b + c
    density = f[0] + axes + diagonals
    inverse = 1.0 / density
    speed = [total * inverse for total in flux]
    square = [total * part for total, part in zip(flux, speed)]
    energy = square[0] + square[1] + square[2]
    d_e = (1.19 / 126.0) * (diagonals - f[0] - energy)
    d_eps = (1.4 / 252.0) * (9.0 * f[0] - 7.0 * axes - 2.0 * diagonals + 5.5 * energy)
    ax_n, dg_n, eq_n = 3.0 * even[1] - axes, diagonals - 3.0 * c, 3.0 * square[0] - energy
    ax_w, dg_w, eq_w = even[3] - even[5], a - b, square[1] - square[2]
    d_pn = (1.4 / 72.0) * (dg_n - 2.0 * ax_n + 0.5 * eq_n)
    d_pw = (1.4 / 24.0) * (dg_w - 2.0 * ax_w + 0.5 * eq_w)
    shear = [
        (1.0 / 36.0) * (ax_n + dg_n - eq_n),
        (1.0 / 12.0) * (ax_w + dg_w - eq_w),
        0.25 * (even[7] - even[9] - flux[0] * speed[1]),
        0.25 * (even[11] - even[13] - flux[0] * speed[2]),
        0.25 * (even[15] - even[17] - flux[1] * speed[2]),
    ]
    base_axis = 11.0 * d_e + 4.0 * d_eps
    base_diag = -8.0 * d_e - d_eps
    base = [None] * 19
    base[0] = f[0] + (30.0 * d_e - 12.0 * d_eps)
    rest = base_axis - 2.0 * d_pn
    for q, change, skew in (
        (1, base_axis + 4.0 * d_pn, axis_odd[0]),
        (3, rest + 2.0 * d_pw, axis_odd[1]),
        (5, rest - 2.0 * d_pw, axis_odd[2]),
    ):
        base[q] = f[q] + (change + skew)
        base[q + 1] = f[q + 1] + (change - skew)
    rest = base_diag - d_pn
    for q, change, one, two in (
        (7, rest - d_pw, up[0], down[1]),
        (11, rest + d_pw, down[0], up[2]),
        (15, base_diag + 2.0 * d_pn, up[1], down[2]),
    ):
        same, other = one + two, one - two
        base[q] = f[q] + (change - same)
        base[q + 1] = f[q + 1] + (change + same)
        base[q + 2] = f[q + 2] + (change - other)
        base[q + 3] = f[q + 3] + (change + other)
    return base, shear


def shear_changes(shear, rate):
    n, w, xy, xz, yz = [rate * part for part in shear]
    lean = n + w
    tilt = n - w
    twice = n + n
    changes = [None] * 19
    changes[1] = changes[2] = -twice
    changes[3] = changes[4] = tilt
    changes[5] = changes[6] = lean
    changes[7] = changes[8] = -(lean + xy)
    changes[9] = changes[10] = xy - lean
    changes[11] = changes[12] = -(tilt + xz)
    changes[13] = changes[14] = xz - tilt
    changes[15] = changes[16] = twice - yz
    changes[17] = changes[18] = twice + yz
    return changes


def relax_rate(eddy, size):
    return 1.0 / (0.5 + 3.0 * (base_visc + eddy * size))


BEFORE = [q for q in range(19) if VELOCITIES[q][1] > 0]
AFTER = [q for q in range(19) if VELOCITIES[q][1] < 0]
RISING = [q for q in range(19) if VELOCITIES[q][2] > 0]
FALLING = [q for q in range(19) if VELOCITIES[q][2] < 0]
FIRST = 8


def ready_kernel(pops, first, second, after_this, base_ref, shear_ref, edge_ref, edge_shear):
    depth, width = pops.shape[1:3]
    rows = [
        below_above("cross", first[q].astype(jnp.float32), second[q].astype(jnp.float32))
        for q in range(19)
    ]
    for side, wanted in enumerate((BEFORE, AFTER)):
        base, shear = relax_parts([pair[side] for pair in rows])
        for index, q in enumerate(wanted):
            edge_ref[side, index] = base[q]
        for k in range(5):
            edge_shear[side, k] = shear[k]

    def plane(z, carry):
        for half in range(width // 16):
            rows = pl.ds(16 * half, 16)
            base, shear = relax_parts([pops[q, z, rows, :].astype(jnp.float32) for q in range(19)])
            for q in range(19):
                base_ref[q, z, rows, :] = base[q]
            for k in range(5):
                shear_ref[k, z, rows, :] = shear[k]
        return carry

    plane_loop(0, depth, plane, 0, 4)


def ready(populations, before, after, after_this):
    _, depth, width, lanes = populations.shape
    return pl.pallas_call(
        ready_kernel,
        out_shape=(
            full((19, depth, width, lanes), jnp.float32),
            full((5, depth, width, lanes), jnp.float32),
            full((2, 5, depth, lanes), jnp.float32),
            full((2, 5, depth, lanes), jnp.float32),
        ),
        in_specs=in_vmem(3) + [pl.BlockSpec(memory_space=pl.ANY)],
        out_specs=tuple(in_vmem(4)),
        compiler_params=params(),
        cost_estimate=cost(2.5),
        name="ready",
    )(populations, before, after, after_this)


def table_rows(table, at, low_at, flux):
    for dim in range(3):
        coarse, fine = split(flux[dim])
        table[at, dim * LANES : (dim + 1) * LANES] = coarse
        table[low_at, dim * LANES : (dim + 1) * LANES] = fine


def add_flux(flux, q, moved):
    for dim in range(3):
        sign = VELOCITIES[q][dim]
        if sign:
            flux[dim] = flux[dim] + moved if sign > 0 else flux[dim] - moved


def marker_force(table, picks, lanes, weights, taps):
    lane_of = lax.broadcasted_iota(jnp.int32, (LANES, lanes[0].shape[1]), 0)
    picked = lax.dot_general(
        table,
        jnp.concatenate(picks, axis=1),
        (((0,), (0,)), ((), ())),
        preferred_element_type=jnp.float32,
    )
    markers = lanes[0].shape[1]
    force = [0.0, 0.0, 0.0]
    for tap, (lane, weight) in enumerate(zip(lanes, weights)):
        mask = jnp.where(lane_of == lane, -weight, 0.0)
        at = slice(tap * markers, (tap + 1) * markers)
        for dim in range(3):
            force[dim] = force[dim] + picked[dim * LANES : (dim + 1) * LANES, at] * mask
        if (tap + 1) % taps == 0:
            yield [jnp.sum(part, axis=0, keepdims=True) for part in force]
            force = [0.0, 0.0, 0.0]


def step_kernel(
    base_ref,
    shear_ref,
    edge_ref,
    edge_shear,
    sums_ref,
    mag_in_ref,
    mag_out_ref,
    cell_ref,
    weight_ref,
    segment_ref,
    note_first,
    note_second,
    next_hbm,
    eddy_ref,
    partial_ref,
    first_ref,
    second_ref,
    post,
    nexts,
    table,
    face_table,
    faces,
    eddy,
    line,
    out_sems,
):
    depth, width = shear_ref.shape[1:3]
    lines = width + 2
    part = depth // 4
    eddy[...] = jnp.zeros_like(eddy)
    eddy[pl.ds(OWN - TOP - 1, lines), :] = jnp.maximum(
        sums_ref[pl.ds(0, lines), :] / (sums_ref[pl.ds(lines, lines), :] + eps_sum), 0.0
    )
    eddy_ref[...] = eddy[pl.ds(OWN - TOP, width), :]

    for side, (wanted, row, place) in enumerate(
        ((BEFORE, OWN - TOP - 1, FIRST - 1), (AFTER, OWN - TOP + width, FIRST + width))
    ):
        for z in range(depth):
            if z == 0:
                size = mag_out_ref[1, pl.ds(row, 1), :]
            elif z == depth - 1:
                size = mag_out_ref[6, pl.ds(row, 1), :]
            else:
                size = mag_in_ref[z - 1, pl.ds(row, 1), :]
            line[pl.ds(z, 1), :] = size
        rate = relax_rate(eddy[pl.ds(row, 1), :], line[...])
        changes = shear_changes([edge_shear[side, k] for k in range(5)], rate)
        for index, q in enumerate(wanted):
            out = edge_ref[side, index] + changes[q]
            for z in range(depth):
                post[q, z, pl.ds(place, 1), :] = out[z : z + 1]

    def collide(z, size_ref, at):
        for half in range(width // 16):
            rows = pl.ds(16 * half, 16)
            around = pl.ds(OWN - TOP + 16 * half, 16)
            rate = relax_rate(eddy[around, :], size_ref[at, around, :])
            changes = shear_changes([shear_ref[k, z, rows, :] for k in range(5)], rate)
            for q in range(19):
                value = base_ref[q, z, rows, :]
                if q:
                    value = value + changes[q]
                post[q, z, pl.ds(FIRST + 16 * half, 16), :] = value

    def inner(z, carry):
        collide(z, mag_in_ref, z - 1)
        return carry

    collide(0, mag_out_ref, 1)
    collide(depth - 1, mag_out_ref, 6)
    plane_loop(1, depth - 1, inner, 0, 7)

    def shifted(q, z, half):
        shift_x, shift_y, _ = VELOCITIES[q]
        piece = post[q, z, pl.ds(FIRST + 16 * half - shift_y, 16), :]
        if shift_x:
            piece = minus(piece) if shift_x > 0 else plus(piece)
        return piece.astype(jnp.bfloat16)

    def run(z, leave_out=()):
        for half in range(width // 16):
            flux = [0.0, 0.0, 0.0]
            for q in range(19):
                if q in leave_out:
                    continue
                moved = shifted(q, z - VELOCITIES[q][2], half)
                nexts[q, z, pl.ds(16 * half, 16), :] = moved
                if q:
                    add_flux(flux, q, moved.astype(jnp.float32))
            row = pl.multiple_of(z * width + 16 * half, 16)
            low_row = pl.multiple_of((depth + z) * width + 16 * half, 16)
            table_rows(table, pl.ds(row, 16), pl.ds(low_row, 16), flux)

    def run_inner(z, carry):
        run(z)
        return carry

    for side, (wanted, z) in enumerate(((RISING, depth - 1), (FALLING, 0))):
        for half in range(width // 16):
            rows = pl.ds(16 * half, 16)
            flux = [0.0, 0.0, 0.0]
            for index, q in enumerate(wanted):
                moved = shifted(q, z, half)
                faces[side, index, rows, :] = moved
                add_flux(flux, q, moved.astype(jnp.float32))
            row = side * width + 16 * half
            table_rows(face_table, pl.ds(row, 16), pl.ds(2 * width + row, 16), flux)
    send_pair("span", faces[0], faces[1], first_ref, second_ref)

    outs = []
    for index in range(4):
        start, stop = index * part, (index + 1) * part
        if index == 0:
            run(0, RISING)
            start += 1
        if index == 3:
            run(depth - 1, FALLING)
            stop -= 1
        plane_loop(start, stop, run_inner, 0, 4)
        place = pl.ds(index * part, part)
        outs.append(
            pltpu.make_async_copy(nexts.at[:, place], next_hbm.at[:, place], out_sems.at[index])
        )
        outs[-1].start()

    owners = partial_ref.shape[0]
    taps, markers = cell_ref.shape
    cells_all = depth * width
    note_below, note_above = free_rows(note_first, note_second, 0, 2 * taps + 1)

    def one_hot(rows, period, wanted):
        row_of = lax.broadcasted_iota(jnp.int32, (period, markers), 0)
        picks = []
        for tap in range(taps):
            hit = jnp.where(row_of == wanted[tap : tap + 1, :], 1.0, 0.0).astype(jnp.bfloat16)
            picks.append(jnp.concatenate([hit] * (rows // period), axis=0))
        return picks

    def row_lane(cells):
        return lax.shift_right_logical(cells, 7), lax.bitwise_and(cells, LANES - 1)

    def each(array):
        return [array[tap : tap + 1, :] for tap in range(taps)]

    row, lane = row_lane(cell_ref[...])
    forces = list(
        marker_force(
            table[...],
            one_hot(2 * cells_all, cells_all, row),
            each(lane),
            each(weight_ref[...]),
            taps,
        )
    )
    segments = [segment_ref[...]]
    picks, lanes, weights = [], [], []
    for side, note in enumerate((note_above, note_below)):
        row, lane = row_lane(note[:taps] + 2**15)
        row = row - side * (cells_all - width)
        inside = jnp.logical_and(row >= 0, row < width)
        picks += one_hot(4 * width, 2 * width, jnp.where(inside, row + side * width, -1))
        lanes += each(lane)
        weights += each(
            (note[taps : 2 * taps].astype(jnp.float32) + 2.0**14) * 2.0**-17
        )
        segments.append(note[2 * taps : 2 * taps + 1])
    forces += list(marker_force(face_table[...], picks, lanes, weights, taps))

    owner_of = lax.broadcasted_iota(jnp.int32, (owners, markers), 0)
    place_of = lax.broadcasted_iota(jnp.int32, (SEG_DEV, markers), 0)
    mine, spread = [], []
    for force, segment in zip(forces, segments):
        hit = jnp.where(owner_of == lax.shift_right_logical(segment, 3), 1.0, 0.0)
        mine.append(hit.astype(jnp.bfloat16))
        place = place_of == lax.bitwise_and(segment, SEG_DEV - 1)
        spread.append(
            jnp.concatenate([jnp.where(place, part, 0.0) for part in force], axis=0)
        )
    mine, rest = jnp.concatenate(mine, axis=1), jnp.concatenate(spread, axis=1)
    rest = jnp.concatenate([rest, jnp.zeros((LANES - 3 * SEG_DEV, 3 * markers), jnp.float32)], axis=0)
    totals = 0.0
    for _ in range(3):
        coarse = rest.astype(jnp.bfloat16)
        rest = rest - coarse.astype(jnp.float32)
        totals = totals + lax.dot_general(
            mine, coarse, (((1,), (1,)), ((), ())), preferred_element_type=jnp.float32
        )
    partial_ref[:, 0, :] = totals
    for copy in outs:
        copy.wait()


def step(parts, sums, mag_in, mag_out, cells, weights, segments, notes, owners):
    _, depth, width, lanes = parts[0].shape
    face = full((5, width, lanes), jnp.bfloat16)
    return pl.pallas_call(
        step_kernel,
        out_shape=(
            full((19, depth, width, lanes), jnp.bfloat16),
            full((width, lanes), jnp.float32),
            full((owners, 1, lanes), jnp.float32),
            face,
            face,
        ),
        in_specs=in_vmem(12),
        out_specs=(pl.BlockSpec(memory_space=pl.ANY),) + tuple(in_vmem(4)),
        scratch_shapes=[
            pltpu.VMEM((19, depth, FIRST + width + 8, lanes), jnp.float32),
            pltpu.VMEM((19, depth, width, lanes), jnp.bfloat16),
            pltpu.VMEM((2 * depth * width, 3 * lanes), jnp.bfloat16),
            pltpu.VMEM((4 * width, 3 * lanes), jnp.bfloat16),
            pltpu.VMEM((2, 5, width, lanes), jnp.bfloat16),
            pltpu.VMEM((EXT, lanes), jnp.float32),
            pltpu.VMEM((depth, lanes), jnp.float32),
            pltpu.SemaphoreType.DMA((4,)),
        ],
        compiler_params=params(),
        cost_estimate=cost(5),
        name="step",
    )(*parts, sums, mag_in, mag_out, cells, weights, segments, *notes)


def arrive_kernel(next_in, first, second, arrived_hbm, next_hbm, force_ref, arrived, sems):
    depth = next_hbm.shape[1]
    odd = is_odd("span")
    shares = pltpu.make_async_copy(arrived_hbm, arrived, sems.at[10])
    shares.start()

    def place(below, above):
        copies = []
        for source, wanted, z in ((below, RISING, 0), (above, FALLING, depth - 1)):
            for index, q in enumerate(wanted):
                copies.append(
                    pltpu.make_async_copy(source.at[index], next_hbm.at[q, z], sems.at[len(copies)])
                )
                copies[-1].start()
        for copy in copies:
            copy.wait()

    @pl.when(odd)
    def _():
        place(first, second)

    @pl.when(jnp.logical_not(odd))
    def _():
        place(second, first)

    shares.wait()
    total = jnp.sum(arrived[:, 0, :], axis=0, keepdims=True)
    for dim in range(3):
        force_ref[pl.ds(dim, 1), :] = total[:, dim * SEG_DEV : (dim + 1) * SEG_DEV]


def arrive(populations_next, first, second, arrived):
    hbm = pl.BlockSpec(memory_space=pl.ANY)
    return pl.pallas_call(
        arrive_kernel,
        out_shape=(
            full(populations_next.shape, jnp.bfloat16),
            full((3, SEG_DEV), jnp.float32),
        ),
        in_specs=[hbm] + in_vmem(2) + [hbm],
        out_specs=(hbm, in_vmem(1)[0]),
        input_output_aliases={0: 0},
        scratch_shapes=[
            pltpu.VMEM(arrived.shape, jnp.float32),
            pltpu.SemaphoreType.DMA((11,)),
        ],
        compiler_params=params(),
        cost_estimate=cost(0.5),
        name="arrive",
    )(populations_next, first, second, arrived)


def local(populations, cell_index, marker_weight, segment_id):
    owners = lax.axis_size("span") * lax.axis_size("cross")
    cells, weights, segments = cell_index.T, marker_weight.T, segment_id[None, :]
    vel, *lines = block_moments(populations)
    lines = swap(*lines, "cross")
    planes = swap(*edge_planes(vel, *lines, cells, weights, segments), "span")
    partial, mag_in = inner_sums(vel, *lines)
    faces = swap(*face_rows(populations, partial), "cross")
    sums, mag_out = outer_sums(vel, *lines, *planes, partial)
    parts = ready(populations, *faces, sums)
    count = lax.axis_size("span")
    if count & (count - 1):
        sums = lax.psum(sums, "span")
    else:
        distance = 1
        while distance < count:
            pairs = [(i, i ^ distance) for i in range(count)]
            sums = sums + lax.ppermute(sums, "span", pairs)
            distance *= 2
    moved, eddy_coeff, packed, *leaving = step(
        parts, sums, mag_in, mag_out, cells, weights, segments, planes, owners
    )
    arrived = lax.all_to_all(packed, ("span", "cross"), 0, 0)
    populations_next, segment_force = arrive(moved, *swap(*leaving, "span"), arrived)
    return (populations_next, eddy_coeff, segment_force)


def solution(mesh):
    in_specs = (
        P(None, "span", "cross", None),
        P(("span", "cross"), None),
        P(("span", "cross"), None),
        P(("span", "cross")),
    )
    out_specs = (P(None, "span", "cross", None), P("cross", None), P(None, ("span", "cross")))
    return jax.shard_map(local, mesh=mesh, in_specs=in_specs, out_specs=out_specs, check_vma=False)
```

```python
import functools

import jax
import jax.numpy as jnp
from jax import lax
from jax.experimental import pallas as pl
from jax.experimental.pallas import tpu as pltpu
from jax.sharding import PartitionSpec as P

SEG_DEV = 8
LANES = 128
HALO = 3
EXT = 40
PAD = 56
OWN = 11
TOP = 8
CHUNKS = (8, 16, 24, 32, 40)
VMEM = 28 * 1024 * 1024

eps_sum = 1e-06
base_visc = 0.005

VELOCITIES = [
    [0, 0, 0],
    [1, 0, 0],
    [-1, 0, 0],
    [0, 1, 0],
    [0, -1, 0],
    [0, 0, 1],
    [0, 0, -1],
    [1, 1, 0],
    [-1, -1, 0],
    [1, -1, 0],
    [-1, 1, 0],
    [1, 0, 1],
    [-1, 0, -1],
    [1, 0, -1],
    [-1, 0, 1],
    [0, 1, 1],
    [0, -1, -1],
    [0, 1, -1],
    [0, -1, 1],
]


def swap(first, second, axis):
    count = lax.axis_size(axis)
    near = [(i, i ^ 1) for i in range(count)]
    other = [(i, (i + 1 if i % 2 else i - 1) % count) for i in range(count)]
    return lax.ppermute(first, axis, near), lax.ppermute(second, axis, other)


def is_odd(axis):
    return lax.rem(lax.axis_index(axis), 2) == 1


def send_pair(axis, upwards, downwards, first, second):
    odd = is_odd(axis)

    @pl.when(odd)
    def _():
        first[...] = downwards
        second[...] = upwards

    @pl.when(jnp.logical_not(odd))
    def _():
        first[...] = upwards
        second[...] = downwards


def below_above(axis, first, second):
    odd = is_odd(axis)
    return jnp.where(odd, first, second), jnp.where(odd, second, first)


def full(shape, dtype):
    return jax.ShapeDtypeStruct(shape, dtype)


def in_vmem(count):
    return [pl.BlockSpec(memory_space=pltpu.VMEM)] * count


def params():
    return pltpu.CompilerParams(vmem_limit_bytes=VMEM)


def cost(micros):
    return pl.CostEstimate(flops=0, bytes_accessed=int(micros * 3.6e6), transcendentals=0)


def plus(array):
    return pltpu.roll(array, LANES - 1, 1)


def minus(array):
    return pltpu.roll(array, 1, 1)


STEP = 2.0**-15


def encode(value):
    return jnp.round(value * (1.0 / STEP)).astype(jnp.int32).astype(jnp.int16)


def decode(coded):
    return coded.astype(jnp.int32).astype(jnp.float32) * STEP


def split(value):
    high = value.astype(jnp.bfloat16)
    return high, (value - high.astype(jnp.float32)).astype(jnp.bfloat16)


def plane_loop(start, stop, body, carry, most):
    count = stop - start
    step = max(size for size in range(1, most + 1) if count % size == 0)

    def block(index, carry):
        for shift in range(step):
            carry = body(start + index * step + shift, carry)
        return carry

    if count == step:
        return block(0, carry)
    return lax.fori_loop(0, count // step, block, carry)


def moments_kernel(pops, vel_ref, first, second, rows):
    depth, width = pops.shape[1:3]

    def plane(z, carry):
        for half in range(width // 16):
            at = pl.ds(16 * half, 16)
            f = [pops[q, z, at, :].astype(jnp.float32) for q in range(19)]
            flux = [0.0, 0.0, 0.0]
            density = f[0]
            for q in range(1, 19, 2):
                even, odd = f[q] + f[q + 1], f[q] - f[q + 1]
                density = density + even
                for dim in range(3):
                    sign = VELOCITIES[q][dim]
                    if sign:
                        flux[dim] = flux[dim] + odd if sign > 0 else flux[dim] - odd
            inverse = 1.0 / density
            for dim in range(3):
                speed = flux[dim] * inverse
                vel_ref[dim, z, at, :] = speed
                for k in range(HALO):
                    if half == 0:
                        rows[0, dim * HALO + k, pl.ds(z, 1), :] = speed[k : k + 1]
                    if half == width // 16 - 1:
                        rows[1, dim * HALO + k, pl.ds(z, 1), :] = speed[15 - k : 16 - k]
        return carry

    plane_loop(0, depth, plane, 0, 4)
    send_pair("cross", encode(rows[1]), encode(rows[0]), first, second)


def block_moments(populations):
    _, depth, width, lanes = populations.shape
    edge = full((3 * HALO, depth, lanes), jnp.int16)
    return pl.pallas_call(
        moments_kernel,
        out_shape=(full((3, depth, width, lanes), jnp.float32), edge, edge),
        in_specs=in_vmem(1),
        out_specs=tuple(in_vmem(3)),
        scratch_shapes=[pltpu.VMEM((2, 3 * HALO, depth, lanes), jnp.float32)],
        compiler_params=params(),
        cost_estimate=cost(1),
        name="moments",
    )(populations)


def decode_rows(first, second, rows):
    rows[0], rows[1] = below_above("cross", decode(first[...]), decode(second[...]))


def place_plane(ext, p, vel_ref, rows, z):
    width = vel_ref.shape[2]
    for dim in range(3):
        ext[dim, p, pl.ds(OWN, width), :] = vel_ref[dim, z]
        for k in range(HALO):
            line = pl.ds(z, 1)
            ext[dim, p, pl.ds(OWN - 1 - k, 1), :] = rows[0, dim * HALO + k, line, :]
            ext[dim, p, pl.ds(OWN + width + k, 1), :] = rows[1, dim * HALO + k, line, :]


TALL = 40
FREE = [(slot, row) for slot in (1, 3, 5) for row in (0, 37, 38, 39)]
FREE += [(slot, row) for slot in (0, 2, 4) for row in (38, 39)]


def edges_kernel(
    vel_ref,
    low_ref,
    high_ref,
    cell_ref,
    weight_ref,
    segment_ref,
    first,
    second,
    rows,
    planes,
    note,
):
    depth, width = vel_ref.shape[1:3]
    taps = cell_ref.shape[0]
    decode_rows(low_ref, high_ref, rows)
    note[pl.ds(0, taps), :] = cell_ref[...].astype(jnp.float32) - 2.0**15
    note[pl.ds(taps, taps), :] = weight_ref[...] * 2.0**17 - 2.0**14
    note[pl.ds(2 * taps, 1), :] = segment_ref[...].astype(jnp.float32)
    coded = []
    for pair in ((0, 1), (depth - 1, depth - 2)):
        planes[...] = jnp.zeros_like(planes)
        for dim in range(3):
            for index, z in enumerate(pair):
                slot = 2 * dim + index
                planes[slot, pl.ds(HALO, width), :] = vel_ref[dim, z]
                for k in range(HALO):
                    line = pl.ds(z, 1)
                    planes[slot, pl.ds(HALO - 1 - k, 1), :] = rows[0, dim * HALO + k, line, :]
                    planes[slot, pl.ds(HALO + width + k, 1), :] = rows[1, dim * HALO + k, line, :]
        for index in range(2 * taps + 1):
            slot, row = FREE[index]
            planes[slot, pl.ds(row, 1), :] = note[pl.ds(index, 1), :] * STEP
        coded.append(encode(planes[...]))
    send_pair("span", coded[1], coded[0], first, second)


def free_rows(first, second, start, count):
    picked = []
    for message in (first, second):
        picked.append(
            jnp.concatenate(
                [
                    message[slot].astype(jnp.int32)[row : row + 1]
                    for slot, row in FREE[start : start + count]
                ],
                axis=0,
            )
        )
    return below_above("span", *picked)


def edge_planes(vel, low, high, cells, weights, segments):
    pair = full((6, TALL, LANES), jnp.int16)
    return pl.pallas_call(
        edges_kernel,
        out_shape=(pair, pair),
        in_specs=in_vmem(6),
        out_specs=tuple(in_vmem(2)),
        scratch_shapes=[
            pltpu.VMEM((2, 3 * HALO, vel.shape[1], LANES), jnp.float32),
            pltpu.VMEM((6, TALL, LANES), jnp.float32),
            pltpu.VMEM((2 * cells.shape[0] + 8, LANES), jnp.float32),
        ],
        compiler_params=params(),
        cost_estimate=cost(0.2),
        name="edges",
    )(vel, low, high, cells, weights, segments)


def strain_parts(ref, p, row, before, here, after):
    grads = [
        (
            plus(here[dim]) - minus(here[dim]),
            ref[dim, p, pl.ds(row + 1, 8), :] - ref[dim, p, pl.ds(row - 1, 8), :],
            after[dim] - before[dim],
        )
        for dim in range(3)
    ]
    parts = [
        grads[0][0],
        grads[1][1],
        grads[2][2],
        grads[0][1] + grads[1][0],
        grads[0][2] + grads[2][0],
        grads[1][2] + grads[2][1],
    ]
    straight = parts[0] * parts[0] + parts[1] * parts[1] + parts[2] * parts[2]
    mixed = parts[3] * parts[3] + parts[4] * parts[4] + parts[5] * parts[5]
    return parts, jnp.sqrt(0.5 * straight + 0.25 * mixed)


def weigh(low, middle, high):
    return (low + high) + (middle + middle)


PAIRS = ((0, 0), (1, 1), (2, 2), (0, 1), (0, 2), (1, 2))


def three(ref, p, rows):
    return [ref[dim, p, rows, :] for dim in range(3)]


def model_sums(planes, ext, hat, zsum, zvel, acc_ref, store_mag):
    for row in CHUNKS:
        rows = pl.ds(row, 8)

        def first_pass(p, carry):
            before, here, lag, last = carry
            after = three(ext, p + 1, rows)
            parts, size = strain_parts(ext, p, row, before, here, after)
            store_mag(p, row, size)
            prods = [size * part for part in parts] + [here[i] * here[j] for i, j in PAIRS]
            for k in range(12):
                zsum[k, p - 1, rows, :] = lag[k] + prods[k]
            for dim in range(3):
                zvel[dim, p, rows, :] = weigh(before[dim], here[dim], after[dim])
            lag = [last[k] + (prods[k] + prods[k]) for k in range(12)]
            return here, after, lag, prods

        none = [jnp.zeros((8, LANES), jnp.float32)] * 12
        carry = (three(ext, 0, rows), three(ext, 1, rows), none, none)
        plane_loop(1, planes - 1, first_pass, carry, 14)

    def second_pass(p, carry):
        for row in CHUNKS:
            for dim in range(3):
                line = weigh(*[zvel[dim, p, pl.ds(row + shift, 8), :] for shift in (-1, 0, 1)])
                hat[dim, p, pl.ds(row, 8), :] = (1.0 / 64.0) * weigh(minus(line), line, plus(line))
        return carry

    plane_loop(1, planes - 1, second_pass, 0, 14)

    for row in CHUNKS:
        rows = pl.ds(row, 8)

        def third_pass(p, carry):
            before, here, lm, mm = carry
            after = three(hat, p + 1, rows)
            parts, size = strain_parts(hat, p, row, before, here, after)
            size = 256.0 * size
            scaled = [64.0 * speed for speed in here]
            squares = [0.0, 0.0]
            for k, (i, j) in enumerate(PAIRS):
                smooth = []
                for field in (k, 6 + k):
                    line = weigh(
                        *[zsum[field, p, pl.ds(row + shift, 8), :] for shift in (-1, 0, 1)]
                    )
                    smooth.append(weigh(minus(line), line, plus(line)))
                model = smooth[0] - size * parts[k]
                lm = lm + (smooth[1] - scaled[i] * here[j]) * model
                squares[k // 3] = squares[k // 3] + model * model
            return here, after, lm, mm + (squares[0] + 0.5 * squares[1])

        none = jnp.zeros((8, LANES), jnp.float32)
        carry = (three(hat, 1, rows), three(hat, 2, rows), none, none)
        _, _, lm, mm = plane_loop(2, planes - 2, third_pass, carry, 12)
        out = pl.ds(row - TOP, 8)
        acc_ref[0, out, :] += (1.0 / 4096.0) * lm
        acc_ref[1, out, :] += (1.0 / 4096.0) * mm


def inner_kernel(vel_ref, low_ref, high_ref, acc_ref, mag_ref, ext, hat, zsum, zvel, rows):
    depth = vel_ref.shape[1]
    decode_rows(low_ref, high_ref, rows)

    def assemble(p, carry):
        place_plane(ext, p, vel_ref, rows, p)
        return carry

    plane_loop(0, depth, assemble, 0, 4)
    acc_ref[...] = jnp.zeros_like(acc_ref)

    def store_mag(p, row, size):
        mag_ref[p - 1, pl.ds(row - TOP, 8), :] = size

    model_sums(depth, ext, hat, zsum, zvel, acc_ref, store_mag)


def model_scratch(planes, depth):
    return [
        pltpu.VMEM((3, planes, PAD, LANES), jnp.float32),
        pltpu.VMEM((3, planes, PAD, LANES), jnp.float32),
        pltpu.VMEM((12, planes, PAD, LANES), jnp.float32),
        pltpu.VMEM((3, planes, PAD, LANES), jnp.float32),
        pltpu.VMEM((2, 3 * HALO, depth, LANES), jnp.float32),
    ]


def inner_sums(vel, low, high):
    depth = vel.shape[1]
    return pl.pallas_call(
        inner_kernel,
        out_shape=(
            full((2, EXT, LANES), jnp.float32),
            full((depth - 2, EXT, LANES), jnp.float32),
        ),
        in_specs=in_vmem(3),
        out_specs=tuple(in_vmem(2)),
        scratch_shapes=model_scratch(depth, depth),
        compiler_params=params(),
        cost_estimate=cost(5),
        name="inner_sums",
    )(vel, low, high)


def outer_kernel(
    vel_ref,
    low_ref,
    high_ref,
    first_ref,
    second_ref,
    partial_ref,
    sums_ref,
    mag_ref,
    words_ref,
    ext,
    hat,
    zsum,
    zvel,
    rows,
    acc,
    stage,
):
    depth, width = vel_ref.shape[1:3]
    decode_rows(low_ref, high_ref, rows)
    acc[...] = partial_ref[...]
    below, above = below_above("span", decode(first_ref[...]), decode(second_ref[...]))
    for side, (message, places, start) in enumerate(
        ((below, (1, 0), 0), (above, (4, 5), depth - 4))
    ):
        for index in range(4):
            place_plane(ext, index + (2 if side == 0 else 0), vel_ref, rows, start + index)
        for dim in range(3):
            for index, p in enumerate(places):
                ext[dim, p, pl.ds(OWN - HALO, TALL), :] = message[2 * dim + index]

        def store_mag(p, row, size):
            mag_ref[4 * side + p - 1, pl.ds(row - TOP, 8), :] = size

        model_sums(6, ext, hat, zsum, zvel, acc, store_mag)
    lines = width + 2
    sums_ref[...] = jnp.zeros_like(sums_ref)
    for index in range(2):
        sums_ref[pl.ds(index * lines, lines), :] = acc[index, pl.ds(OWN - TOP - 1, lines), :]
    stage[...] = jnp.zeros_like(stage)
    words = pack(*[acc[index, pl.ds(OWN - TOP - 1, lines), :] for index in range(2)])
    store_words(words, stage, words_ref)


def outer_sums(vel, low, high, below, above, partial):
    depth, width = vel.shape[1:3]
    words = -(-3 * (width + 2) // 8) * 8
    return pl.pallas_call(
        outer_kernel,
        out_shape=(
            full((-(-2 * (width + 2) // 8) * 8, LANES), jnp.float32),
            full((8, EXT, LANES), jnp.float32),
            full((words, LANES), jnp.int16),
        ),
        in_specs=in_vmem(6),
        out_specs=tuple(in_vmem(3)),
        scratch_shapes=model_scratch(6, depth) + [
            pltpu.VMEM((2, EXT, LANES), jnp.float32),
            pltpu.VMEM((words, LANES), jnp.float32),
        ],
        compiler_params=params(),
        cost_estimate=cost(2),
        name="outer_sums",
    )(vel, low, high, below, above, partial)


def to_code(value):
    size = jnp.clip(jnp.abs(value), 2.0**-63, 2.0**63)
    steps = jnp.round((jnp.log(size) * 1.4426950408889634 + 64.0) * 2.0**16).astype(jnp.int32)
    return jnp.where(value < 0.0, steps + 2**23, steps)


def from_code(code):
    steps = lax.bitwise_and(code, 2**23 - 1).astype(jnp.float32)
    size = jnp.exp((steps * 2.0**-16 - 64.0) * 0.6931471805599453)
    return jnp.where(code >= 2**23, -size, size)


def pack(lm, mm):
    lm, mm = to_code(lm), to_code(mm)
    low = lax.bitwise_and(lm, 255) * 256 + lax.bitwise_and(mm, 255)
    words = [lax.shift_right_logical(lm, 8), lax.shift_right_logical(mm, 8), low]
    return [(word - 2**15).astype(jnp.float32) for word in words]


def unpack(words):
    lm, mm, low = [word + 2**15 for word in words]
    return (
        from_code(lm * 256 + lax.shift_right_logical(low, 8)),
        from_code(mm * 256 + lax.bitwise_and(low, 255)),
    )


def store_words(words, stage, out):
    lines = words[0].shape[0]
    for index, word in enumerate(words):
        stage[pl.ds(index * lines, lines), :] = word
    out[...] = stage[...].astype(jnp.int32).astype(jnp.int16)


def combine_kernel(lines, own, other, out, stage):
    total = (0.0, 0.0)
    for message in (own, other):
        stage[...] = message[...].astype(jnp.int32).astype(jnp.float32)
        words = [stage[pl.ds(index * lines, lines), :].astype(jnp.int32) for index in range(3)]
        total = [before + value for before, value in zip(total, unpack(words))]
    if out.dtype == jnp.int16:
        store_words(pack(*total), stage, out)
    else:
        out[...] = jnp.zeros_like(out)
        for index in range(2):
            out[pl.ds(index * lines, lines), :] = total[index]


def combine(own, other, lines, like):
    return pl.pallas_call(
        functools.partial(combine_kernel, lines),
        out_shape=full(like.shape, like.dtype),
        in_specs=in_vmem(2),
        out_specs=in_vmem(1)[0],
        scratch_shapes=[pltpu.VMEM(own.shape, jnp.float32)],
        compiler_params=params(),
        cost_estimate=cost(0.1),
        name="combine",
    )(own, other)


def rows_kernel(pops, after_this, first, second, rows):
    depth, width = pops.shape[1:3]

    def plane(z, carry):
        for q in range(19):
            low = pops[q, z, pl.ds(0, 16), :].astype(jnp.float32)
            high = pops[q, z, pl.ds(width - 16, 16), :].astype(jnp.float32)
            rows[0, q, pl.ds(z, 1), :] = low[:1]
            rows[1, q, pl.ds(z, 1), :] = high[15:]
        return carry

    plane_loop(0, depth, plane, 0, 4)
    send_pair(
        "cross", rows[1].astype(jnp.bfloat16), rows[0].astype(jnp.bfloat16), first, second
    )


def face_rows(populations, after_this):
    _, depth, width, lanes = populations.shape
    edge = full((19, depth, lanes), jnp.bfloat16)
    return pl.pallas_call(
        rows_kernel,
        out_shape=(edge, edge),
        in_specs=in_vmem(1) + [pl.BlockSpec(memory_space=pl.ANY)],
        out_specs=tuple(in_vmem(2)),
        scratch_shapes=[pltpu.VMEM((2, 19, depth, lanes), jnp.float32)],
        compiler_params=params(),
        cost_estimate=cost(0.5),
        name="face_rows",
    )(populations, after_this)


def relax_parts(f):
    even = {q: f[q] + f[q + 1] for q in range(1, 19, 2)}
    odd = {q: f[q] - f[q + 1] for q in range(1, 19, 2)}
    x_xy, x_xz = odd[7] + odd[9], odd[11] + odd[13]
    y_yz, y_xy = odd[15] + odd[17], odd[7] - odd[9]
    z_xz, z_yz = odd[11] - odd[13], odd[15] - odd[17]
    flux, up, down, axis_odd = [], [], [], []
    for first, second, along in ((x_xy, x_xz, 1), (y_yz, y_xy, 3), (z_xz, z_yz, 5)):
        sides = first + second
        total = odd[along] + sides
        heat = 0.15 * (sides - (2.0 / 3.0) * total)
        twist = (1.98 / 8.0) * (first - second)
        flux.append(total)
        up.append(heat + twist)
        down.append(heat - twist)
        axis_odd.append(4.0 * heat)
    a, b, c = even[7] + even[9], even[11] + even[13], even[15] + even[17]
    axes = even[1] + even[3] + even[5]
    diagonals = a + b + c
    density = f[0] + axes + diagonals
    inverse = 1.0 / density
    speed = [total * inverse for total in flux]
    square = [total * part for total, part in zip(flux, speed)]
    energy = square[0] + square[1] + square[2]
    d_e = (1.19 / 126.0) * (diagonals - f[0] - energy)
    d_eps = (1.4 / 252.0) * (9.0 * f[0] - 7.0 * axes - 2.0 * diagonals + 5.5 * energy)
    ax_n, dg_n, eq_n = 3.0 * even[1] - axes, diagonals - 3.0 * c, 3.0 * square[0] - energy
    ax_w, dg_w, eq_w = even[3] - even[5], a - b, square[1] - square[2]
    d_pn = (1.4 / 72.0) * (dg_n - 2.0 * ax_n + 0.5 * eq_n)
    d_pw = (1.4 / 24.0) * (dg_w - 2.0 * ax_w + 0.5 * eq_w)
    shear = [
        (1.0 / 36.0) * (ax_n + dg_n - eq_n),
        (1.0 / 12.0) * (ax_w + dg_w - eq_w),
        0.25 * (even[7] - even[9] - flux[0] * speed[1]),
        0.25 * (even[11] - even[13] - flux[0] * speed[2]),
        0.25 * (even[15] - even[17] - flux[1] * speed[2]),
    ]
    base_axis = 11.0 * d_e + 4.0 * d_eps
    base_diag = -8.0 * d_e - d_eps
    base = [None] * 19
    base[0] = f[0] + (30.0 * d_e - 12.0 * d_eps)
    rest = base_axis - 2.0 * d_pn
    for q, change, skew in (
        (1, base_axis + 4.0 * d_pn, axis_odd[0]),
        (3, rest + 2.0 * d_pw, axis_odd[1]),
        (5, rest - 2.0 * d_pw, axis_odd[2]),
    ):
        base[q] = f[q] + (change + skew)
        base[q + 1] = f[q + 1] + (change - skew)
    rest = base_diag - d_pn
    for q, change, one, two in (
        (7, rest - d_pw, up[0], down[1]),
        (11, rest + d_pw, down[0], up[2]),
        (15, base_diag + 2.0 * d_pn, up[1], down[2]),
    ):
        same, other = one + two, one - two
        base[q] = f[q] + (change - same)
        base[q + 1] = f[q + 1] + (change + same)
        base[q + 2] = f[q + 2] + (change - other)
        base[q + 3] = f[q + 3] + (change + other)
    return base, shear


def shear_changes(shear, rate):
    n, w, xy, xz, yz = [rate * part for part in shear]
    lean = n + w
    tilt = n - w
    twice = n + n
    changes = [None] * 19
    changes[1] = changes[2] = -twice
    changes[3] = changes[4] = tilt
    changes[5] = changes[6] = lean
    changes[7] = changes[8] = -(lean + xy)
    changes[9] = changes[10] = xy - lean
    changes[11] = changes[12] = -(tilt + xz)
    changes[13] = changes[14] = xz - tilt
    changes[15] = changes[16] = twice - yz
    changes[17] = changes[18] = twice + yz
    return changes


def relax_rate(eddy, size):
    return 1.0 / (0.5 + 3.0 * (base_visc + eddy * size))


BEFORE = [q for q in range(19) if VELOCITIES[q][1] > 0]
AFTER = [q for q in range(19) if VELOCITIES[q][1] < 0]
RISING = [q for q in range(19) if VELOCITIES[q][2] > 0]
FALLING = [q for q in range(19) if VELOCITIES[q][2] < 0]
FIRST = 8


def ready_kernel(pops, first, second, after_this, base_ref, shear_ref, edge_ref, edge_shear):
    depth, width = pops.shape[1:3]
    rows = [
        below_above("cross", first[q].astype(jnp.float32), second[q].astype(jnp.float32))
        for q in range(19)
    ]
    for side, wanted in enumerate((BEFORE, AFTER)):
        base, shear = relax_parts([pair[side] for pair in rows])
        for index, q in enumerate(wanted):
            edge_ref[side, index] = base[q]
        for k in range(5):
            edge_shear[side, k] = shear[k]

    def plane(z, carry):
        for half in range(width // 16):
            rows = pl.ds(16 * half, 16)
            base, shear = relax_parts([pops[q, z, rows, :].astype(jnp.float32) for q in range(19)])
            for q in range(19):
                base_ref[q, z, rows, :] = base[q]
            for k in range(5):
                shear_ref[k, z, rows, :] = shear[k]
        return carry

    plane_loop(0, depth, plane, 0, 4)


def ready(populations, before, after, after_this):
    _, depth, width, lanes = populations.shape
    return pl.pallas_call(
        ready_kernel,
        out_shape=(
            full((19, depth, width, lanes), jnp.float32),
            full((5, depth, width, lanes), jnp.float32),
            full((2, 5, depth, lanes), jnp.float32),
            full((2, 5, depth, lanes), jnp.float32),
        ),
        in_specs=in_vmem(3) + [pl.BlockSpec(memory_space=pl.ANY)],
        out_specs=tuple(in_vmem(4)),
        compiler_params=params(),
        cost_estimate=cost(2.5),
        name="ready",
    )(populations, before, after, after_this)


def table_rows(table, at, low_at, flux):
    for dim in range(3):
        coarse, fine = split(flux[dim])
        table[at, dim * LANES : (dim + 1) * LANES] = coarse
        table[low_at, dim * LANES : (dim + 1) * LANES] = fine


def add_flux(flux, q, moved):
    for dim in range(3):
        sign = VELOCITIES[q][dim]
        if sign:
            flux[dim] = flux[dim] + moved if sign > 0 else flux[dim] - moved


def marker_force(table, picks, lanes, weights, taps):
    lane_of = lax.broadcasted_iota(jnp.int32, (LANES, lanes[0].shape[1]), 0)
    picked = lax.dot_general(
        table,
        jnp.concatenate(picks, axis=1),
        (((0,), (0,)), ((), ())),
        preferred_element_type=jnp.float32,
    )
    markers = lanes[0].shape[1]
    force = [0.0, 0.0, 0.0]
    for tap, (lane, weight) in enumerate(zip(lanes, weights)):
        mask = jnp.where(lane_of == lane, -weight, 0.0)
        at = slice(tap * markers, (tap + 1) * markers)
        for dim in range(3):
            force[dim] = force[dim] + picked[dim * LANES : (dim + 1) * LANES, at] * mask
        if (tap + 1) % taps == 0:
            yield [jnp.sum(part, axis=0, keepdims=True) for part in force]
            force = [0.0, 0.0, 0.0]


def step_kernel(
    base_ref,
    shear_ref,
    edge_ref,
    edge_shear,
    sums_ref,
    mag_in_ref,
    mag_out_ref,
    cell_ref,
    weight_ref,
    segment_ref,
    note_first,
    note_second,
    next_hbm,
    eddy_ref,
    partial_ref,
    first_ref,
    second_ref,
    post,
    nexts,
    table,
    face_table,
    faces,
    eddy,
    line,
    out_sems,
):
    depth, width = shear_ref.shape[1:3]
    lines = width + 2
    part = depth // 4
    eddy[...] = jnp.zeros_like(eddy)
    eddy[pl.ds(OWN - TOP - 1, lines), :] = jnp.maximum(
        sums_ref[pl.ds(0, lines), :] / (sums_ref[pl.ds(lines, lines), :] + eps_sum), 0.0
    )
    eddy_ref[...] = eddy[pl.ds(OWN - TOP, width), :]

    for side, (wanted, row, place) in enumerate(
        ((BEFORE, OWN - TOP - 1, FIRST - 1), (AFTER, OWN - TOP + width, FIRST + width))
    ):
        for z in range(depth):
            if z == 0:
                size = mag_out_ref[1, pl.ds(row, 1), :]
            elif z == depth - 1:
                size = mag_out_ref[6, pl.ds(row, 1), :]
            else:
                size = mag_in_ref[z - 1, pl.ds(row, 1), :]
            line[pl.ds(z, 1), :] = size
        rate = relax_rate(eddy[pl.ds(row, 1), :], line[...])
        changes = shear_changes([edge_shear[side, k] for k in range(5)], rate)
        for index, q in enumerate(wanted):
            out = edge_ref[side, index] + changes[q]
            for z in range(depth):
                post[q, z, pl.ds(place, 1), :] = out[z : z + 1]

    def collide(z, size_ref, at):
        for half in range(width // 16):
            rows = pl.ds(16 * half, 16)
            around = pl.ds(OWN - TOP + 16 * half, 16)
            rate = relax_rate(eddy[around, :], size_ref[at, around, :])
            changes = shear_changes([shear_ref[k, z, rows, :] for k in range(5)], rate)
            for q in range(19):
                value = base_ref[q, z, rows, :]
                if q:
                    value = value + changes[q]
                post[q, z, pl.ds(FIRST + 16 * half, 16), :] = value

    def inner(z, carry):
        collide(z, mag_in_ref, z - 1)
        return carry

    collide(0, mag_out_ref, 1)
    collide(depth - 1, mag_out_ref, 6)
    plane_loop(1, depth - 1, inner, 0, 7)

    def shifted(q, z, half):
        shift_x, shift_y, _ = VELOCITIES[q]
        piece = post[q, z, pl.ds(FIRST + 16 * half - shift_y, 16), :]
        if shift_x:
            piece = minus(piece) if shift_x > 0 else plus(piece)
        return piece.astype(jnp.bfloat16)

    def run(z, leave_out=()):
        for half in range(width // 16):
            flux = [0.0, 0.0, 0.0]
            for q in range(19):
                if q in leave_out:
                    continue
                moved = shifted(q, z - VELOCITIES[q][2], half)
                nexts[q, z, pl.ds(16 * half, 16), :] = moved
                if q:
                    add_flux(flux, q, moved.astype(jnp.float32))
            row = pl.multiple_of(z * width + 16 * half, 16)
            low_row = pl.multiple_of((depth + z) * width + 16 * half, 16)
            table_rows(table, pl.ds(row, 16), pl.ds(low_row, 16), flux)

    def run_inner(z, carry):
        run(z)
        return carry

    for side, (wanted, z) in enumerate(((RISING, depth - 1), (FALLING, 0))):
        for half in range(width // 16):
            rows = pl.ds(16 * half, 16)
            flux = [0.0, 0.0, 0.0]
            for index, q in enumerate(wanted):
                moved = shifted(q, z, half)
                faces[side, index, rows, :] = moved
                add_flux(flux, q, moved.astype(jnp.float32))
            row = side * width + 16 * half
            table_rows(face_table, pl.ds(row, 16), pl.ds(2 * width + row, 16), flux)
    send_pair("span", faces[0], faces[1], first_ref, second_ref)

    outs = []
    for index in range(4):
        start, stop = index * part, (index + 1) * part
        if index == 0:
            run(0, RISING)
            start += 1
        if index == 3:
            run(depth - 1, FALLING)
            stop -= 1
        plane_loop(start, stop, run_inner, 0, 4)
        place = pl.ds(index * part, part)
        outs.append(
            pltpu.make_async_copy(nexts.at[:, place], next_hbm.at[:, place], out_sems.at[index])
        )
        outs[-1].start()

    owners = partial_ref.shape[0]
    taps, markers = cell_ref.shape
    cells_all = depth * width
    note_below, note_above = free_rows(note_first, note_second, 0, 2 * taps + 1)

    def one_hot(rows, period, wanted):
        row_of = lax.broadcasted_iota(jnp.int32, (period, markers), 0)
        picks = []
        for tap in range(taps):
            hit = jnp.where(row_of == wanted[tap : tap + 1, :], 1.0, 0.0).astype(jnp.bfloat16)
            picks.append(jnp.concatenate([hit] * (rows // period), axis=0))
        return picks

    def row_lane(cells):
        return lax.shift_right_logical(cells, 7), lax.bitwise_and(cells, LANES - 1)

    def each(array):
        return [array[tap : tap + 1, :] for tap in range(taps)]

    row, lane = row_lane(cell_ref[...])
    forces = list(
        marker_force(
            table[...],
            one_hot(2 * cells_all, cells_all, row),
            each(lane),
            each(weight_ref[...]),
            taps,
        )
    )
    segments = [segment_ref[...]]
    picks, lanes, weights = [], [], []
    for side, note in enumerate((note_above, note_below)):
        row, lane = row_lane(note[:taps] + 2**15)
        row = row - side * (cells_all - width)
        inside = jnp.logical_and(row >= 0, row < width)
        picks += one_hot(4 * width, 2 * width, jnp.where(inside, row + side * width, -1))
        lanes += each(lane)
        weights += each(
            (note[taps : 2 * taps].astype(jnp.float32) + 2.0**14) * 2.0**-17
        )
        segments.append(note[2 * taps : 2 * taps + 1])
    forces += list(marker_force(face_table[...], picks, lanes, weights, taps))

    owner_of = lax.broadcasted_iota(jnp.int32, (owners, markers), 0)
    place_of = lax.broadcasted_iota(jnp.int32, (SEG_DEV, markers), 0)
    mine, spread = [], []
    for force, segment in zip(forces, segments):
        hit = jnp.where(owner_of == lax.shift_right_logical(segment, 3), 1.0, 0.0)
        mine.append(hit.astype(jnp.bfloat16))
        place = place_of == lax.bitwise_and(segment, SEG_DEV - 1)
        spread.append(
            jnp.concatenate([jnp.where(place, part, 0.0) for part in force], axis=0)
        )
    mine, rest = jnp.concatenate(mine, axis=1), jnp.concatenate(spread, axis=1)
    rest = jnp.concatenate([rest, jnp.zeros((LANES - 3 * SEG_DEV, 3 * markers), jnp.float32)], axis=0)
    totals = 0.0
    for _ in range(3):
        coarse = rest.astype(jnp.bfloat16)
        rest = rest - coarse.astype(jnp.float32)
        totals = totals + lax.dot_general(
            mine, coarse, (((1,), (1,)), ((), ())), preferred_element_type=jnp.float32
        )
    partial_ref[:, 0, :] = totals
    for copy in outs:
        copy.wait()


def step(parts, sums, mag_in, mag_out, cells, weights, segments, notes, owners):
    _, depth, width, lanes = parts[0].shape
    face = full((5, width, lanes), jnp.bfloat16)
    return pl.pallas_call(
        step_kernel,
        out_shape=(
            full((19, depth, width, lanes), jnp.bfloat16),
            full((width, lanes), jnp.float32),
            full((owners, 1, lanes), jnp.float32),
            face,
            face,
        ),
        in_specs=in_vmem(12),
        out_specs=(pl.BlockSpec(memory_space=pl.ANY),) + tuple(in_vmem(4)),
        scratch_shapes=[
            pltpu.VMEM((19, depth, FIRST + width + 8, lanes), jnp.float32),
            pltpu.VMEM((19, depth, width, lanes), jnp.bfloat16),
            pltpu.VMEM((2 * depth * width, 3 * lanes), jnp.bfloat16),
            pltpu.VMEM((4 * width, 3 * lanes), jnp.bfloat16),
            pltpu.VMEM((2, 5, width, lanes), jnp.bfloat16),
            pltpu.VMEM((EXT, lanes), jnp.float32),
            pltpu.VMEM((depth, lanes), jnp.float32),
            pltpu.SemaphoreType.DMA((4,)),
        ],
        compiler_params=params(),
        cost_estimate=cost(5),
        name="step",
    )(*parts, sums, mag_in, mag_out, cells, weights, segments, *notes)


def arrive_kernel(next_in, first, second, arrived_hbm, next_hbm, force_ref, arrived, sems):
    depth = next_hbm.shape[1]
    odd = is_odd("span")
    shares = pltpu.make_async_copy(arrived_hbm, arrived, sems.at[10])
    shares.start()

    def place(below, above):
        copies = []
        for source, wanted, z in ((below, RISING, 0), (above, FALLING, depth - 1)):
            for index, q in enumerate(wanted):
                copies.append(
                    pltpu.make_async_copy(source.at[index], next_hbm.at[q, z], sems.at[len(copies)])
                )
                copies[-1].start()
        for copy in copies:
            copy.wait()

    @pl.when(odd)
    def _():
        place(first, second)

    @pl.when(jnp.logical_not(odd))
    def _():
        place(second, first)

    shares.wait()
    total = jnp.sum(arrived[:, 0, :], axis=0, keepdims=True)
    for dim in range(3):
        force_ref[pl.ds(dim, 1), :] = total[:, dim * SEG_DEV : (dim + 1) * SEG_DEV]


def arrive(populations_next, first, second, arrived):
    hbm = pl.BlockSpec(memory_space=pl.ANY)
    return pl.pallas_call(
        arrive_kernel,
        out_shape=(
            full(populations_next.shape, jnp.bfloat16),
            full((3, SEG_DEV), jnp.float32),
        ),
        in_specs=[hbm] + in_vmem(2) + [hbm],
        out_specs=(hbm, in_vmem(1)[0]),
        input_output_aliases={0: 0},
        scratch_shapes=[
            pltpu.VMEM(arrived.shape, jnp.float32),
            pltpu.SemaphoreType.DMA((11,)),
        ],
        compiler_params=params(),
        cost_estimate=cost(0.5),
        name="arrive",
    )(populations_next, first, second, arrived)


def local(populations, cell_index, marker_weight, segment_id):
    owners = lax.axis_size("span") * lax.axis_size("cross")
    cells, weights, segments = cell_index.T, marker_weight.T, segment_id[None, :]
    vel, *lines = block_moments(populations)
    lines = swap(*lines, "cross")
    planes = swap(*edge_planes(vel, *lines, cells, weights, segments), "span")
    partial, mag_in = inner_sums(vel, *lines)
    faces = swap(*face_rows(populations, partial), "cross")
    sums, mag_out, words = outer_sums(vel, *lines, *planes, partial)
    parts = ready(populations, *faces, sums)
    count = lax.axis_size("span")
    if count & (count - 1):
        sums = lax.psum(sums, "span")
    else:
        distance = 1
        lines = populations.shape[2] + 2
        while distance < count:
            pairs = [(i, i ^ distance) for i in range(count)]
            other = lax.ppermute(words, "span", pairs)
            distance *= 2
            words = combine(words, other, lines, words if distance < count else sums)
        sums = words
    moved, eddy_coeff, packed, *leaving = step(
        parts, sums, mag_in, mag_out, cells, weights, segments, planes, owners
    )
    arrived = lax.all_to_all(packed, ("span", "cross"), 0, 0)
    populations_next, segment_force = arrive(moved, *swap(*leaving, "span"), arrived)
    return (populations_next, eddy_coeff, segment_force)


def solution(mesh):
    in_specs = (
        P(None, "span", "cross", None),
        P(("span", "cross"), None),
        P(("span", "cross"), None),
        P(("span", "cross")),
    )
    out_specs = (P(None, "span", "cross", None), P("cross", None), P(None, ("span", "cross")))
    return jax.shard_map(local, mesh=mesh, in_specs=in_specs, out_specs=out_specs, check_vma=False)
```

```python
import functools

import jax
import jax.numpy as jnp
from jax import lax
from jax.experimental import pallas as pl
from jax.experimental.pallas import tpu as pltpu
from jax.sharding import PartitionSpec as P

SEG_DEV = 8
LANES = 128
HALO = 3
EXT = 40
PAD = 56
OWN = 11
TOP = 8
CHUNKS = (8, 16, 24, 32, 40)
VMEM = 28 * 1024 * 1024

eps_sum = 1e-06
base_visc = 0.005

VELOCITIES = [
    [0, 0, 0],
    [1, 0, 0],
    [-1, 0, 0],
    [0, 1, 0],
    [0, -1, 0],
    [0, 0, 1],
    [0, 0, -1],
    [1, 1, 0],
    [-1, -1, 0],
    [1, -1, 0],
    [-1, 1, 0],
    [1, 0, 1],
    [-1, 0, -1],
    [1, 0, -1],
    [-1, 0, 1],
    [0, 1, 1],
    [0, -1, -1],
    [0, 1, -1],
    [0, -1, 1],
]


def swap(first, second, axis):
    count = lax.axis_size(axis)
    near = [(i, i ^ 1) for i in range(count)]
    other = [(i, (i + 1 if i % 2 else i - 1) % count) for i in range(count)]
    return lax.ppermute(first, axis, near), lax.ppermute(second, axis, other)


def is_odd(axis):
    return lax.rem(lax.axis_index(axis), 2) == 1


def send_pair(axis, upwards, downwards, first, second):
    odd = is_odd(axis)

    @pl.when(odd)
    def _():
        first[...] = downwards
        second[...] = upwards

    @pl.when(jnp.logical_not(odd))
    def _():
        first[...] = upwards
        second[...] = downwards


def below_above(axis, first, second):
    odd = is_odd(axis)
    return jnp.where(odd, first, second), jnp.where(odd, second, first)


def full(shape, dtype):
    return jax.ShapeDtypeStruct(shape, dtype)


def in_vmem(count):
    return [pl.BlockSpec(memory_space=pltpu.VMEM)] * count


def params():
    return pltpu.CompilerParams(vmem_limit_bytes=VMEM)


def cost(micros):
    return pl.CostEstimate(flops=0, bytes_accessed=int(micros * 3.6e6), transcendentals=0)


def plus(array):
    return pltpu.roll(array, LANES - 1, 1)


def minus(array):
    return pltpu.roll(array, 1, 1)


STEP = 2.0**-15


def encode(value):
    return jnp.round(value * (1.0 / STEP)).astype(jnp.int32).astype(jnp.int16)


def decode(coded):
    return coded.astype(jnp.int32).astype(jnp.float32) * STEP


def split(value):
    high = value.astype(jnp.bfloat16)
    return high, (value - high.astype(jnp.float32)).astype(jnp.bfloat16)


def plane_loop(start, stop, body, carry, most):
    count = stop - start
    step = max(size for size in range(1, most + 1) if count % size == 0)

    def block(index, carry):
        for shift in range(step):
            carry = body(start + index * step + shift, carry)
        return carry

    if count == step:
        return block(0, carry)
    return lax.fori_loop(0, count // step, block, carry)


def moments_kernel(pops, vel_ref, first, second, rows):
    depth, width = pops.shape[1:3]

    def plane(z, carry):
        for half in range(width // 16):
            at = pl.ds(16 * half, 16)
            f = [pops[q, z, at, :].astype(jnp.float32) for q in range(19)]
            flux = [0.0, 0.0, 0.0]
            density = f[0]
            for q in range(1, 19, 2):
                even, odd = f[q] + f[q + 1], f[q] - f[q + 1]
                density = density + even
                for dim in range(3):
                    sign = VELOCITIES[q][dim]
                    if sign:
                        flux[dim] = flux[dim] + odd if sign > 0 else flux[dim] - odd
            inverse = 1.0 / density
            for dim in range(3):
                speed = flux[dim] * inverse
                vel_ref[dim, z, at, :] = speed
                for k in range(HALO):
                    if half == 0:
                        rows[0, dim * HALO + k, pl.ds(z, 1), :] = speed[k : k + 1]
                    if half == width // 16 - 1:
                        rows[1, dim * HALO + k, pl.ds(z, 1), :] = speed[15 - k : 16 - k]
        return carry

    plane_loop(0, depth, plane, 0, 4)
    send_pair("cross", encode(rows[1]), encode(rows[0]), first, second)


def block_moments(populations):
    _, depth, width, lanes = populations.shape
    edge = full((3 * HALO, depth, lanes), jnp.int16)
    return pl.pallas_call(
        moments_kernel,
        out_shape=(full((3, depth, width, lanes), jnp.float32), edge, edge),
        in_specs=in_vmem(1),
        out_specs=tuple(in_vmem(3)),
        scratch_shapes=[pltpu.VMEM((2, 3 * HALO, depth, lanes), jnp.float32)],
        compiler_params=params(),
        cost_estimate=cost(1),
        name="moments",
    )(populations)


def decode_rows(first, second, rows):
    rows[0], rows[1] = below_above("cross", decode(first[...]), decode(second[...]))


def place_plane(ext, p, vel_ref, rows, z):
    width = vel_ref.shape[2]
    for dim in range(3):
        ext[dim, p, pl.ds(OWN, width), :] = vel_ref[dim, z]
        for k in range(HALO):
            line = pl.ds(z, 1)
            ext[dim, p, pl.ds(OWN - 1 - k, 1), :] = rows[0, dim * HALO + k, line, :]
            ext[dim, p, pl.ds(OWN + width + k, 1), :] = rows[1, dim * HALO + k, line, :]


TALL = 40


def edges_kernel(vel_ref, low_ref, high_ref, first, second, rows, planes):
    depth, width = vel_ref.shape[1:3]
    decode_rows(low_ref, high_ref, rows)
    coded = []
    for pair in ((0, 1), (depth - 1, depth - 2)):
        planes[...] = jnp.zeros_like(planes)
        for dim in range(3):
            for index, z in enumerate(pair):
                slot = 2 * dim + index
                planes[slot, pl.ds(HALO, width), :] = vel_ref[dim, z]
                for k in range(HALO):
                    line = pl.ds(z, 1)
                    planes[slot, pl.ds(HALO - 1 - k, 1), :] = rows[0, dim * HALO + k, line, :]
                    planes[slot, pl.ds(HALO + width + k, 1), :] = rows[1, dim * HALO + k, line, :]
        coded.append(encode(planes[...]))
    send_pair("span", coded[1], coded[0], first, second)


def edge_planes(vel, low, high):
    pair = full((6, TALL, LANES), jnp.int16)
    return pl.pallas_call(
        edges_kernel,
        out_shape=(pair, pair),
        in_specs=in_vmem(3),
        out_specs=tuple(in_vmem(2)),
        scratch_shapes=[
            pltpu.VMEM((2, 3 * HALO, vel.shape[1], LANES), jnp.float32),
            pltpu.VMEM((6, TALL, LANES), jnp.float32),
        ],
        compiler_params=params(),
        cost_estimate=cost(0.2),
        name="edges",
    )(vel, low, high)


def strain_parts(ref, p, row, before, here, after):
    grads = [
        (
            plus(here[dim]) - minus(here[dim]),
            ref[dim, p, pl.ds(row + 1, 8), :] - ref[dim, p, pl.ds(row - 1, 8), :],
            after[dim] - before[dim],
        )
        for dim in range(3)
    ]
    parts = [
        grads[0][0],
        grads[1][1],
        grads[2][2],
        grads[0][1] + grads[1][0],
        grads[0][2] + grads[2][0],
        grads[1][2] + grads[2][1],
    ]
    straight = parts[0] * parts[0] + parts[1] * parts[1] + parts[2] * parts[2]
    mixed = parts[3] * parts[3] + parts[4] * parts[4] + parts[5] * parts[5]
    return parts, jnp.sqrt(0.5 * straight + 0.25 * mixed)


def weigh(low, middle, high):
    return (low + high) + (middle + middle)


PAIRS = ((0, 0), (1, 1), (2, 2), (0, 1), (0, 2), (1, 2))


def three(ref, p, rows):
    return [ref[dim, p, rows, :] for dim in range(3)]


def model_sums(planes, ext, hat, zsum, zvel, acc_ref, store_mag):
    for row in CHUNKS:
        rows = pl.ds(row, 8)

        def first_pass(p, carry):
            before, here, lag, last = carry
            after = three(ext, p + 1, rows)
            parts, size = strain_parts(ext, p, row, before, here, after)
            store_mag(p, row, size)
            prods = [size * part for part in parts] + [here[i] * here[j] for i, j in PAIRS]
            for k in range(12):
                zsum[k, p - 1, rows, :] = lag[k] + prods[k]
            for dim in range(3):
                zvel[dim, p, rows, :] = weigh(before[dim], here[dim], after[dim])
            lag = [last[k] + (prods[k] + prods[k]) for k in range(12)]
            return here, after, lag, prods

        none = [jnp.zeros((8, LANES), jnp.float32)] * 12
        carry = (three(ext, 0, rows), three(ext, 1, rows), none, none)
        plane_loop(1, planes - 1, first_pass, carry, 14)

    def second_pass(p, carry):
        for row in CHUNKS:
            for dim in range(3):
                line = weigh(*[zvel[dim, p, pl.ds(row + shift, 8), :] for shift in (-1, 0, 1)])
                hat[dim, p, pl.ds(row, 8), :] = (1.0 / 64.0) * weigh(minus(line), line, plus(line))
        return carry

    plane_loop(1, planes - 1, second_pass, 0, 14)

    for row in CHUNKS:
        rows = pl.ds(row, 8)

        def third_pass(p, carry):
            before, here, lm, mm = carry
            after = three(hat, p + 1, rows)
            parts, size = strain_parts(hat, p, row, before, here, after)
            size = 256.0 * size
            scaled = [64.0 * speed for speed in here]
            squares = [0.0, 0.0]
            for k, (i, j) in enumerate(PAIRS):
                smooth = []
                for field in (k, 6 + k):
                    line = weigh(
                        *[zsum[field, p, pl.ds(row + shift, 8), :] for shift in (-1, 0, 1)]
                    )
                    smooth.append(weigh(minus(line), line, plus(line)))
                model = smooth[0] - size * parts[k]
                lm = lm + (smooth[1] - scaled[i] * here[j]) * model
                squares[k // 3] = squares[k // 3] + model * model
            return here, after, lm, mm + (squares[0] + 0.5 * squares[1])

        none = jnp.zeros((8, LANES), jnp.float32)
        carry = (three(hat, 1, rows), three(hat, 2, rows), none, none)
        _, _, lm, mm = plane_loop(2, planes - 2, third_pass, carry, 12)
        out = pl.ds(row - TOP, 8)
        acc_ref[0, out, :] += (1.0 / 4096.0) * lm
        acc_ref[1, out, :] += (1.0 / 4096.0) * mm


def inner_kernel(vel_ref, low_ref, high_ref, acc_ref, mag_ref, ext, hat, zsum, zvel, rows):
    depth = vel_ref.shape[1]
    decode_rows(low_ref, high_ref, rows)

    def assemble(p, carry):
        place_plane(ext, p, vel_ref, rows, p)
        return carry

    plane_loop(0, depth, assemble, 0, 4)
    acc_ref[...] = jnp.zeros_like(acc_ref)

    def store_mag(p, row, size):
        mag_ref[p - 1, pl.ds(row - TOP, 8), :] = size

    model_sums(depth, ext, hat, zsum, zvel, acc_ref, store_mag)


def model_scratch(planes, depth):
    return [
        pltpu.VMEM((3, planes, PAD, LANES), jnp.float32),
        pltpu.VMEM((3, planes, PAD, LANES), jnp.float32),
        pltpu.VMEM((12, planes, PAD, LANES), jnp.float32),
        pltpu.VMEM((3, planes, PAD, LANES), jnp.float32),
        pltpu.VMEM((2, 3 * HALO, depth, LANES), jnp.float32),
    ]


def inner_sums(vel, low, high):
    depth = vel.shape[1]
    return pl.pallas_call(
        inner_kernel,
        out_shape=(
            full((2, EXT, LANES), jnp.float32),
            full((depth - 2, EXT, LANES), jnp.float32),
        ),
        in_specs=in_vmem(3),
        out_specs=tuple(in_vmem(2)),
        scratch_shapes=model_scratch(depth, depth),
        compiler_params=params(),
        cost_estimate=cost(5),
        name="inner_sums",
    )(vel, low, high)


def outer_kernel(
    vel_ref,
    low_ref,
    high_ref,
    first_ref,
    second_ref,
    partial_ref,
    after_this,
    sums_ref,
    mag_ref,
    ext,
    hat,
    zsum,
    zvel,
    rows,
    acc,
):
    depth, width = vel_ref.shape[1:3]
    decode_rows(low_ref, high_ref, rows)
    acc[...] = partial_ref[...]
    below, above = below_above("span", decode(first_ref[...]), decode(second_ref[...]))
    for side, (message, places, start) in enumerate(
        ((below, (1, 0), 0), (above, (4, 5), depth - 4))
    ):
        for index in range(4):
            place_plane(ext, index + (2 if side == 0 else 0), vel_ref, rows, start + index)
        for dim in range(3):
            for index, p in enumerate(places):
                ext[dim, p, pl.ds(OWN - HALO, TALL), :] = message[2 * dim + index]

        def store_mag(p, row, size):
            mag_ref[4 * side + p - 1, pl.ds(row - TOP, 8), :] = size

        model_sums(6, ext, hat, zsum, zvel, acc, store_mag)
    lines = width + 2
    sums_ref[...] = jnp.zeros_like(sums_ref)
    for index in range(2):
        sums_ref[pl.ds(index * lines, lines), :] = acc[index, pl.ds(OWN - TOP - 1, lines), :]


def outer_sums(vel, low, high, below, above, partial, after_this):
    depth, width = vel.shape[1:3]
    return pl.pallas_call(
        outer_kernel,
        out_shape=(
            full((-(-2 * (width + 2) // 8) * 8, LANES), jnp.float32),
            full((8, EXT, LANES), jnp.float32),
        ),
        in_specs=in_vmem(6) + [pl.BlockSpec(memory_space=pl.ANY)],
        out_specs=tuple(in_vmem(2)),
        scratch_shapes=model_scratch(6, depth) + [pltpu.VMEM((2, EXT, LANES), jnp.float32)],
        compiler_params=params(),
        cost_estimate=cost(2),
        name="outer_sums",
    )(vel, low, high, below, above, partial, after_this)


def rows_kernel(pops, after_this, first, second, rows):
    depth, width = pops.shape[1:3]

    def plane(z, carry):
        for q in range(19):
            low = pops[q, z, pl.ds(0, 16), :].astype(jnp.float32)
            high = pops[q, z, pl.ds(width - 16, 16), :].astype(jnp.float32)
            rows[0, q, pl.ds(z, 1), :] = low[:1]
            rows[1, q, pl.ds(z, 1), :] = high[15:]
        return carry

    plane_loop(0, depth, plane, 0, 4)
    send_pair(
        "cross", rows[1].astype(jnp.bfloat16), rows[0].astype(jnp.bfloat16), first, second
    )


def face_rows(populations, after_this):
    _, depth, width, lanes = populations.shape
    edge = full((19, depth, lanes), jnp.bfloat16)
    return pl.pallas_call(
        rows_kernel,
        out_shape=(edge, edge),
        in_specs=in_vmem(1) + [pl.BlockSpec(memory_space=pl.ANY)],
        out_specs=tuple(in_vmem(2)),
        scratch_shapes=[pltpu.VMEM((2, 19, depth, lanes), jnp.float32)],
        compiler_params=params(),
        cost_estimate=cost(0.5),
        name="face_rows",
    )(populations, after_this)


def relax_parts(f):
    even = {q: f[q] + f[q + 1] for q in range(1, 19, 2)}
    odd = {q: f[q] - f[q + 1] for q in range(1, 19, 2)}
    x_xy, x_xz = odd[7] + odd[9], odd[11] + odd[13]
    y_yz, y_xy = odd[15] + odd[17], odd[7] - odd[9]
    z_xz, z_yz = odd[11] - odd[13], odd[15] - odd[17]
    flux, up, down, axis_odd = [], [], [], []
    for first, second, along in ((x_xy, x_xz, 1), (y_yz, y_xy, 3), (z_xz, z_yz, 5)):
        sides = first + second
        total = odd[along] + sides
        heat = 0.15 * (sides - (2.0 / 3.0) * total)
        twist = (1.98 / 8.0) * (first - second)
        flux.append(total)
        up.append(heat + twist)
        down.append(heat - twist)
        axis_odd.append(4.0 * heat)
    a, b, c = even[7] + even[9], even[11] + even[13], even[15] + even[17]
    axes = even[1] + even[3] + even[5]
    diagonals = a + b + c
    density = f[0] + axes + diagonals
    inverse = 1.0 / density
    speed = [total * inverse for total in flux]
    square = [total * part for total, part in zip(flux, speed)]
    energy = square[0] + square[1] + square[2]
    d_e = (1.19 / 126.0) * (diagonals - f[0] - energy)
    d_eps = (1.4 / 252.0) * (9.0 * f[0] - 7.0 * axes - 2.0 * diagonals + 5.5 * energy)
    ax_n, dg_n, eq_n = 3.0 * even[1] - axes, diagonals - 3.0 * c, 3.0 * square[0] - energy
    ax_w, dg_w, eq_w = even[3] - even[5], a - b, square[1] - square[2]
    d_pn = (1.4 / 72.0) * (dg_n - 2.0 * ax_n + 0.5 * eq_n)
    d_pw = (1.4 / 24.0) * (dg_w - 2.0 * ax_w + 0.5 * eq_w)
    shear = [
        (1.0 / 36.0) * (ax_n + dg_n - eq_n),
        (1.0 / 12.0) * (ax_w + dg_w - eq_w),
        0.25 * (even[7] - even[9] - flux[0] * speed[1]),
        0.25 * (even[11] - even[13] - flux[0] * speed[2]),
        0.25 * (even[15] - even[17] - flux[1] * speed[2]),
    ]
    base_axis = 11.0 * d_e + 4.0 * d_eps
    base_diag = -8.0 * d_e - d_eps
    base = [None] * 19
    base[0] = f[0] + (30.0 * d_e - 12.0 * d_eps)
    rest = base_axis - 2.0 * d_pn
    for q, change, skew in (
        (1, base_axis + 4.0 * d_pn, axis_odd[0]),
        (3, rest + 2.0 * d_pw, axis_odd[1]),
        (5, rest - 2.0 * d_pw, axis_odd[2]),
    ):
        base[q] = f[q] + (change + skew)
        base[q + 1] = f[q + 1] + (change - skew)
    rest = base_diag - d_pn
    for q, change, one, two in (
        (7, rest - d_pw, up[0], down[1]),
        (11, rest + d_pw, down[0], up[2]),
        (15, base_diag + 2.0 * d_pn, up[1], down[2]),
    ):
        same, other = one + two, one - two
        base[q] = f[q] + (change - same)
        base[q + 1] = f[q + 1] + (change + same)
        base[q + 2] = f[q + 2] + (change - other)
        base[q + 3] = f[q + 3] + (change + other)
    return base, shear


def shear_changes(shear, rate):
    n, w, xy, xz, yz = [rate * part for part in shear]
    lean = n + w
    tilt = n - w
    twice = n + n
    changes = [None] * 19
    changes[1] = changes[2] = -twice
    changes[3] = changes[4] = tilt
    changes[5] = changes[6] = lean
    changes[7] = changes[8] = -(lean + xy)
    changes[9] = changes[10] = xy - lean
    changes[11] = changes[12] = -(tilt + xz)
    changes[13] = changes[14] = xz - tilt
    changes[15] = changes[16] = twice - yz
    changes[17] = changes[18] = twice + yz
    return changes


def relax_rate(eddy, size):
    return 1.0 / (0.5 + 3.0 * (base_visc + eddy * size))


BEFORE = [q for q in range(19) if VELOCITIES[q][1] > 0]
AFTER = [q for q in range(19) if VELOCITIES[q][1] < 0]
RISING = [q for q in range(19) if VELOCITIES[q][2] > 0]
FALLING = [q for q in range(19) if VELOCITIES[q][2] < 0]
FIRST = 8


def ready_kernel(pops, first, second, after_this, base_ref, shear_ref, edge_ref, edge_shear):
    depth, width = pops.shape[1:3]
    rows = [
        below_above("cross", first[q].astype(jnp.float32), second[q].astype(jnp.float32))
        for q in range(19)
    ]
    for side, wanted in enumerate((BEFORE, AFTER)):
        base, shear = relax_parts([pair[side] for pair in rows])
        for index, q in enumerate(wanted):
            edge_ref[side, index] = base[q]
        for k in range(5):
            edge_shear[side, k] = shear[k]

    def plane(z, carry):
        for half in range(width // 16):
            rows = pl.ds(16 * half, 16)
            base, shear = relax_parts([pops[q, z, rows, :].astype(jnp.float32) for q in range(19)])
            for q in range(19):
                base_ref[q, z, rows, :] = base[q]
            for k in range(5):
                shear_ref[k, z, rows, :] = shear[k]
        return carry

    plane_loop(0, depth, plane, 0, 4)


def ready(populations, before, after, after_this):
    _, depth, width, lanes = populations.shape
    return pl.pallas_call(
        ready_kernel,
        out_shape=(
            full((19, depth, width, lanes), jnp.float32),
            full((5, depth, width, lanes), jnp.float32),
            full((2, 5, depth, lanes), jnp.float32),
            full((2, 5, depth, lanes), jnp.float32),
        ),
        in_specs=in_vmem(3) + [pl.BlockSpec(memory_space=pl.ANY)],
        out_specs=tuple(in_vmem(4)),
        compiler_params=params(),
        cost_estimate=cost(2.5),
        name="ready",
    )(populations, before, after, after_this)


PART_STEP = 2.0**-13
ACTING = (0, 1, 3, 4)


def leaving_kernel(pops, first, second, after_this, out_first, out_second, stage):
    depth, width = pops.shape[1:3]
    rows = [
        below_above("cross", first[q].astype(jnp.float32), second[q].astype(jnp.float32))
        for q in range(19)
    ]
    halo = [relax_parts([pair[side] for pair in rows]) for side in range(2)]
    coded = []
    for wanted, z in ((FALLING, 0), (RISING, depth - 1)):
        stage[...] = jnp.zeros_like(stage)
        for half in range(width // 16):
            at = pl.ds(16 * half, 16)
            base, shear = relax_parts([pops[q, z, at, :].astype(jnp.float32) for q in range(19)])
            for index, q in enumerate(wanted):
                stage[index, at, :] = base[q]
            for index, k in enumerate(ACTING):
                stage[5 + index, at, :] = 2.0 * shear[k]
        for side, (base, shear) in enumerate(halo):
            at = pl.ds(width + side, 1)
            for index, q in enumerate(wanted):
                stage[index, at, :] = base[q][z : z + 1]
            for index, k in enumerate(ACTING):
                stage[5 + index, at, :] = 2.0 * shear[k][z : z + 1]
        coded.append(
            jnp.round(stage[...] * (1.0 / PART_STEP)).astype(jnp.int32).astype(jnp.int16)
        )
    send_pair("span", coded[1], coded[0], out_first, out_second)


def leaving(populations, first, second, after_this):
    part = full((9, TALL, LANES), jnp.int16)
    return pl.pallas_call(
        leaving_kernel,
        out_shape=(part, part),
        in_specs=in_vmem(3) + [pl.BlockSpec(memory_space=pl.ANY)],
        out_specs=tuple(in_vmem(2)),
        scratch_shapes=[pltpu.VMEM((9, TALL, LANES), jnp.float32)],
        compiler_params=params(),
        cost_estimate=cost(0.5),
        name="leaving",
    )(populations, first, second, after_this)


def table_rows(table, at, low_at, flux):
    for dim in range(3):
        coarse, fine = split(flux[dim])
        table[at, dim * LANES : (dim + 1) * LANES] = coarse
        table[low_at, dim * LANES : (dim + 1) * LANES] = fine


def add_flux(flux, q, moved):
    for dim in range(3):
        sign = VELOCITIES[q][dim]
        if sign:
            flux[dim] = flux[dim] + moved if sign > 0 else flux[dim] - moved


def marker_force(table, picks, lanes, weights):
    lane_of = lax.broadcasted_iota(jnp.int32, (LANES, lanes[0].shape[1]), 0)
    picked = lax.dot_general(
        table,
        jnp.concatenate(picks, axis=1),
        (((0,), (0,)), ((), ())),
        preferred_element_type=jnp.float32,
    )
    markers = lanes[0].shape[1]
    force = [0.0, 0.0, 0.0]
    for tap, (lane, weight) in enumerate(zip(lanes, weights)):
        mask = jnp.where(lane_of == lane, -weight, 0.0)
        at = slice(tap * markers, (tap + 1) * markers)
        for dim in range(3):
            force[dim] = force[dim] + picked[dim * LANES : (dim + 1) * LANES, at] * mask
    return [jnp.sum(part, axis=0, keepdims=True) for part in force]


def step_kernel(
    base_ref,
    shear_ref,
    edge_ref,
    edge_shear,
    sums_ref,
    mag_in_ref,
    mag_out_ref,
    cell_ref,
    weight_ref,
    segment_ref,
    part_first,
    part_second,
    next_hbm,
    eddy_ref,
    partial_ref,
    post,
    nexts,
    table,
    arrived,
    eddy,
    line,
    out_sems,
):
    depth, width = shear_ref.shape[1:3]
    lines = width + 2
    part = depth // 4
    eddy[...] = jnp.zeros_like(eddy)
    eddy[pl.ds(OWN - TOP - 1, lines), :] = jnp.maximum(
        sums_ref[pl.ds(0, lines), :] / (sums_ref[pl.ds(lines, lines), :] + eps_sum), 0.0
    )
    eddy_ref[...] = eddy[pl.ds(OWN - TOP, width), :]

    for side, (wanted, row, place) in enumerate(
        ((BEFORE, OWN - TOP - 1, FIRST - 1), (AFTER, OWN - TOP + width, FIRST + width))
    ):
        for z in range(depth):
            if z == 0:
                size = mag_out_ref[1, pl.ds(row, 1), :]
            elif z == depth - 1:
                size = mag_out_ref[6, pl.ds(row, 1), :]
            else:
                size = mag_in_ref[z - 1, pl.ds(row, 1), :]
            line[pl.ds(z, 1), :] = size
        rate = relax_rate(eddy[pl.ds(row, 1), :], line[...])
        changes = shear_changes([edge_shear[side, k] for k in range(5)], rate)
        for index, q in enumerate(wanted):
            out = edge_ref[side, index] + changes[q]
            for z in range(depth):
                post[q, z + 1, pl.ds(place, 1), :] = out[z : z + 1]

    parts = [
        message[...].astype(jnp.int32).astype(jnp.float32) for message in (part_first, part_second)
    ]
    arrived[0], arrived[1] = below_above("span", *parts)
    for side, (wanted, p, slot) in enumerate(((RISING, 0, 0), (FALLING, depth + 1, 7))):
        pieces = [(16 * half, 16, OWN - TOP + 16 * half, FIRST + 16 * half, wanted) for half in range(width // 16)]
        pieces.append((width, 1, OWN - TOP - 1, FIRST - 1, BEFORE))
        pieces.append((width + 1, 1, OWN - TOP + width, FIRST + width, AFTER))
        for start, count, around, place, needed in pieces:
            at, around = pl.ds(start, count), pl.ds(around, count)
            rate = relax_rate(eddy[around, :], mag_out_ref[slot, around, :])
            n, w, xz, yz = [arrived[side, 5 + k, at, :] * (0.5 * PART_STEP) for k in range(4)]
            changes = shear_changes([n, w, jnp.zeros_like(n), xz, yz], rate)
            for index, q in enumerate(wanted):
                if q in needed:
                    value = arrived[side, index, at, :] * PART_STEP + changes[q]
                    post[q, p, pl.ds(place, count), :] = value

    def collide(z, size_ref, at):
        for half in range(width // 16):
            rows = pl.ds(16 * half, 16)
            around = pl.ds(OWN - TOP + 16 * half, 16)
            rate = relax_rate(eddy[around, :], size_ref[at, around, :])
            changes = shear_changes([shear_ref[k, z, rows, :] for k in range(5)], rate)
            for q in range(19):
                value = base_ref[q, z, rows, :]
                if q:
                    value = value + changes[q]
                post[q, z + 1, pl.ds(FIRST + 16 * half, 16), :] = value

    def inner(z, carry):
        collide(z, mag_in_ref, z - 1)
        return carry

    collide(0, mag_out_ref, 1)
    collide(depth - 1, mag_out_ref, 6)
    plane_loop(1, depth - 1, inner, 0, 7)

    def shifted(q, z, half):
        shift_x, shift_y, _ = VELOCITIES[q]
        piece = post[q, z + 1, pl.ds(FIRST + 16 * half - shift_y, 16), :]
        if shift_x:
            piece = minus(piece) if shift_x > 0 else plus(piece)
        return piece.astype(jnp.bfloat16)

    def run(z, carry):
        for half in range(width // 16):
            flux = [0.0, 0.0, 0.0]
            for q in range(19):
                moved = shifted(q, z - VELOCITIES[q][2], half)
                nexts[q, z, pl.ds(16 * half, 16), :] = moved
                if q:
                    add_flux(flux, q, moved.astype(jnp.float32))
            row = pl.multiple_of(z * width + 16 * half, 16)
            low_row = pl.multiple_of((depth + z) * width + 16 * half, 16)
            table_rows(table, pl.ds(row, 16), pl.ds(low_row, 16), flux)
        return carry

    outs = []
    for index in range(4):
        start, stop = index * part, (index + 1) * part
        plane_loop(start, stop, run, 0, 4)
        place = pl.ds(index * part, part)
        outs.append(
            pltpu.make_async_copy(nexts.at[:, place], next_hbm.at[:, place], out_sems.at[index])
        )
        outs[-1].start()

    owners = partial_ref.shape[0]
    taps, markers = cell_ref.shape
    cells_all = depth * width
    def one_hot(rows, period, wanted):
        row_of = lax.broadcasted_iota(jnp.int32, (period, markers), 0)
        picks = []
        for tap in range(taps):
            hit = jnp.where(row_of == wanted[tap : tap + 1, :], 1.0, 0.0).astype(jnp.bfloat16)
            picks.append(jnp.concatenate([hit] * (rows // period), axis=0))
        return picks

    def row_lane(cells):
        return lax.shift_right_logical(cells, 7), lax.bitwise_and(cells, LANES - 1)

    def each(array):
        return [array[tap : tap + 1, :] for tap in range(taps)]

    row, lane = row_lane(cell_ref[...])
    force = marker_force(
        table[...],
        one_hot(2 * cells_all, cells_all, row),
        each(lane),
        each(weight_ref[...]),
    )

    owner_of = lax.broadcasted_iota(jnp.int32, (owners, markers), 0)
    place_of = lax.broadcasted_iota(jnp.int32, (SEG_DEV, markers), 0)
    segment = segment_ref[...]
    mine = jnp.where(owner_of == lax.shift_right_logical(segment, 3), 1.0, 0.0)
    mine = mine.astype(jnp.bfloat16)
    place = place_of == lax.bitwise_and(segment, SEG_DEV - 1)
    rest = [jnp.where(place, part, 0.0) for part in force]
    rest.append(jnp.zeros((LANES - 3 * SEG_DEV, markers), jnp.float32))
    rest = jnp.concatenate(rest, axis=0)
    totals = 0.0
    for _ in range(3):
        coarse = rest.astype(jnp.bfloat16)
        rest = rest - coarse.astype(jnp.float32)
        totals = totals + lax.dot_general(
            mine, coarse, (((1,), (1,)), ((), ())), preferred_element_type=jnp.float32
        )
    partial_ref[:, 0, :] = totals
    for copy in outs:
        copy.wait()


def step(parts, sums, mag_in, mag_out, cells, weights, segments, messages, owners):
    _, depth, width, lanes = parts[0].shape
    return pl.pallas_call(
        step_kernel,
        out_shape=(
            full((19, depth, width, lanes), jnp.bfloat16),
            full((width, lanes), jnp.float32),
            full((owners, 1, lanes), jnp.float32),
        ),
        in_specs=in_vmem(12),
        out_specs=(pl.BlockSpec(memory_space=pl.ANY),) + tuple(in_vmem(2)),
        scratch_shapes=[
            pltpu.VMEM((19, depth + 2, FIRST + width + 8, lanes), jnp.float32),
            pltpu.VMEM((19, depth, width, lanes), jnp.bfloat16),
            pltpu.VMEM((2 * depth * width, 3 * lanes), jnp.bfloat16),
            pltpu.VMEM((2, 9, TALL, lanes), jnp.float32),
            pltpu.VMEM((EXT, lanes), jnp.float32),
            pltpu.VMEM((depth, lanes), jnp.float32),
            pltpu.SemaphoreType.DMA((4,)),
        ],
        compiler_params=params(),
        cost_estimate=cost(5),
        name="step",
    )(*parts, sums, mag_in, mag_out, cells, weights, segments, *messages)


def finish_kernel(arrived_ref, out_ref):
    total = jnp.sum(arrived_ref[:, 0, :], axis=0, keepdims=True)
    for dim in range(3):
        out_ref[pl.ds(dim, 1), :] = total[:, dim * SEG_DEV : (dim + 1) * SEG_DEV]


def finish(arrived):
    return pl.pallas_call(
        finish_kernel,
        out_shape=full((3, SEG_DEV), jnp.float32),
        in_specs=in_vmem(1),
        out_specs=in_vmem(1)[0],
        name="finish",
    )(arrived)


def local(populations, cell_index, marker_weight, segment_id):
    owners = lax.axis_size("span") * lax.axis_size("cross")
    cells, weights, segments = cell_index.T, marker_weight.T, segment_id[None, :]
    vel, *lines = block_moments(populations)
    lines = swap(*lines, "cross")
    planes = swap(*edge_planes(vel, *lines), "span")
    partial, mag_in = inner_sums(vel, *lines)
    faces = face_rows(populations, partial)
    sums, mag_out = outer_sums(vel, *lines, *planes, partial, faces[0])
    faces = swap(*faces, "cross")
    messages = leaving(populations, *faces, sums)
    parts = ready(populations, *faces, sums)
    count = lax.axis_size("span")
    if count & (count - 1):
        sums = lax.psum(sums, "span")
        messages = swap(*messages, "span")
    else:
        distance = 1
        while distance < count:
            pairs = [(i, i ^ distance) for i in range(count)]
            sums = sums + lax.ppermute(sums, "span", pairs)
            if distance == 1:
                arriving = swap(*messages, "span")
                sums, _ = lax.optimization_barrier((sums, messages))
            distance *= 2
        messages = arriving
    populations_next, eddy_coeff, packed = step(
        parts, sums, mag_in, mag_out, cells, weights, segments, messages, owners
    )
    arrived = lax.all_to_all(packed, ("span", "cross"), 0, 0)
    return (populations_next, eddy_coeff, finish(arrived))


def solution(mesh):
    in_specs = (
        P(None, "span", "cross", None),
        P(("span", "cross"), None),
        P(("span", "cross"), None),
        P(("span", "cross")),
    )
    out_specs = (P(None, "span", "cross", None), P("cross", None), P(None, ("span", "cross")))
    return jax.shard_map(local, mesh=mesh, in_specs=in_specs, out_specs=out_specs, check_vma=False)
```

```python
import functools

import jax
import jax.numpy as jnp
from jax import lax
from jax.experimental import pallas as pl
from jax.experimental.pallas import tpu as pltpu
from jax.sharding import PartitionSpec as P

SEG_DEV = 8
LANES = 128
HALO = 3
EXT = 40
PAD = 56
OWN = 11
TOP = 8
CHUNKS = (8, 16, 24, 32, 40)
VMEM = 28 * 1024 * 1024

eps_sum = 1e-06
base_visc = 0.005

VELOCITIES = [
    [0, 0, 0],
    [1, 0, 0],
    [-1, 0, 0],
    [0, 1, 0],
    [0, -1, 0],
    [0, 0, 1],
    [0, 0, -1],
    [1, 1, 0],
    [-1, -1, 0],
    [1, -1, 0],
    [-1, 1, 0],
    [1, 0, 1],
    [-1, 0, -1],
    [1, 0, -1],
    [-1, 0, 1],
    [0, 1, 1],
    [0, -1, -1],
    [0, 1, -1],
    [0, -1, 1],
]


def swap(first, second, axis):
    count = lax.axis_size(axis)
    near = [(i, i ^ 1) for i in range(count)]
    other = [(i, (i + 1 if i % 2 else i - 1) % count) for i in range(count)]
    return lax.ppermute(first, axis, near), lax.ppermute(second, axis, other)


def is_odd(axis):
    return lax.rem(lax.axis_index(axis), 2) == 1


def send_pair(axis, upwards, downwards, first, second):
    odd = is_odd(axis)

    @pl.when(odd)
    def _():
        first[...] = downwards
        second[...] = upwards

    @pl.when(jnp.logical_not(odd))
    def _():
        first[...] = upwards
        second[...] = downwards


def below_above(axis, first, second):
    odd = is_odd(axis)
    return jnp.where(odd, first, second), jnp.where(odd, second, first)


def full(shape, dtype):
    return jax.ShapeDtypeStruct(shape, dtype)


def in_vmem(count):
    return [pl.BlockSpec(memory_space=pltpu.VMEM)] * count


def params():
    return pltpu.CompilerParams(vmem_limit_bytes=VMEM)


def cost(micros):
    return pl.CostEstimate(flops=0, bytes_accessed=int(micros * 3.6e6), transcendentals=0)


def plus(array):
    return pltpu.roll(array, LANES - 1, 1)


def minus(array):
    return pltpu.roll(array, 1, 1)


STEP = 2.0**-15


def encode(value):
    return jnp.round(value * (1.0 / STEP)).astype(jnp.int32).astype(jnp.int16)


def decode(coded):
    return coded.astype(jnp.int32).astype(jnp.float32) * STEP


def split(value):
    high = value.astype(jnp.bfloat16)
    return high, (value - high.astype(jnp.float32)).astype(jnp.bfloat16)


def plane_loop(start, stop, body, carry, most):
    count = stop - start
    step = max(size for size in range(1, most + 1) if count % size == 0)

    def block(index, carry):
        for shift in range(step):
            carry = body(start + index * step + shift, carry)
        return carry

    if count == step:
        return block(0, carry)
    return lax.fori_loop(0, count // step, block, carry)


def moments_kernel(pops, vel_ref, first, second, rows):
    depth, width = pops.shape[1:3]

    def plane(z, carry):
        for half in range(width // 16):
            at = pl.ds(16 * half, 16)
            f = [pops[q, z, at, :].astype(jnp.float32) for q in range(19)]
            flux = [0.0, 0.0, 0.0]
            density = f[0]
            for q in range(1, 19, 2):
                even, odd = f[q] + f[q + 1], f[q] - f[q + 1]
                density = density + even
                for dim in range(3):
                    sign = VELOCITIES[q][dim]
                    if sign:
                        flux[dim] = flux[dim] + odd if sign > 0 else flux[dim] - odd
            inverse = 1.0 / density
            for dim in range(3):
                speed = flux[dim] * inverse
                vel_ref[dim, z, at, :] = speed
                for k in range(HALO):
                    if half == 0:
                        rows[0, dim * HALO + k, pl.ds(z, 1), :] = speed[k : k + 1]
                    if half == width // 16 - 1:
                        rows[1, dim * HALO + k, pl.ds(z, 1), :] = speed[15 - k : 16 - k]
        return carry

    plane_loop(0, depth, plane, 0, 4)
    send_pair("cross", encode(rows[1]), encode(rows[0]), first, second)


def block_moments(populations):
    _, depth, width, lanes = populations.shape
    edge = full((3 * HALO, depth, lanes), jnp.int16)
    return pl.pallas_call(
        moments_kernel,
        out_shape=(full((3, depth, width, lanes), jnp.float32), edge, edge),
        in_specs=in_vmem(1),
        out_specs=tuple(in_vmem(3)),
        scratch_shapes=[pltpu.VMEM((2, 3 * HALO, depth, lanes), jnp.float32)],
        compiler_params=params(),
        cost_estimate=cost(1),
        name="moments",
    )(populations)


def decode_rows(first, second, rows):
    rows[0], rows[1] = below_above("cross", decode(first[...]), decode(second[...]))


def place_plane(ext, p, vel_ref, rows, z):
    width = vel_ref.shape[2]
    for dim in range(3):
        ext[dim, p, pl.ds(OWN, width), :] = vel_ref[dim, z]
        for k in range(HALO):
            line = pl.ds(z, 1)
            ext[dim, p, pl.ds(OWN - 1 - k, 1), :] = rows[0, dim * HALO + k, line, :]
            ext[dim, p, pl.ds(OWN + width + k, 1), :] = rows[1, dim * HALO + k, line, :]


TALL = 40


def edges_kernel(vel_ref, low_ref, high_ref, first, second, rows, planes):
    depth, width = vel_ref.shape[1:3]
    decode_rows(low_ref, high_ref, rows)
    coded = []
    for pair in ((0, 1), (depth - 1, depth - 2)):
        planes[...] = jnp.zeros_like(planes)
        for dim in range(3):
            for index, z in enumerate(pair):
                slot = 2 * dim + index
                planes[slot, pl.ds(HALO, width), :] = vel_ref[dim, z]
                for k in range(HALO):
                    line = pl.ds(z, 1)
                    planes[slot, pl.ds(HALO - 1 - k, 1), :] = rows[0, dim * HALO + k, line, :]
                    planes[slot, pl.ds(HALO + width + k, 1), :] = rows[1, dim * HALO + k, line, :]
        coded.append(encode(planes[...]))
    send_pair("span", coded[1], coded[0], first, second)


def edge_planes(vel, low, high):
    pair = full((6, TALL, LANES), jnp.int16)
    return pl.pallas_call(
        edges_kernel,
        out_shape=(pair, pair),
        in_specs=in_vmem(3),
        out_specs=tuple(in_vmem(2)),
        scratch_shapes=[
            pltpu.VMEM((2, 3 * HALO, vel.shape[1], LANES), jnp.float32),
            pltpu.VMEM((6, TALL, LANES), jnp.float32),
        ],
        compiler_params=params(),
        cost_estimate=cost(0.2),
        name="edges",
    )(vel, low, high)


def strain_parts(ref, p, row, before, here, after):
    grads = [
        (
            plus(here[dim]) - minus(here[dim]),
            ref[dim, p, pl.ds(row + 1, 8), :] - ref[dim, p, pl.ds(row - 1, 8), :],
            after[dim] - before[dim],
        )
        for dim in range(3)
    ]
    parts = [
        grads[0][0],
        grads[1][1],
        grads[2][2],
        grads[0][1] + grads[1][0],
        grads[0][2] + grads[2][0],
        grads[1][2] + grads[2][1],
    ]
    straight = parts[0] * parts[0] + parts[1] * parts[1] + parts[2] * parts[2]
    mixed = parts[3] * parts[3] + parts[4] * parts[4] + parts[5] * parts[5]
    return parts, jnp.sqrt(0.5 * straight + 0.25 * mixed)


def weigh(low, middle, high):
    return (low + high) + (middle + middle)


PAIRS = ((0, 0), (1, 1), (2, 2), (0, 1), (0, 2), (1, 2))


def three(ref, p, rows):
    return [ref[dim, p, rows, :] for dim in range(3)]


def model_sums(planes, ext, hat, zsum, zvel, acc_ref, store_mag):
    for row in CHUNKS:
        rows = pl.ds(row, 8)

        def first_pass(p, carry):
            before, here, lag, last = carry
            after = three(ext, p + 1, rows)
            parts, size = strain_parts(ext, p, row, before, here, after)
            store_mag(p, row, size)
            prods = [size * part for part in parts] + [here[i] * here[j] for i, j in PAIRS]
            for k in range(12):
                zsum[k, p - 1, rows, :] = lag[k] + prods[k]
            for dim in range(3):
                zvel[dim, p, rows, :] = weigh(before[dim], here[dim], after[dim])
            lag = [last[k] + (prods[k] + prods[k]) for k in range(12)]
            return here, after, lag, prods

        none = [jnp.zeros((8, LANES), jnp.float32)] * 12
        carry = (three(ext, 0, rows), three(ext, 1, rows), none, none)
        plane_loop(1, planes - 1, first_pass, carry, 14)

    def second_pass(p, carry):
        for row in CHUNKS:
            for dim in range(3):
                line = weigh(*[zvel[dim, p, pl.ds(row + shift, 8), :] for shift in (-1, 0, 1)])
                hat[dim, p, pl.ds(row, 8), :] = (1.0 / 64.0) * weigh(minus(line), line, plus(line))
        return carry

    plane_loop(1, planes - 1, second_pass, 0, 14)

    for row in CHUNKS:
        rows = pl.ds(row, 8)

        def third_pass(p, carry):
            before, here, lm, mm = carry
            after = three(hat, p + 1, rows)
            parts, size = strain_parts(hat, p, row, before, here, after)
            size = 256.0 * size
            scaled = [64.0 * speed for speed in here]
            squares = [0.0, 0.0]
            for k, (i, j) in enumerate(PAIRS):
                smooth = []
                for field in (k, 6 + k):
                    line = weigh(
                        *[zsum[field, p, pl.ds(row + shift, 8), :] for shift in (-1, 0, 1)]
                    )
                    smooth.append(weigh(minus(line), line, plus(line)))
                model = smooth[0] - size * parts[k]
                lm = lm + (smooth[1] - scaled[i] * here[j]) * model
                squares[k // 3] = squares[k // 3] + model * model
            return here, after, lm, mm + (squares[0] + 0.5 * squares[1])

        none = jnp.zeros((8, LANES), jnp.float32)
        carry = (three(hat, 1, rows), three(hat, 2, rows), none, none)
        _, _, lm, mm = plane_loop(2, planes - 2, third_pass, carry, 12)
        out = pl.ds(row - TOP, 8)
        acc_ref[0, out, :] += (1.0 / 4096.0) * lm
        acc_ref[1, out, :] += (1.0 / 4096.0) * mm


def inner_kernel(vel_ref, low_ref, high_ref, acc_ref, mag_ref, ext, hat, zsum, zvel, rows):
    depth = vel_ref.shape[1]
    decode_rows(low_ref, high_ref, rows)

    def assemble(p, carry):
        place_plane(ext, p, vel_ref, rows, p)
        return carry

    plane_loop(0, depth, assemble, 0, 4)
    acc_ref[...] = jnp.zeros_like(acc_ref)

    def store_mag(p, row, size):
        mag_ref[p - 1, pl.ds(row - TOP, 8), :] = size

    model_sums(depth, ext, hat, zsum, zvel, acc_ref, store_mag)


def model_scratch(planes, depth):
    return [
        pltpu.VMEM((3, planes, PAD, LANES), jnp.float32),
        pltpu.VMEM((3, planes, PAD, LANES), jnp.float32),
        pltpu.VMEM((12, planes, PAD, LANES), jnp.float32),
        pltpu.VMEM((3, planes, PAD, LANES), jnp.float32),
        pltpu.VMEM((2, 3 * HALO, depth, LANES), jnp.float32),
    ]


def inner_sums(vel, low, high):
    depth = vel.shape[1]
    return pl.pallas_call(
        inner_kernel,
        out_shape=(
            full((2, EXT, LANES), jnp.float32),
            full((depth - 2, EXT, LANES), jnp.float32),
        ),
        in_specs=in_vmem(3),
        out_specs=tuple(in_vmem(2)),
        scratch_shapes=model_scratch(depth, depth),
        compiler_params=params(),
        cost_estimate=cost(5),
        name="inner_sums",
    )(vel, low, high)


def outer_kernel(
    vel_ref,
    low_ref,
    high_ref,
    first_ref,
    second_ref,
    partial_ref,
    after_this,
    sums_ref,
    mag_ref,
    ext,
    hat,
    zsum,
    zvel,
    rows,
    acc,
):
    depth, width = vel_ref.shape[1:3]
    decode_rows(low_ref, high_ref, rows)
    acc[...] = partial_ref[...]
    below, above = below_above("span", decode(first_ref[...]), decode(second_ref[...]))
    for side, (message, places, start) in enumerate(
        ((below, (1, 0), 0), (above, (4, 5), depth - 4))
    ):
        for index in range(4):
            place_plane(ext, index + (2 if side == 0 else 0), vel_ref, rows, start + index)
        for dim in range(3):
            for index, p in enumerate(places):
                ext[dim, p, pl.ds(OWN - HALO, TALL), :] = message[2 * dim + index]

        def store_mag(p, row, size):
            mag_ref[4 * side + p - 1, pl.ds(row - TOP, 8), :] = size

        model_sums(6, ext, hat, zsum, zvel, acc, store_mag)
    lines = width + 2
    sums_ref[...] = jnp.zeros_like(sums_ref)
    for index in range(2):
        sums_ref[pl.ds(index * lines, lines), :] = acc[index, pl.ds(OWN - TOP - 1, lines), :]


def outer_sums(vel, low, high, below, above, partial, after_this):
    depth, width = vel.shape[1:3]
    return pl.pallas_call(
        outer_kernel,
        out_shape=(
            full((-(-2 * (width + 2) // 8) * 8, LANES), jnp.float32),
            full((8, EXT, LANES), jnp.float32),
        ),
        in_specs=in_vmem(6) + [pl.BlockSpec(memory_space=pl.ANY)],
        out_specs=tuple(in_vmem(2)),
        scratch_shapes=model_scratch(6, depth) + [pltpu.VMEM((2, EXT, LANES), jnp.float32)],
        compiler_params=params(),
        cost_estimate=cost(2),
        name="outer_sums",
    )(vel, low, high, below, above, partial, after_this)


def rows_kernel(pops, after_this, first, second, rows):
    depth, width = pops.shape[1:3]

    def plane(z, carry):
        for q in range(19):
            low = pops[q, z, pl.ds(0, 16), :].astype(jnp.float32)
            high = pops[q, z, pl.ds(width - 16, 16), :].astype(jnp.float32)
            rows[0, q, pl.ds(z, 1), :] = low[:1]
            rows[1, q, pl.ds(z, 1), :] = high[15:]
        return carry

    plane_loop(0, depth, plane, 0, 4)
    send_pair(
        "cross", rows[1].astype(jnp.bfloat16), rows[0].astype(jnp.bfloat16), first, second
    )


def face_rows(populations, after_this):
    _, depth, width, lanes = populations.shape
    edge = full((19, depth, lanes), jnp.bfloat16)
    return pl.pallas_call(
        rows_kernel,
        out_shape=(edge, edge),
        in_specs=in_vmem(1) + [pl.BlockSpec(memory_space=pl.ANY)],
        out_specs=tuple(in_vmem(2)),
        scratch_shapes=[pltpu.VMEM((2, 19, depth, lanes), jnp.float32)],
        compiler_params=params(),
        cost_estimate=cost(0.5),
        name="face_rows",
    )(populations, after_this)


def relax_parts(f):
    even = {q: f[q] + f[q + 1] for q in range(1, 19, 2)}
    odd = {q: f[q] - f[q + 1] for q in range(1, 19, 2)}
    x_xy, x_xz = odd[7] + odd[9], odd[11] + odd[13]
    y_yz, y_xy = odd[15] + odd[17], odd[7] - odd[9]
    z_xz, z_yz = odd[11] - odd[13], odd[15] - odd[17]
    flux, up, down, axis_odd = [], [], [], []
    for first, second, along in ((x_xy, x_xz, 1), (y_yz, y_xy, 3), (z_xz, z_yz, 5)):
        sides = first + second
        total = odd[along] + sides
        heat = 0.15 * (sides - (2.0 / 3.0) * total)
        twist = (1.98 / 8.0) * (first - second)
        flux.append(total)
        up.append(heat + twist)
        down.append(heat - twist)
        axis_odd.append(4.0 * heat)
    a, b, c = even[7] + even[9], even[11] + even[13], even[15] + even[17]
    axes = even[1] + even[3] + even[5]
    diagonals = a + b + c
    density = f[0] + axes + diagonals
    inverse = 1.0 / density
    speed = [total * inverse for total in flux]
    square = [total * part for total, part in zip(flux, speed)]
    energy = square[0] + square[1] + square[2]
    d_e = (1.19 / 126.0) * (diagonals - f[0] - energy)
    d_eps = (1.4 / 252.0) * (9.0 * f[0] - 7.0 * axes - 2.0 * diagonals + 5.5 * energy)
    ax_n, dg_n, eq_n = 3.0 * even[1] - axes, diagonals - 3.0 * c, 3.0 * square[0] - energy
    ax_w, dg_w, eq_w = even[3] - even[5], a - b, square[1] - square[2]
    d_pn = (1.4 / 72.0) * (dg_n - 2.0 * ax_n + 0.5 * eq_n)
    d_pw = (1.4 / 24.0) * (dg_w - 2.0 * ax_w + 0.5 * eq_w)
    shear = [
        (1.0 / 36.0) * (ax_n + dg_n - eq_n),
        (1.0 / 12.0) * (ax_w + dg_w - eq_w),
        0.25 * (even[7] - even[9] - flux[0] * speed[1]),
        0.25 * (even[11] - even[13] - flux[0] * speed[2]),
        0.25 * (even[15] - even[17] - flux[1] * speed[2]),
    ]
    base_axis = 11.0 * d_e + 4.0 * d_eps
    base_diag = -8.0 * d_e - d_eps
    base = [None] * 19
    base[0] = f[0] + (30.0 * d_e - 12.0 * d_eps)
    rest = base_axis - 2.0 * d_pn
    for q, change, skew in (
        (1, base_axis + 4.0 * d_pn, axis_odd[0]),
        (3, rest + 2.0 * d_pw, axis_odd[1]),
        (5, rest - 2.0 * d_pw, axis_odd[2]),
    ):
        base[q] = f[q] + (change + skew)
        base[q + 1] = f[q + 1] + (change - skew)
    rest = base_diag - d_pn
    for q, change, one, two in (
        (7, rest - d_pw, up[0], down[1]),
        (11, rest + d_pw, down[0], up[2]),
        (15, base_diag + 2.0 * d_pn, up[1], down[2]),
    ):
        same, other = one + two, one - two
        base[q] = f[q] + (change - same)
        base[q + 1] = f[q + 1] + (change + same)
        base[q + 2] = f[q + 2] + (change - other)
        base[q + 3] = f[q + 3] + (change + other)
    return base, shear


def shear_changes(shear, rate):
    n, w, xy, xz, yz = [rate * part for part in shear]
    lean = n + w
    tilt = n - w
    twice = n + n
    changes = [None] * 19
    changes[1] = changes[2] = -twice
    changes[3] = changes[4] = tilt
    changes[5] = changes[6] = lean
    changes[7] = changes[8] = -(lean + xy)
    changes[9] = changes[10] = xy - lean
    changes[11] = changes[12] = -(tilt + xz)
    changes[13] = changes[14] = xz - tilt
    changes[15] = changes[16] = twice - yz
    changes[17] = changes[18] = twice + yz
    return changes


def relax_rate(eddy, size):
    return 1.0 / (0.5 + 3.0 * (base_visc + eddy * size))


BEFORE = [q for q in range(19) if VELOCITIES[q][1] > 0]
AFTER = [q for q in range(19) if VELOCITIES[q][1] < 0]
RISING = [q for q in range(19) if VELOCITIES[q][2] > 0]
FALLING = [q for q in range(19) if VELOCITIES[q][2] < 0]
FIRST = 8


def ready_kernel(pops, first, second, after_this, base_ref, shear_ref, edge_ref, edge_shear):
    depth, width = pops.shape[1:3]
    rows = [
        below_above("cross", first[q].astype(jnp.float32), second[q].astype(jnp.float32))
        for q in range(19)
    ]
    for side, wanted in enumerate((BEFORE, AFTER)):
        base, shear = relax_parts([pair[side] for pair in rows])
        for index, q in enumerate(wanted):
            edge_ref[side, index] = base[q]
        for k in range(5):
            edge_shear[side, k] = shear[k]

    def plane(z, carry):
        for half in range(width // 16):
            rows = pl.ds(16 * half, 16)
            base, shear = relax_parts([pops[q, z, rows, :].astype(jnp.float32) for q in range(19)])
            for q in range(19):
                base_ref[q, z, rows, :] = base[q]
            for k in range(5):
                shear_ref[k, z, rows, :] = shear[k]
        return carry

    plane_loop(0, depth, plane, 0, 4)


def ready(populations, before, after, after_this):
    _, depth, width, lanes = populations.shape
    return pl.pallas_call(
        ready_kernel,
        out_shape=(
            full((19, depth, width, lanes), jnp.float32),
            full((5, depth, width, lanes), jnp.float32),
            full((2, 5, depth, lanes), jnp.float32),
            full((2, 5, depth, lanes), jnp.float32),
        ),
        in_specs=in_vmem(3) + [pl.BlockSpec(memory_space=pl.ANY)],
        out_specs=tuple(in_vmem(4)),
        compiler_params=params(),
        cost_estimate=cost(2.5),
        name="ready",
    )(populations, before, after, after_this)


PART_STEP = 1.0 / 11500.0
ACTING = (0, 1, 3, 4)


def leaving_kernel(pops, first, second, after_this, out_first, out_second, stage):
    depth, width = pops.shape[1:3]
    rows = [
        below_above("cross", first[q].astype(jnp.float32), second[q].astype(jnp.float32))
        for q in range(19)
    ]
    halo = [relax_parts([pair[side] for pair in rows]) for side in range(2)]
    coded = []
    for wanted, z in ((FALLING, 0), (RISING, depth - 1)):
        stage[...] = jnp.zeros_like(stage)
        for half in range(width // 16):
            at = pl.ds(16 * half, 16)
            base, shear = relax_parts([pops[q, z, at, :].astype(jnp.float32) for q in range(19)])
            for index, q in enumerate(wanted):
                stage[index, at, :] = base[q] - 0.5
            for index, k in enumerate(ACTING):
                stage[5 + index, at, :] = 2.0 * shear[k]
        for side, (base, shear) in enumerate(halo):
            at = pl.ds(width + side, 1)
            for index, q in enumerate(wanted):
                stage[index, at, :] = base[q][z : z + 1] - 0.5
            for index, k in enumerate(ACTING):
                stage[5 + index, at, :] = 2.0 * shear[k][z : z + 1]
        coded.append(
            jnp.round(stage[...] * (1.0 / PART_STEP)).astype(jnp.int32).astype(jnp.int16)
        )
    send_pair("span", coded[1], coded[0], out_first, out_second)


def leaving(populations, first, second, after_this):
    part = full((9, TALL, LANES), jnp.int16)
    return pl.pallas_call(
        leaving_kernel,
        out_shape=(part, part),
        in_specs=in_vmem(3) + [pl.BlockSpec(memory_space=pl.ANY)],
        out_specs=tuple(in_vmem(2)),
        scratch_shapes=[pltpu.VMEM((9, TALL, LANES), jnp.float32)],
        compiler_params=params(),
        cost_estimate=cost(0.5),
        name="leaving",
    )(populations, first, second, after_this)


def table_rows(table, at, low_at, flux):
    for dim in range(3):
        coarse, fine = split(flux[dim])
        table[at, dim * LANES : (dim + 1) * LANES] = coarse
        table[low_at, dim * LANES : (dim + 1) * LANES] = fine


def add_flux(flux, q, moved):
    for dim in range(3):
        sign = VELOCITIES[q][dim]
        if sign:
            flux[dim] = flux[dim] + moved if sign > 0 else flux[dim] - moved


def picks_kernel(cell_ref, weight_ref, after_this, pick_ref, mask_ref):
    taps, markers = cell_ref.shape
    cells_all = pick_ref.shape[0] // 2
    row_of = lax.broadcasted_iota(jnp.int32, (cells_all, markers), 0)
    lane_of = lax.broadcasted_iota(jnp.int32, (LANES, markers), 0)
    for tap in range(taps):
        cell = cell_ref[pl.ds(tap, 1), :]
        at = pl.ds(tap * markers, markers)
        hit = jnp.where(row_of == lax.shift_right_logical(cell, 7), 1.0, 0.0)
        hit = hit.astype(jnp.bfloat16)
        pick_ref[pl.ds(0, cells_all), at] = hit
        pick_ref[pl.ds(cells_all, cells_all), at] = hit
        lane = lax.bitwise_and(cell, LANES - 1)
        mask_ref[:, at] = jnp.where(lane_of == lane, -weight_ref[pl.ds(tap, 1), :], 0.0)


def marker_picks(cells, weights, after_this, rows):
    taps, markers = cells.shape
    return pl.pallas_call(
        picks_kernel,
        out_shape=(
            full((2 * rows, taps * markers), jnp.bfloat16),
            full((LANES, taps * markers), jnp.float32),
        ),
        in_specs=in_vmem(2) + [pl.BlockSpec(memory_space=pl.ANY)],
        out_specs=tuple(in_vmem(2)),
        compiler_params=params(),
        cost_estimate=cost(0.7),
        name="picks",
    )(cells, weights, after_this)


def marker_force(table, pick_ref, mask_ref, markers):
    picked = lax.dot_general(
        table[...],
        pick_ref[...],
        (((0,), (0,)), ((), ())),
        preferred_element_type=jnp.float32,
    )
    force = [0.0, 0.0, 0.0]
    for start in range(0, pick_ref.shape[1], markers):
        at = slice(start, start + markers)
        mask = mask_ref[:, pl.ds(start, markers)]
        for dim in range(3):
            force[dim] = force[dim] + picked[dim * LANES : (dim + 1) * LANES, at] * mask
    return [jnp.sum(part, axis=0, keepdims=True) for part in force]


def step_kernel(
    base_ref,
    shear_ref,
    edge_ref,
    edge_shear,
    sums_ref,
    mag_in_ref,
    mag_out_ref,
    pick_ref,
    mask_ref,
    segment_ref,
    part_first,
    part_second,
    next_hbm,
    eddy_ref,
    partial_ref,
    post,
    nexts,
    table,
    arrived,
    eddy,
    line,
    out_sems,
):
    depth, width = shear_ref.shape[1:3]
    lines = width + 2
    part = depth // 4
    eddy[...] = jnp.zeros_like(eddy)
    eddy[pl.ds(OWN - TOP - 1, lines), :] = jnp.maximum(
        sums_ref[pl.ds(0, lines), :] / (sums_ref[pl.ds(lines, lines), :] + eps_sum), 0.0
    )
    eddy_ref[...] = eddy[pl.ds(OWN - TOP, width), :]

    for side, (wanted, row, place) in enumerate(
        ((BEFORE, OWN - TOP - 1, FIRST - 1), (AFTER, OWN - TOP + width, FIRST + width))
    ):
        for z in range(depth):
            if z == 0:
                size = mag_out_ref[1, pl.ds(row, 1), :]
            elif z == depth - 1:
                size = mag_out_ref[6, pl.ds(row, 1), :]
            else:
                size = mag_in_ref[z - 1, pl.ds(row, 1), :]
            line[pl.ds(z, 1), :] = size
        rate = relax_rate(eddy[pl.ds(row, 1), :], line[...])
        changes = shear_changes([edge_shear[side, k] for k in range(5)], rate)
        for index, q in enumerate(wanted):
            out = edge_ref[side, index] + changes[q]
            for z in range(depth):
                post[q, z + 1, pl.ds(place, 1), :] = out[z : z + 1]

    parts = [
        message[...].astype(jnp.int32).astype(jnp.float32) for message in (part_first, part_second)
    ]
    arrived[0], arrived[1] = below_above("span", *parts)
    for side, (wanted, p, slot) in enumerate(((RISING, 0, 0), (FALLING, depth + 1, 7))):
        pieces = [(16 * half, 16, OWN - TOP + 16 * half, FIRST + 16 * half, wanted) for half in range(width // 16)]
        pieces.append((width, 1, OWN - TOP - 1, FIRST - 1, BEFORE))
        pieces.append((width + 1, 1, OWN - TOP + width, FIRST + width, AFTER))
        for start, count, around, place, needed in pieces:
            at, around = pl.ds(start, count), pl.ds(around, count)
            rate = relax_rate(eddy[around, :], mag_out_ref[slot, around, :])
            n, w, xz, yz = [arrived[side, 5 + k, at, :] * (0.5 * PART_STEP) for k in range(4)]
            changes = shear_changes([n, w, jnp.zeros_like(n), xz, yz], rate)
            for index, q in enumerate(wanted):
                if q in needed:
                    value = (arrived[side, index, at, :] * PART_STEP + 0.5) + changes[q]
                    post[q, p, pl.ds(place, count), :] = value

    def collide(z, size_ref, at):
        for half in range(width // 16):
            rows = pl.ds(16 * half, 16)
            around = pl.ds(OWN - TOP + 16 * half, 16)
            rate = relax_rate(eddy[around, :], size_ref[at, around, :])
            changes = shear_changes([shear_ref[k, z, rows, :] for k in range(5)], rate)
            for q in range(19):
                value = base_ref[q, z, rows, :]
                if q:
                    value = value + changes[q]
                post[q, z + 1, pl.ds(FIRST + 16 * half, 16), :] = value

    def inner(z, carry):
        collide(z, mag_in_ref, z - 1)
        return carry

    collide(0, mag_out_ref, 1)
    collide(depth - 1, mag_out_ref, 6)
    plane_loop(1, depth - 1, inner, 0, 7)

    def shifted(q, z, half):
        shift_x, shift_y, _ = VELOCITIES[q]
        piece = post[q, z + 1, pl.ds(FIRST + 16 * half - shift_y, 16), :]
        if shift_x:
            piece = minus(piece) if shift_x > 0 else plus(piece)
        return piece.astype(jnp.bfloat16)

    def run(z, carry):
        for half in range(width // 16):
            flux = [0.0, 0.0, 0.0]
            for q in range(19):
                moved = shifted(q, z - VELOCITIES[q][2], half)
                nexts[q, z, pl.ds(16 * half, 16), :] = moved
                if q:
                    add_flux(flux, q, moved.astype(jnp.float32))
            row = pl.multiple_of(z * width + 16 * half, 16)
            low_row = pl.multiple_of((depth + z) * width + 16 * half, 16)
            table_rows(table, pl.ds(row, 16), pl.ds(low_row, 16), flux)
        return carry

    outs = []
    for index in range(4):
        start, stop = index * part, (index + 1) * part
        plane_loop(start, stop, run, 0, 4)
        place = pl.ds(index * part, part)
        outs.append(
            pltpu.make_async_copy(nexts.at[:, place], next_hbm.at[:, place], out_sems.at[index])
        )
        outs[-1].start()

    owners = partial_ref.shape[0]
    markers = segment_ref.shape[1]
    force = marker_force(table, pick_ref, mask_ref, markers)

    owner_of = lax.broadcasted_iota(jnp.int32, (owners, markers), 0)
    place_of = lax.broadcasted_iota(jnp.int32, (SEG_DEV, markers), 0)
    segment = segment_ref[...]
    mine = jnp.where(owner_of == lax.shift_right_logical(segment, 3), 1.0, 0.0)
    mine = mine.astype(jnp.bfloat16)
    place = place_of == lax.bitwise_and(segment, SEG_DEV - 1)
    rest = [jnp.where(place, part, 0.0) for part in force]
    rest.append(jnp.zeros((LANES - 3 * SEG_DEV, markers), jnp.float32))
    rest = jnp.concatenate(rest, axis=0)
    totals = 0.0
    for _ in range(3):
        coarse = rest.astype(jnp.bfloat16)
        rest = rest - coarse.astype(jnp.float32)
        totals = totals + lax.dot_general(
            mine, coarse, (((1,), (1,)), ((), ())), preferred_element_type=jnp.float32
        )
    partial_ref[:, 0, :] = totals
    for copy in outs:
        copy.wait()


def step(parts, sums, mag_in, mag_out, picks, segments, messages, owners):
    _, depth, width, lanes = parts[0].shape
    return pl.pallas_call(
        step_kernel,
        out_shape=(
            full((19, depth, width, lanes), jnp.bfloat16),
            full((width, lanes), jnp.float32),
            full((owners, 1, lanes), jnp.float32),
        ),
        in_specs=in_vmem(12),
        out_specs=(pl.BlockSpec(memory_space=pl.ANY),) + tuple(in_vmem(2)),
        scratch_shapes=[
            pltpu.VMEM((19, depth + 2, FIRST + width + 8, lanes), jnp.float32),
            pltpu.VMEM((19, depth, width, lanes), jnp.bfloat16),
            pltpu.VMEM((2 * depth * width, 3 * lanes), jnp.bfloat16),
            pltpu.VMEM((2, 9, TALL, lanes), jnp.float32),
            pltpu.VMEM((EXT, lanes), jnp.float32),
            pltpu.VMEM((depth, lanes), jnp.float32),
            pltpu.SemaphoreType.DMA((4,)),
        ],
        compiler_params=params(),
        cost_estimate=cost(5),
        name="step",
    )(*parts, sums, mag_in, mag_out, *picks, segments, *messages)


def finish_kernel(arrived_ref, out_ref):
    total = jnp.sum(arrived_ref[:, 0, :], axis=0, keepdims=True)
    for dim in range(3):
        out_ref[pl.ds(dim, 1), :] = total[:, dim * SEG_DEV : (dim + 1) * SEG_DEV]


def finish(arrived):
    return pl.pallas_call(
        finish_kernel,
        out_shape=full((3, SEG_DEV), jnp.float32),
        in_specs=in_vmem(1),
        out_specs=in_vmem(1)[0],
        name="finish",
    )(arrived)


def local(populations, cell_index, marker_weight, segment_id):
    owners = lax.axis_size("span") * lax.axis_size("cross")
    cells, weights, segments = cell_index.T, marker_weight.T, segment_id[None, :]
    vel, *lines = block_moments(populations)
    lines = swap(*lines, "cross")
    planes = swap(*edge_planes(vel, *lines), "span")
    partial, mag_in = inner_sums(vel, *lines)
    faces = face_rows(populations, partial)
    sums, mag_out = outer_sums(vel, *lines, *planes, partial, faces[0])
    faces = swap(*faces, "cross")
    parts = ready(populations, *faces, sums)
    flat_rows = populations.shape[1] * populations.shape[2]
    count = lax.axis_size("span")
    if count & (count - 1):
        arriving = swap(*leaving(populations, *faces, sums), "span")
        picks = marker_picks(cells, weights, sums, flat_rows)
        sums = lax.psum(sums, "span")
    else:
        distance = 1
        messages = leaving(populations, *faces, sums)
        while distance < count:
            pairs = [(i, i ^ distance) for i in range(count)]
            other = lax.ppermute(sums, "span", pairs)
            if distance == 1:
                arriving = swap(*messages, "span")
                sums, _ = lax.optimization_barrier((sums + other, messages))
                picks = marker_picks(cells, weights, sums, flat_rows)
            elif distance == 2:
                sums, picks = lax.optimization_barrier((sums + other, picks))
            else:
                sums = sums + other
            distance *= 2
    populations_next, eddy_coeff, packed = step(
        parts, sums, mag_in, mag_out, picks, segments, arriving, owners
    )
    arrived = lax.all_to_all(packed, ("span", "cross"), 0, 0)
    return (populations_next, eddy_coeff, finish(arrived))


def solution(mesh):
    in_specs = (
        P(None, "span", "cross", None),
        P(("span", "cross"), None),
        P(("span", "cross"), None),
        P(("span", "cross")),
    )
    out_specs = (P(None, "span", "cross", None), P("cross", None), P(None, ("span", "cross")))
    return jax.shard_map(local, mesh=mesh, in_specs=in_specs, out_specs=out_specs, check_vma=False)
```

```python
import functools

import jax
import jax.numpy as jnp
from jax import lax
from jax.experimental import pallas as pl
from jax.experimental.pallas import tpu as pltpu
from jax.sharding import PartitionSpec as P

SEG_DEV = 8
LANES = 128
HALO = 3
EXT = 40
PAD = 56
OWN = 11
TOP = 8
CHUNKS = (8, 16, 24, 32, 40)
VMEM = 28 * 1024 * 1024

eps_sum = 1e-06
base_visc = 0.005

VELOCITIES = [
    [0, 0, 0],
    [1, 0, 0],
    [-1, 0, 0],
    [0, 1, 0],
    [0, -1, 0],
    [0, 0, 1],
    [0, 0, -1],
    [1, 1, 0],
    [-1, -1, 0],
    [1, -1, 0],
    [-1, 1, 0],
    [1, 0, 1],
    [-1, 0, -1],
    [1, 0, -1],
    [-1, 0, 1],
    [0, 1, 1],
    [0, -1, -1],
    [0, 1, -1],
    [0, -1, 1],
]


def swap(first, second, axis):
    count = lax.axis_size(axis)
    near = [(i, i ^ 1) for i in range(count)]
    other = [(i, (i + 1 if i % 2 else i - 1) % count) for i in range(count)]
    return lax.ppermute(first, axis, other), lax.ppermute(second, axis, near)


def is_odd(axis):
    return lax.rem(lax.axis_index(axis), 2) == 1


def send_pair(axis, upwards, downwards, first, second):
    odd = is_odd(axis)

    @pl.when(odd)
    def _():
        first[...] = upwards
        second[...] = downwards

    @pl.when(jnp.logical_not(odd))
    def _():
        first[...] = downwards
        second[...] = upwards


def below_above(axis, first, second):
    odd = is_odd(axis)
    return jnp.where(odd, second, first), jnp.where(odd, first, second)


def full(shape, dtype):
    return jax.ShapeDtypeStruct(shape, dtype)


def in_vmem(count):
    return [pl.BlockSpec(memory_space=pltpu.VMEM)] * count


def params():
    return pltpu.CompilerParams(vmem_limit_bytes=VMEM)


def cost(micros):
    return pl.CostEstimate(flops=0, bytes_accessed=int(micros * 3.6e6), transcendentals=0)


def plus(array):
    return pltpu.roll(array, LANES - 1, 1)


def minus(array):
    return pltpu.roll(array, 1, 1)


STEP = 2.0**-15


def encode(value):
    return jnp.round(value * (1.0 / STEP)).astype(jnp.int32).astype(jnp.int16)


def decode(coded):
    return coded.astype(jnp.int32).astype(jnp.float32) * STEP


def split(value):
    high = value.astype(jnp.bfloat16)
    return high, (value - high.astype(jnp.float32)).astype(jnp.bfloat16)


def plane_loop(start, stop, body, carry, most):
    count = stop - start
    step = max(size for size in range(1, most + 1) if count % size == 0)

    def block(index, carry):
        for shift in range(step):
            carry = body(start + index * step + shift, carry)
        return carry

    if count == step:
        return block(0, carry)
    return lax.fori_loop(0, count // step, block, carry)


def moments_kernel(pops, vel_ref, first, second, rows):
    depth, width = pops.shape[1:3]

    def plane(z, carry):
        for half in range(width // 16):
            at = pl.ds(16 * half, 16)
            f = [pops[q, z, at, :].astype(jnp.float32) for q in range(19)]
            flux = [0.0, 0.0, 0.0]
            density = f[0]
            for q in range(1, 19, 2):
                even, odd = f[q] + f[q + 1], f[q] - f[q + 1]
                density = density + even
                for dim in range(3):
                    sign = VELOCITIES[q][dim]
                    if sign:
                        flux[dim] = flux[dim] + odd if sign > 0 else flux[dim] - odd
            inverse = 1.0 / density
            for dim in range(3):
                speed = flux[dim] * inverse
                vel_ref[dim, z, at, :] = speed
                for k in range(HALO):
                    if half == 0:
                        rows[0, dim * HALO + k, pl.ds(z, 1), :] = speed[k : k + 1]
                    if half == width // 16 - 1:
                        rows[1, dim * HALO + k, pl.ds(z, 1), :] = speed[15 - k : 16 - k]
        return carry

    plane_loop(0, depth, plane, 0, 4)
    send_pair("cross", encode(rows[1]), encode(rows[0]), first, second)


def block_moments(populations):
    _, depth, width, lanes = populations.shape
    edge = full((3 * HALO, depth, lanes), jnp.int16)
    return pl.pallas_call(
        moments_kernel,
        out_shape=(full((3, depth, width, lanes), jnp.float32), edge, edge),
        in_specs=in_vmem(1),
        out_specs=tuple(in_vmem(3)),
        scratch_shapes=[pltpu.VMEM((2, 3 * HALO, depth, lanes), jnp.float32)],
        compiler_params=params(),
        cost_estimate=cost(1),
        name="moments",
    )(populations)


def decode_rows(first, second, rows):
    rows[0], rows[1] = below_above("cross", decode(first[...]), decode(second[...]))


def place_plane(ext, p, vel_ref, rows, z):
    width = vel_ref.shape[2]
    for dim in range(3):
        ext[dim, p, pl.ds(OWN, width), :] = vel_ref[dim, z]
        for k in range(HALO):
            line = pl.ds(z, 1)
            ext[dim, p, pl.ds(OWN - 1 - k, 1), :] = rows[0, dim * HALO + k, line, :]
            ext[dim, p, pl.ds(OWN + width + k, 1), :] = rows[1, dim * HALO + k, line, :]


TALL = 40


def edges_kernel(vel_ref, low_ref, high_ref, first, second, rows, planes):
    depth, width = vel_ref.shape[1:3]
    decode_rows(low_ref, high_ref, rows)
    coded = []
    for pair in ((0, 1), (depth - 1, depth - 2)):
        planes[...] = jnp.zeros_like(planes)
        for dim in range(3):
            for index, z in enumerate(pair):
                slot = 2 * dim + index
                planes[slot, pl.ds(HALO, width), :] = vel_ref[dim, z]
                for k in range(HALO):
                    line = pl.ds(z, 1)
                    planes[slot, pl.ds(HALO - 1 - k, 1), :] = rows[0, dim * HALO + k, line, :]
                    planes[slot, pl.ds(HALO + width + k, 1), :] = rows[1, dim * HALO + k, line, :]
        coded.append(encode(planes[...]))
    send_pair("span", coded[1], coded[0], first, second)


def edge_planes(vel, low, high):
    pair = full((6, TALL, LANES), jnp.int16)
    return pl.pallas_call(
        edges_kernel,
        out_shape=(pair, pair),
        in_specs=in_vmem(3),
        out_specs=tuple(in_vmem(2)),
        scratch_shapes=[
            pltpu.VMEM((2, 3 * HALO, vel.shape[1], LANES), jnp.float32),
            pltpu.VMEM((6, TALL, LANES), jnp.float32),
        ],
        compiler_params=params(),
        cost_estimate=cost(0.2),
        name="edges",
    )(vel, low, high)


def strain_parts(ref, p, row, before, here, after):
    grads = [
        (
            plus(here[dim]) - minus(here[dim]),
            ref[dim, p, pl.ds(row + 1, 8), :] - ref[dim, p, pl.ds(row - 1, 8), :],
            after[dim] - before[dim],
        )
        for dim in range(3)
    ]
    parts = [
        grads[0][0],
        grads[1][1],
        grads[2][2],
        grads[0][1] + grads[1][0],
        grads[0][2] + grads[2][0],
        grads[1][2] + grads[2][1],
    ]
    straight = parts[0] * parts[0] + parts[1] * parts[1] + parts[2] * parts[2]
    mixed = parts[3] * parts[3] + parts[4] * parts[4] + parts[5] * parts[5]
    return parts, jnp.sqrt(0.5 * straight + 0.25 * mixed)


def weigh(low, middle, high):
    return (low + high) + (middle + middle)


PAIRS = ((0, 0), (1, 1), (2, 2), (0, 1), (0, 2), (1, 2))


def three(ref, p, rows):
    return [ref[dim, p, rows, :] for dim in range(3)]


def model_sums(planes, ext, hat, zsum, zvel, acc_ref, store_mag):
    for row in CHUNKS:
        rows = pl.ds(row, 8)

        def first_pass(p, carry):
            before, here, lag, last = carry
            after = three(ext, p + 1, rows)
            parts, size = strain_parts(ext, p, row, before, here, after)
            store_mag(p, row, size)
            prods = [size * part for part in parts] + [here[i] * here[j] for i, j in PAIRS]
            for k in range(12):
                zsum[k, p - 1, rows, :] = lag[k] + prods[k]
            for dim in range(3):
                zvel[dim, p, rows, :] = weigh(before[dim], here[dim], after[dim])
            lag = [last[k] + (prods[k] + prods[k]) for k in range(12)]
            return here, after, lag, prods

        none = [jnp.zeros((8, LANES), jnp.float32)] * 12
        carry = (three(ext, 0, rows), three(ext, 1, rows), none, none)
        plane_loop(1, planes - 1, first_pass, carry, 14)

    def second_pass(p, carry):
        for row in CHUNKS:
            for dim in range(3):
                line = weigh(*[zvel[dim, p, pl.ds(row + shift, 8), :] for shift in (-1, 0, 1)])
                hat[dim, p, pl.ds(row, 8), :] = (1.0 / 64.0) * weigh(minus(line), line, plus(line))
        return carry

    plane_loop(1, planes - 1, second_pass, 0, 14)

    for row in CHUNKS:
        rows = pl.ds(row, 8)

        def third_pass(p, carry):
            before, here, lm, mm = carry
            after = three(hat, p + 1, rows)
            parts, size = strain_parts(hat, p, row, before, here, after)
            size = 256.0 * size
            scaled = [64.0 * speed for speed in here]
            squares = [0.0, 0.0]
            for k, (i, j) in enumerate(PAIRS):
                smooth = []
                for field in (k, 6 + k):
                    line = weigh(
                        *[zsum[field, p, pl.ds(row + shift, 8), :] for shift in (-1, 0, 1)]
                    )
                    smooth.append(weigh(minus(line), line, plus(line)))
                model = smooth[0] - size * parts[k]
                lm = lm + (smooth[1] - scaled[i] * here[j]) * model
                squares[k // 3] = squares[k // 3] + model * model
            return here, after, lm, mm + (squares[0] + 0.5 * squares[1])

        none = jnp.zeros((8, LANES), jnp.float32)
        carry = (three(hat, 1, rows), three(hat, 2, rows), none, none)
        _, _, lm, mm = plane_loop(2, planes - 2, third_pass, carry, 12)
        out = pl.ds(row - TOP, 8)
        acc_ref[0, out, :] += (1.0 / 4096.0) * lm
        acc_ref[1, out, :] += (1.0 / 4096.0) * mm


def inner_kernel(vel_ref, low_ref, high_ref, acc_ref, mag_ref, ext, hat, zsum, zvel, rows):
    depth = vel_ref.shape[1]
    decode_rows(low_ref, high_ref, rows)

    def assemble(p, carry):
        place_plane(ext, p, vel_ref, rows, p)
        return carry

    plane_loop(0, depth, assemble, 0, 4)
    acc_ref[...] = jnp.zeros_like(acc_ref)

    def store_mag(p, row, size):
        mag_ref[p - 1, pl.ds(row - TOP, 8), :] = size

    model_sums(depth, ext, hat, zsum, zvel, acc_ref, store_mag)


def model_scratch(planes, depth):
    return [
        pltpu.VMEM((3, planes, PAD, LANES), jnp.float32),
        pltpu.VMEM((3, planes, PAD, LANES), jnp.float32),
        pltpu.VMEM((12, planes, PAD, LANES), jnp.float32),
        pltpu.VMEM((3, planes, PAD, LANES), jnp.float32),
        pltpu.VMEM((2, 3 * HALO, depth, LANES), jnp.float32),
    ]


def inner_sums(vel, low, high):
    depth = vel.shape[1]
    return pl.pallas_call(
        inner_kernel,
        out_shape=(
            full((2, EXT, LANES), jnp.float32),
            full((depth - 2, EXT, LANES), jnp.float32),
        ),
        in_specs=in_vmem(3),
        out_specs=tuple(in_vmem(2)),
        scratch_shapes=model_scratch(depth, depth),
        compiler_params=params(),
        cost_estimate=cost(5),
        name="inner_sums",
    )(vel, low, high)


def outer_kernel(
    vel_ref,
    low_ref,
    high_ref,
    first_ref,
    second_ref,
    partial_ref,
    after_this,
    sums_ref,
    mag_ref,
    ext,
    hat,
    zsum,
    zvel,
    rows,
    acc,
):
    depth, width = vel_ref.shape[1:3]
    decode_rows(low_ref, high_ref, rows)
    acc[...] = partial_ref[...]
    below, above = below_above("span", decode(first_ref[...]), decode(second_ref[...]))
    for side, (message, places, start) in enumerate(
        ((below, (1, 0), 0), (above, (4, 5), depth - 4))
    ):
        for index in range(4):
            place_plane(ext, index + (2 if side == 0 else 0), vel_ref, rows, start + index)
        for dim in range(3):
            for index, p in enumerate(places):
                ext[dim, p, pl.ds(OWN - HALO, TALL), :] = message[2 * dim + index]

        def store_mag(p, row, size):
            mag_ref[4 * side + p - 1, pl.ds(row - TOP, 8), :] = size

        model_sums(6, ext, hat, zsum, zvel, acc, store_mag)
    lines = width + 2
    sums_ref[...] = jnp.zeros_like(sums_ref)
    for index in range(2):
        sums_ref[pl.ds(index * lines, lines), :] = acc[index, pl.ds(OWN - TOP - 1, lines), :]


def outer_sums(vel, low, high, below, above, partial, after_this):
    depth, width = vel.shape[1:3]
    return pl.pallas_call(
        outer_kernel,
        out_shape=(
            full((-(-2 * (width + 2) // 8) * 8, LANES), jnp.float32),
            full((8, EXT, LANES), jnp.float32),
        ),
        in_specs=in_vmem(6) + [pl.BlockSpec(memory_space=pl.ANY)],
        out_specs=tuple(in_vmem(2)),
        scratch_shapes=model_scratch(6, depth) + [pltpu.VMEM((2, EXT, LANES), jnp.float32)],
        compiler_params=params(),
        cost_estimate=cost(2),
        name="outer_sums",
    )(vel, low, high, below, above, partial, after_this)


def rows_kernel(pops, after_this, first, second, rows):
    depth, width = pops.shape[1:3]

    def plane(z, carry):
        for q in range(19):
            low = pops[q, z, pl.ds(0, 16), :].astype(jnp.float32)
            high = pops[q, z, pl.ds(width - 16, 16), :].astype(jnp.float32)
            rows[0, q, pl.ds(z, 1), :] = low[:1]
            rows[1, q, pl.ds(z, 1), :] = high[15:]
        return carry

    plane_loop(0, depth, plane, 0, 4)
    send_pair(
        "cross", rows[1].astype(jnp.bfloat16), rows[0].astype(jnp.bfloat16), first, second
    )


def face_rows(populations, after_this):
    _, depth, width, lanes = populations.shape
    edge = full((19, depth, lanes), jnp.bfloat16)
    return pl.pallas_call(
        rows_kernel,
        out_shape=(edge, edge),
        in_specs=in_vmem(1) + [pl.BlockSpec(memory_space=pl.ANY)],
        out_specs=tuple(in_vmem(2)),
        scratch_shapes=[pltpu.VMEM((2, 19, depth, lanes), jnp.float32)],
        compiler_params=params(),
        cost_estimate=cost(0.5),
        name="face_rows",
    )(populations, after_this)


def relax_parts(f):
    even = {q: f[q] + f[q + 1] for q in range(1, 19, 2)}
    odd = {q: f[q] - f[q + 1] for q in range(1, 19, 2)}
    x_xy, x_xz = odd[7] + odd[9], odd[11] + odd[13]
    y_yz, y_xy = odd[15] + odd[17], odd[7] - odd[9]
    z_xz, z_yz = odd[11] - odd[13], odd[15] - odd[17]
    flux, up, down, axis_odd = [], [], [], []
    for first, second, along in ((x_xy, x_xz, 1), (y_yz, y_xy, 3), (z_xz, z_yz, 5)):
        sides = first + second
        total = odd[along] + sides
        heat = 0.15 * (sides - (2.0 / 3.0) * total)
        twist = (1.98 / 8.0) * (first - second)
        flux.append(total)
        up.append(heat + twist)
        down.append(heat - twist)
        axis_odd.append(4.0 * heat)
    a, b, c = even[7] + even[9], even[11] + even[13], even[15] + even[17]
    axes = even[1] + even[3] + even[5]
    diagonals = a + b + c
    density = f[0] + axes + diagonals
    inverse = 1.0 / density
    speed = [total * inverse for total in flux]
    square = [total * part for total, part in zip(flux, speed)]
    energy = square[0] + square[1] + square[2]
    d_e = (1.19 / 126.0) * (diagonals - f[0] - energy)
    d_eps = (1.4 / 252.0) * (9.0 * f[0] - 7.0 * axes - 2.0 * diagonals + 5.5 * energy)
    ax_n, dg_n, eq_n = 3.0 * even[1] - axes, diagonals - 3.0 * c, 3.0 * square[0] - energy
    ax_w, dg_w, eq_w = even[3] - even[5], a - b, square[1] - square[2]
    d_pn = (1.4 / 72.0) * (dg_n - 2.0 * ax_n + 0.5 * eq_n)
    d_pw = (1.4 / 24.0) * (dg_w - 2.0 * ax_w + 0.5 * eq_w)
    shear = [
        (1.0 / 36.0) * (ax_n + dg_n - eq_n),
        (1.0 / 12.0) * (ax_w + dg_w - eq_w),
        0.25 * (even[7] - even[9] - flux[0] * speed[1]),
        0.25 * (even[11] - even[13] - flux[0] * speed[2]),
        0.25 * (even[15] - even[17] - flux[1] * speed[2]),
    ]
    base_axis = 11.0 * d_e + 4.0 * d_eps
    base_diag = -8.0 * d_e - d_eps
    base = [None] * 19
    base[0] = f[0] + (30.0 * d_e - 12.0 * d_eps)
    rest = base_axis - 2.0 * d_pn
    for q, change, skew in (
        (1, base_axis + 4.0 * d_pn, axis_odd[0]),
        (3, rest + 2.0 * d_pw, axis_odd[1]),
        (5, rest - 2.0 * d_pw, axis_odd[2]),
    ):
        base[q] = f[q] + (change + skew)
        base[q + 1] = f[q + 1] + (change - skew)
    rest = base_diag - d_pn
    for q, change, one, two in (
        (7, rest - d_pw, up[0], down[1]),
        (11, rest + d_pw, down[0], up[2]),
        (15, base_diag + 2.0 * d_pn, up[1], down[2]),
    ):
        same, other = one + two, one - two
        base[q] = f[q] + (change - same)
        base[q + 1] = f[q + 1] + (change + same)
        base[q + 2] = f[q + 2] + (change - other)
        base[q + 3] = f[q + 3] + (change + other)
    return base, shear


def shear_changes(shear, rate):
    n, w, xy, xz, yz = [rate * part for part in shear]
    lean = n + w
    tilt = n - w
    twice = n + n
    changes = [None] * 19
    changes[1] = changes[2] = -twice
    changes[3] = changes[4] = tilt
    changes[5] = changes[6] = lean
    changes[7] = changes[8] = -(lean + xy)
    changes[9] = changes[10] = xy - lean
    changes[11] = changes[12] = -(tilt + xz)
    changes[13] = changes[14] = xz - tilt
    changes[15] = changes[16] = twice - yz
    changes[17] = changes[18] = twice + yz
    return changes


def relax_rate(eddy, size):
    return 1.0 / (0.5 + 3.0 * (base_visc + eddy * size))


BEFORE = [q for q in range(19) if VELOCITIES[q][1] > 0]
AFTER = [q for q in range(19) if VELOCITIES[q][1] < 0]
RISING = [q for q in range(19) if VELOCITIES[q][2] > 0]
FALLING = [q for q in range(19) if VELOCITIES[q][2] < 0]
FIRST = 8


def ready_kernel(pops, first, second, after_this, base_ref, shear_ref, edge_ref, edge_shear):
    depth, width = pops.shape[1:3]
    rows = [
        below_above("cross", first[q].astype(jnp.float32), second[q].astype(jnp.float32))
        for q in range(19)
    ]
    for side, wanted in enumerate((BEFORE, AFTER)):
        base, shear = relax_parts([pair[side] for pair in rows])
        for index, q in enumerate(wanted):
            edge_ref[side, index] = base[q]
        for k in range(5):
            edge_shear[side, k] = shear[k]

    def plane(z, carry):
        for half in range(width // 16):
            rows = pl.ds(16 * half, 16)
            base, shear = relax_parts([pops[q, z, rows, :].astype(jnp.float32) for q in range(19)])
            for q in range(19):
                base_ref[q, z, rows, :] = base[q]
            for k in range(5):
                shear_ref[k, z, rows, :] = shear[k]
        return carry

    plane_loop(0, depth, plane, 0, 4)


def ready(populations, before, after, after_this):
    _, depth, width, lanes = populations.shape
    return pl.pallas_call(
        ready_kernel,
        out_shape=(
            full((19, depth, width, lanes), jnp.float32),
            full((5, depth, width, lanes), jnp.float32),
            full((2, 5, depth, lanes), jnp.float32),
            full((2, 5, depth, lanes), jnp.float32),
        ),
        in_specs=in_vmem(3) + [pl.BlockSpec(memory_space=pl.ANY)],
        out_specs=tuple(in_vmem(4)),
        compiler_params=params(),
        cost_estimate=cost(2.5),
        name="ready",
    )(populations, before, after, after_this)


PART_STEP = 1.0 / 11500.0
ACTING = (0, 1, 3, 4)


def leaving_kernel(pops, first, second, after_this, out_first, out_second, stage):
    depth, width = pops.shape[1:3]
    rows = [
        below_above("cross", first[q].astype(jnp.float32), second[q].astype(jnp.float32))
        for q in range(19)
    ]
    halo = [relax_parts([pair[side] for pair in rows]) for side in range(2)]
    coded = []
    for wanted, z in ((FALLING, 0), (RISING, depth - 1)):
        stage[...] = jnp.zeros_like(stage)
        for half in range(width // 16):
            at = pl.ds(16 * half, 16)
            base, shear = relax_parts([pops[q, z, at, :].astype(jnp.float32) for q in range(19)])
            for index, q in enumerate(wanted):
                stage[index, at, :] = base[q] - 0.5
            for index, k in enumerate(ACTING):
                stage[5 + index, at, :] = 2.0 * shear[k]
        for side, (base, shear) in enumerate(halo):
            at = pl.ds(width + side, 1)
            for index, q in enumerate(wanted):
                stage[index, at, :] = base[q][z : z + 1] - 0.5
            for index, k in enumerate(ACTING):
                stage[5 + index, at, :] = 2.0 * shear[k][z : z + 1]
        coded.append(
            jnp.round(stage[...] * (1.0 / PART_STEP)).astype(jnp.int32).astype(jnp.int16)
        )
    send_pair("span", coded[1], coded[0], out_first, out_second)


def leaving(populations, first, second, after_this):
    part = full((9, TALL, LANES), jnp.int16)
    return pl.pallas_call(
        leaving_kernel,
        out_shape=(part, part),
        in_specs=in_vmem(3) + [pl.BlockSpec(memory_space=pl.ANY)],
        out_specs=tuple(in_vmem(2)),
        scratch_shapes=[pltpu.VMEM((9, TALL, LANES), jnp.float32)],
        compiler_params=params(),
        cost_estimate=cost(0.5),
        name="leaving",
    )(populations, first, second, after_this)


def table_rows(table, at, low_at, flux):
    for dim in range(3):
        coarse, fine = split(flux[dim])
        table[at, dim * LANES : (dim + 1) * LANES] = coarse
        table[low_at, dim * LANES : (dim + 1) * LANES] = fine


def add_flux(flux, q, moved):
    for dim in range(3):
        sign = VELOCITIES[q][dim]
        if sign:
            flux[dim] = flux[dim] + moved if sign > 0 else flux[dim] - moved


def picks_kernel(cell_ref, weight_ref, after_this, pick_ref, mask_ref):
    taps, markers = cell_ref.shape
    cells_all = pick_ref.shape[0] // 2
    row_of = lax.broadcasted_iota(jnp.int32, (cells_all, markers), 0)
    lane_of = lax.broadcasted_iota(jnp.int32, (LANES, markers), 0)
    for tap in range(taps):
        cell = cell_ref[pl.ds(tap, 1), :]
        at = pl.ds(tap * markers, markers)
        hit = jnp.where(row_of == lax.shift_right_logical(cell, 7), 1.0, 0.0)
        hit = hit.astype(jnp.bfloat16)
        pick_ref[pl.ds(0, cells_all), at] = hit
        pick_ref[pl.ds(cells_all, cells_all), at] = hit
        lane = lax.bitwise_and(cell, LANES - 1)
        mask_ref[:, at] = jnp.where(lane_of == lane, -weight_ref[pl.ds(tap, 1), :], 0.0)


def marker_picks(cells, weights, after_this, rows):
    taps, markers = cells.shape
    return pl.pallas_call(
        picks_kernel,
        out_shape=(
            full((2 * rows, taps * markers), jnp.bfloat16),
            full((LANES, taps * markers), jnp.float32),
        ),
        in_specs=in_vmem(2) + [pl.BlockSpec(memory_space=pl.ANY)],
        out_specs=tuple(in_vmem(2)),
        compiler_params=params(),
        cost_estimate=cost(0.7),
        name="picks",
    )(cells, weights, after_this)


def marker_force(table, pick_ref, mask_ref, markers):
    picked = lax.dot_general(
        table[...],
        pick_ref[...],
        (((0,), (0,)), ((), ())),
        preferred_element_type=jnp.float32,
    )
    force = [0.0, 0.0, 0.0]
    for start in range(0, pick_ref.shape[1], markers):
        at = slice(start, start + markers)
        mask = mask_ref[:, pl.ds(start, markers)]
        for dim in range(3):
            force[dim] = force[dim] + picked[dim * LANES : (dim + 1) * LANES, at] * mask
    return [jnp.sum(part, axis=0, keepdims=True) for part in force]


def step_kernel(
    base_ref,
    shear_ref,
    edge_ref,
    edge_shear,
    sums_ref,
    mag_in_ref,
    mag_out_ref,
    pick_ref,
    mask_ref,
    segment_ref,
    part_first,
    part_second,
    next_hbm,
    eddy_ref,
    partial_ref,
    post,
    nexts,
    table,
    arrived,
    eddy,
    line,
    out_sems,
):
    depth, width = shear_ref.shape[1:3]
    lines = width + 2
    part = depth // 4
    eddy[...] = jnp.zeros_like(eddy)
    eddy[pl.ds(OWN - TOP - 1, lines), :] = jnp.maximum(
        sums_ref[pl.ds(0, lines), :] / (sums_ref[pl.ds(lines, lines), :] + eps_sum), 0.0
    )
    eddy_ref[...] = eddy[pl.ds(OWN - TOP, width), :]

    for side, (wanted, row, place) in enumerate(
        ((BEFORE, OWN - TOP - 1, FIRST - 1), (AFTER, OWN - TOP + width, FIRST + width))
    ):
        for z in range(depth):
            if z == 0:
                size = mag_out_ref[1, pl.ds(row, 1), :]
            elif z == depth - 1:
                size = mag_out_ref[6, pl.ds(row, 1), :]
            else:
                size = mag_in_ref[z - 1, pl.ds(row, 1), :]
            line[pl.ds(z, 1), :] = size
        rate = relax_rate(eddy[pl.ds(row, 1), :], line[...])
        changes = shear_changes([edge_shear[side, k] for k in range(5)], rate)
        for index, q in enumerate(wanted):
            out = edge_ref[side, index] + changes[q]
            for z in range(depth):
                post[q, z + 1, pl.ds(place, 1), :] = out[z : z + 1]

    parts = [
        message[...].astype(jnp.int32).astype(jnp.float32) for message in (part_first, part_second)
    ]
    arrived[0], arrived[1] = below_above("span", *parts)
    for side, (wanted, p, slot) in enumerate(((RISING, 0, 0), (FALLING, depth + 1, 7))):
        pieces = [(16 * half, 16, OWN - TOP + 16 * half, FIRST + 16 * half, wanted) for half in range(width // 16)]
        pieces.append((width, 1, OWN - TOP - 1, FIRST - 1, BEFORE))
        pieces.append((width + 1, 1, OWN - TOP + width, FIRST + width, AFTER))
        for start, count, around, place, needed in pieces:
            at, around = pl.ds(start, count), pl.ds(around, count)
            rate = relax_rate(eddy[around, :], mag_out_ref[slot, around, :])
            n, w, xz, yz = [arrived[side, 5 + k, at, :] * (0.5 * PART_STEP) for k in range(4)]
            changes = shear_changes([n, w, jnp.zeros_like(n), xz, yz], rate)
            for index, q in enumerate(wanted):
                if q in needed:
                    value = (arrived[side, index, at, :] * PART_STEP + 0.5) + changes[q]
                    post[q, p, pl.ds(place, count), :] = value

    def collide(z, size_ref, at):
        for half in range(width // 16):
            rows = pl.ds(16 * half, 16)
            around = pl.ds(OWN - TOP + 16 * half, 16)
            rate = relax_rate(eddy[around, :], size_ref[at, around, :])
            changes = shear_changes([shear_ref[k, z, rows, :] for k in range(5)], rate)
            for q in range(19):
                value = base_ref[q, z, rows, :]
                if q:
                    value = value + changes[q]
                post[q, z + 1, pl.ds(FIRST + 16 * half, 16), :] = value

    def inner(z, carry):
        collide(z, mag_in_ref, z - 1)
        return carry

    collide(0, mag_out_ref, 1)
    collide(depth - 1, mag_out_ref, 6)
    plane_loop(1, depth - 1, inner, 0, 7)

    def shifted(q, z, half):
        shift_x, shift_y, _ = VELOCITIES[q]
        piece = post[q, z + 1, pl.ds(FIRST + 16 * half - shift_y, 16), :]
        if shift_x:
            piece = minus(piece) if shift_x > 0 else plus(piece)
        return piece.astype(jnp.bfloat16)

    def run(z, carry):
        for half in range(width // 16):
            flux = [0.0, 0.0, 0.0]
            for q in range(19):
                moved = shifted(q, z - VELOCITIES[q][2], half)
                nexts[q, z, pl.ds(16 * half, 16), :] = moved
                if q:
                    add_flux(flux, q, moved.astype(jnp.float32))
            row = pl.multiple_of(z * width + 16 * half, 16)
            low_row = pl.multiple_of((depth + z) * width + 16 * half, 16)
            table_rows(table, pl.ds(row, 16), pl.ds(low_row, 16), flux)
        return carry

    outs = []
    for index in range(4):
        start, stop = index * part, (index + 1) * part
        plane_loop(start, stop, run, 0, 4)
        place = pl.ds(index * part, part)
        outs.append(
            pltpu.make_async_copy(nexts.at[:, place], next_hbm.at[:, place], out_sems.at[index])
        )
        outs[-1].start()

    owners = partial_ref.shape[0]
    markers = segment_ref.shape[1]
    force = marker_force(table, pick_ref, mask_ref, markers)

    owner_of = lax.broadcasted_iota(jnp.int32, (owners, markers), 0)
    place_of = lax.broadcasted_iota(jnp.int32, (SEG_DEV, markers), 0)
    segment = segment_ref[...]
    mine = jnp.where(owner_of == lax.shift_right_logical(segment, 3), 1.0, 0.0)
    mine = mine.astype(jnp.bfloat16)
    place = place_of == lax.bitwise_and(segment, SEG_DEV - 1)
    rest = [jnp.where(place, part, 0.0) for part in force]
    rest.append(jnp.zeros((LANES - 3 * SEG_DEV, markers), jnp.float32))
    rest = jnp.concatenate(rest, axis=0)
    totals = 0.0
    for _ in range(3):
        coarse = rest.astype(jnp.bfloat16)
        rest = rest - coarse.astype(jnp.float32)
        totals = totals + lax.dot_general(
            mine, coarse, (((1,), (1,)), ((), ())), preferred_element_type=jnp.float32
        )
    partial_ref[:, 0, :] = totals
    for copy in outs:
        copy.wait()


def step(parts, sums, mag_in, mag_out, picks, segments, messages, owners):
    _, depth, width, lanes = parts[0].shape
    return pl.pallas_call(
        step_kernel,
        out_shape=(
            full((19, depth, width, lanes), jnp.bfloat16),
            full((width, lanes), jnp.float32),
            full((owners, 1, lanes), jnp.float32),
        ),
        in_specs=in_vmem(12),
        out_specs=(pl.BlockSpec(memory_space=pl.ANY),) + tuple(in_vmem(2)),
        scratch_shapes=[
            pltpu.VMEM((19, depth + 2, FIRST + width + 8, lanes), jnp.float32),
            pltpu.VMEM((19, depth, width, lanes), jnp.bfloat16),
            pltpu.VMEM((2 * depth * width, 3 * lanes), jnp.bfloat16),
            pltpu.VMEM((2, 9, TALL, lanes), jnp.float32),
            pltpu.VMEM((EXT, lanes), jnp.float32),
            pltpu.VMEM((depth, lanes), jnp.float32),
            pltpu.SemaphoreType.DMA((4,)),
        ],
        compiler_params=params(),
        cost_estimate=cost(5),
        name="step",
    )(*parts, sums, mag_in, mag_out, *picks, segments, *messages)


def finish_kernel(arrived_ref, out_ref):
    total = jnp.sum(arrived_ref[:, 0, :], axis=0, keepdims=True)
    for dim in range(3):
        out_ref[pl.ds(dim, 1), :] = total[:, dim * SEG_DEV : (dim + 1) * SEG_DEV]


def finish(arrived):
    return pl.pallas_call(
        finish_kernel,
        out_shape=full((3, SEG_DEV), jnp.float32),
        in_specs=in_vmem(1),
        out_specs=in_vmem(1)[0],
        name="finish",
    )(arrived)


def local(populations, cell_index, marker_weight, segment_id):
    owners = lax.axis_size("span") * lax.axis_size("cross")
    cells, weights, segments = cell_index.T, marker_weight.T, segment_id[None, :]
    vel, *lines = block_moments(populations)
    lines = swap(*lines, "cross")
    planes = swap(*edge_planes(vel, *lines), "span")
    partial, mag_in = inner_sums(vel, *lines)
    faces = face_rows(populations, partial)
    sums, mag_out = outer_sums(vel, *lines, *planes, partial, faces[0])
    faces = swap(*faces, "cross")
    parts = ready(populations, *faces, sums)
    flat_rows = populations.shape[1] * populations.shape[2]
    count = lax.axis_size("span")
    if count & (count - 1):
        arriving = swap(*leaving(populations, *faces, sums), "span")
        picks = marker_picks(cells, weights, sums, flat_rows)
        sums = lax.psum(sums, "span")
    else:
        distance = 1
        messages = leaving(populations, *faces, sums)
        while distance < count:
            pairs = [(i, i ^ distance) for i in range(count)]
            other = lax.ppermute(sums, "span", pairs)
            if distance == 1:
                arriving = swap(*messages, "span")
                sums, _ = lax.optimization_barrier((sums + other, messages))
                picks = marker_picks(cells, weights, sums, flat_rows)
            elif distance == 2:
                sums, picks = lax.optimization_barrier((sums + other, picks))
            else:
                sums = sums + other
            distance *= 2
    populations_next, eddy_coeff, packed = step(
        parts, sums, mag_in, mag_out, picks, segments, arriving, owners
    )
    arrived = lax.all_to_all(packed, ("span", "cross"), 0, 0)
    return (populations_next, eddy_coeff, finish(arrived))


def solution(mesh):
    in_specs = (
        P(None, "span", "cross", None),
        P(("span", "cross"), None),
        P(("span", "cross"), None),
        P(("span", "cross")),
    )
    out_specs = (P(None, "span", "cross", None), P("cross", None), P(None, ("span", "cross")))
    return jax.shard_map(local, mesh=mesh, in_specs=in_specs, out_specs=out_specs, check_vma=False)
```

```python
import functools

import jax
import jax.numpy as jnp
from jax import lax
from jax.experimental import pallas as pl
from jax.experimental.pallas import tpu as pltpu
from jax.sharding import PartitionSpec as P

SEG_DEV = 8
LANES = 128
HALO = 3
EXT = 40
PAD = 56
OWN = 11
TOP = 8
CHUNKS = (8, 16, 24, 32, 40)
VMEM = 28 * 1024 * 1024

eps_sum = 1e-06
base_visc = 0.005

VELOCITIES = [
    [0, 0, 0],
    [1, 0, 0],
    [-1, 0, 0],
    [0, 1, 0],
    [0, -1, 0],
    [0, 0, 1],
    [0, 0, -1],
    [1, 1, 0],
    [-1, -1, 0],
    [1, -1, 0],
    [-1, 1, 0],
    [1, 0, 1],
    [-1, 0, -1],
    [1, 0, -1],
    [-1, 0, 1],
    [0, 1, 1],
    [0, -1, -1],
    [0, 1, -1],
    [0, -1, 1],
]


def swap(first, second, axis):
    count = lax.axis_size(axis)
    near = [(i, i ^ 1) for i in range(count)]
    other = [(i, (i + 1 if i % 2 else i - 1) % count) for i in range(count)]
    return lax.ppermute(first, axis, near), lax.ppermute(second, axis, other)


def is_odd(axis):
    return lax.rem(lax.axis_index(axis), 2) == 1


def send_pair(axis, upwards, downwards, first, second):
    odd = is_odd(axis)

    @pl.when(odd)
    def _():
        first[...] = downwards
        second[...] = upwards

    @pl.when(jnp.logical_not(odd))
    def _():
        first[...] = upwards
        second[...] = downwards


def below_above(axis, first, second):
    odd = is_odd(axis)
    return jnp.where(odd, first, second), jnp.where(odd, second, first)


def full(shape, dtype):
    return jax.ShapeDtypeStruct(shape, dtype)


def in_vmem(count):
    return [pl.BlockSpec(memory_space=pltpu.VMEM)] * count


def params():
    return pltpu.CompilerParams(vmem_limit_bytes=VMEM)


def cost(micros):
    return pl.CostEstimate(flops=0, bytes_accessed=int(micros * 3.6e6), transcendentals=0)


def plus(array):
    return pltpu.roll(array, LANES - 1, 1)


def minus(array):
    return pltpu.roll(array, 1, 1)


STEP = 2.0**-15


def encode(value):
    return jnp.round(value * (1.0 / STEP)).astype(jnp.int32).astype(jnp.int16)


def decode(coded):
    return coded.astype(jnp.int32).astype(jnp.float32) * STEP


def split(value):
    high = value.astype(jnp.bfloat16)
    return high, (value - high.astype(jnp.float32)).astype(jnp.bfloat16)


def plane_loop(start, stop, body, carry, most):
    count = stop - start
    step = max(size for size in range(1, most + 1) if count % size == 0)

    def block(index, carry):
        for shift in range(step):
            carry = body(start + index * step + shift, carry)
        return carry

    if count == step:
        return block(0, carry)
    return lax.fori_loop(0, count // step, block, carry)


def moments_kernel(pops, vel_ref, first, second, rows):
    depth, width = pops.shape[1:3]

    def plane(z, carry):
        for half in range(width // 16):
            at = pl.ds(16 * half, 16)
            f = [pops[q, z, at, :].astype(jnp.float32) for q in range(19)]
            flux = [0.0, 0.0, 0.0]
            density = f[0]
            for q in range(1, 19, 2):
                even, odd = f[q] + f[q + 1], f[q] - f[q + 1]
                density = density + even
                for dim in range(3):
                    sign = VELOCITIES[q][dim]
                    if sign:
                        flux[dim] = flux[dim] + odd if sign > 0 else flux[dim] - odd
            inverse = 1.0 / density
            for dim in range(3):
                speed = flux[dim] * inverse
                vel_ref[dim, z, at, :] = speed
                for k in range(HALO):
                    if half == 0:
                        rows[0, dim * HALO + k, pl.ds(z, 1), :] = speed[k : k + 1]
                    if half == width // 16 - 1:
                        rows[1, dim * HALO + k, pl.ds(z, 1), :] = speed[15 - k : 16 - k]
        return carry

    plane_loop(0, depth, plane, 0, 4)
    send_pair("cross", encode(rows[1]), encode(rows[0]), first, second)


def block_moments(populations):
    _, depth, width, lanes = populations.shape
    edge = full((3 * HALO, depth, lanes), jnp.int16)
    return pl.pallas_call(
        moments_kernel,
        out_shape=(full((3, depth, width, lanes), jnp.float32), edge, edge),
        in_specs=in_vmem(1),
        out_specs=tuple(in_vmem(3)),
        scratch_shapes=[pltpu.VMEM((2, 3 * HALO, depth, lanes), jnp.float32)],
        compiler_params=params(),
        cost_estimate=cost(1),
        name="moments",
    )(populations)


def decode_rows(first, second, rows):
    rows[0], rows[1] = below_above("cross", decode(first[...]), decode(second[...]))


def place_plane(ext, p, vel_ref, rows, z):
    width = vel_ref.shape[2]
    for dim in range(3):
        ext[dim, p, pl.ds(OWN, width), :] = vel_ref[dim, z]
        for k in range(HALO):
            line = pl.ds(z, 1)
            ext[dim, p, pl.ds(OWN - 1 - k, 1), :] = rows[0, dim * HALO + k, line, :]
            ext[dim, p, pl.ds(OWN + width + k, 1), :] = rows[1, dim * HALO + k, line, :]


TALL = 40


def edges_kernel(vel_ref, low_ref, high_ref, first, second, rows, planes):
    depth, width = vel_ref.shape[1:3]
    decode_rows(low_ref, high_ref, rows)
    coded = []
    for pair in ((0, 1), (depth - 1, depth - 2)):
        planes[...] = jnp.zeros_like(planes)
        for dim in range(3):
            for index, z in enumerate(pair):
                slot = 2 * dim + index
                planes[slot, pl.ds(HALO, width), :] = vel_ref[dim, z]
                for k in range(HALO):
                    line = pl.ds(z, 1)
                    planes[slot, pl.ds(HALO - 1 - k, 1), :] = rows[0, dim * HALO + k, line, :]
                    planes[slot, pl.ds(HALO + width + k, 1), :] = rows[1, dim * HALO + k, line, :]
        coded.append(encode(planes[...]))
    send_pair("span", coded[1], coded[0], first, second)


def edge_planes(vel, low, high):
    pair = full((6, TALL, LANES), jnp.int16)
    return pl.pallas_call(
        edges_kernel,
        out_shape=(pair, pair),
        in_specs=in_vmem(3),
        out_specs=tuple(in_vmem(2)),
        scratch_shapes=[
            pltpu.VMEM((2, 3 * HALO, vel.shape[1], LANES), jnp.float32),
            pltpu.VMEM((6, TALL, LANES), jnp.float32),
        ],
        compiler_params=params(),
        cost_estimate=cost(0.2),
        name="edges",
    )(vel, low, high)


def strain_parts(ref, p, row, before, here, after):
    grads = [
        (
            plus(here[dim]) - minus(here[dim]),
            ref[dim, p, pl.ds(row + 1, 8), :] - ref[dim, p, pl.ds(row - 1, 8), :],
            after[dim] - before[dim],
        )
        for dim in range(3)
    ]
    parts = [
        grads[0][0],
        grads[1][1],
        grads[2][2],
        grads[0][1] + grads[1][0],
        grads[0][2] + grads[2][0],
        grads[1][2] + grads[2][1],
    ]
    straight = parts[0] * parts[0] + parts[1] * parts[1] + parts[2] * parts[2]
    mixed = parts[3] * parts[3] + parts[4] * parts[4] + parts[5] * parts[5]
    return parts, jnp.sqrt(0.5 * straight + 0.25 * mixed)


def weigh(low, middle, high):
    return (low + high) + (middle + middle)


PAIRS = ((0, 0), (1, 1), (2, 2), (0, 1), (0, 2), (1, 2))


def three(ref, p, rows):
    return [ref[dim, p, rows, :] for dim in range(3)]


def model_sums(planes, ext, hat, zsum, zvel, acc_ref, store_mag):
    for row in CHUNKS:
        rows = pl.ds(row, 8)

        def first_pass(p, carry):
            before, here, lag, last = carry
            after = three(ext, p + 1, rows)
            parts, size = strain_parts(ext, p, row, before, here, after)
            store_mag(p, row, size)
            prods = [size * part for part in parts] + [here[i] * here[j] for i, j in PAIRS]
            for k in range(12):
                zsum[k, p - 1, rows, :] = lag[k] + prods[k]
            for dim in range(3):
                zvel[dim, p, rows, :] = weigh(before[dim], here[dim], after[dim])
            lag = [last[k] + (prods[k] + prods[k]) for k in range(12)]
            return here, after, lag, prods

        none = [jnp.zeros((8, LANES), jnp.float32)] * 12
        carry = (three(ext, 0, rows), three(ext, 1, rows), none, none)
        plane_loop(1, planes - 1, first_pass, carry, 14)

    def second_pass(p, carry):
        for row in CHUNKS:
            for dim in range(3):
                line = weigh(*[zvel[dim, p, pl.ds(row + shift, 8), :] for shift in (-1, 0, 1)])
                hat[dim, p, pl.ds(row, 8), :] = (1.0 / 64.0) * weigh(minus(line), line, plus(line))
        return carry

    plane_loop(1, planes - 1, second_pass, 0, 14)

    for row in CHUNKS:
        rows = pl.ds(row, 8)

        def third_pass(p, carry):
            before, here, lm, mm = carry
            after = three(hat, p + 1, rows)
            parts, size = strain_parts(hat, p, row, before, here, after)
            size = 256.0 * size
            scaled = [64.0 * speed for speed in here]
            squares = [0.0, 0.0]
            for k, (i, j) in enumerate(PAIRS):
                smooth = []
                for field in (k, 6 + k):
                    line = weigh(
                        *[zsum[field, p, pl.ds(row + shift, 8), :] for shift in (-1, 0, 1)]
                    )
                    smooth.append(weigh(minus(line), line, plus(line)))
                model = smooth[0] - size * parts[k]
                lm = lm + (smooth[1] - scaled[i] * here[j]) * model
                squares[k // 3] = squares[k // 3] + model * model
            return here, after, lm, mm + (squares[0] + 0.5 * squares[1])

        none = jnp.zeros((8, LANES), jnp.float32)
        carry = (three(hat, 1, rows), three(hat, 2, rows), none, none)
        _, _, lm, mm = plane_loop(2, planes - 2, third_pass, carry, 12)
        out = pl.ds(row - TOP, 8)
        acc_ref[0, out, :] += (1.0 / 4096.0) * lm
        acc_ref[1, out, :] += (1.0 / 4096.0) * mm


def inner_kernel(vel_ref, low_ref, high_ref, acc_ref, mag_ref, ext, hat, zsum, zvel, rows):
    depth = vel_ref.shape[1]
    decode_rows(low_ref, high_ref, rows)

    def assemble(p, carry):
        place_plane(ext, p, vel_ref, rows, p)
        return carry

    plane_loop(0, depth, assemble, 0, 4)
    acc_ref[...] = jnp.zeros_like(acc_ref)

    def store_mag(p, row, size):
        mag_ref[p - 1, pl.ds(row - TOP, 8), :] = size

    model_sums(depth, ext, hat, zsum, zvel, acc_ref, store_mag)


def model_scratch(planes, depth):
    return [
        pltpu.VMEM((3, planes, PAD, LANES), jnp.float32),
        pltpu.VMEM((3, planes, PAD, LANES), jnp.float32),
        pltpu.VMEM((12, planes, PAD, LANES), jnp.float32),
        pltpu.VMEM((3, planes, PAD, LANES), jnp.float32),
        pltpu.VMEM((2, 3 * HALO, depth, LANES), jnp.float32),
    ]


def inner_sums(vel, low, high):
    depth = vel.shape[1]
    return pl.pallas_call(
        inner_kernel,
        out_shape=(
            full((2, EXT, LANES), jnp.float32),
            full((depth - 2, EXT, LANES), jnp.float32),
        ),
        in_specs=in_vmem(3),
        out_specs=tuple(in_vmem(2)),
        scratch_shapes=model_scratch(depth, depth),
        compiler_params=params(),
        cost_estimate=cost(5),
        name="inner_sums",
    )(vel, low, high)


def outer_kernel(
    vel_ref,
    low_ref,
    high_ref,
    first_ref,
    second_ref,
    partial_ref,
    after_this,
    sums_ref,
    mag_ref,
    ext,
    hat,
    zsum,
    zvel,
    rows,
    acc,
):
    depth, width = vel_ref.shape[1:3]
    decode_rows(low_ref, high_ref, rows)
    acc[...] = partial_ref[...]
    below, above = below_above("span", decode(first_ref[...]), decode(second_ref[...]))
    for side, (message, places, start) in enumerate(
        ((below, (1, 0), 0), (above, (4, 5), depth - 4))
    ):
        for index in range(4):
            place_plane(ext, index + (2 if side == 0 else 0), vel_ref, rows, start + index)
        for dim in range(3):
            for index, p in enumerate(places):
                ext[dim, p, pl.ds(OWN - HALO, TALL), :] = message[2 * dim + index]

        def store_mag(p, row, size):
            mag_ref[4 * side + p - 1, pl.ds(row - TOP, 8), :] = size

        model_sums(6, ext, hat, zsum, zvel, acc, store_mag)
    lines = width + 2
    sums_ref[...] = jnp.zeros_like(sums_ref)
    for index in range(2):
        sums_ref[pl.ds(index * lines, lines), :] = acc[index, pl.ds(OWN - TOP - 1, lines), :]


def outer_sums(vel, low, high, below, above, partial, after_this):
    depth, width = vel.shape[1:3]
    return pl.pallas_call(
        outer_kernel,
        out_shape=(
            full((-(-2 * (width + 2) // 8) * 8, LANES), jnp.float32),
            full((8, EXT, LANES), jnp.float32),
        ),
        in_specs=in_vmem(6) + [pl.BlockSpec(memory_space=pl.ANY)],
        out_specs=tuple(in_vmem(2)),
        scratch_shapes=model_scratch(6, depth) + [pltpu.VMEM((2, EXT, LANES), jnp.float32)],
        compiler_params=params(),
        cost_estimate=cost(2),
        name="outer_sums",
    )(vel, low, high, below, above, partial, after_this)


def rows_kernel(pops, after_this, first, second, rows):
    depth, width = pops.shape[1:3]

    def plane(z, carry):
        for q in range(19):
            low = pops[q, z, pl.ds(0, 16), :].astype(jnp.float32)
            high = pops[q, z, pl.ds(width - 16, 16), :].astype(jnp.float32)
            rows[0, q, pl.ds(z, 1), :] = low[:1]
            rows[1, q, pl.ds(z, 1), :] = high[15:]
        return carry

    plane_loop(0, depth, plane, 0, 4)
    send_pair(
        "cross", rows[1].astype(jnp.bfloat16), rows[0].astype(jnp.bfloat16), first, second
    )


def face_rows(populations, after_this):
    _, depth, width, lanes = populations.shape
    edge = full((19, depth, lanes), jnp.bfloat16)
    return pl.pallas_call(
        rows_kernel,
        out_shape=(edge, edge),
        in_specs=in_vmem(1) + [pl.BlockSpec(memory_space=pl.ANY)],
        out_specs=tuple(in_vmem(2)),
        scratch_shapes=[pltpu.VMEM((2, 19, depth, lanes), jnp.float32)],
        compiler_params=params(),
        cost_estimate=cost(0.5),
        name="face_rows",
    )(populations, after_this)


def relax_parts(f):
    even = {q: f[q] + f[q + 1] for q in range(1, 19, 2)}
    odd = {q: f[q] - f[q + 1] for q in range(1, 19, 2)}
    x_xy, x_xz = odd[7] + odd[9], odd[11] + odd[13]
    y_yz, y_xy = odd[15] + odd[17], odd[7] - odd[9]
    z_xz, z_yz = odd[11] - odd[13], odd[15] - odd[17]
    flux, up, down, axis_odd = [], [], [], []
    for first, second, along in ((x_xy, x_xz, 1), (y_yz, y_xy, 3), (z_xz, z_yz, 5)):
        sides = first + second
        total = odd[along] + sides
        heat = 0.15 * (sides - (2.0 / 3.0) * total)
        twist = (1.98 / 8.0) * (first - second)
        flux.append(total)
        up.append(heat + twist)
        down.append(heat - twist)
        axis_odd.append(4.0 * heat)
    a, b, c = even[7] + even[9], even[11] + even[13], even[15] + even[17]
    axes = even[1] + even[3] + even[5]
    diagonals = a + b + c
    density = f[0] + axes + diagonals
    inverse = 1.0 / density
    speed = [total * inverse for total in flux]
    square = [total * part for total, part in zip(flux, speed)]
    energy = square[0] + square[1] + square[2]
    d_e = (1.19 / 126.0) * (diagonals - f[0] - energy)
    d_eps = (1.4 / 252.0) * (9.0 * f[0] - 7.0 * axes - 2.0 * diagonals + 5.5 * energy)
    ax_n, dg_n, eq_n = 3.0 * even[1] - axes, diagonals - 3.0 * c, 3.0 * square[0] - energy
    ax_w, dg_w, eq_w = even[3] - even[5], a - b, square[1] - square[2]
    d_pn = (1.4 / 72.0) * (dg_n - 2.0 * ax_n + 0.5 * eq_n)
    d_pw = (1.4 / 24.0) * (dg_w - 2.0 * ax_w + 0.5 * eq_w)
    shear = [
        (1.0 / 36.0) * (ax_n + dg_n - eq_n),
        (1.0 / 12.0) * (ax_w + dg_w - eq_w),
        0.25 * (even[7] - even[9] - flux[0] * speed[1]),
        0.25 * (even[11] - even[13] - flux[0] * speed[2]),
        0.25 * (even[15] - even[17] - flux[1] * speed[2]),
    ]
    base_axis = 11.0 * d_e + 4.0 * d_eps
    base_diag = -8.0 * d_e - d_eps
    base = [None] * 19
    base[0] = f[0] + (30.0 * d_e - 12.0 * d_eps)
    rest = base_axis - 2.0 * d_pn
    for q, change, skew in (
        (1, base_axis + 4.0 * d_pn, axis_odd[0]),
        (3, rest + 2.0 * d_pw, axis_odd[1]),
        (5, rest - 2.0 * d_pw, axis_odd[2]),
    ):
        base[q] = f[q] + (change + skew)
        base[q + 1] = f[q + 1] + (change - skew)
    rest = base_diag - d_pn
    for q, change, one, two in (
        (7, rest - d_pw, up[0], down[1]),
        (11, rest + d_pw, down[0], up[2]),
        (15, base_diag + 2.0 * d_pn, up[1], down[2]),
    ):
        same, other = one + two, one - two
        base[q] = f[q] + (change - same)
        base[q + 1] = f[q + 1] + (change + same)
        base[q + 2] = f[q + 2] + (change - other)
        base[q + 3] = f[q + 3] + (change + other)
    return base, shear


def shear_changes(shear, rate):
    n, w, xy, xz, yz = [rate * part for part in shear]
    lean = n + w
    tilt = n - w
    twice = n + n
    changes = [None] * 19
    changes[1] = changes[2] = -twice
    changes[3] = changes[4] = tilt
    changes[5] = changes[6] = lean
    changes[7] = changes[8] = -(lean + xy)
    changes[9] = changes[10] = xy - lean
    changes[11] = changes[12] = -(tilt + xz)
    changes[13] = changes[14] = xz - tilt
    changes[15] = changes[16] = twice - yz
    changes[17] = changes[18] = twice + yz
    return changes


def relax_rate(eddy, size):
    return 1.0 / (0.5 + 3.0 * (base_visc + eddy * size))


BEFORE = [q for q in range(19) if VELOCITIES[q][1] > 0]
AFTER = [q for q in range(19) if VELOCITIES[q][1] < 0]
RISING = [q for q in range(19) if VELOCITIES[q][2] > 0]
FALLING = [q for q in range(19) if VELOCITIES[q][2] < 0]
FIRST = 8


def ready_kernel(pops, first, second, after_this, base_ref, shear_ref, edge_ref, edge_shear):
    depth, width = pops.shape[1:3]
    rows = [
        below_above("cross", first[q].astype(jnp.float32), second[q].astype(jnp.float32))
        for q in range(19)
    ]
    for side, wanted in enumerate((BEFORE, AFTER)):
        base, shear = relax_parts([pair[side] for pair in rows])
        for index, q in enumerate(wanted):
            edge_ref[side, index] = base[q]
        for k in range(5):
            edge_shear[side, k] = shear[k]

    def plane(z, carry):
        for half in range(width // 16):
            rows = pl.ds(16 * half, 16)
            base, shear = relax_parts([pops[q, z, rows, :].astype(jnp.float32) for q in range(19)])
            for q in range(19):
                base_ref[q, z, rows, :] = base[q]
            for k in range(5):
                shear_ref[k, z, rows, :] = shear[k]
        return carry

    plane_loop(0, depth, plane, 0, 4)


def ready(populations, before, after, after_this):
    _, depth, width, lanes = populations.shape
    return pl.pallas_call(
        ready_kernel,
        out_shape=(
            full((19, depth, width, lanes), jnp.float32),
            full((5, depth, width, lanes), jnp.float32),
            full((2, 5, depth, lanes), jnp.float32),
            full((2, 5, depth, lanes), jnp.float32),
        ),
        in_specs=in_vmem(3) + [pl.BlockSpec(memory_space=pl.ANY)],
        out_specs=tuple(in_vmem(4)),
        compiler_params=params(),
        cost_estimate=cost(2.5),
        name="ready",
    )(populations, before, after, after_this)


PART_STEP = 1.0 / 11500.0
ACTING = (0, 1, 3, 4)


def leaving_kernel(pops, first, second, after_this, out_first, out_second, stage):
    depth, width = pops.shape[1:3]
    rows = [
        below_above("cross", first[q].astype(jnp.float32), second[q].astype(jnp.float32))
        for q in range(19)
    ]
    halo = [relax_parts([pair[side] for pair in rows]) for side in range(2)]
    coded = []
    for wanted, z in ((FALLING, 0), (RISING, depth - 1)):
        stage[...] = jnp.zeros_like(stage)
        for half in range(width // 16):
            at = pl.ds(16 * half, 16)
            base, shear = relax_parts([pops[q, z, at, :].astype(jnp.float32) for q in range(19)])
            for index, q in enumerate(wanted):
                stage[index, at, :] = base[q] - 0.5
            for index, k in enumerate(ACTING):
                stage[5 + index, at, :] = 2.0 * shear[k]
        for side, (base, shear) in enumerate(halo):
            at = pl.ds(width + side, 1)
            for index, q in enumerate(wanted):
                stage[index, at, :] = base[q][z : z + 1] - 0.5
            for index, k in enumerate(ACTING):
                stage[5 + index, at, :] = 2.0 * shear[k][z : z + 1]
        coded.append(
            jnp.round(stage[...] * (1.0 / PART_STEP)).astype(jnp.int32).astype(jnp.int16)
        )
    send_pair("span", coded[1], coded[0], out_first, out_second)


def leaving(populations, first, second, after_this):
    part = full((9, TALL, LANES), jnp.int16)
    return pl.pallas_call(
        leaving_kernel,
        out_shape=(part, part),
        in_specs=in_vmem(3) + [pl.BlockSpec(memory_space=pl.ANY)],
        out_specs=tuple(in_vmem(2)),
        scratch_shapes=[pltpu.VMEM((9, TALL, LANES), jnp.float32)],
        compiler_params=params(),
        cost_estimate=cost(0.5),
        name="leaving",
    )(populations, first, second, after_this)


def table_rows(table, at, low_at, flux):
    for dim in range(3):
        coarse, fine = split(flux[dim])
        table[at, dim * LANES : (dim + 1) * LANES] = coarse
        table[low_at, dim * LANES : (dim + 1) * LANES] = fine


def add_flux(flux, q, moved):
    for dim in range(3):
        sign = VELOCITIES[q][dim]
        if sign:
            flux[dim] = flux[dim] + moved if sign > 0 else flux[dim] - moved


def picks_kernel(cell_ref, weight_ref, after_this, pick_ref, mask_ref):
    taps, markers = cell_ref.shape
    cells_all = pick_ref.shape[0] // 2
    row_of = lax.broadcasted_iota(jnp.int32, (cells_all, markers), 0)
    lane_of = lax.broadcasted_iota(jnp.int32, (LANES, markers), 0)
    for tap in range(taps):
        cell = cell_ref[pl.ds(tap, 1), :]
        at = pl.ds(tap * markers, markers)
        hit = jnp.where(row_of == lax.shift_right_logical(cell, 7), 1.0, 0.0)
        hit = hit.astype(jnp.bfloat16)
        pick_ref[pl.ds(0, cells_all), at] = hit
        pick_ref[pl.ds(cells_all, cells_all), at] = hit
        lane = lax.bitwise_and(cell, LANES - 1)
        mask_ref[:, at] = jnp.where(lane_of == lane, -weight_ref[pl.ds(tap, 1), :], 0.0)


def marker_picks(cells, weights, after_this, rows):
    taps, markers = cells.shape
    return pl.pallas_call(
        picks_kernel,
        out_shape=(
            full((2 * rows, taps * markers), jnp.bfloat16),
            full((LANES, taps * markers), jnp.float32),
        ),
        in_specs=in_vmem(2) + [pl.BlockSpec(memory_space=pl.ANY)],
        out_specs=tuple(in_vmem(2)),
        compiler_params=params(),
        cost_estimate=cost(0.7),
        name="picks",
    )(cells, weights, after_this)


def marker_force(table, pick_ref, mask_ref, markers):
    picked = lax.dot_general(
        table[...],
        pick_ref[...],
        (((0,), (0,)), ((), ())),
        preferred_element_type=jnp.float32,
    )
    force = [0.0, 0.0, 0.0]
    for start in range(0, pick_ref.shape[1], markers):
        at = slice(start, start + markers)
        mask = mask_ref[:, pl.ds(start, markers)]
        for dim in range(3):
            force[dim] = force[dim] + picked[dim * LANES : (dim + 1) * LANES, at] * mask
    return [jnp.sum(part, axis=0, keepdims=True) for part in force]


def step_kernel(
    base_ref,
    shear_ref,
    edge_ref,
    edge_shear,
    sums_ref,
    mag_in_ref,
    mag_out_ref,
    pick_ref,
    mask_ref,
    segment_ref,
    part_first,
    part_second,
    next_hbm,
    eddy_ref,
    partial_ref,
    post,
    nexts,
    table,
    arrived,
    eddy,
    line,
    out_sems,
):
    depth, width = shear_ref.shape[1:3]
    lines = width + 2
    part = depth // 4
    eddy[...] = jnp.zeros_like(eddy)
    eddy[pl.ds(OWN - TOP - 1, lines), :] = jnp.maximum(
        sums_ref[pl.ds(0, lines), :] / (sums_ref[pl.ds(lines, lines), :] + eps_sum), 0.0
    )
    eddy_ref[...] = eddy[pl.ds(OWN - TOP, width), :]

    for side, (wanted, row, place) in enumerate(
        ((BEFORE, OWN - TOP - 1, FIRST - 1), (AFTER, OWN - TOP + width, FIRST + width))
    ):
        for z in range(depth):
            if z == 0:
                size = mag_out_ref[1, pl.ds(row, 1), :]
            elif z == depth - 1:
                size = mag_out_ref[6, pl.ds(row, 1), :]
            else:
                size = mag_in_ref[z - 1, pl.ds(row, 1), :]
            line[pl.ds(z, 1), :] = size
        rate = relax_rate(eddy[pl.ds(row, 1), :], line[...])
        changes = shear_changes([edge_shear[side, k] for k in range(5)], rate)
        for index, q in enumerate(wanted):
            out = edge_ref[side, index] + changes[q]
            for z in range(depth):
                post[q, z + 1, pl.ds(place, 1), :] = out[z : z + 1]

    parts = [
        message[...].astype(jnp.int32).astype(jnp.float32) for message in (part_first, part_second)
    ]
    arrived[0], arrived[1] = below_above("span", *parts)
    for side, (wanted, p, slot) in enumerate(((RISING, 0, 0), (FALLING, depth + 1, 7))):
        pieces = [(16 * half, 16, OWN - TOP + 16 * half, FIRST + 16 * half, wanted) for half in range(width // 16)]
        pieces.append((width, 1, OWN - TOP - 1, FIRST - 1, BEFORE))
        pieces.append((width + 1, 1, OWN - TOP + width, FIRST + width, AFTER))
        for start, count, around, place, needed in pieces:
            at, around = pl.ds(start, count), pl.ds(around, count)
            rate = relax_rate(eddy[around, :], mag_out_ref[slot, around, :])
            n, w, xz, yz = [arrived[side, 5 + k, at, :] * (0.5 * PART_STEP) for k in range(4)]
            changes = shear_changes([n, w, jnp.zeros_like(n), xz, yz], rate)
            for index, q in enumerate(wanted):
                if q in needed:
                    value = (arrived[side, index, at, :] * PART_STEP + 0.5) + changes[q]
                    post[q, p, pl.ds(place, count), :] = value

    def collide(z, size_ref, at):
        for half in range(width // 16):
            rows = pl.ds(16 * half, 16)
            around = pl.ds(OWN - TOP + 16 * half, 16)
            rate = relax_rate(eddy[around, :], size_ref[at, around, :])
            changes = shear_changes([shear_ref[k, z, rows, :] for k in range(5)], rate)
            for q in range(19):
                value = base_ref[q, z, rows, :]
                if q:
                    value = value + changes[q]
                post[q, z + 1, pl.ds(FIRST + 16 * half, 16), :] = value

    def inner(z, carry):
        collide(z, mag_in_ref, z - 1)
        return carry

    collide(0, mag_out_ref, 1)
    collide(depth - 1, mag_out_ref, 6)
    plane_loop(1, depth - 1, inner, 0, 7)

    def shifted(q, z, half):
        shift_x, shift_y, _ = VELOCITIES[q]
        piece = post[q, z + 1, pl.ds(FIRST + 16 * half - shift_y, 16), :]
        if shift_x:
            piece = minus(piece) if shift_x > 0 else plus(piece)
        return piece.astype(jnp.bfloat16)

    def run(z, carry):
        for half in range(width // 16):
            flux = [0.0, 0.0, 0.0]
            for q in range(19):
                moved = shifted(q, z - VELOCITIES[q][2], half)
                nexts[q, z, pl.ds(16 * half, 16), :] = moved
                if q:
                    add_flux(flux, q, moved.astype(jnp.float32))
            row = pl.multiple_of(z * width + 16 * half, 16)
            low_row = pl.multiple_of((depth + z) * width + 16 * half, 16)
            table_rows(table, pl.ds(row, 16), pl.ds(low_row, 16), flux)
        return carry

    outs = []
    for index in range(4):
        start, stop = index * part, (index + 1) * part
        plane_loop(start, stop, run, 0, 4)
        place = pl.ds(index * part, part)
        outs.append(
            pltpu.make_async_copy(nexts.at[:, place], next_hbm.at[:, place], out_sems.at[index])
        )
        outs[-1].start()

    owners = partial_ref.shape[0]
    markers = segment_ref.shape[1]
    force = marker_force(table, pick_ref, mask_ref, markers)

    owner_of = lax.broadcasted_iota(jnp.int32, (owners, markers), 0)
    place_of = lax.broadcasted_iota(jnp.int32, (SEG_DEV, markers), 0)
    segment = segment_ref[...]
    mine = jnp.where(owner_of == lax.shift_right_logical(segment, 3), 1.0, 0.0)
    mine = mine.astype(jnp.bfloat16)
    place = place_of == lax.bitwise_and(segment, SEG_DEV - 1)
    rest = [jnp.where(place, part, 0.0) for part in force]
    rest.append(jnp.zeros((LANES - 3 * SEG_DEV, markers), jnp.float32))
    rest = jnp.concatenate(rest, axis=0)
    totals = 0.0
    for _ in range(3):
        coarse = rest.astype(jnp.bfloat16)
        rest = rest - coarse.astype(jnp.float32)
        totals = totals + lax.dot_general(
            mine, coarse, (((1,), (1,)), ((), ())), preferred_element_type=jnp.float32
        )
    partial_ref[:, 0, :] = totals
    for copy in outs:
        copy.wait()


def step(parts, sums, mag_in, mag_out, picks, segments, messages, owners):
    _, depth, width, lanes = parts[0].shape
    return pl.pallas_call(
        step_kernel,
        out_shape=(
            full((19, depth, width, lanes), jnp.bfloat16),
            full((width, lanes), jnp.float32),
            full((owners, 1, lanes), jnp.float32),
        ),
        in_specs=in_vmem(12),
        out_specs=(pl.BlockSpec(memory_space=pl.ANY),) + tuple(in_vmem(2)),
        scratch_shapes=[
            pltpu.VMEM((19, depth + 2, FIRST + width + 8, lanes), jnp.float32),
            pltpu.VMEM((19, depth, width, lanes), jnp.bfloat16),
            pltpu.VMEM((2 * depth * width, 3 * lanes), jnp.bfloat16),
            pltpu.VMEM((2, 9, TALL, lanes), jnp.float32),
            pltpu.VMEM((EXT, lanes), jnp.float32),
            pltpu.VMEM((depth, lanes), jnp.float32),
            pltpu.SemaphoreType.DMA((4,)),
        ],
        compiler_params=params(),
        cost_estimate=cost(5),
        name="step",
    )(*parts, sums, mag_in, mag_out, *picks, segments, *messages)


def local(populations, cell_index, marker_weight, segment_id):
    owners = lax.axis_size("span") * lax.axis_size("cross")
    cells, weights, segments = cell_index.T, marker_weight.T, segment_id[None, :]
    vel, *lines = block_moments(populations)
    lines = swap(*lines, "cross")
    planes = swap(*edge_planes(vel, *lines), "span")
    partial, mag_in = inner_sums(vel, *lines)
    faces = face_rows(populations, partial)
    sums, mag_out = outer_sums(vel, *lines, *planes, partial, faces[0])
    faces = swap(*faces, "cross")
    parts = ready(populations, *faces, sums)
    flat_rows = populations.shape[1] * populations.shape[2]
    count = lax.axis_size("span")
    if count & (count - 1):
        arriving = swap(*leaving(populations, *faces, sums), "span")
        picks = marker_picks(cells, weights, sums, flat_rows)
        sums = lax.psum(sums, "span")
    else:
        distance = 1
        messages = leaving(populations, *faces, sums)
        while distance < count:
            pairs = [(i, i ^ distance) for i in range(count)]
            other = lax.ppermute(sums, "span", pairs)
            if distance == 1:
                arriving = swap(*messages, "span")
                sums, _ = lax.optimization_barrier((sums + other, messages))
                picks = marker_picks(cells, weights, sums, flat_rows)
            elif distance == 2:
                sums, picks = lax.optimization_barrier((sums + other, picks))
            else:
                sums = sums + other
            distance *= 2
    populations_next, eddy_coeff, packed = step(
        parts, sums, mag_in, mag_out, picks, segments, arriving, owners
    )
    arrived = lax.all_to_all(packed, ("span", "cross"), 0, 0)
    forces = jnp.sum(arrived, axis=(0, 1))[: 3 * SEG_DEV].reshape(3, SEG_DEV)
    return (populations_next, eddy_coeff, forces)


def solution(mesh):
    in_specs = (
        P(None, "span", "cross", None),
        P(("span", "cross"), None),
        P(("span", "cross"), None),
        P(("span", "cross")),
    )
    out_specs = (P(None, "span", "cross", None), P("cross", None), P(None, ("span", "cross")))
    return jax.shard_map(local, mesh=mesh, in_specs=in_specs, out_specs=out_specs, check_vma=False)
```
